32 devices in a mesh: dp: 8 (over z, x), tile: 4 (over y, core).
Axes of the slice: x: 2, y: 2, z: 4, core: 2. Of those that a mesh axis runs over, the one named last changes fastest.
Arguments:
- patches: bfloat16 [256, 4, 7, 7, 320], P('dp', 'tile'), may hold values from -41 to 41
- conv_kernel: float32 [2, 3, 3, 320], replicated, may hold values from -1.5 to 1.5
- batch_gain: float32 [2, 320], replicated, may hold values from 0.5 to 1.5
- batch_shift: float32 [2, 320], replicated, may hold values from -3 to 3
- mix_width: bfloat16 [2, 14, 14], replicated, may hold values from -1.5 to 1.5
- mix_width_bias: float32 [2, 14], replicated, may hold values from -3 to 3
- mix_height: bfloat16 [2, 14, 14], replicated, may hold values from -1.5 to 1.5
- mix_height_bias: float32 [2, 14], replicated, may hold values from -3 to 3
- unite_weight: bfloat16 [2, 960, 320], replicated, may hold values from -0.1875 to 0.1875
- unite_bias: float32 [2, 320], replicated, may hold values from -2 to 2
- norm_gain: float32 [2, 320], replicated, may hold values from 0.5 to 1.5
- norm_shift: float32 [2, 320], replicated, may hold values from -2 to 2
- up_weight: bfloat16 [2, 320, 1280], replicated, may hold values from -0.3125 to 0.3125
- up_bias: float32 [2, 1280], replicated, may hold values from -2 to 2
- down_weight: bfloat16 [2, 1280, 320], replicated, may hold values from -0.15625 to 0.15625
- down_bias: float32 [2, 320], replicated, may hold values from -2 to 2
- cotangent: bfloat16 [256, 4, 7, 7, 320], P('dp', 'tile'), may hold values from -35 to 35
Outputs:
- features_out: bfloat16 [256, 4, 7, 7, 320], P('dp', 'tile')
- patches_grad: bfloat16 [256, 4, 7, 7, 320], P('dp', 'tile')
- conv_kernel_grad: float32 [2, 3, 3, 320], replicated
- batch_gain_grad: float32 [2, 320], replicated
- batch_shift_grad: float32 [2, 320], replicated
- mix_width_grad: float32 [2, 14, 14], replicated
- mix_width_bias_grad: float32 [2, 14], replicated
- mix_height_grad: float32 [2, 14, 14], replicated
- mix_height_bias_grad: float32 [2, 14], replicated
- unite_weight_grad: float32 [2, 960, 320], replicated
- unite_bias_grad: float32 [2, 320], replicated
- norm_gain_grad: float32 [2, 320], replicated
- norm_shift_grad: float32 [2, 320], replicated
- up_weight_grad: float32 [2, 320, 1280], replicated
- up_bias_grad: float32 [2, 1280], replicated
- down_weight_grad: float32 [2, 1280, 320], replicated
- down_bias_grad: float32 [2, 320], replicated
The draws below stay inside these ranges and needn't reach their ends.
All inputs are finite; a program needn't handle non-finite values.
Results may differ from the reference program's by a relative error of at most 0.0085.
Values may be sent and summed in bfloat16 or wider, within the bound.
No kernel may reach another device: no remote copies, remote signals or barrier semaphores. Data moves between devices by JAX's collectives and lax.ppermute only.
A program may use at most 192 MiB of HBM per device.

```python
import math
import jax
import jax.numpy as jnp
from jax import lax

C = 320
HID = 1280
IMG_DEV = 32
LAYERS = 2
TSIDE = 7
GRID = 2
MAP = 14
TILES = 4
IMAGES = 256
N_DP = 8


def scaled_field(key, random_part, row_low, row_high, offset_size):
    images = random_part.shape[0]
    chan_key = jax.random.fold_in(key, 11)
    offset_key = jax.random.fold_in(key, 12)
    position_ramp = jnp.arange(images, dtype=jnp.float32) / max(images - 1, 1)
    row_scale = row_low * jnp.exp(position_ramp * math.log(row_high / row_low))
    channel_scale = jnp.exp(jax.random.uniform(chan_key, (random_part.shape[-1],), jnp.float32, math.log(0.3), math.log(3.0)))
    channel_offset = jax.random.uniform(offset_key, (random_part.shape[-1],), jnp.float32, -1.0, 1.0) * offset_size
    return row_scale[:, None, None, None, None] * channel_scale * (random_part + channel_offset)


def draw_patches(key, part):
    key = jax.random.fold_in(key, 3)
    noise_key = jax.random.fold_in(key, 1)
    field_dims = (IMAGES, TILES, TSIDE, TSIDE, C)
    random_part = jnp.clip(jax.random.normal(noise_key, field_dims, jnp.float32), -3.5, 3.5)
    result = scaled_field(key, random_part, 0.3, 3.0, 1.0)
    return result.astype(jnp.bfloat16)


def draw_cotangent(key, part):
    key = jax.random.fold_in(key, 5)
    noise_key = jax.random.fold_in(key, 1)
    field_dims = (IMAGES, TILES, TSIDE, TSIDE, C)
    random_part = jnp.clip(jax.random.normal(noise_key, field_dims, jnp.float32), -3.5, 3.5)
    result = scaled_field(key, random_part, 0.3, 3.0, 0.3)
    return result.astype(jnp.bfloat16)


def scatter_about(stream_key, dims, width, limit, kind=jnp.bfloat16):
    values = width * jax.random.normal(stream_key, dims, jnp.float32)
    return jnp.clip(values, min=-limit, max=limit).astype(kind)


def setup_inputs(seed: int = 0) -> dict:
    streams_of = jax.random.split(jax.random.key(seed), 18)
    return {
        "patches": draw_patches(jax.random.fold_in(streams_of[17], 71), 0),
        "conv_kernel": scatter_about(streams_of[1], (LAYERS, 3, 3, C), 0.33, 1.5, jnp.float32),
        "batch_gain": jnp.clip(1.0 + 0.1 * jax.random.normal(streams_of[2], (LAYERS, C), jnp.float32), 0.5, 1.5),
        "batch_shift": scatter_about(streams_of[3], (LAYERS, C), 0.5, 3.0, jnp.float32),
        "mix_width": scatter_about(streams_of[4], (LAYERS, MAP, MAP), MAP ** -0.5, 1.5),
        "mix_width_bias": scatter_about(streams_of[5], (LAYERS, MAP), 0.5, 3.0, jnp.float32),
        "mix_height": scatter_about(streams_of[6], (LAYERS, MAP, MAP), MAP ** -0.5, 1.5),
        "mix_height_bias": scatter_about(streams_of[7], (LAYERS, MAP), 0.5, 3.0, jnp.float32),
        "unite_weight": scatter_about(streams_of[8], (LAYERS, 3 * C, C), (3 * C) ** -0.5, 0.1875),
        "unite_bias": scatter_about(streams_of[9], (LAYERS, C), 0.3, 2.0, jnp.float32),
        "norm_gain": jnp.clip(1.0 + 0.1 * jax.random.normal(streams_of[10], (LAYERS, C), jnp.float32), 0.5, 1.5),
        "norm_shift": scatter_about(streams_of[11], (LAYERS, C), 0.3, 2.0, jnp.float32),
        "up_weight": scatter_about(streams_of[12], (LAYERS, C, HID), C ** -0.5, 0.3125),
        "up_bias": scatter_about(streams_of[13], (LAYERS, HID), 0.3, 2.0, jnp.float32),
        "down_weight": scatter_about(streams_of[14], (LAYERS, HID, C), HID ** -0.5, 0.15625),
        "down_bias": scatter_about(streams_of[15], (LAYERS, C), 0.3, 2.0, jnp.float32),
        "cotangent": draw_cotangent(jax.random.fold_in(streams_of[17], 71), 0),
    }


@jax.custom_vjp
def low(v):
    return lax.optimization_barrier(v.astype(jnp.bfloat16)).astype(jnp.float32)

@jax.custom_vjp
def low_back(v):
    return v

def low_keep(v):
    return (low(v), None)

def low_pass(kept, grad):
    return (grad,)

def back_keep(v):
    return (v, None)

def back_low(kept, grad):
    return (low(grad),)
low.defvjp(low_keep, low_pass)
low_back.defvjp(back_keep, back_low)
highest = lax.Precision.HIGHEST
norm_epsilon = 1e-05
layer_epsilon = 1e-06

def to_maps(tiles):
    images = tiles.shape[0]
    channels = tiles.shape[4]
    layout = tiles.reshape(images, GRID, GRID, TSIDE, TSIDE, channels)
    return layout.transpose(0, 1, 3, 2, 4, 5).reshape(images, GRID * TSIDE, GRID * TSIDE, channels)

def to_tiles(maps):
    images = maps.shape[0]
    channels = maps.shape[3]
    layout = maps.reshape(images, GRID, TSIDE, GRID, TSIDE, channels)
    return layout.transpose(0, 1, 3, 2, 4, 5).reshape(images, GRID * GRID, TSIDE, TSIDE, channels)

def depthwise(padded, kernel):
    height = padded.shape[1] - 2
    breadth = padded.shape[2] - 2
    result = jnp.zeros((padded.shape[0], height, breadth, padded.shape[3]), jnp.float32)
    for offset_row in range(3):
        for offset_col in range(3):
            result = result + padded[:, offset_row:offset_row + height, offset_col:offset_col + breadth, :] * kernel[offset_row, offset_col]
    return result

def one_layer(stream, params):
    kernel, batch_gain, batch_shift, width_mix, width_bias, height_mix, height_bias, unite_matrix, unite_offset, layer_gain, layer_shift, up_matrix, up_offset, down_matrix, down_offset = params
    rounded = low(stream)
    padded = jnp.pad(rounded, ((0, 0), (0, 0), (1, 1), (1, 1), (0, 0)))
    conved = lax.map(jax.checkpoint(lambda blocked: depthwise(blocked, kernel)), padded)
    average = lax.optimization_barrier(jnp.mean(conved, axis=(0, 1, 2, 3)))
    variance = lax.optimization_barrier(jnp.mean(jnp.square(conved - average), axis=(0, 1, 2, 3)))
    scaled = lax.rsqrt(variance + norm_epsilon)
    normed = (conved - average) * scaled * batch_gain + batch_shift

    def branch(inputs):
        residual, normal_part = inputs
        rounded_norm = low(normal_part)
        along_width = jnp.einsum('bhwc,vw->bhvc', rounded_norm, width_mix, precision=highest) + width_bias[None, None, :, None]
        along_height = jnp.einsum('bhwc,vh->bvwc', rounded_norm, height_mix, precision=highest) + height_bias[None, :, None, None]
        along_width = low(low_back(along_width))
        along_height = low(low_back(along_height))
        joined = jnp.concatenate([rounded_norm, along_width, along_height], axis=-1)
        united = low_back(jnp.einsum('bhwk,kc->bhwc', joined, unite_matrix, precision=highest) + unite_offset)
        middle = residual + united
        centre = lax.optimization_barrier(jnp.mean(middle, axis=-1, keepdims=True))
        spread = lax.optimization_barrier(jnp.mean(jnp.square(middle - centre), axis=-1, keepdims=True))
        normal_tokens = (middle - centre) * lax.rsqrt(spread + layer_epsilon) * layer_gain + layer_shift
        hidden = low_back(jnp.einsum('bhwc,cf->bhwf', low(normal_tokens), up_matrix, precision=highest) + up_offset)
        active = low(jax.nn.gelu(hidden, approximate=False))
        return middle + low_back(jnp.einsum('bhwf,fc->bhwc', active, down_matrix, precision=highest) + down_offset)
    return lax.map(jax.checkpoint(branch), (stream, normed))

def forward(start, params):
    stream = to_maps(start).reshape(N_DP, IMG_DEV, MAP, MAP, C)
    for layer_index in range(LAYERS):
        stream = one_layer(stream, tuple((weight[layer_index] for weight in params)))
    return stream

def reference(patches, conv_kernel, batch_gain, batch_shift, mix_width, mix_width_bias, mix_height, mix_height_bias, unite_weight, unite_bias, norm_gain, norm_shift, up_weight, up_bias, down_weight, down_bias, cotangent):
    params = tuple((weight.astype(jnp.float32) for weight in (conv_kernel, batch_gain, batch_shift, mix_width, mix_width_bias, mix_height, mix_height_bias, unite_weight, unite_bias, norm_gain, norm_shift, up_weight, up_bias, down_weight, down_bias)))
    start = patches.astype(jnp.float32)
    output, pullback = jax.vjp(forward, start, params)
    seed_grad = to_maps(cotangent.astype(jnp.float32)).reshape(output.shape)
    start_grad, param_grads = pullback(seed_grad)
    features_out = to_tiles(output.reshape(-1, MAP, MAP, C)).astype(jnp.bfloat16)
    return (features_out, start_grad.astype(jnp.bfloat16), param_grads[0], param_grads[1], param_grads[2], param_grads[3], param_grads[4], param_grads[5], param_grads[6], param_grads[7], param_grads[8], param_grads[9], param_grads[10], param_grads[11], param_grads[12], param_grads[13], param_grads[14])
```

```python
import jax
import jax.numpy as jnp
from jax import lax
from jax.experimental import pallas as pl
from jax.experimental.pallas import tpu as pltpu
from jax.sharding import PartitionSpec as P

F32 = jnp.float32
BF16 = jnp.bfloat16
norm_epsilon = 1e-05
layer_epsilon = 1e-06
ROOT_HALF = 0.7071067811865476
INV_ROOT_TAU = 0.3989422804014327
LOG2E = 1.4426950408889634

TS = 7
MAP = 14
IMG = 8
ROW = MAP * IMG
PIECE = TS * TS * IMG
VMEM_BYTES = 58 * 1024 * 1024
BLK = 256


def partner(x, axis, distance):
    count = lax.axis_size(axis)
    return lax.ppermute(x, axis, [(i, i ^ distance) for i in range(count)])


def stages():
    result = [("tile", (1, 2, 3))]
    count = lax.axis_size("dp")
    step = 1
    if count > 1 and (count.bit_length() - 1) % 2 == 1:
        result.append(("dp", (1,)))
        step = 2
    while step < count:
        result.append(("dp", (step, 2 * step, 3 * step)))
        step *= 4
    return result


def total_sum(x):
    for axis, distances in stages():
        got = [partner(x, axis, d) for d in distances]
        if len(got) == 1:
            x = x + got[0]
        else:
            x = (x + got[0]) + (got[1] + got[2])
    return x


def total_moments(stats, count):
    for axis, distances in stages():
        parts = [stats] + [partner(stats, axis, d) for d in distances]
        if len(parts) == 2:
            mean = (parts[0][0] + parts[1][0]) * 0.5
            dev = [jnp.square(p[0] - mean) for p in parts]
            square = (parts[0][1] + parts[1][1]) + count * (dev[0] + dev[1])
        else:
            mean = ((parts[0][0] + parts[1][0]) + (parts[2][0] + parts[3][0])) * 0.25
            dev = [jnp.square(p[0] - mean) for p in parts]
            square = ((parts[0][1] + parts[1][1]) + (parts[2][1] + parts[3][1])) + count * (
                (dev[0] + dev[1]) + (dev[2] + dev[3])
            )
        count = count * len(parts)
        stats = jnp.stack([mean, square])
    return stats


def to_whole(field, tile):
    share = field.shape[2] // lax.axis_size("tile")
    pieces = []
    for k in range(4):
        part = lax.dynamic_slice_in_dim(field, (tile ^ k) * share, share, 2)
        part = part.reshape(TS * TS * share, field.shape[3])
        pieces.append(part if k == 0 else partner(part, "tile", k))
    return pieces


def to_tiled(pieces, tile):
    channels = pieces[0].shape[-1]
    share = pieces[0].shape[0] // (TS * TS)
    result = jnp.zeros((TS, TS, share * lax.axis_size("tile"), channels), pieces[0].dtype)
    for k in range(4):
        part = pieces[k] if k == 0 else partner(pieces[k], "tile", k)
        part = part.reshape(TS, TS, share, channels)
        result = lax.dynamic_update_slice_in_dim(result, part, (tile ^ k) * share, 2)
    return result


def halving_plan():
    count = lax.axis_size("dp")
    far = [("dp", 1 << b) for b in range(1, count.bit_length() - 1)]
    first = [("tile", 2)] + ([("dp", 1)] if count > 1 else [])
    return [first + far, first[::-1] + far]


def bit_of(axis, distance):
    return (lax.axis_index(axis) & distance) != 0


def halve(x, axis, distance):
    rows = x.shape[0] // 2
    high = bit_of(axis, distance)
    low_part, high_part = x[:rows], x[rows:]
    mine = jnp.where(high, high_part, low_part)
    sent = jnp.where(high, low_part, high_part)
    got = partner(sent, axis, distance)
    return (mine.astype(F32) + got.astype(F32)).astype(BF16)


def double(x, axis, distance):
    got = partner(x, axis, distance)
    high = bit_of(axis, distance)
    return jnp.concatenate([jnp.where(high, got, x), jnp.where(high, x, got)], 0)


def sum_gradients(buffer):
    half = halve(buffer, "tile", 1)
    cut = 512
    sides = [half[:, :cut], half[:, cut:]]
    done = []
    for side, plan in zip(sides, halving_plan()):
        for axis, distance in plan:
            side = halve(side, axis, distance)
        for axis, distance in reversed(plan):
            side = double(side, axis, distance)
        done.append(side)
    return double(jnp.concatenate(done, 1), "tile", 1)


def dot(a, b):
    return lax.dot_general(a, b, (((1,), (0,)), ((), ())), preferred_element_type=F32)


def dot_nt(a, b):
    return lax.dot_general(a, b, (((1,), (1,)), ((), ())), preferred_element_type=F32)


def dot_tn(a, b):
    return lax.dot_general(a, b, (((0,), (0,)), ((), ())), preferred_element_type=F32)


def spread(matrix, repeat):
    size = MAP * repeat
    shift = repeat.bit_length() - 1
    row = lax.broadcasted_iota(jnp.int32, (size, MAP), 0)
    col = lax.broadcasted_iota(jnp.int32, (size, MAP), 1)
    pick = jnp.where((row >> shift) == col, 1.0, 0.0).astype(BF16)
    wide = dot_nt(dot(pick, matrix).astype(BF16), pick)
    row = lax.broadcasted_iota(jnp.int32, (size, size), 0)
    col = lax.broadcasted_iota(jnp.int32, (size, size), 1)
    return jnp.where((row & (repeat - 1)) == (col & (repeat - 1)), wide, 0.0).astype(BF16)


def collapse(product, repeat):
    size = MAP * repeat
    shift = repeat.bit_length() - 1
    row = lax.broadcasted_iota(jnp.int32, (size, size), 0)
    col = lax.broadcasted_iota(jnp.int32, (size, size), 1)
    kept = jnp.where((row & (repeat - 1)) == (col & (repeat - 1)), product, 0.0)
    kept = jnp.sum(kept.reshape(MAP, repeat, size), axis=1)
    row = lax.broadcasted_iota(jnp.int32, (size, MAP), 0)
    col = lax.broadcasted_iota(jnp.int32, (size, MAP), 1)
    pick = jnp.where((row >> shift) == col, 1.0, 0.0).astype(F32)
    return lax.dot_general(
        kept, pick, (((1,), (0,)), ((), ())), preferred_element_type=F32, precision=lax.Precision.HIGHEST
    )


def lane_groups(channels):
    return [(lo, min(lo + 128, channels)) for lo in range(0, channels, 128)]


def zero_border(pad):
    shape = pad.shape
    pad[0] = jnp.zeros(shape[1:], F32)
    pad[MAP + 1] = jnp.zeros(shape[1:], F32)
    for h in range(1, MAP + 1):
        pad[h, 0] = jnp.zeros(shape[2:], F32)
        pad[h, MAP + 1] = jnp.zeros(shape[2:], F32)


def corner(tile, k):
    other = tile ^ k
    return (other >> 1) * TS, (other & 1) * TS


def conv_rows(pad, kernel_ref, layer, out_ref, stats_ref, sums):
    channels = pad.shape[-1]
    sums[...] = jnp.zeros(sums.shape, F32)

    def body(h, carry):
        for lo, hi in lane_groups(channels):
            acc = None
            for r in range(3):
                for s in range(3):
                    term = pad[h + r, s : s + MAP, :, lo:hi] * kernel_ref[r, s, layer : layer + 1, lo:hi]
                    acc = term if acc is None else acc + term
            out_ref[h, :, lo:hi] = acc.reshape(ROW, hi - lo)
            sums[0, :, lo:hi] += jnp.sum(acc, axis=0)
        return carry

    lax.fori_loop(0, MAP, body, 0)
    count = MAP * ROW
    mean = jnp.sum(sums[0], axis=0, keepdims=True) * (1.0 / count)

    def again(h, carry):
        for lo, hi in lane_groups(channels):
            dev = out_ref[h, :, lo:hi] - mean[:, lo:hi]
            sums[1, :, lo:hi] += jnp.sum((dev * dev).reshape(MAP, IMG, hi - lo), axis=0)
        return carry

    lax.fori_loop(0, MAP, again, 0)
    stats_ref[0:1] = mean
    stats_ref[1:2] = jnp.sum(sums[1], axis=0, keepdims=True)


def kernel_first(tile_ref, p0, p1, p2, p3, kernel_ref, x_ref, a_ref, stats_ref, pad, sums):
    tile = tile_ref[0]
    zero_border(pad)
    for k, piece in enumerate((p0, p1, p2, p3)):
        h0, w0 = corner(tile, k)
        value = piece[...].astype(F32).reshape(TS, TS, IMG, -1)
        pad[pl.ds(1 + h0, TS), pl.ds(1 + w0, TS)] = value

    def body(h, carry):
        x_ref[h] = pad[h + 1, 1 : MAP + 1].reshape(ROW, -1).astype(BF16)
        return carry

    lax.fori_loop(0, MAP, body, 0)
    conv_rows(pad, kernel_ref, 0, a_ref, stats_ref, sums)


def scale_of(stats_ref, cells):
    mean = stats_ref[0:1]
    return mean, lax.rsqrt(stats_ref[1:2] * (1.0 / cells) + norm_epsilon)


def mix_forward(layer, cells, a_ref, stats_ref, gain_ref, shift_ref, mw_ref, mwb_ref, mh_ref, mhb_ref, nb, pw, ph):
    mean, rstd = scale_of(stats_ref, cells)
    gain = gain_ref[layer : layer + 1]
    shift = shift_ref[layer : layer + 1]
    width = spread(mw_ref[layer], IMG)
    height = spread(mh_ref[layer], 16)

    def body(h, carry):
        value = (((a_ref[h] - mean) * rstd) * gain + shift).astype(BF16)
        nb[h] = value
        pw[h] = (dot(width, value) + mwb_ref[layer]).astype(BF16)
        return carry

    lax.fori_loop(0, MAP, body, 0)
    for j in range(ROW // 16):
        value = nb[:, 16 * j : 16 * j + 16, :].reshape(MAP * 16, -1)
        mixed = (dot(height, value) + mhb_ref[layer]).astype(BF16)
        ph[:, 16 * j : 16 * j + 16, :] = mixed.reshape(MAP, 16, -1)


def gelu_pair(v):
    t = 1.0 / (1.0 + (0.3275911 * ROOT_HALF) * jnp.abs(v))
    e = jnp.exp2(v * v * (-0.5 * LOG2E))
    q = ((((0.5 * 1.061405429 * t - 0.5 * 1.453152027) * t + 0.5 * 1.421413741) * t - 0.5 * 0.284496736) * t + 0.5 * 0.254829592) * t * e
    phi = jnp.where(v >= 0, 1.0 - q, q)
    return v * phi, phi + v * e * INV_ROOT_TAU


def chunk_rows(ref, c):
    value = ref[pl.ds(2 * c, 2)]
    return value.reshape(2 * ROW, value.shape[-1])


def put_rows(ref, c, value):
    ref[pl.ds(2 * c, 2)] = value.reshape(2, ROW, value.shape[-1])


def mlp_forward(layer, c, residual, nb, pw, ph, unite_ref, unite_b, ng, ns, up_ref, up_b, down_ref, down_b, g_ref, d_ref):
    one = slice(layer, layer + 1)
    channels = residual.shape[-1]
    m = residual + unite_b[one]
    for i, part in enumerate((nb, pw, ph)):
        m = m + dot(chunk_rows(part, c), unite_ref[i * channels : (i + 1) * channels])
    centre = jnp.mean(m, axis=-1, keepdims=True)
    dev = m - centre
    s = lax.rsqrt(jnp.mean(dev * dev, axis=-1, keepdims=True) + layer_epsilon)
    zhat = dev * s
    zb = (zhat * ng[one] + ns[one]).astype(BF16)
    out = m + down_b[one]
    for lo in range(0, up_ref.shape[-1], BLK):
        blk = slice(lo, lo + BLK)
        h = dot(zb, up_ref[:, blk]) + up_b[one, blk]
        g, d = gelu_pair(h)
        g = g.astype(BF16)
        g_ref[pl.ds(2 * c, 2), :, blk] = g.reshape(2, ROW, BLK)
        d_ref[pl.ds(2 * c, 2), :, blk] = d.astype(BF16).reshape(2, ROW, BLK)
        out = out + dot_nt(g, down_ref[:, blk])
    return zhat, s, zb, out


def mlp_backward(layer, c, do32, zhat, s, d_ref, down_ref, up_ref, unite_ref, ng, do_ref, dh_ref, dm_ref, df_ref, dn_ref, dpw, dph, small, upsum):
    one = slice(layer, layer + 1)
    channels = do32.shape[-1]
    dob = do32.astype(BF16)
    put_rows(do_ref, c, dob)
    dz = None
    for lo in range(0, up_ref.shape[-1], BLK):
        blk = slice(lo, lo + BLK)
        dg = dot(dob, down_ref[:, blk])
        d = d_ref[pl.ds(2 * c, 2), :, blk].reshape(2 * ROW, BLK).astype(F32)
        dh = (dg * d).astype(BF16)
        dh_ref[pl.ds(2 * c, 2), :, blk] = dh.reshape(2, ROW, BLK)
        upsum[:, blk] += jnp.sum(dh.astype(F32).reshape(-1, 8, BLK), axis=0)
        term = dot_nt(dh, up_ref[:, blk])
        dz = term if dz is None else dz + term
    e = dz * ng[one]
    mean_e = jnp.mean(e, axis=-1, keepdims=True)
    mean_ez = jnp.mean(e * zhat, axis=-1, keepdims=True)
    dm = do32 + s * (e - mean_e - zhat * mean_ez)
    put_rows(dm_ref, c, dm)
    df = dm.astype(BF16)
    put_rows(df_ref, c, df)
    small[2] += jnp.sum((dz * zhat).reshape(-1, 8, channels), axis=0)
    small[3] += jnp.sum(dz.reshape(-1, 8, channels), axis=0)
    small[4] += jnp.sum(dob.astype(F32).reshape(-1, 8, channels), axis=0)
    small[5] += jnp.sum(df.astype(F32).reshape(-1, 8, channels), axis=0)
    put_rows(dn_ref, c, dot_nt(df, unite_ref[0:channels]))
    put_rows(dpw, c, dot_nt(df, unite_ref[channels : 2 * channels]).astype(BF16))
    put_rows(dph, c, dot_nt(df, unite_ref[2 * channels : 3 * channels]).astype(BF16))


def mix_backward(layer, cells, a_ref, stats_ref, mwt_ref, mht_ref, dpw, dph, dn_ref, small):
    mean, rstd = scale_of(stats_ref, cells)
    width = spread(mwt_ref[layer], IMG)
    height = spread(mht_ref[layer], 16)
    for j in range(ROW // 16):
        cols = slice(16 * j, 16 * j + 16)
        value = dph[:, cols, :].reshape(MAP * 16, -1)
        dn_ref[:, cols, :] += dot(height, value).reshape(MAP, 16, -1)

    def body(h, carry):
        dn = dn_ref[h] + dot(width, dpw[h])
        dn_ref[h] = dn
        xhat = (a_ref[h] - mean) * rstd
        small[0] += jnp.sum(dn.reshape(MAP, IMG, -1), axis=0)
        small[1] += jnp.sum((dn * xhat).reshape(MAP, IMG, -1), axis=0)
        return carry

    lax.fori_loop(0, MAP, body, 0)


def put_small(out_ref, small, upsum):
    channels = out_ref.shape[-1]
    out_ref[...] = jnp.zeros(out_ref.shape, F32)
    for i in range(6):
        out_ref[i : i + 1] = jnp.sum(small[i], axis=0, keepdims=True)
    up = jnp.sum(upsum[...], axis=0, keepdims=True)
    for i in range(up.shape[-1] // channels):
        out_ref[6 + i : 7 + i] = up[:, i * channels : (i + 1) * channels]


def kernel_forward(cells, a_ref, stats_ref, x_ref, gain, shift, mw, mwb, mh, mhb, unite, unite_b, ng, ns, up, up_b, down, down_b, kernel_ref,
                   nb, pw, ph, zhat_ref, s_ref, zb_ref, g_ref, d_ref, u_ref, a2_ref, stats2_ref, pad, sums):
    mix_forward(0, cells, a_ref, stats_ref, gain, shift, mw, mwb, mh, mhb, nb, pw, ph)
    zero_border(pad)

    def body(c, carry):
        residual = chunk_rows(x_ref, c).astype(F32)
        zhat, s, zb, out = mlp_forward(0, c, residual, nb, pw, ph, unite, unite_b, ng, ns, up, up_b, down, down_b, g_ref, d_ref)
        put_rows(zhat_ref, c, zhat)
        put_rows(s_ref, c, s)
        put_rows(zb_ref, c, zb)
        put_rows(u_ref, c, out)
        rounded = out.astype(BF16).astype(F32)
        pad[pl.ds(2 * c + 1, 2), 1 : MAP + 1] = rounded.reshape(2, MAP, IMG, -1)
        return carry

    lax.fori_loop(0, MAP // 2, body, 0)
    conv_rows(pad, kernel_ref, 1, a2_ref, stats2_ref, sums)


def kernel_turn(cells, tile_ref, a_ref, stats_ref, u_ref, c0, c1, c2, c3, gain, shift, mw, mwb, mh, mhb, unite, unite_b, ng, ns, up, up_b, down, down_b, mwt, mht,
                nb, pw, ph, zb_ref, g_ref, f0, f1, f2, f3, do_ref, dh_ref, dm_ref, df_ref, dn_ref, dpw, dph, small_ref,
                cot, d_ref, small, upsum):
    tile = tile_ref[0]
    small[...] = jnp.zeros(small.shape, F32)
    upsum[...] = jnp.zeros(upsum.shape, F32)
    for k, piece in enumerate((c0, c1, c2, c3)):
        h0, w0 = corner(tile, k)
        cot[pl.ds(h0, TS), pl.ds(w0, TS)] = piece[...].astype(F32).reshape(TS, TS, IMG, -1)
    mix_forward(1, cells, a_ref, stats_ref, gain, shift, mw, mwb, mh, mhb, nb, pw, ph)

    def body(c, carry):
        residual = chunk_rows(u_ref, c)
        zhat, s, zb, out = mlp_forward(1, c, residual, nb, pw, ph, unite, unite_b, ng, ns, up, up_b, down, down_b, g_ref, d_ref)
        put_rows(zb_ref, c, zb)
        do32 = cot[pl.ds(2 * c, 2)].reshape(2 * ROW, -1)
        cot[pl.ds(2 * c, 2)] = out.reshape(2, MAP, IMG, -1)
        mlp_backward(1, c, do32, zhat, s, d_ref, down, up, unite, ng, do_ref, dh_ref, dm_ref, df_ref, dn_ref, dpw, dph, small, upsum)
        return carry

    lax.fori_loop(0, MAP // 2, body, 0)
    mix_backward(1, cells, a_ref, stats_ref, mwt, mht, dpw, dph, dn_ref, small)
    put_small(small_ref, small, upsum)
    for k, piece in enumerate((f0, f1, f2, f3)):
        h0, w0 = corner(tile, k)
        piece[...] = cot[pl.ds(h0, TS), pl.ds(w0, TS)].reshape(PIECE, -1).astype(BF16)


def conv_backward(layer, cells, a_ref, stats_ref, totals_ref, gain, kernel_ref, dn_ref, dm_ref, x_of, emit, kgrad_ref, padx, padd, ksum):
    mean, rstd = scale_of(stats_ref, cells)
    scale = rstd * gain[layer : layer + 1]
    shift_mean = totals_ref[0:1] * (1.0 / cells)
    gain_mean = totals_ref[1:2] * (1.0 / cells)
    channels = padx.shape[-1]
    zero_border(padx)
    zero_border(padd)
    ksum[...] = jnp.zeros(ksum.shape, F32)

    def fill(h, carry):
        xhat = (a_ref[h] - mean) * rstd
        da = scale * (dn_ref[h] - shift_mean - xhat * gain_mean)
        padd[h + 1, 1 : MAP + 1] = da.reshape(MAP, IMG, -1)
        padx[h + 1, 1 : MAP + 1] = x_of(h).reshape(MAP, IMG, -1)
        return carry

    lax.fori_loop(0, MAP, fill, 0)

    def body(h, carry):
        for lo, hi in lane_groups(channels):
            acc = dm_ref[h, :, lo:hi].reshape(MAP, IMG, hi - lo)
            da = padd[h + 1, 1 : MAP + 1, :, lo:hi]
            for r in range(3):
                for s in range(3):
                    acc = acc + padd[h + 2 - r, 2 - s : 2 - s + MAP, :, lo:hi] * kernel_ref[r, s, layer : layer + 1, lo:hi]
                    ksum[3 * r + s, :, lo:hi] += jnp.sum(da * padx[h + r, s : s + MAP, :, lo:hi], axis=0)
            emit(h, lo, hi, acc)
        return carry

    lax.fori_loop(0, MAP, body, 0)
    kgrad_ref[...] = jnp.zeros(kgrad_ref.shape, F32)
    for i in range(9):
        kgrad_ref[i : i + 1] = jnp.sum(ksum[i], axis=0, keepdims=True)


def kernel_middle(cells, a2_ref, stats2_ref, totals_ref, dn2_ref, dm2_ref, u_ref, kernel_ref, gain, a_ref, stats_ref, zhat_ref, s_ref, d_ref, up, down, unite, ng, mwt, mht,
                  kgrad_ref, do_ref, dh_ref, dm_ref, df_ref, dn_ref, dpw, dph, small_ref, padx, padd, ksum, du, small, upsum):
    small[...] = jnp.zeros(small.shape, F32)
    upsum[...] = jnp.zeros(upsum.shape, F32)

    def x_of(h):
        return u_ref[h].astype(BF16).astype(F32)

    def emit(h, lo, hi, value):
        du[h, :, lo:hi] = value.reshape(ROW, hi - lo)

    conv_backward(1, cells, a2_ref, stats2_ref, totals_ref, gain, kernel_ref, dn2_ref, dm2_ref, x_of, emit, kgrad_ref, padx, padd, ksum)

    def body(c, carry):
        mlp_backward(0, c, chunk_rows(du, c), chunk_rows(zhat_ref, c), chunk_rows(s_ref, c), d_ref, down, up, unite, ng, do_ref, dh_ref, dm_ref, df_ref, dn_ref, dpw, dph, small, upsum)
        return carry

    lax.fori_loop(0, MAP // 2, body, 0)
    mix_backward(0, cells, a_ref, stats_ref, mwt, mht, dpw, dph, dn_ref, small)
    put_small(small_ref, small, upsum)


def kernel_last(cells, tile_ref, a_ref, stats_ref, totals_ref, dn_ref, dm_ref, x_ref, kernel_ref, gain,
                kgrad_ref, o0, o1, o2, o3, padx, padd, ksum, du):
    tile = tile_ref[0]

    def x_of(h):
        return x_ref[h].astype(F32)

    def emit(h, lo, hi, value):
        du[h, :, :, lo:hi] = value

    conv_backward(0, cells, a_ref, stats_ref, totals_ref, gain, kernel_ref, dn_ref, dm_ref, x_of, emit, kgrad_ref, padx, padd, ksum)
    for k, piece in enumerate((o0, o1, o2, o3)):
        h0, w0 = corner(tile, k)
        piece[...] = du[pl.ds(h0, TS), pl.ds(w0, TS)].reshape(PIECE, -1).astype(BF16)


def kernel_weights(do_ref, g_ref, zb_ref, dh_ref, df_ref, nb, pw, ph, dpw, dph, buf, mix_ref):
    channels = do_ref.shape[-1]
    rows = MAP * ROW

    def flat(ref):
        return ref[...].reshape(rows, ref.shape[-1])

    def put(base, value):
        lo = 0
        while lo < value.shape[-1]:
            quarter, lane = divmod(base + lo, buf.shape[-1])
            size = min(value.shape[-1] - lo, buf.shape[-1] - lane)
            buf[quarter * channels : (quarter + 1) * channels, lane : lane + size] = value[:, lo : lo + size].astype(BF16)
            lo += size

    hidden = g_ref.shape[-1]
    dob, zb, df = flat(do_ref), flat(zb_ref), flat(df_ref)
    for lo in range(0, hidden, BLK):
        put(lo, dot_tn(zb, dh_ref[:, :, lo : lo + BLK].reshape(rows, BLK)))
        put(hidden + lo, dot_tn(dob, g_ref[:, :, lo : lo + BLK].reshape(rows, BLK)))
    parts = [dot_tn(df, flat(part)) for part in (nb, pw, ph)]
    pad = 4 * buf.shape[-1] - 2 * hidden - 3 * channels
    whole = jnp.concatenate(parts + [jnp.zeros((channels, pad), F32)], axis=1)
    put(2 * hidden, whole)

    wide = jnp.zeros((ROW, ROW), F32)
    bias = jnp.zeros((ROW, channels), F32)
    for h in range(MAP):
        wide = wide + dot_nt(dpw[h], nb[h])
        bias = bias + dpw[h].astype(F32)
    tall = jnp.zeros((MAP * 16, MAP * 16), F32)
    tall_bias = jnp.zeros((MAP, 16, channels), F32)
    for j in range(ROW // 16):
        cols = slice(16 * j, 16 * j + 16)
        value = dph[:, cols, :]
        tall = tall + dot_nt(value.reshape(MAP * 16, channels), nb[:, cols, :].reshape(MAP * 16, channels))
        tall_bias = tall_bias + value.astype(F32)
    mix_ref[...] = jnp.zeros(mix_ref.shape, F32)
    mix_ref[0:MAP, 0:MAP] = collapse(wide, IMG)
    mix_ref[0:MAP, 128 : 128 + MAP] = collapse(tall, 16)
    col = jnp.sum(jnp.sum(bias.reshape(MAP, IMG, channels), axis=1), axis=-1, keepdims=True)
    mix_ref[0:MAP, 256:257] = col
    col = jnp.sum(jnp.sum(tall_bias, axis=1), axis=-1, keepdims=True)
    mix_ref[0:MAP, 257:258] = col


SMEM = pl.BlockSpec(memory_space=pltpu.SMEM)


def layered(array, layer):
    shape = array.shape
    return pl.BlockSpec((None,) + shape[1:], lambda i: (layer,) + (0,) * (len(shape) - 1))


def full(array):
    rank = len(array.shape)
    return pl.BlockSpec(array.shape, lambda i: (0,) * rank)


def run(body, operands, outs, scratch, name, flops):
    arrays, specs = [], []
    for operand in operands:
        if isinstance(operand, tuple):
            what, array = operand
            arrays.append(array)
            specs.append(SMEM if what == "smem" else layered(array, what))
        else:
            arrays.append(operand)
            specs.append(full(operand))
    size = sum(a.size * a.dtype.itemsize for a in arrays) + sum(o.size * o.dtype.itemsize for o in outs)
    return pl.pallas_call(
        body,
        grid=(1,),
        in_specs=specs,
        out_specs=[full(o) for o in outs],
        out_shape=outs,
        scratch_shapes=scratch,
        compiler_params=pltpu.CompilerParams(vmem_limit_bytes=VMEM_BYTES),
        cost_estimate=pl.CostEstimate(flops=flops, bytes_accessed=size, transcendentals=0),
        name=name,
    )(*arrays)


def on_device(
    patches,
    conv_kernel,
    batch_gain,
    batch_shift,
    mix_width,
    mix_width_bias,
    mix_height,
    mix_height_bias,
    unite_weight,
    unite_bias,
    norm_gain,
    norm_shift,
    up_weight,
    up_bias,
    down_weight,
    down_bias,
    cotangent,
):
    channels = patches.shape[-1]
    hidden = up_weight.shape[-1]
    tile = lax.axis_index("tile")
    tile_arg = ("smem", tile.astype(jnp.int32).reshape(1))
    local_cells = MAP * ROW
    cells = local_cells * lax.axis_size("dp") * lax.axis_size("tile")

    def rows(lanes, dtype):
        return jax.ShapeDtypeStruct((MAP, ROW, lanes), dtype)

    def shape(*dims, dtype=F32):
        return jax.ShapeDtypeStruct(dims, dtype)

    piece = shape(PIECE, channels, dtype=BF16)
    c_bf, c_f32, h_bf = rows(channels, BF16), rows(channels, F32), rows(hidden, BF16)
    pad = pltpu.VMEM((MAP + 2, MAP + 2, IMG, channels), F32)
    sums = pltpu.VMEM((2, 8, channels), F32)
    small = pltpu.VMEM((6, 8, channels), F32)
    upsum = pltpu.VMEM((8, hidden), F32)
    ksum = pltpu.VMEM((9, 8, channels), F32)

    kernels = conv_kernel.transpose(1, 2, 0, 3)
    down_t = down_weight.transpose(0, 2, 1)
    mwb = jnp.repeat(mix_width_bias, IMG, axis=1)[:, :, None]
    mhb = jnp.repeat(mix_height_bias, 16, axis=1)[:, :, None]
    mwt, mht = mix_width.transpose(0, 2, 1), mix_height.transpose(0, 2, 1)

    x_pieces = to_whole(patches[:, 0].transpose(1, 2, 0, 3), tile)
    x0, a0, stats0 = run(
        kernel_first,
        [tile_arg, *x_pieces, kernels],
        [c_bf, c_f32, shape(2, channels)],
        [pad, sums],
        "conv_first",
        10**7,
    )
    stats0 = total_moments(stats0, float(local_cells))
    cot_pieces = to_whole(cotangent[:, 0].transpose(1, 2, 0, 3), tile)

    def forward_args(layer):
        return [
            batch_gain, batch_shift, mix_width, mwb, mix_height, mhb,
            (layer, unite_weight), unite_bias, norm_gain, norm_shift,
            (layer, up_weight), up_bias, (layer, down_t), down_bias,
        ]

    def body_forward(*refs):
        kernel_forward(cells, *refs)

    nb0, pw0, ph0, zhat0, s0, zb0, g0, d0, u1, a1, stats1 = run(
        body_forward,
        [a0, stats0, x0, *forward_args(0), kernels],
        [c_bf, c_bf, c_bf, c_f32, rows(1, F32), c_bf, h_bf, h_bf, c_f32, c_f32, shape(2, channels)],
        [pad, sums],
        "block_forward",
        4 * 10**9,
    )
    stats1 = total_moments(stats1, float(local_cells))

    def body_turn(*refs):
        kernel_turn(cells, *refs)

    nb1, pw1, ph1, zb1, g1, f0, f1, f2, f3, do1, dh1, dm1, df1, dn1, dpw1, dph1, small1 = run(
        body_turn,
        [tile_arg, a1, stats1, u1, *cot_pieces, *forward_args(1), mwt, mht],
        [c_bf, c_bf, c_bf, c_bf, h_bf, piece, piece, piece, piece, c_bf, h_bf, c_f32, c_bf, c_f32, c_bf, c_bf, shape(16, channels)],
        [pltpu.VMEM((MAP, MAP, IMG, channels), F32), pltpu.VMEM((MAP, ROW, hidden), BF16), small, upsum],
        "block_turn",
        8 * 10**9,
    )
    features = to_tiled([f0, f1, f2, f3], tile)
    total1 = total_sum(small1)
    buffer_shape = shape(4 * channels, (2 * hidden + 1024) // 4, dtype=BF16)
    buf1, mix1 = run(
        kernel_weights,
        [do1, g1, zb1, dh1, df1, nb1, pw1, ph1, dpw1, dph1],
        [buffer_shape, shape(16, channels)],
        [],
        "weights_1",
        4 * 10**9,
    )
    sum1 = sum_gradients(buf1)

    def body_middle(*refs):
        kernel_middle(cells, *refs)

    kgrad1, do0, dh0, dm0, df0, dn0, dpw0, dph0, small0 = run(
        body_middle,
        [a1, stats1, total1, dn1, dm1, u1, kernels, batch_gain, a0, stats0, zhat0, s0, d0, (0, up_weight), (0, down_t), (0, unite_weight), norm_gain, mwt, mht],
        [shape(16, channels), c_bf, h_bf, c_f32, c_bf, c_f32, c_bf, c_bf, shape(16, channels)],
        [pad, pad, ksum, pltpu.VMEM((MAP, ROW, channels), F32), small, upsum],
        "block_back",
        4 * 10**9,
    )
    total0 = total_sum(small0)
    buf0, mix0 = run(
        kernel_weights,
        [do0, g0, zb0, dh0, df0, nb0, pw0, ph0, dpw0, dph0],
        [buffer_shape, shape(16, channels)],
        [],
        "weights_0",
        4 * 10**9,
    )
    sum0 = sum_gradients(buf0)

    def body_last(*refs):
        kernel_last(cells, *refs)

    kgrad0, o0, o1, o2, o3 = run(
        body_last,
        [tile_arg, a0, stats0, total0, dn0, dm0, x0, kernels, batch_gain],
        [shape(16, channels), piece, piece, piece, piece],
        [pad, pad, ksum, pltpu.VMEM((MAP, MAP, IMG, channels), F32)],
        "conv_last",
        10**7,
    )
    grads = to_tiled([o0, o1, o2, o3], tile)
    last = total_sum(jnp.concatenate([kgrad0, kgrad1, mix0, mix1], 0))

    def to_output(field):
        return field.transpose(2, 0, 1, 3)[:, None]

    def unpack(total):
        quarters = [total[i * channels : (i + 1) * channels] for i in range(4)]
        whole = jnp.concatenate(quarters, 1).astype(F32)
        return (
            whole[:, :hidden],
            whole[:, hidden : 2 * hidden],
            whole[:, 2 * hidden : 2 * hidden + 3 * channels],
        )

    packed = [unpack(sum0), unpack(sum1)]
    up_grad = jnp.stack([p[0] for p in packed])
    down_grad = jnp.stack([p[1] for p in packed]).transpose(0, 2, 1)
    unite_grad = jnp.stack([p[2] for p in packed]).transpose(0, 2, 1)
    totals = jnp.stack([total0, total1])
    kgrads = jnp.stack([last[0:9], last[16:25]]).reshape(2, 3, 3, channels)
    mixes = jnp.stack([last[32:48], last[48:64]])[:, :MAP]
    return (
        to_output(features),
        to_output(grads),
        kgrads,
        totals[:, 1],
        totals[:, 0],
        mixes[:, :, 0:MAP],
        mixes[:, :, 256],
        mixes[:, :, 128 : 128 + MAP],
        mixes[:, :, 257],
        unite_grad,
        totals[:, 5],
        totals[:, 2],
        totals[:, 3],
        up_grad,
        totals[:, 6:10].reshape(2, hidden),
        down_grad,
        totals[:, 4],
    )


def solution(mesh):
    field = P("dp", "tile", None, None, None)
    return jax.shard_map(
        on_device,
        mesh=mesh,
        in_specs=(field,) + (P(),) * 15 + (field,),
        out_specs=(field, field) + (P(),) * 15,
        check_vma=False,
    )
```

```python
import jax
import jax.numpy as jnp
from jax import lax
from jax.experimental import pallas as pl
from jax.experimental.pallas import tpu as pltpu
from jax.sharding import PartitionSpec as P

F32 = jnp.float32
BF16 = jnp.bfloat16
norm_epsilon = 1e-05
layer_epsilon = 1e-06
ROOT_HALF = 0.7071067811865476
INV_ROOT_TAU = 0.3989422804014327
LOG2E = 1.4426950408889634

TS = 7
MAP = 14
IMG = 8
ROW = MAP * IMG
PIECE = TS * TS * IMG
VMEM_BYTES = 58 * 1024 * 1024
BLK = 256


def partner(x, axis, distance):
    count = lax.axis_size(axis)
    return lax.ppermute(x, axis, [(i, i ^ distance) for i in range(count)])


def stages():
    result = [("tile", (1, 2, 3))]
    count = lax.axis_size("dp")
    step = 1
    if count > 1 and (count.bit_length() - 1) % 2 == 1:
        result.append(("dp", (1,)))
        step = 2
    while step < count:
        result.append(("dp", (step, 2 * step, 3 * step)))
        step *= 4
    return result


def total_sum(x, after=None):
    for step, (axis, distances) in enumerate(stages()):
        if step == 2 and after is not None:
            x, *after = tie(x, *after)
        got = [partner(x, axis, d) for d in distances]
        if len(got) == 1:
            x = x + got[0]
        else:
            x = (x + got[0]) + (got[1] + got[2])
    return x if after is None else (x, after)


def total_moments(stats, count):
    for axis, distances in stages():
        parts = [stats] + [partner(stats, axis, d) for d in distances]
        if len(parts) == 2:
            mean = (parts[0][0] + parts[1][0]) * 0.5
            dev = [jnp.square(p[0] - mean) for p in parts]
            square = (parts[0][1] + parts[1][1]) + count * (dev[0] + dev[1])
        else:
            mean = ((parts[0][0] + parts[1][0]) + (parts[2][0] + parts[3][0])) * 0.25
            dev = [jnp.square(p[0] - mean) for p in parts]
            square = ((parts[0][1] + parts[1][1]) + (parts[2][1] + parts[3][1])) + count * (
                (dev[0] + dev[1]) + (dev[2] + dev[3])
            )
        count = count * len(parts)
        stats = jnp.stack([mean, square])
    return stats


def to_whole(field, tile):
    share = field.shape[2] // lax.axis_size("tile")
    pieces = []
    for k in range(4):
        part = lax.dynamic_slice_in_dim(field, (tile ^ k) * share, share, 2)
        part = part.reshape(TS * TS * share, field.shape[3])
        pieces.append(part if k == 0 else partner(part, "tile", k))
    return pieces


def to_tiled(pieces, tile):
    channels = pieces[0].shape[-1]
    share = pieces[0].shape[0] // (TS * TS)
    result = jnp.zeros((TS, TS, share * lax.axis_size("tile"), channels), pieces[0].dtype)
    for k in range(4):
        part = pieces[k] if k == 0 else partner(pieces[k], "tile", k)
        part = part.reshape(TS, TS, share, channels)
        result = lax.dynamic_update_slice_in_dim(result, part, (tile ^ k) * share, 2)
    return result


def flat_partner(x, mask):
    axes = ("dp", "tile")
    count = lax.axis_size("dp") * lax.axis_size("tile")
    return lax.ppermute(x, axes, [(i, i ^ mask) for i in range(count)])


GROUPS = ((0,), (1, 2), (3, 4))
BLOCKS = 32


def block_index():
    flat = lax.axis_index("dp") * lax.axis_size("tile") + lax.axis_index("tile")
    index = jnp.zeros((), jnp.int32)
    for group in GROUPS:
        for bit in group:
            index = index * 2 + ((flat >> bit) & 1)
    return index


def masks(group):
    if len(group) == 1:
        return [1 << group[0]]
    return [1 << group[1], 1 << group[0], (1 << group[0]) | (1 << group[1])]


def narrow_add(parts):
    parts = [p.astype(F32) for p in parts]
    total = parts[0] + parts[1]
    if len(parts) == 4:
        total = total + (parts[2] + parts[3])
    return total.astype(BF16)


def scatter_stage(x, group):
    wide = masks(group)
    size = x.shape[0] // (len(wide) + 1)
    got = [flat_partner(x[(j + 1) * size : (j + 2) * size], mask) for j, mask in enumerate(wide)]
    return narrow_add([x[:size]] + got)


def extra_sum(x):
    count = lax.axis_size("dp") * lax.axis_size("tile")
    mask = BLOCKS
    while mask < count:
        x = narrow_add([x, flat_partner(x, mask)])
        mask *= 2
    return x


def gather_stage(x, group):
    return jnp.concatenate([x] + [flat_partner(x, mask) for mask in masks(group)], 0)


def tie(*values):
    return lax.optimization_barrier(values)


def dot(a, b):
    return lax.dot_general(a, b, (((1,), (0,)), ((), ())), preferred_element_type=F32)


def dot_nt(a, b):
    return lax.dot_general(a, b, (((1,), (1,)), ((), ())), preferred_element_type=F32)


def dot_tn(a, b):
    return lax.dot_general(a, b, (((0,), (0,)), ((), ())), preferred_element_type=F32)


def spread(matrix, repeat):
    size = MAP * repeat
    shift = repeat.bit_length() - 1
    row = lax.broadcasted_iota(jnp.int32, (size, MAP), 0)
    col = lax.broadcasted_iota(jnp.int32, (size, MAP), 1)
    pick = jnp.where((row >> shift) == col, 1.0, 0.0).astype(BF16)
    wide = dot_nt(dot(pick, matrix).astype(BF16), pick)
    row = lax.broadcasted_iota(jnp.int32, (size, size), 0)
    col = lax.broadcasted_iota(jnp.int32, (size, size), 1)
    return jnp.where((row & (repeat - 1)) == (col & (repeat - 1)), wide, 0.0).astype(BF16)


def collapse(product, repeat):
    size = MAP * repeat
    shift = repeat.bit_length() - 1
    row = lax.broadcasted_iota(jnp.int32, (size, size), 0)
    col = lax.broadcasted_iota(jnp.int32, (size, size), 1)
    kept = jnp.where((row & (repeat - 1)) == (col & (repeat - 1)), product, 0.0)
    kept = jnp.sum(kept.reshape(MAP, repeat, size), axis=1)
    row = lax.broadcasted_iota(jnp.int32, (size, MAP), 0)
    col = lax.broadcasted_iota(jnp.int32, (size, MAP), 1)
    pick = jnp.where((row >> shift) == col, 1.0, 0.0).astype(F32)
    return lax.dot_general(
        kept, pick, (((1,), (0,)), ((), ())), preferred_element_type=F32, precision=lax.Precision.HIGHEST
    )


def lane_groups(channels):
    return [(lo, min(lo + 128, channels)) for lo in range(0, channels, 128)]


def zero_border(pad):
    shape = pad.shape
    pad[0] = jnp.zeros(shape[1:], F32)
    pad[MAP + 1] = jnp.zeros(shape[1:], F32)
    for h in range(1, MAP + 1):
        pad[h, 0] = jnp.zeros(shape[2:], F32)
        pad[h, MAP + 1] = jnp.zeros(shape[2:], F32)


def corner(tile, k):
    other = tile ^ k
    return (other >> 1) * TS, (other & 1) * TS


def conv_rows(pad, kernel_ref, layer, out_ref, stats_ref, sums):
    channels = pad.shape[-1]
    sums[...] = jnp.zeros(sums.shape, F32)

    def body(h, carry):
        for lo, hi in lane_groups(channels):
            acc = None
            for r in range(3):
                for s in range(3):
                    term = pad[h + r, s : s + MAP, :, lo:hi] * kernel_ref[r, s, layer : layer + 1, lo:hi]
                    acc = term if acc is None else acc + term
            out_ref[h, :, lo:hi] = acc.reshape(ROW, hi - lo)
            sums[0, :, lo:hi] += jnp.sum(acc, axis=0)
        return carry

    lax.fori_loop(0, MAP, body, 0)
    count = MAP * ROW
    mean = jnp.sum(sums[0], axis=0, keepdims=True) * (1.0 / count)

    def again(h, carry):
        for lo, hi in lane_groups(channels):
            dev = out_ref[h, :, lo:hi] - mean[:, lo:hi]
            sums[1, :, lo:hi] += jnp.sum((dev * dev).reshape(MAP, IMG, hi - lo), axis=0)
        return carry

    lax.fori_loop(0, MAP, again, 0)
    stats_ref[0:1] = mean
    stats_ref[1:2] = jnp.sum(sums[1], axis=0, keepdims=True)


def scale_of(stats_ref, cells):
    mean = stats_ref[0:1]
    return mean, lax.rsqrt(stats_ref[1:2] * (1.0 / cells) + norm_epsilon)


def mix_forward(layer, cells, a_ref, stats_ref, gain_ref, shift_ref, mw_ref, mwb_ref, mh_ref, mhb_ref, nb, pw, ph):
    mean, rstd = scale_of(stats_ref, cells)
    gain = gain_ref[layer : layer + 1]
    shift = shift_ref[layer : layer + 1]
    width = spread(mw_ref[layer], IMG)
    height = spread(mh_ref[layer], 16)

    def body(h, carry):
        value = (((a_ref[h] - mean) * rstd) * gain + shift).astype(BF16)
        nb[h] = value
        pw[h] = (dot(width, value) + mwb_ref[layer]).astype(BF16)
        return carry

    lax.fori_loop(0, MAP, body, 0)
    for j in range(ROW // 16):
        value = nb[:, 16 * j : 16 * j + 16, :].reshape(MAP * 16, -1)
        mixed = (dot(height, value) + mhb_ref[layer]).astype(BF16)
        ph[:, 16 * j : 16 * j + 16, :] = mixed.reshape(MAP, 16, -1)


def gelu_pair(v):
    t = 1.0 / (1.0 + (0.3275911 * ROOT_HALF) * jnp.abs(v))
    e = jnp.exp2(v * v * (-0.5 * LOG2E))
    q = ((((0.5 * 1.061405429 * t - 0.5 * 1.453152027) * t + 0.5 * 1.421413741) * t - 0.5 * 0.284496736) * t + 0.5 * 0.254829592) * t * e
    phi = jnp.where(v >= 0, 1.0 - q, q)
    return v * phi, phi + v * e * INV_ROOT_TAU


def chunk_rows(ref, c):
    value = ref[pl.ds(2 * c, 2)]
    return value.reshape(2 * ROW, value.shape[-1])


def put_rows(ref, c, value):
    ref[pl.ds(2 * c, 2)] = value.reshape(2, ROW, value.shape[-1])


def mlp_forward(layer, c, residual, nb, pw, ph, unite_ref, unite_b, ng, ns, up_ref, up_b, down_ref, down_b, g_ref, d_ref, d_row):
    one = slice(layer, layer + 1)
    channels = residual.shape[-1]
    m = residual + unite_b[one]
    for i, part in enumerate((nb, pw, ph)):
        m = m + dot(chunk_rows(part, c), unite_ref[i * channels : (i + 1) * channels])
    centre = jnp.mean(m, axis=-1, keepdims=True)
    dev = m - centre
    s = lax.rsqrt(jnp.mean(dev * dev, axis=-1, keepdims=True) + layer_epsilon)
    zhat = dev * s
    zb = (zhat * ng[one] + ns[one]).astype(BF16)
    out = m + down_b[one]
    for lo in range(0, up_ref.shape[-1], BLK):
        blk = slice(lo, lo + BLK)
        h = dot(zb, up_ref[:, blk]) + up_b[one, blk]
        g, d = gelu_pair(h)
        g = g.astype(BF16)
        g_ref[pl.ds(2 * c, 2), :, blk] = g.reshape(2, ROW, BLK)
        d_ref[pl.ds(d_row, 2), :, blk] = d.astype(BF16).reshape(2, ROW, BLK)
        out = out + dot_nt(g, down_ref[:, blk])
    return zhat, s, zb, out


def mlp_backward(layer, c, do32, zhat, s, d_ref, d_row, down_ref, up_ref, unite_ref, ng, do_ref, dh_ref, dm_ref, df_ref, dn_ref, dpw, dph, small, upsum):
    one = slice(layer, layer + 1)
    channels = do32.shape[-1]
    dob = do32.astype(BF16)
    put_rows(do_ref, c, dob)
    dz = None
    for lo in range(0, up_ref.shape[-1], BLK):
        blk = slice(lo, lo + BLK)
        dg = dot(dob, down_ref[:, blk])
        d = d_ref[pl.ds(d_row, 2), :, blk].reshape(2 * ROW, BLK).astype(F32)
        dh = (dg * d).astype(BF16)
        dh_ref[pl.ds(2 * c, 2), :, blk] = dh.reshape(2, ROW, BLK)
        upsum[:, blk] += jnp.sum(dh.astype(F32).reshape(-1, 8, BLK), axis=0)
        term = dot_nt(dh, up_ref[:, blk])
        dz = term if dz is None else dz + term
    e = dz * ng[one]
    mean_e = jnp.mean(e, axis=-1, keepdims=True)
    mean_ez = jnp.mean(e * zhat, axis=-1, keepdims=True)
    dm = do32 + s * (e - mean_e - zhat * mean_ez)
    put_rows(dm_ref, c, dm)
    df = dm.astype(BF16)
    put_rows(df_ref, c, df)
    small[2] += jnp.sum((dz * zhat).reshape(-1, 8, channels), axis=0)
    small[3] += jnp.sum(dz.reshape(-1, 8, channels), axis=0)
    small[4] += jnp.sum(dob.astype(F32).reshape(-1, 8, channels), axis=0)
    small[5] += jnp.sum(df.astype(F32).reshape(-1, 8, channels), axis=0)
    put_rows(dn_ref, c, dot_nt(df, unite_ref[0:channels]))
    put_rows(dpw, c, dot_nt(df, unite_ref[channels : 2 * channels]).astype(BF16))
    put_rows(dph, c, dot_nt(df, unite_ref[2 * channels : 3 * channels]).astype(BF16))


def mix_backward(layer, cells, a_ref, stats_ref, mwt_ref, mht_ref, dpw, dph, dn_ref, small, send):
    mean, rstd = scale_of(stats_ref, cells)
    width = spread(mwt_ref[layer], IMG)
    height = spread(mht_ref[layer], 16)
    for j in range(ROW // 16):
        cols = slice(16 * j, 16 * j + 16)
        value = dph[:, cols, :].reshape(MAP * 16, -1)
        dn_ref[:, cols, :] += dot(height, value).reshape(MAP, 16, -1)

    def body(c, carry):
        for i in range(2):
            h = 2 * c + i
            dn = dn_ref[h] + dot(width, dpw[h])
            dn_ref[h] = dn
            xhat = (a_ref[h] - mean) * rstd
            small[0] += jnp.sum(dn.reshape(MAP, IMG, -1), axis=0)
            small[1] += jnp.sum((dn * xhat).reshape(MAP, IMG, -1), axis=0)
        send(c)
        return carry

    lax.fori_loop(0, MAP // 2, body, 0)


def weight_gradients(index, do_ref, g_ref, zb_ref, dh_ref, df_ref, nb, pw, ph, dpw, dph, buf, mix_ref):
    channels = do_ref.shape[-1]
    rows = MAP * ROW
    lanes = buf.shape[-1]
    size = buf.shape[1]

    def flat(ref):
        return ref[...].reshape(rows, ref.shape[-1])

    def put(base, value):
        lo = 0
        while lo < value.shape[-1]:
            quarter, lane = divmod(base + lo, lanes)
            step = min(value.shape[-1] - lo, lanes - lane)
            for b in range(channels // size):
                place = (quarter * (channels // size) + b) ^ index
                buf[place, :, lane : lane + step] = value[b * size : (b + 1) * size, lo : lo + step].astype(BF16)
            lo += step

    hidden = g_ref.shape[-1]
    dob, zb, df = flat(do_ref), flat(zb_ref), flat(df_ref)
    for lo in range(0, hidden, BLK):
        put(lo, dot_tn(zb, dh_ref[:, :, lo : lo + BLK].reshape(rows, BLK)))
        put(hidden + lo, dot_tn(dob, g_ref[:, :, lo : lo + BLK].reshape(rows, BLK)))
    parts = [dot_tn(df, flat(part)) for part in (nb, pw, ph)]
    pad = 4 * lanes - 2 * hidden - 3 * channels
    put(2 * hidden, jnp.concatenate(parts + [jnp.zeros((channels, pad), F32)], axis=1))

    wide = jnp.zeros((ROW, ROW), F32)
    bias = jnp.zeros((ROW, channels), F32)
    for h in range(MAP):
        wide = wide + dot_nt(dpw[h], nb[h])
        bias = bias + dpw[h].astype(F32)
    tall = jnp.zeros((MAP * 16, MAP * 16), F32)
    tall_bias = jnp.zeros((MAP, 16, channels), F32)
    for j in range(ROW // 16):
        cols = slice(16 * j, 16 * j + 16)
        value = dph[:, cols, :]
        tall = tall + dot_nt(value.reshape(MAP * 16, channels), nb[:, cols, :].reshape(MAP * 16, channels))
        tall_bias = tall_bias + value.astype(F32)
    mix_ref[...] = jnp.zeros(mix_ref.shape, F32)
    mix_ref[0:MAP, 0:MAP] = collapse(wide, IMG)
    mix_ref[0:MAP, 128 : 128 + MAP] = collapse(tall, 16)
    col = jnp.sum(jnp.sum(bias.reshape(MAP, IMG, channels), axis=1), axis=-1, keepdims=True)
    mix_ref[0:MAP, 256:257] = col
    col = jnp.sum(jnp.sum(tall_bias, axis=1), axis=-1, keepdims=True)
    mix_ref[0:MAP, 257:258] = col


def put_small(out_ref, small, upsum):
    channels = out_ref.shape[-1]
    out_ref[...] = jnp.zeros(out_ref.shape, F32)
    for i in range(6):
        out_ref[i : i + 1] = jnp.sum(small[i], axis=0, keepdims=True)
    up = jnp.sum(upsum[...], axis=0, keepdims=True)
    for i in range(up.shape[-1] // channels):
        out_ref[6 + i : 7 + i] = up[:, i * channels : (i + 1) * channels]


def conv_backward(layer, cells, a, stats_ref, totals_ref, gain, kernel_ref, dn, dm, x, emit, kgrad_ref, padx, padd, ksum):
    mean, rstd = scale_of(stats_ref, cells)
    scale = rstd * gain[layer : layer + 1]
    shift_mean = totals_ref[0:1] * (1.0 / cells)
    gain_mean = totals_ref[1:2] * (1.0 / cells)
    channels = padx.shape[-1]
    zero_border(padx)
    zero_border(padd)
    ksum[...] = jnp.zeros(ksum.shape, F32)

    def fill(c, carry):
        for part in (a, dn, x):
            part.wait(c)
        for i in range(2):
            h = 2 * c + i
            xhat = (a.ref[h] - mean) * rstd
            da = scale * (dn.ref[h] - shift_mean - xhat * gain_mean)
            padd[h + 1, 1 : MAP + 1] = da.reshape(MAP, IMG, -1)
            padx[h + 1, 1 : MAP + 1] = x.ref[h].astype(BF16).astype(F32).reshape(MAP, IMG, -1)
        return carry

    lax.fori_loop(0, MAP // 2, fill, 0)
    dm.wait_all()

    def body(h, carry):
        for lo, hi in lane_groups(channels):
            acc = dm.ref[h, :, lo:hi].reshape(MAP, IMG, hi - lo)
            da = padd[h + 1, 1 : MAP + 1, :, lo:hi]
            for r in range(3):
                for s in range(3):
                    acc = acc + padd[h + 2 - r, 2 - s : 2 - s + MAP, :, lo:hi] * kernel_ref[r, s, layer : layer + 1, lo:hi]
                    ksum[3 * r + s, :, lo:hi] += jnp.sum(da * padx[h + r, s : s + MAP, :, lo:hi], axis=0)
            emit(h, lo, hi, acc)
        return carry

    lax.fori_loop(0, MAP, body, 0)
    kgrad_ref[...] = jnp.zeros(kgrad_ref.shape, F32)
    for i in range(9):
        kgrad_ref[i : i + 1] = jnp.sum(ksum[i], axis=0, keepdims=True)


def kernel_first(r):
    tile = r.tile[0]
    zero_border(r.pad)
    for k, piece in enumerate((r.p0, r.p1, r.p2, r.p3)):
        h0, w0 = corner(tile, k)
        value = piece[...].astype(F32).reshape(TS, TS, IMG, -1)
        r.pad[pl.ds(1 + h0, TS), pl.ds(1 + w0, TS)] = value

    def body(h, carry):
        r.x[h] = r.pad[h + 1, 1 : MAP + 1].reshape(ROW, -1).astype(BF16)
        return carry

    lax.fori_loop(0, MAP, body, 0)
    conv_rows(r.pad, r.kernels, 0, r.a, r.stats, r.sums)


def forward_front(r, layer, cells):
    r.a.wait_all()
    mix_forward(layer, cells, r.a.ref, r.stats, r.batch_gain, r.batch_shift, r.mix_width, r.mwb, r.mix_height, r.mhb, r.nb.ref, r.pw.ref, r.ph.ref)


def forward_chunk(r, layer, c, residual, d_ref, d_row):
    return mlp_forward(layer, c, residual, r.nb.ref, r.pw.ref, r.ph.ref, r.unite.ref, r.unite_bias, r.norm_gain, r.norm_shift, r.up.ref, r.up_bias, r.down.ref, r.down_bias, r.g.ref, d_ref, d_row)


def kernel_forward(cells, r):
    forward_front(r, 0, cells)
    for out in (r.nb, r.pw, r.ph):
        out.send_all()
    zero_border(r.pad)
    for part in (r.unite, r.up, r.down, r.x):
        part.wait_all()

    def body(c, carry):
        residual = chunk_rows(r.x.ref, c).astype(F32)
        zhat, s, zb, out = forward_chunk(r, 0, c, residual, r.d.ref, 2 * c)
        put_rows(r.zhat.ref, c, zhat)
        put_rows(r.s.ref, c, s)
        put_rows(r.zb.ref, c, zb)
        put_rows(r.u.ref, c, out)
        for stream in (r.zhat, r.s, r.zb, r.u, r.g, r.d):
            stream.send(c)
        rounded = out.astype(BF16).astype(F32)
        r.pad[pl.ds(2 * c + 1, 2), 1 : MAP + 1] = rounded.reshape(2, MAP, IMG, -1)
        return carry

    lax.fori_loop(0, MAP // 2, body, 0)
    conv_rows(r.pad, r.kernels, 1, r.a2.ref, r.stats2, r.sums)
    r.a2.send_all()


def clear(r):
    r.small[...] = jnp.zeros(r.small.shape, F32)
    r.upsum[...] = jnp.zeros(r.upsum.shape, F32)


def send_blocks(r):
    half = BLOCKS // 2
    r.mine.start(r.buf.at[pl.ds(0, half)])
    r.sent.start(r.buf.at[pl.ds(half, half)])


def kernel_turn(cells, r):
    tile = r.tile[0]
    clear(r)
    for key in ("nb", "pw", "ph", "g"):
        setattr(r, key, Held(getattr(r, key)))
    forward_front(r, 1, cells)
    for k, piece in enumerate((r.c0, r.c1, r.c2, r.c3)):
        piece.wait_all()
        h0, w0 = corner(tile, k)
        r.cot[pl.ds(h0, TS), pl.ds(w0, TS)] = piece.ref[...].astype(F32).reshape(TS, TS, IMG, -1)
    for part in (r.u, r.unite, r.up, r.down):
        part.wait_all()

    def body(c, carry):
        residual = chunk_rows(r.u.ref, c)
        zhat, s, zb, out = forward_chunk(r, 1, c, residual, r.d, 0)
        put_rows(r.zb, c, zb)
        do32 = r.cot[pl.ds(2 * c, 2)].reshape(2 * ROW, -1)
        r.cot[pl.ds(2 * c, 2)] = out.reshape(2, MAP, IMG, -1)
        mlp_backward(1, c, do32, zhat, s, r.d, 0, r.down.ref, r.up.ref, r.unite.ref, r.norm_gain, r.do, r.dh, r.dm.ref, r.df, r.dn.ref, r.dpw, r.dph, r.small, r.upsum)
        r.dm.send(c)
        return carry

    lax.fori_loop(0, MAP // 2, body, 0)
    mix_backward(1, cells, r.a.ref, r.stats, r.mwt, r.mht, r.dpw, r.dph, r.dn.ref, r.small, r.dn.send)
    put_small(r.small_out, r.small, r.upsum)
    for k, piece in enumerate((r.f0, r.f1, r.f2, r.f3)):
        h0, w0 = corner(tile, k)
        piece.ref[...] = r.cot[pl.ds(h0, TS), pl.ds(w0, TS)].reshape(PIECE, -1).astype(BF16)
        piece.send_all()
    weight_gradients(r.index[0], r.do, r.g.ref, r.zb, r.dh, r.df, r.nb.ref, r.pw.ref, r.ph.ref, r.dpw, r.dph, r.buf, r.mix)
    send_blocks(r)


def kernel_conv_middle(cells, r):
    def emit(h, lo, hi, value):
        r.du.ref[h, :, lo:hi] = value.reshape(ROW, hi - lo)

    conv_backward(1, cells, r.a, r.stats, r.totals, r.batch_gain, r.kernels, r.dn, r.dm, r.x, emit, r.kgrad, r.padx, r.padd, r.ksum)
    r.du.send_all()


def kernel_mlp_back(r):
    clear(r)
    for part in (r.down, r.up, r.unite):
        part.wait_all()

    def body(c, carry):
        for part in (r.du, r.d, r.zhat, r.s):
            part.wait(c)
        mlp_backward(0, c, chunk_rows(r.du.ref, c), chunk_rows(r.zhat.ref, c), chunk_rows(r.s.ref, c), r.d.ref, 2 * c, r.down.ref, r.up.ref, r.unite.ref, r.norm_gain,
                     r.do, r.dh, r.dm.ref, r.df, r.dn.ref, r.dpw.ref, r.dph.ref, r.small, r.upsum)
        for stream in (r.dm, r.dn, r.dpw, r.dph):
            stream.send(c)
        return carry

    lax.fori_loop(0, MAP // 2, body, 0)
    put_small(r.small_out, r.small, r.upsum)
    for part in (r.zb, r.g, r.nb, r.pw, r.ph):
        part.wait_all()
    weight_gradients(r.index[0], r.do, r.g.ref, r.zb.ref, r.dh, r.df, r.nb.ref, r.pw.ref, r.ph.ref, r.dpw.ref, r.dph.ref, r.buf, r.mix)
    send_blocks(r)


def kernel_mix_back(cells, r):
    r.small[...] = jnp.zeros(r.small.shape, F32)
    for part in (r.dph, r.dn_in, r.dpw, r.a):
        part.wait_all()
    r.dn.ref[...] = r.dn_in.ref[...]
    mix_backward(0, cells, r.a.ref, r.stats, r.mwt, r.mht, r.dpw.ref, r.dph.ref, r.dn.ref, r.small, r.dn.send)
    r.small_out[...] = r.small_in[...]
    for i in range(2):
        r.small_out[i : i + 1] = jnp.sum(r.small[i], axis=0, keepdims=True)


def kernel_last(cells, r):
    tile = r.tile[0]

    def emit(h, lo, hi, value):
        r.du[h, :, :, lo:hi] = value

    conv_backward(0, cells, r.a, r.stats, r.totals, r.batch_gain, r.kernels, r.dn, r.dm, r.x, emit, r.kgrad, r.padx, r.padd, r.ksum)
    for k, piece in enumerate((r.o0, r.o1, r.o2, r.o3)):
        h0, w0 = corner(tile, k)
        piece[...] = r.du[pl.ds(h0, TS), pl.ds(w0, TS)].reshape(PIECE, -1).astype(BF16)


def unpack_body(r):
    index = r.index[0]
    channels = r.up.shape[0]
    hidden = r.up.shape[1]
    lanes = r.near.shape[-1]
    size = r.near.shape[1]
    per = channels // size
    flip = index & (BLOCKS // 2 - 1)
    own = (index >> (BLOCKS.bit_length() - 2)) & 1

    def put(value, quarter, row):
        lo = 0
        while lo < lanes:
            base = quarter * lanes + lo
            if base < hidden:
                ref, lane, end = r.up, base, hidden
            elif base < 2 * hidden:
                ref, lane, end = r.down, base - hidden, hidden
            else:
                ref, lane, end = r.unite, base - 2 * hidden, 3 * channels
            if lane >= end:
                break
            step = min(end - lane, lanes - lo)
            ref[row : row + size, lane : lane + step] = value[:, lo : lo + step]
            lo += step

    for p in range(BLOCKS):
        low = p & (BLOCKS // 2 - 1)
        high = p // (BLOCKS // 2)
        place = low ^ flip
        value = jnp.where(own == high, r.near[place].astype(F32), r.far[place].astype(F32))
        put(value, p // per, (p % per) * size)


def kernel_finish(r):
    channels = r.last.shape[-1]
    for layer, total in enumerate((r.total0, r.total1)):
        one = slice(layer, layer + 1)
        r.batch_shift[one] = total[0:1]
        r.batch_gain[one] = total[1:2]
        r.norm_gain[one] = total[2:3]
        r.norm_shift[one] = total[3:4]
        r.down_bias[one] = total[4:5]
        r.unite_bias[one] = total[5:6]
        for i in range(r.up_bias.shape[-1] // channels):
            r.up_bias[one, i * channels : (i + 1) * channels] = total[6 + i : 7 + i]
        for i in range(9):
            r.kernel[i // 3, i % 3, one] = r.last[16 * layer + i : 16 * layer + i + 1]
        base = 32 + 16 * layer
        r.mix[layer] = r.last[base : base + 16]


class Kept:
    def __init__(self, array):
        self.array = array


class Smem:
    def __init__(self, array):
        self.array = array


class Layer:
    def __init__(self, array, layer):
        self.array, self.layer = array, layer


class Late:
    def __init__(self, array, layer=None):
        self.array, self.layer = array, layer

    @property
    def shape(self):
        return self.array.shape if self.layer is None else self.array.shape[1:]

    @property
    def parts(self):
        return MAP // 2 if self.shape[0] == MAP else 1


class LateRef:
    def __init__(self, late, source, ref, sems):
        self.parts = late.parts
        self.source = source if late.layer is None else source.at[late.layer]
        self.ref, self.sems = ref, sems

    def copy(self, c):
        if self.parts == 1:
            return pltpu.make_async_copy(self.source, self.ref, self.sems.at[0])
        rows = pl.ds(2 * c, 2)
        return pltpu.make_async_copy(self.source.at[rows], self.ref.at[rows], self.sems.at[c])

    def start(self):
        for c in range(self.parts):
            self.copy(c).start()

    def wait(self, c):
        self.copy(c).wait()

    def wait_all(self):
        for c in range(self.parts):
            self.copy(c).wait()


class Stream:
    def __init__(self, out):
        self.out = out


class Place:
    def __init__(self, out):
        self.out = out


class StreamRef:
    def __init__(self, target, ref, sem):
        self.target, self.ref, self.sem = target, ref, sem

    def send(self, c):
        rows = pl.ds(2 * c, 2)
        pltpu.make_async_copy(self.ref.at[rows], self.target.at[rows], self.sem).start()

    def send_all(self):
        pltpu.make_async_copy(self.ref, self.target, self.sem).start()

    def finish(self):
        pltpu.make_async_copy(self.ref, self.target, self.sem).wait()


class PlaceRef:
    def __init__(self, target, sem):
        self.target, self.sem = target, sem

    def start(self, source):
        self.copy = pltpu.make_async_copy(source, self.target, self.sem)
        self.copy.start()

    def finish(self):
        self.copy.wait()


class Held:
    def __init__(self, ref):
        self.ref = ref


class Refs:
    pass


def full(array):
    rank = len(array.shape)
    return pl.BlockSpec(array.shape, lambda i: (0,) * rank)


ANY = pl.BlockSpec(memory_space=pl.ANY)


def run(body, name, flops, ins, outs, scratch=None, aliases=None):
    scratch = dict(scratch or {})
    arrays, in_specs, out_specs, out_shapes, spaces = [], [], [], [], []
    for key, operand in ins.items():
        if isinstance(operand, Smem):
            in_specs.append(pl.BlockSpec(memory_space=pltpu.SMEM))
        elif isinstance(operand, Layer):
            shape, layer = operand.array.shape, operand.layer
            in_specs.append(pl.BlockSpec((None,) + shape[1:], lambda i, layer=layer, rank=len(shape): (layer,) + (0,) * (rank - 1)))
        elif isinstance(operand, Kept):
            in_specs.append(ANY)
        elif isinstance(operand, Late):
            in_specs.append(ANY)
            spaces += [pltpu.VMEM(operand.shape, operand.array.dtype), pltpu.SemaphoreType.DMA((operand.parts,))]
        else:
            in_specs.append(full(operand))
        arrays.append(getattr(operand, "array", operand))
    for key, out in outs.items():
        if isinstance(out, (Stream, Place)):
            out_specs.append(ANY)
            out_shapes.append(out.out)
            if isinstance(out, Stream):
                spaces.append(pltpu.VMEM(out.out.shape, out.out.dtype))
            spaces.append(pltpu.SemaphoreType.DMA)
        elif isinstance(out, Layer):
            shape, layer = out.array.shape, out.layer
            out_specs.append(pl.BlockSpec((None,) + shape[1:], lambda i, layer=layer, rank=len(shape): (layer,) + (0,) * (rank - 1)))
            out_shapes.append(out.array)
        else:
            out_specs.append(full(out))
            out_shapes.append(out)
    spaces += list(scratch.values())

    def wrapped(*refs):
        refs = list(refs)
        r = Refs()
        main, extra = refs[: len(ins) + len(outs)], refs[len(ins) + len(outs) :]
        late, streams = [], []
        for key, operand in ins.items():
            ref = main.pop(0)
            if isinstance(operand, Late):
                ref = LateRef(operand, ref, extra.pop(0), extra.pop(0))
                late.append(ref)
            setattr(r, key, ref)
        for key, out in outs.items():
            ref = main.pop(0)
            if isinstance(out, Stream):
                ref = StreamRef(ref, extra.pop(0), extra.pop(0))
                streams.append(ref)
            elif isinstance(out, Place):
                ref = PlaceRef(ref, extra.pop(0))
                streams.append(ref)
            setattr(r, key, ref)
        for key in scratch:
            setattr(r, key, extra.pop(0))
        for part in late:
            part.start()
        body(r)
        for stream in streams:
            stream.finish()

    size = sum(a.size * a.dtype.itemsize for a in arrays) + sum(o.size * o.dtype.itemsize for o in out_shapes)
    results = pl.pallas_call(
        wrapped,
        grid=(1,),
        in_specs=in_specs,
        out_specs=out_specs,
        out_shape=out_shapes,
        scratch_shapes=spaces,
        input_output_aliases=aliases or {},
        compiler_params=pltpu.CompilerParams(vmem_limit_bytes=VMEM_BYTES),
        cost_estimate=pl.CostEstimate(flops=flops, bytes_accessed=size, transcendentals=0),
        name=name,
    )(*arrays)
    named = Refs()
    for key, value in zip(outs, results):
        setattr(named, key, value)
    return named


def on_device(
    patches,
    conv_kernel,
    batch_gain,
    batch_shift,
    mix_width,
    mix_width_bias,
    mix_height,
    mix_height_bias,
    unite_weight,
    unite_bias,
    norm_gain,
    norm_shift,
    up_weight,
    up_bias,
    down_weight,
    down_bias,
    cotangent,
):
    channels = patches.shape[-1]
    hidden = up_weight.shape[-1]
    tile = lax.axis_index("tile")
    tile_arg = Smem(tile.astype(jnp.int32).reshape(1))
    index_arg = Smem(block_index().reshape(1))
    local_cells = MAP * ROW
    cells = local_cells * lax.axis_size("dp") * lax.axis_size("tile")

    def rows(lanes, dtype):
        return jax.ShapeDtypeStruct((MAP, ROW, lanes), dtype)

    def shape(*dims, dtype=F32):
        return jax.ShapeDtypeStruct(dims, dtype)

    def vmem(struct):
        return pltpu.VMEM(struct.shape, struct.dtype)

    piece = shape(PIECE, channels, dtype=BF16)
    c_bf, c_f32, h_bf = rows(channels, BF16), rows(channels, F32), rows(hidden, BF16)
    map4 = pltpu.VMEM((MAP, MAP, IMG, channels), F32)
    pad = pltpu.VMEM((MAP + 2, MAP + 2, IMG, channels), F32)
    sums = pltpu.VMEM((2, 8, channels), F32)
    small = pltpu.VMEM((6, 8, channels), F32)
    upsum = pltpu.VMEM((8, hidden), F32)
    ksum = pltpu.VMEM((9, 8, channels), F32)
    lanes = (2 * hidden + 1024) // 4
    block_rows = 4 * channels // BLOCKS
    half = shape(BLOCKS // 2, block_rows, lanes, dtype=BF16)
    buf = pltpu.VMEM((BLOCKS, block_rows, lanes), BF16)

    kernels = conv_kernel.transpose(1, 2, 0, 3)
    down_t = down_weight.transpose(0, 2, 1)
    mwb = jnp.repeat(mix_width_bias, IMG, axis=1)[:, :, None]
    mhb = jnp.repeat(mix_height_bias, 16, axis=1)[:, :, None]
    mwt, mht = mix_width.transpose(0, 2, 1), mix_height.transpose(0, 2, 1)

    x_pieces = to_whole(patches[:, 0].transpose(1, 2, 0, 3), tile)
    prepared = [unite_weight, mix_width, mix_height, mwt, mht, mwb, mhb]
    *x_pieces, unite_weight, mix_width, mix_height, mwt, mht, mwb, mhb = tie(*x_pieces, *prepared)
    first = run(
        kernel_first,
        "conv_first",
        10**7,
        dict(tile=tile_arg, **{f"p{k}": x_pieces[k] for k in range(4)}, kernels=kernels),
        dict(x=c_bf, a=c_f32, stats=shape(2, channels)),
        dict(pad=pad, sums=sums),
    )
    stats0 = total_moments(first.stats, float(local_cells))
    stats0, cotangent = tie(stats0, cotangent)
    cot_pieces = to_whole(cotangent[:, 0].transpose(1, 2, 0, 3), tile)

    def forward_ins(layer):
        return dict(
            batch_gain=batch_gain, batch_shift=batch_shift, mix_width=mix_width, mwb=mwb, mix_height=mix_height, mhb=mhb,
            unite=Late(unite_weight, layer), up=Late(up_weight, layer), down=Late(down_t, layer),
            unite_bias=unite_bias, norm_gain=norm_gain, norm_shift=norm_shift, up_bias=up_bias, down_bias=down_bias,
        )

    fwd = run(
        lambda r: kernel_forward(cells, r),
        "block_forward",
        6 * 10**9,
        dict(a=Late(first.a), stats=stats0, **forward_ins(0), x=Late(first.x), kernels=kernels),
        dict(
            nb=Stream(c_bf), pw=Stream(c_bf), ph=Stream(c_bf), zhat=Stream(c_f32), s=Stream(rows(1, F32)), zb=Stream(c_bf),
            g=Stream(h_bf), d=Stream(h_bf), u=Stream(c_f32), a2=Stream(c_f32), stats2=shape(2, channels),
        ),
        dict(pad=pad, sums=sums),
    )
    stats1, *cot_pieces = tie(fwd.stats2, *cot_pieces)
    stats1 = total_moments(stats1, float(local_cells))

    turn = run(
        lambda r: kernel_turn(cells, r),
        "block_turn",
        14 * 10**9,
        dict(
            tile=tile_arg, index=index_arg, a=Late(fwd.a2), stats=stats1, u=Late(fwd.u), **{f"c{k}": Late(cot_pieces[k]) for k in range(4)},
            **forward_ins(1), mwt=mwt, mht=mht,
        ),
        dict(
            **{f"f{k}": Stream(piece) for k in range(4)}, dm=Stream(c_f32), dn=Stream(c_f32), small_out=shape(16, channels), mix=shape(16, channels),
            mine=Place(half), sent=Place(half),
        ),
        dict(
            nb=vmem(c_bf), pw=vmem(c_bf), ph=vmem(c_bf), zb=vmem(c_bf), g=vmem(h_bf), do=vmem(c_bf), dh=vmem(h_bf), df=vmem(c_bf), dpw=vmem(c_bf), dph=vmem(c_bf),
            cot=map4, d=pltpu.VMEM((2, ROW, hidden), BF16), small=small, upsum=upsum, buf=buf,
        ),
    )
    features = [turn.f0, turn.f1, turn.f2, turn.f3]

    got = flat_partner(turn.sent, masks(GROUPS[0])[0])
    total1 = total_sum(turn.small_out)
    part1 = narrow_add([turn.mine, got])
    total1, part1 = tie(total1, part1)
    mid = run(
        lambda r: kernel_conv_middle(cells, r),
        "conv_middle",
        2 * 10**9,
        dict(a=Late(fwd.a2), dn=Late(turn.dn), x=Late(fwd.u), dm=Late(turn.dm), stats=stats1, totals=total1, kernels=kernels, batch_gain=batch_gain),
        dict(du=Stream(c_f32), kgrad=shape(16, channels)),
        dict(padx=pad, padd=pad, ksum=ksum),
    )
    part1 = scatter_stage(part1, GROUPS[1])
    du, part1, *features = tie(mid.du, part1, *features)
    back = run(
        kernel_mlp_back,
        "mlp_back",
        10 * 10**9,
        dict(
            index=index_arg, down=Late(down_t, 0), du=Late(du), d=Late(fwd.d), up=Late(up_weight, 0), zhat=Late(fwd.zhat), s=Late(fwd.s), unite=Late(unite_weight, 0), norm_gain=norm_gain,
            zb=Late(fwd.zb), g=Late(fwd.g), nb=Late(fwd.nb), pw=Late(fwd.pw), ph=Late(fwd.ph),
        ),
        dict(
            dm=Stream(c_f32), dn=Stream(c_f32), dpw=Stream(c_bf), dph=Stream(c_bf), small_out=shape(16, channels), mix=shape(16, channels), mine=Place(half), sent=Place(half),
        ),
        dict(do=vmem(c_bf), dh=vmem(h_bf), df=vmem(c_bf), small=small, upsum=upsum, buf=buf),
    )
    features_out = to_tiled(features, tile)
    part1 = extra_sum(scatter_stage(part1, GROUPS[2]))
    dn, features_out, part1 = tie(back.dn, features_out, part1)
    mixed = run(
        lambda r: kernel_mix_back(cells, r),
        "mix_back",
        2 * 10**9,
        dict(dph=Late(back.dph), dn_in=Late(dn), dpw=Late(back.dpw), a=Late(first.a), stats=stats0, mwt=mwt, mht=mht, small_in=back.small_out),
        dict(dn=Stream(c_f32), small_out=shape(16, channels)),
        dict(small=small),
    )
    part1 = gather_stage(part1, GROUPS[2])
    part0 = narrow_add([back.mine, flat_partner(back.sent, masks(GROUPS[0])[0])])
    small0, part0, part1 = tie(mixed.small_out, part0, part1)
    total0, (part0, part1) = total_sum(small0, [part0, part1])
    part0 = scatter_stage(part0, GROUPS[1])
    part1 = gather_stage(part1, GROUPS[1])
    last = run(
        lambda r: kernel_last(cells, r),
        "conv_last",
        2 * 10**9,
        dict(tile=tile_arg, a=Late(first.a), dn=Late(mixed.dn), x=Late(first.x), dm=Late(back.dm), stats=stats0, totals=total0, kernels=kernels, batch_gain=batch_gain),
        dict(kgrad=shape(16, channels), **{f"o{k}": piece for k in range(4)}),
        dict(padx=pad, padd=pad, ksum=ksum, du=map4),
    )
    kgrad0, part0, part1 = tie(last.kgrad, part0, part1)
    last_small = total_sum(jnp.concatenate([kgrad0, mid.kgrad, back.mix, turn.mix], 0))
    grads = to_tiled([last.o0, last.o1, last.o2, last.o3], tile)

    far1 = flat_partner(part1, masks(GROUPS[0])[0])
    part0 = extra_sum(scatter_stage(part0, GROUPS[2]))
    part0 = gather_stage(part0, GROUPS[2])
    part0 = gather_stage(part0, GROUPS[1])
    far0 = flat_partner(part0, masks(GROUPS[0])[0])

    grad_shapes = dict(up=shape(2, channels, hidden), down=shape(2, channels, hidden), unite=shape(2, channels, 3 * channels))
    whole = run(
        unpack_body,
        "unpack_1",
        10**7,
        dict(index=index_arg, near=part1, far=far1),
        {key: Layer(value, 1) for key, value in grad_shapes.items()},
    )
    whole = run(
        unpack_body,
        "unpack_0",
        10**7,
        dict(index=index_arg, near=part0, far=far0, up_in=Kept(whole.up), down_in=Kept(whole.down), unite_in=Kept(whole.unite)),
        {key: Layer(value, 0) for key, value in grad_shapes.items()},
        aliases={3: 0, 4: 1, 5: 2},
    )
    line = shape(2, channels)
    fin = run(
        kernel_finish,
        "finish",
        10**6,
        dict(total0=total0, total1=total1, last=last_small),
        dict(
            batch_shift=line, batch_gain=line, norm_gain=line, norm_shift=line, down_bias=line, unite_bias=line, up_bias=shape(2, hidden),
            kernel=shape(3, 3, 2, channels), mix=shape(2, 16, channels),
        ),
    )

    def to_output(field):
        return field.transpose(2, 0, 1, 3)[:, None]

    mixes = fin.mix[:, :MAP]
    return (
        to_output(features_out),
        to_output(grads),
        fin.kernel.transpose(2, 0, 1, 3),
        fin.batch_gain,
        fin.batch_shift,
        mixes[:, :, 0:MAP],
        mixes[:, :, 256],
        mixes[:, :, 128 : 128 + MAP],
        mixes[:, :, 257],
        whole.unite.transpose(0, 2, 1),
        fin.unite_bias,
        fin.norm_gain,
        fin.norm_shift,
        whole.up,
        fin.up_bias,
        whole.down.transpose(0, 2, 1),
        fin.down_bias,
    )


def solution(mesh):
    field = P("dp", "tile", None, None, None)
    return jax.shard_map(
        on_device,
        mesh=mesh,
        in_specs=(field,) + (P(),) * 15 + (field,),
        out_specs=(field, field) + (P(),) * 15,
        check_vma=False,
    )
```

```python
import math

import jax
import jax.numpy as jnp
from jax import lax
from jax.experimental import pallas as pl
from jax.experimental.pallas import tpu as pltpu
from jax.sharding import PartitionSpec as P

F32 = jnp.float32
BF16 = jnp.bfloat16
norm_epsilon = 1e-05
layer_epsilon = 1e-06
ROOT_HALF = 0.7071067811865476
INV_ROOT_TAU = 0.3989422804014327
LOG2E = 1.4426950408889634

TS = 7
MAP = 14
IMG = 8
ROW = MAP * IMG
PIECE = TS * TS * IMG
VMEM_BYTES = 58 * 1024 * 1024
MARGIN = 8 * 1024 * 1024
BLK = 256


def partner(x, axis, distance):
    count = lax.axis_size(axis)
    return lax.ppermute(x, axis, [(i, i ^ distance) for i in range(count)])


def stages():
    result = [("tile", (1, 2, 3))]
    count = lax.axis_size("dp")
    step = 1
    if count > 1 and (count.bit_length() - 1) % 2 == 1:
        result.append(("dp", (1,)))
        step = 2
    while step < count:
        result.append(("dp", (step, 2 * step, 3 * step)))
        step *= 4
    return result


def total_sum(x, after=None, when=2):
    for step, (axis, distances) in enumerate(stages()):
        if step == when and after is not None:
            x, *after = tie(x, *after)
        got = [partner(x, axis, d) for d in distances]
        if len(got) == 1:
            x = x + got[0]
        else:
            x = (x + got[0]) + (got[1] + got[2])
    return x if after is None else (x, after)


def total_moments(stats, count, after=None):
    for step, (axis, distances) in enumerate(stages()):
        if step == 2 and after is not None:
            stats, *after = tie(stats, *after)
        parts = [stats] + [partner(stats, axis, d) for d in distances]
        if len(parts) == 2:
            mean = (parts[0][0] + parts[1][0]) * 0.5
            dev = [jnp.square(p[0] - mean) for p in parts]
            square = (parts[0][1] + parts[1][1]) + count * (dev[0] + dev[1])
        else:
            mean = ((parts[0][0] + parts[1][0]) + (parts[2][0] + parts[3][0])) * 0.25
            dev = [jnp.square(p[0] - mean) for p in parts]
            square = ((parts[0][1] + parts[1][1]) + (parts[2][1] + parts[3][1])) + count * (
                (dev[0] + dev[1]) + (dev[2] + dev[3])
            )
        count = count * len(parts)
        stats = jnp.stack([mean, square])
    return stats if after is None else (stats, after)


def to_whole(field, tile):
    share = field.shape[2] // lax.axis_size("tile")
    pieces = []
    for k in range(4):
        part = lax.dynamic_slice_in_dim(field, (tile ^ k) * share, share, 2)
        part = part.reshape(TS * TS * share, field.shape[3])
        pieces.append(part if k == 0 else partner(part, "tile", k))
    return pieces


def swap_pieces(pieces):
    return [pieces[0]] + [partner(pieces[k], "tile", k) for k in range(1, 4)]


def join_pieces(pieces, tile):
    channels = pieces[0].shape[-1]
    share = pieces[0].shape[0] // (TS * TS)
    result = jnp.zeros((TS, TS, share * lax.axis_size("tile"), channels), pieces[0].dtype)
    for k in range(4):
        part = pieces[k].reshape(TS, TS, share, channels)
        result = lax.dynamic_update_slice_in_dim(result, part, (tile ^ k) * share, 2)
    return result


def flat_partner(x, mask):
    axes = ("dp", "tile")
    count = lax.axis_size("dp") * lax.axis_size("tile")
    return lax.ppermute(x, axes, [(i, i ^ mask) for i in range(count)])


GROUPS = ((0,), (1, 2), (3, 4))
BLOCKS = 32


def block_index():
    flat = lax.axis_index("dp") * lax.axis_size("tile") + lax.axis_index("tile")
    index = jnp.zeros((), jnp.int32)
    for group in GROUPS:
        for bit in group:
            index = index * 2 + ((flat >> bit) & 1)
    return index


def masks(group):
    if len(group) == 1:
        return [1 << group[0]]
    return [1 << group[1], 1 << group[0], (1 << group[0]) | (1 << group[1])]


def narrow_add(parts):
    parts = [p.astype(F32) for p in parts]
    total = parts[0] + parts[1]
    if len(parts) == 4:
        total = total + (parts[2] + parts[3])
    return total.astype(BF16)


def scatter_stage(x, group):
    wide = masks(group)
    size = x.shape[0] // (len(wide) + 1)
    got = [flat_partner(x[(j + 1) * size : (j + 2) * size], mask) for j, mask in enumerate(wide)]
    return narrow_add([x[:size]] + got)


def extra_sum(x):
    count = lax.axis_size("dp") * lax.axis_size("tile")
    mask = BLOCKS
    while mask < count:
        x = narrow_add([x, flat_partner(x, mask)])
        mask *= 2
    return x


def gather_stage(x, group):
    return jnp.concatenate([x] + [flat_partner(x, mask) for mask in masks(group)], 0)


def tie(*values):
    return lax.optimization_barrier(values)


def dot(a, b):
    return lax.dot_general(a, b, (((1,), (0,)), ((), ())), preferred_element_type=F32)


def dot_nt(a, b):
    return lax.dot_general(a, b, (((1,), (1,)), ((), ())), preferred_element_type=F32)


def dot_tn(a, b):
    return lax.dot_general(a, b, (((0,), (0,)), ((), ())), preferred_element_type=F32)


def spread(ref, layer, repeat, turned=False):
    matrix = ref[...].astype(F32)[:, layer, :].astype(BF16)
    size = MAP * repeat
    shift = repeat.bit_length() - 1
    row = lax.broadcasted_iota(jnp.int32, (size, MAP), 0)
    col = lax.broadcasted_iota(jnp.int32, (size, MAP), 1)
    pick = jnp.where((row >> shift) == col, 1.0, 0.0).astype(BF16)
    half = dot_nt(pick, matrix) if turned else dot(pick, matrix)
    wide = dot_nt(half.astype(BF16), pick)
    row = lax.broadcasted_iota(jnp.int32, (size, size), 0)
    col = lax.broadcasted_iota(jnp.int32, (size, size), 1)
    return jnp.where((row & (repeat - 1)) == (col & (repeat - 1)), wide, 0.0).astype(BF16)


def spread_bias(ref, layer, repeat):
    size = MAP * repeat
    shift = repeat.bit_length() - 1
    row = lax.broadcasted_iota(jnp.int32, (size, MAP), 0)
    col = lax.broadcasted_iota(jnp.int32, (size, MAP), 1)
    return jnp.sum(jnp.where((row >> shift) == col, ref[layer : layer + 1], 0.0), axis=1, keepdims=True)


def collapse(product, repeat):
    size = MAP * repeat
    shift = repeat.bit_length() - 1
    row = lax.broadcasted_iota(jnp.int32, (size, size), 0)
    col = lax.broadcasted_iota(jnp.int32, (size, size), 1)
    kept = jnp.where((row & (repeat - 1)) == (col & (repeat - 1)), product, 0.0)
    kept = jnp.sum(kept.reshape(MAP, repeat, size), axis=1)
    row = lax.broadcasted_iota(jnp.int32, (size, MAP), 0)
    col = lax.broadcasted_iota(jnp.int32, (size, MAP), 1)
    pick = jnp.where((row >> shift) == col, 1.0, 0.0).astype(F32)
    return lax.dot_general(
        kept, pick, (((1,), (0,)), ((), ())), preferred_element_type=F32, precision=lax.Precision.HIGHEST
    )


def lane_groups(channels):
    return [(lo, min(lo + 128, channels)) for lo in range(0, channels, 128)]


def zero_border(pad):
    shape = pad.shape
    pad[0] = jnp.zeros(shape[1:], F32)
    pad[MAP + 1] = jnp.zeros(shape[1:], F32)
    for h in range(1, MAP + 1):
        pad[h, 0] = jnp.zeros(shape[2:], F32)
        pad[h, MAP + 1] = jnp.zeros(shape[2:], F32)


def pick_columns(field, w0):
    return jnp.where(w0 == 0, field[:, :TS], field[:, TS:])


def corner(tile, k):
    other = tile ^ k
    return (other >> 1) * TS, (other & 1) * TS


def conv_rows(pad, kernel_ref, layer, out_ref, stats_ref, sums):
    channels = pad.shape[-1]
    sums[...] = jnp.zeros(sums.shape, F32)

    def body(h, carry):
        for lo, hi in lane_groups(channels):
            acc = None
            for r in range(3):
                for s in range(3):
                    term = pad[h + r, s : s + MAP, :, lo:hi] * kernel_ref[r, s, layer : layer + 1, lo:hi]
                    acc = term if acc is None else acc + term
            out_ref[h, :, lo:hi] = acc.reshape(ROW, hi - lo)
            sums[0, :, lo:hi] += jnp.sum(acc, axis=0)
        return carry

    lax.fori_loop(0, MAP, body, 0)
    count = MAP * ROW
    mean = jnp.sum(sums[0], axis=0, keepdims=True) * (1.0 / count)

    def again(h, carry):
        for lo, hi in lane_groups(channels):
            dev = out_ref[h, :, lo:hi] - mean[:, lo:hi]
            sums[1, :, lo:hi] += jnp.sum((dev * dev).reshape(MAP, IMG, hi - lo), axis=0)
        return carry

    lax.fori_loop(0, MAP, again, 0)
    stats_ref[0:1] = mean
    stats_ref[1:2] = jnp.sum(sums[1], axis=0, keepdims=True)


def scale_of(stats_ref, cells):
    mean = stats_ref[0:1]
    return mean, lax.rsqrt(stats_ref[1:2] * (1.0 / cells) + norm_epsilon)


def mix_forward(layer, cells, a_ref, stats_ref, gain_ref, shift_ref, mw_ref, mwb_ref, mh_ref, mhb_ref, nb, pw, ph):
    mean, rstd = scale_of(stats_ref, cells)
    gain = gain_ref[layer : layer + 1]
    shift = shift_ref[layer : layer + 1]
    width = spread(mw_ref, layer, IMG)
    height = spread(mh_ref, layer, 16)
    width_bias = spread_bias(mwb_ref, layer, IMG)
    height_bias = spread_bias(mhb_ref, layer, 16)

    def body(h, carry):
        value = (((a_ref[h] - mean) * rstd) * gain + shift).astype(BF16)
        nb[h] = value
        pw[h] = (dot(width, value) + width_bias).astype(BF16)
        return carry

    lax.fori_loop(0, MAP, body, 0)
    for j in range(ROW // 16):
        value = nb[:, 16 * j : 16 * j + 16, :].reshape(MAP * 16, -1)
        mixed = (dot(height, value) + height_bias).astype(BF16)
        ph[:, 16 * j : 16 * j + 16, :] = mixed.reshape(MAP, 16, -1)


def gelu_pair(v):
    t = 1.0 / (1.0 + (0.3275911 * ROOT_HALF) * jnp.abs(v))
    e = jnp.exp2(v * v * (-0.5 * LOG2E))
    q = ((((0.5 * 1.061405429 * t - 0.5 * 1.453152027) * t + 0.5 * 1.421413741) * t - 0.5 * 0.284496736) * t + 0.5 * 0.254829592) * t * e
    phi = jnp.where(v >= 0, 1.0 - q, q)
    return v * phi, phi + v * e * INV_ROOT_TAU


HALVES = 2
PART = MAP // HALVES


def half_rows(ref, p):
    value = ref[p * PART : (p + 1) * PART]
    return value.reshape(PART * ROW, value.shape[-1])


def put_half(ref, p, value):
    ref[p * PART : (p + 1) * PART] = value.reshape(PART, ROW, value.shape[-1])


def add_half(ref, p, value):
    ref[p * PART : (p + 1) * PART] += value.reshape(PART, ROW, value.shape[-1])


def column_sums(value):
    return jnp.sum(value.reshape(-1, 8, value.shape[-1]), axis=0)


def unite_norm(r, layer, p, residual):
    one = slice(layer, layer + 1)
    channels = residual.shape[-1]
    m = residual + r.unite_bias[one]
    for i, part in enumerate((r.nb, r.pw, r.ph)):
        m = m + dot(half_rows(part.ref, p), r.unite[i * channels : (i + 1) * channels])
    centre = jnp.mean(m, axis=-1, keepdims=True)
    dev = m - centre
    s = lax.rsqrt(jnp.mean(dev * dev, axis=-1, keepdims=True) + layer_epsilon)
    zhat = dev * s
    zb = (zhat * r.norm_gain[one] + r.norm_shift[one]).astype(BF16)
    return m, zhat, s, zb


def hidden_block(r, layer, j):
    blk = pl.ds(pl.multiple_of(j * BLK, BLK), BLK)
    return blk, r.up.ref[:, blk], r.down.ref[:, blk]


def block_half(value):
    return value.reshape(PART, ROW, BLK)


def norm_backward(r, layer, p, do32, zhat, s, dz, df_ref):
    one = slice(layer, layer + 1)
    channels = do32.shape[-1]
    e = dz * r.norm_gain[one]
    mean_e = jnp.mean(e, axis=-1, keepdims=True)
    mean_ez = jnp.mean(e * zhat, axis=-1, keepdims=True)
    dm = do32 + s * (e - mean_e - zhat * mean_ez)
    put_half(r.dm.ref, p, dm)
    df = dm.astype(BF16)
    put_half(df_ref, p, df)
    r.small[2] += column_sums(dz * zhat)
    r.small[3] += column_sums(dz)
    r.small[4] += column_sums(do32)
    r.small[5] += column_sums(dm)
    put_half(r.dn.ref, p, dot_nt(df, r.unite[0:channels]))
    put_half(r.dpw, p, dot_nt(df, r.unite[channels : 2 * channels]).astype(BF16))
    put_half(r.dph, p, dot_nt(df, r.unite[2 * channels : 3 * channels]).astype(BF16))


GROUP_LANES = 128
PER_QUARTER = 7


def put_group(r, q, value):
    size = r.buf.shape[2]
    count = value.shape[0] // size
    quarter = q // PER_QUARTER if isinstance(q, int) else lax.div(q, PER_QUARTER)
    lane = q - quarter * PER_QUARTER
    for b in range(count):
        r.buf[(quarter * count + b) ^ r.index[0], lane] = value[b * size : (b + 1) * size].astype(BF16)


def put_columns(r, q, value):
    for i in range(value.shape[-1] // GROUP_LANES):
        put_group(r, q + i, value[:, i * GROUP_LANES : (i + 1) * GROUP_LANES])


def flat_rows(value):
    return value.reshape(MAP * ROW, value.shape[-1])


def hidden_gradients(r, j, blocks, zb, do, g, dh):
    per = BLK // GROUP_LANES
    put_columns(r, per * j, dot_tn(flat_rows(zb[...]), dh))
    put_columns(r, per * (j + blocks), dot_tn(flat_rows(do[...]), g))


def mix_backward(layer, cells, a_ref, stats_ref, mw_ref, mh_ref, dpw, dph, dn_ref, small, then=None):
    mean, rstd = scale_of(stats_ref, cells)
    width = spread(mw_ref, layer, IMG, turned=True)
    height = spread(mh_ref, layer, 16, turned=True)
    for j in range(ROW // 16):
        cols = slice(16 * j, 16 * j + 16)
        value = dph[:, cols, :].reshape(MAP * 16, -1)
        dn_ref[:, cols, :] += dot(height, value).reshape(MAP, 16, -1)

    def body(h, carry):
        dn = dn_ref[h] + dot(width, dpw[h])
        dn_ref[h] = dn
        xhat = (a_ref[h] - mean) * rstd
        small[0] += jnp.sum(dn.reshape(MAP, IMG, -1), axis=0)
        small[1] += jnp.sum((dn * xhat).reshape(MAP, IMG, -1), axis=0)
        if then is not None:
            then(h)
        return carry

    lax.fori_loop(0, MAP, body, 0)


def unite_gradients(r, blocks, df_ref, out_ref):
    df = flat_rows(df_ref[...])
    channels = df.shape[-1]
    nb, dpw, dph = r.nb.ref, r.dpw, r.dph
    parts = [dot_tn(df, flat_rows(part.ref[...])) for part in (r.nb, r.pw, r.ph)]
    lanes = -(-3 * channels // GROUP_LANES) * GROUP_LANES
    whole = jnp.concatenate(parts + [jnp.zeros((channels, lanes - 3 * channels), F32)], axis=1)
    put_columns(r, 2 * blocks * (BLK // GROUP_LANES), whole)

    wide = jnp.zeros((ROW, ROW), F32)
    bias = jnp.zeros((ROW, channels), F32)
    for h in range(MAP):
        wide = wide + dot_nt(dpw[h], nb[h])
        bias = bias + dpw[h].astype(F32)
    tall = jnp.zeros((MAP * 16, MAP * 16), F32)
    tall_bias = jnp.zeros((MAP, 16, channels), F32)
    for j in range(ROW // 16):
        cols = slice(16 * j, 16 * j + 16)
        value = dph[:, cols, :]
        tall = tall + dot_nt(value.reshape(MAP * 16, channels), nb[:, cols, :].reshape(MAP * 16, channels))
        tall_bias = tall_bias + value.astype(F32)
    diagonal = lax.broadcasted_iota(jnp.int32, (MAP, MAP), 0) == lax.broadcasted_iota(jnp.int32, (MAP, MAP), 1)

    def as_row(field):
        col = jnp.sum(jnp.sum(field, axis=1), axis=-1, keepdims=True)
        return jnp.sum(jnp.where(diagonal, col, 0.0), axis=0, keepdims=True)

    width = jnp.concatenate([collapse(wide, IMG), as_row(bias.reshape(MAP, IMG, channels))], axis=0)
    height = jnp.concatenate([collapse(tall, 16), as_row(tall_bias)], axis=0)
    for v in range(MAP + 1):
        row, lane = mix_place(v)
        out_ref[row : row + 1, lane : lane + MAP] = width[v : v + 1]
        out_ref[row : row + 1, lane + 16 : lane + 16 + MAP] = height[v : v + 1]


MIX_ROW = 10
TAPS_ROW = 12
KERNEL_ROW = 21
SMALL_ROWS = 32


def mix_place(v):
    return MIX_ROW + v // 10, 32 * (v % 10)


def put_small(out_ref, small, upsum):
    channels = out_ref.shape[-1]
    for i in range(6):
        out_ref[i : i + 1] = jnp.sum(small[i], axis=0, keepdims=True)
    up = jnp.sum(upsum[...], axis=0, keepdims=True)
    for i in range(up.shape[-1] // channels):
        out_ref[6 + i : 7 + i] = up[:, i * channels : (i + 1) * channels]


def tap_sums(value, pad, h, lo, hi, total):
    for r in range(3):
        for s in range(3):
            total[3 * r + s, :, lo:hi] += jnp.sum(value * pad[h + r, s : s + MAP, :, lo:hi], axis=0)


def put_taps(out_ref, row, total):
    for i in range(9):
        out_ref[row + i : row + i + 1] = jnp.sum(total[i], axis=0, keepdims=True)


def conv_backward(layer, cells, a, stats_ref, totals_ref, gain, kernel_ref, dn, dm, emit, padd, x=None, padx=None, ksum=None):
    mean, rstd = scale_of(stats_ref, cells)
    scale = rstd * gain[layer : layer + 1]
    shift_mean = totals_ref[0:1] * (1.0 / cells)
    gain_mean = totals_ref[1:2] * (1.0 / cells)
    channels = padd.shape[-1]
    zero_border(padd)
    if x is not None:
        zero_border(padx)
        ksum[...] = jnp.zeros(ksum.shape, F32)

    def fill(c, carry):
        for part in (a, dn) if x is None else (a, dn, x):
            part.wait(c)
        for i in range(2):
            h = 2 * c + i
            xhat = (a.ref[h] - mean) * rstd
            da = scale * (dn.ref[h] - shift_mean - xhat * gain_mean)
            padd[h + 1, 1 : MAP + 1] = da.reshape(MAP, IMG, -1)
            if x is not None:
                padx[h + 1, 1 : MAP + 1] = x.ref[h].astype(BF16).astype(F32).reshape(MAP, IMG, -1)
        return carry

    lax.fori_loop(0, MAP // 2, fill, 0)
    dm.wait_all()

    def body(h, carry):
        for lo, hi in lane_groups(channels):
            acc = dm.ref[h, :, lo:hi].reshape(MAP, IMG, hi - lo)
            da = padd[h + 1, 1 : MAP + 1, :, lo:hi]
            for r in range(3):
                for s in range(3):
                    acc = acc + padd[h + 2 - r, 2 - s : 2 - s + MAP, :, lo:hi] * kernel_ref[r, s, layer : layer + 1, lo:hi]
            if x is not None:
                tap_sums(da, padx, h, lo, hi, ksum)
            emit(h, lo, hi, acc)
        return carry

    lax.fori_loop(0, MAP, body, 0)


def fill_pad(pad, x_ref):
    def body(h, carry):
        pad[h + 1, 1 : MAP + 1] = x_ref[h].astype(F32).reshape(MAP, IMG, -1)
        return carry

    lax.fori_loop(0, MAP, body, 0)


def kernel_taps(r):
    r.x.wait_all()
    zero_border(r.pad)
    fill_pad(r.pad, r.x.ref)
    r.a.wait_all()
    mean = r.stats[0:1]
    for total in (r.alone, r.times):
        total[...] = jnp.zeros(total.shape, F32)

    def body(h, carry):
        for lo, hi in lane_groups(r.pad.shape[-1]):
            value = (r.a.ref[h, :, lo:hi] - mean[:, lo:hi]).reshape(MAP, IMG, hi - lo)
            for i in range(3):
                for s in range(3):
                    window = r.pad[h + i, s : s + MAP, :, lo:hi]
                    r.alone[3 * i + s, :, lo:hi] += jnp.sum(window, axis=0)
                    r.times[3 * i + s, :, lo:hi] += jnp.sum(value * window, axis=0)
        return carry

    lax.fori_loop(0, MAP, body, 0)
    r.out[...] = jnp.zeros(r.out.shape, F32)
    put_taps(r.out, 0, r.alone)
    put_taps(r.out, 9, r.times)
    r.out[18:19] = mean


def kernel_first(r):
    tile = r.tile[0]
    zero_border(r.pad)
    for k, piece in enumerate((r.p0, r.p1, r.p2, r.p3)):
        h0, w0 = corner(tile, k)
        value = piece[...].astype(F32).reshape(TS, TS, IMG, -1)
        r.pad[pl.ds(1 + h0, TS), pl.ds(1 + w0, TS)] = value

    def body(h, carry):
        r.x[h] = r.pad[h + 1, 1 : MAP + 1].reshape(ROW, -1).astype(BF16)
        return carry

    lax.fori_loop(0, MAP, body, 0)
    conv_rows(r.pad, r.kernels, 0, r.a, r.stats, r.sums)


def turn_unite(r):
    r.unite_t.wait_all()
    r.unite[...] = r.unite_t.ref[...].T


def forward_front(r, layer, cells):
    r.a.wait_all()
    mix_forward(layer, cells, r.a.ref, r.stats, r.batch_gain, r.batch_shift, r.mix_width, r.mix_width_bias, r.mix_height, r.mix_height_bias, r.nb.ref, r.pw.ref, r.ph.ref)


def kernel_forward(cells, r):
    forward_front(r, 0, cells)
    for out in (r.nb, r.pw, r.ph):
        out.send_all()
    turn_unite(r)
    zero_border(r.pad)
    r.x.wait_all()
    for p in range(HALVES):
        m, zhat, s, zb = unite_norm(r, 0, p, half_rows(r.x.ref, p).astype(F32))
        put_half(r.u.ref, p, m + r.down_bias[0:1])
        put_half(r.zhat.ref, p, zhat)
        put_half(r.s.ref, p, s)
        put_half(r.zb.ref, p, zb)
        for stream in (r.zhat, r.s, r.zb):
            stream.send(p)
    r.up.wait_all()
    r.down.wait_all()

    def body(j, carry):
        blk, up, down = hidden_block(r, 0, j)
        for p in range(HALVES):
            g, d = gelu_pair(dot(half_rows(r.zb.ref, p), up) + r.up_bias[0:1, blk])
            g = g.astype(BF16)
            r.g.ref[j, p * PART : (p + 1) * PART] = block_half(g)
            r.d.ref[j, p * PART : (p + 1) * PART] = block_half(d.astype(BF16))
            add_half(r.u.ref, p, dot_nt(g, down))
        r.g.send(j)
        r.d.send(j)
        return carry

    lax.fori_loop(0, r.up_bias.shape[-1] // BLK, body, 0)
    r.u.send_all()

    def fill(h, carry):
        rounded = r.u.ref[h].astype(BF16).astype(F32)
        r.pad[h + 1, 1 : MAP + 1] = rounded.reshape(MAP, IMG, -1)
        return carry

    lax.fori_loop(0, MAP, fill, 0)
    conv_rows(r.pad, r.kernels, 1, r.a2.ref, r.stats2, r.sums)
    r.a2.send_all()


def clear(r):
    r.small[...] = jnp.zeros(r.small.shape, F32)
    r.upsum[...] = jnp.zeros(r.upsum.shape, F32)


def send_blocks(r):
    half = BLOCKS // 2
    r.mine.start(r.buf.at[pl.ds(0, half)])
    r.sent.start(r.buf.at[pl.ds(half, half)])


def kernel_turn(cells, r):
    tile = r.tile[0]
    clear(r)
    for key in ("nb", "pw", "ph"):
        setattr(r, key, Held(getattr(r, key)))
    forward_front(r, 1, cells)
    turn_unite(r)
    for k, piece in enumerate((r.c0, r.c1, r.c2, r.c3)):
        piece.wait_all()
        h0, w0 = corner(tile, k)
        r.cot[pl.ds(h0, TS), pl.ds(w0, TS)] = piece.ref[...].astype(F32).reshape(TS, TS, IMG, -1)
    r.u.wait_all()

    def cotangent(p):
        return r.cot[p * PART : (p + 1) * PART].reshape(PART * ROW, -1)

    for p in range(HALVES):
        m, zhat, s, zb = unite_norm(r, 1, p, half_rows(r.u.ref, p))
        put_half(r.out, p, m + r.down_bias[1:2])
        put_half(r.zhat, p, zhat)
        put_half(r.s, p, s)
        put_half(r.zb, p, zb)
        put_half(r.do, p, cotangent(p).astype(BF16))
    r.up.wait_all()
    r.down.wait_all()
    r.dz[...] = jnp.zeros(r.dz.shape, F32)
    blocks = r.up_bias.shape[-1] // BLK

    def body(j, carry):
        blk, up, down = hidden_block(r, 1, j)
        gs, dhs = [], []
        for p in range(HALVES):
            g, d = gelu_pair(dot(half_rows(r.zb, p), up) + r.up_bias[1:2, blk])
            g = g.astype(BF16)
            add_half(r.out, p, dot_nt(g, down))
            dh = dot(half_rows(r.do, p), down) * d
            r.upsum[:, blk] += column_sums(dh)
            dh = dh.astype(BF16)
            add_half(r.dz, p, dot_nt(dh, up))
            gs.append(g)
            dhs.append(dh)
        hidden_gradients(r, j, blocks, r.zb, r.do, jnp.concatenate(gs, 0), jnp.concatenate(dhs, 0))
        return carry

    lax.fori_loop(0, blocks, body, 0)
    for k, piece in enumerate((r.f0, r.f1, r.f2, r.f3)):
        h0, w0 = corner(tile, k)
        field = r.out[pl.ds(h0, TS)].reshape(TS, MAP, IMG, -1)
        piece.ref[...] = pick_columns(field, w0).reshape(PIECE, -1).astype(BF16)
        piece.send_all()
    for p in range(HALVES):
        norm_backward(r, 1, p, cotangent(p), half_rows(r.zhat, p), half_rows(r.s, p), half_rows(r.dz, p), r.df)
        r.dm.send(p)
    mix_backward(1, cells, r.a.ref, r.stats, r.mix_width, r.mix_height, r.dpw, r.dph, r.dn.ref, r.small)
    r.dn.send_all()
    r.small_out[...] = jnp.zeros(r.small_out.shape, F32)
    put_small(r.small_out, r.small, r.upsum)
    unite_gradients(r, blocks, r.df, r.small_out)
    send_blocks(r)


def kernel_conv_middle(cells, r):
    def emit(h, lo, hi, value):
        r.du.ref[h, :, lo:hi] = value.reshape(ROW, hi - lo)

    conv_backward(1, cells, r.a, r.stats, r.totals, r.batch_gain, r.kernels, r.dn, r.dm, emit, r.padd, r.x, r.padx, r.ksum)
    r.du.send_all()
    put_taps(r.kgrad, 0, r.ksum)


def kernel_back(cells, r):
    clear(r)
    turn_unite(r)
    for part in (r.up, r.down, r.zb):
        part.wait_all()
    for p in range(HALVES):
        r.du.wait(p)
        put_half(r.do, p, half_rows(r.du.ref, p).astype(BF16))
    r.dz[...] = jnp.zeros(r.dz.shape, F32)
    blocks = r.upsum.shape[-1] // BLK

    def body(j, carry):
        blk, up, down = hidden_block(r, 0, j)
        r.d.wait(j)
        dhs = []
        for p in range(HALVES):
            d = r.d.ref[j, p * PART : (p + 1) * PART].reshape(PART * ROW, BLK).astype(F32)
            dh = dot(half_rows(r.do, p), down) * d
            r.upsum[:, blk] += column_sums(dh)
            dh = dh.astype(BF16)
            add_half(r.dz, p, dot_nt(dh, up))
            dhs.append(dh)
        r.g.wait(j)
        hidden_gradients(r, j, blocks, r.zb.ref, r.do, flat_rows(r.g.ref[j]), jnp.concatenate(dhs, 0))
        return carry

    lax.fori_loop(0, blocks, body, 0)
    r.zhat.wait_all()
    r.s.wait_all()
    for p in range(HALVES):
        norm_backward(r, 0, p, half_rows(r.du.ref, p), half_rows(r.zhat.ref, p), half_rows(r.s.ref, p), half_rows(r.dz, p), r.df)
        r.dm.send(p)
    for part in (r.nb, r.pw, r.ph):
        part.wait_all()
    r.small_out[...] = jnp.zeros(r.small_out.shape, F32)
    unite_gradients(r, blocks, r.df, r.small_out)
    send_blocks(r)
    for part in (r.a, r.x):
        part.wait_all()
    zero_border(r.pad)
    fill_pad(r.pad, r.x.ref)
    r.taps[...] = jnp.zeros(r.taps.shape, F32)

    def then(h):
        for lo, hi in lane_groups(r.pad.shape[-1]):
            tap_sums(r.dn.ref[h, :, lo:hi].reshape(MAP, IMG, hi - lo), r.pad, h, lo, hi, r.taps)

    mix_backward(0, cells, r.a.ref, r.stats, r.mix_width, r.mix_height, r.dpw, r.dph, r.dn.ref, r.small, then)
    r.dn.send_all()
    put_small(r.small_out, r.small, r.upsum)
    put_taps(r.small_out, TAPS_ROW, r.taps)
    r.small_out[KERNEL_ROW : KERNEL_ROW + 9] = r.kgrad[0:9]


def kernel_last(cells, r):
    tile = r.tile[0]

    def emit(h, lo, hi, value):
        r.du[h, :, :, lo:hi] = value

    conv_backward(0, cells, r.a, r.stats, r.totals, r.batch_gain, r.kernels, r.dn, r.dm, emit, r.padd)
    for k, piece in enumerate((r.o0, r.o1, r.o2, r.o3)):
        h0, w0 = corner(tile, k)
        piece[...] = r.du[pl.ds(h0, TS), pl.ds(w0, TS)].reshape(PIECE, -1).astype(BF16)


def unpack_put(r, value, quarter, row):
    channels, hidden = r.up.ref.shape
    rows = pl.ds(row, value.shape[1])
    for i in range(value.shape[0]):
        base = (quarter * value.shape[0] + i) * GROUP_LANES
        if base < hidden:
            ref, lane, end = r.up.ref, base, hidden
        elif base < 2 * hidden:
            ref, lane, end = r.down.ref, base - hidden, hidden
        else:
            ref, lane, end = r.unite.ref, base - 2 * hidden, 3 * channels
        step = min(GROUP_LANES, end - lane)
        ref[rows, lane : lane + step] = value[i, :, 0:step]


def unpack_all(r, block):
    channels, hidden = r.up.ref.shape
    size = 4 * channels // BLOCKS
    per = channels // size
    lanes = PER_QUARTER * GROUP_LANES
    for quarter in range(4):
        for b in range(per):
            unpack_put(r, block(quarter * per + b), quarter, b * size)
        if (quarter + 1) * lanes >= hidden and quarter * lanes < hidden:
            r.up.send_all()
        if (quarter + 1) * lanes >= 2 * hidden and quarter * lanes < 2 * hidden:
            r.down.send_all()
    r.unite.send_all()


def kernel_unpack_gathered(r):
    r.blocks.wait_all()
    bits = [bit for group in GROUPS for bit in group]

    def block(p):
        place = sum(((p >> (len(bits) - 1 - i)) & 1) << bit for i, bit in enumerate(bits))
        return r.blocks.ref[place].astype(F32)

    unpack_all(r, block)


def kernel_unpack(r):
    index = r.index[0]
    half = BLOCKS // 2
    flip = index & (half - 1)
    own = index // half
    r.near.wait_all()
    r.far.wait_all()

    def block(p):
        place = (p & (half - 1)) ^ flip
        near, far = r.near.ref[place].astype(F32), r.far.ref[place].astype(F32)
        return jnp.where(own == p // half, near, far)

    unpack_all(r, block)


def kernel_finish(cells, r):
    channels = r.total0.shape[-1]
    for layer, total in enumerate((r.total0, r.total1)):
        one = slice(layer, layer + 1)
        r.batch_shift[one] = total[0:1]
        r.batch_gain[one] = total[1:2]
        r.norm_gain[one] = total[2:3]
        r.norm_shift[one] = total[3:4]
        r.down_bias[one] = total[4:5]
        r.unite_bias[one] = total[5:6]
        for i in range(r.up_bias.shape[-1] // channels):
            r.up_bias[one, i * channels : (i + 1) * channels] = total[6 + i : 7 + i]
        for v in range(MAP + 1):
            row, lane = mix_place(v)
            width, height = total[row : row + 1, lane : lane + MAP], total[row : row + 1, lane + 16 : lane + 16 + MAP]
            if v < MAP:
                r.mix_width[v, one], r.mix_height[v, one] = width, height
            else:
                r.mix_width_bias[one], r.mix_height_bias[one] = width, height
    mean, rstd = scale_of(r.stats, cells)
    shift_mean, gain_mean = r.total0[0:1] * (1.0 / cells), r.total0[1:2] * (1.0 / cells)
    for i in range(9):
        alone, times = r.total1[TAPS_ROW + i : TAPS_ROW + i + 1], r.total1[KERNEL_ROW + i : KERNEL_ROW + i + 1]
        value = r.total0[TAPS_ROW + i : TAPS_ROW + i + 1] - shift_mean * alone - gain_mean * rstd * times
        r.kernel[i // 3, i % 3, 0:1] = rstd * r.gain[0:1] * value
        r.kernel[i // 3, i % 3, 1:2] = r.total0[KERNEL_ROW + i : KERNEL_ROW + i + 1]


class Kept:
    def __init__(self, array):
        self.array = array


class Smem:
    def __init__(self, array):
        self.array = array


class Layer:
    def __init__(self, array, layer):
        self.array, self.layer = array, layer


def chunk_step(shape, step=None):
    if len(shape) == 4 and shape[1:3] == (MAP, ROW):
        return 1
    if len(shape) == 3 and shape[:2] == (MAP, ROW):
        return step or PART
    return shape[0]


class Late:
    def __init__(self, array, layer=None, step=None):
        self.array, self.layer = array, layer
        self.step = chunk_step(self.shape, step)

    @property
    def shape(self):
        return self.array.shape if self.layer is None else self.array.shape[1:]

    @property
    def parts(self):
        return self.shape[0] // self.step


class LateRef:
    def __init__(self, late, source, ref, sems):
        self.parts, self.step = late.parts, late.step
        self.source = source if late.layer is None else source.at[late.layer]
        self.ref, self.sems = ref, sems

    def copy(self, c):
        if self.parts == 1:
            return pltpu.make_async_copy(self.source, self.ref, self.sems.at[0])
        rows = pl.ds(self.step * c, self.step)
        return pltpu.make_async_copy(self.source.at[rows], self.ref.at[rows], self.sems.at[c])

    def start(self):
        for c in range(self.parts):
            self.copy(c).start()

    def wait(self, c):
        self.copy(c).wait()

    def wait_all(self):
        for c in range(self.parts):
            self.copy(c).wait()


class Stream:
    def __init__(self, out, layer=None):
        self.out, self.layer = out, layer

    @property
    def shape(self):
        return self.out.shape if self.layer is None else self.out.shape[1:]


class Place:
    def __init__(self, out):
        self.out = out


class StreamRef:
    def __init__(self, target, ref, sem):
        self.target, self.ref, self.sem = target, ref, sem
        self.step = chunk_step(ref.shape)

    def send(self, c):
        rows = pl.ds(self.step * c, self.step)
        pltpu.make_async_copy(self.ref.at[rows], self.target.at[rows], self.sem).start()

    def send_all(self):
        pltpu.make_async_copy(self.ref, self.target, self.sem).start()

    def finish(self):
        pltpu.make_async_copy(self.ref, self.target, self.sem).wait()


class PlaceRef:
    def __init__(self, target, sem):
        self.target, self.sem = target, sem

    def start(self, source):
        self.copy = pltpu.make_async_copy(source, self.target, self.sem)
        self.copy.start()

    def finish(self):
        self.copy.wait()


class Held:
    def __init__(self, ref):
        self.ref = ref


class Refs:
    pass


def full(array):
    rank = len(array.shape)
    return pl.BlockSpec(array.shape, lambda i: (0,) * rank)


ANY = pl.BlockSpec(memory_space=pl.ANY)


def _padded(array):
    shape = list(array.shape)
    if len(shape) > 1:
        shape[-2] = -(-shape[-2] // 16) * 16
    shape[-1] = -(-shape[-1] // 128) * 128
    return math.prod(shape) * jnp.dtype(array.dtype).itemsize


def run(body, name, flops, ins, outs, scratch=None, aliases=None, tight=False):
    scratch = dict(scratch or {})
    arrays, in_specs, out_specs, out_shapes, spaces = [], [], [], [], []
    for key, operand in ins.items():
        if isinstance(operand, Smem):
            in_specs.append(pl.BlockSpec(memory_space=pltpu.SMEM))
        elif isinstance(operand, Layer):
            shape, layer = operand.array.shape, operand.layer
            in_specs.append(pl.BlockSpec((None,) + shape[1:], lambda i, layer=layer, rank=len(shape): (layer,) + (0,) * (rank - 1)))
        elif isinstance(operand, Kept):
            in_specs.append(ANY)
        elif isinstance(operand, Late):
            in_specs.append(ANY)
            spaces += [pltpu.VMEM(operand.shape, operand.array.dtype), pltpu.SemaphoreType.DMA((operand.parts,))]
        else:
            in_specs.append(full(operand))
        arrays.append(getattr(operand, "array", operand))
    for key, out in outs.items():
        if isinstance(out, (Stream, Place)):
            out_specs.append(ANY)
            out_shapes.append(out.out)
            if isinstance(out, Stream):
                spaces.append(pltpu.VMEM(out.shape, out.out.dtype))
            spaces.append(pltpu.SemaphoreType.DMA)
        elif isinstance(out, Layer):
            shape, layer = out.array.shape, out.layer
            out_specs.append(pl.BlockSpec((None,) + shape[1:], lambda i, layer=layer, rank=len(shape): (layer,) + (0,) * (rank - 1)))
            out_shapes.append(out.array)
        else:
            out_specs.append(full(out))
            out_shapes.append(out)
    spaces += list(scratch.values())

    def wrapped(*refs):
        refs = list(refs)
        r = Refs()
        main, extra = refs[: len(ins) + len(outs)], refs[len(ins) + len(outs) :]
        late, streams = [], []
        for key, operand in ins.items():
            ref = main.pop(0)
            if isinstance(operand, Late):
                ref = LateRef(operand, ref, extra.pop(0), extra.pop(0))
                late.append(ref)
            setattr(r, key, ref)
        for key, out in outs.items():
            ref = main.pop(0)
            if isinstance(out, Stream):
                ref = StreamRef(ref if out.layer is None else ref.at[out.layer], extra.pop(0), extra.pop(0))
                streams.append(ref)
            elif isinstance(out, Place):
                ref = PlaceRef(ref, extra.pop(0))
                streams.append(ref)
            setattr(r, key, ref)
        for key in scratch:
            setattr(r, key, extra.pop(0))
        for part in late:
            part.start()
        body(r)
        for stream in streams:
            stream.finish()

    held = [a for a, spec in zip(arrays + out_shapes, in_specs + out_specs) if spec is not ANY]
    held += [space for space in spaces if getattr(space, "memory_space", None) == pltpu.VMEM]
    need = sum(_padded(a) for a in held)
    limit = min(VMEM_BYTES, need + need // 4 + MARGIN) if tight else VMEM_BYTES
    size = sum(a.size * a.dtype.itemsize for a in arrays) + sum(o.size * o.dtype.itemsize for o in out_shapes)
    results = pl.pallas_call(
        wrapped,
        grid=(1,),
        in_specs=in_specs,
        out_specs=out_specs,
        out_shape=out_shapes,
        scratch_shapes=spaces,
        input_output_aliases=aliases or {},
        compiler_params=pltpu.CompilerParams(vmem_limit_bytes=limit),
        cost_estimate=pl.CostEstimate(flops=flops, bytes_accessed=size, transcendentals=0),
        name=name,
    )(*arrays)
    named = Refs()
    for key, value in zip(outs, results):
        setattr(named, key, value)
    return named


def on_device(
    patches,
    conv_kernel,
    batch_gain,
    batch_shift,
    mix_width,
    mix_width_bias,
    mix_height,
    mix_height_bias,
    unite_weight,
    unite_bias,
    norm_gain,
    norm_shift,
    up_weight,
    up_bias,
    down_weight,
    down_bias,
    cotangent,
):
    channels = patches.shape[-1]
    hidden = up_weight.shape[-1]
    tile = lax.axis_index("tile")
    tile_arg = Smem(tile.astype(jnp.int32).reshape(1))
    index_arg = Smem(block_index().reshape(1))
    local_cells = MAP * ROW
    cells = local_cells * lax.axis_size("dp") * lax.axis_size("tile")

    def rows(lanes, dtype):
        return jax.ShapeDtypeStruct((MAP, ROW, lanes), dtype)

    def shape(*dims, dtype=F32):
        return jax.ShapeDtypeStruct(dims, dtype)

    def vmem(struct):
        return pltpu.VMEM(struct.shape, struct.dtype)

    piece = shape(PIECE, channels, dtype=BF16)
    c_bf, c_f32, h_bf = rows(channels, BF16), rows(channels, F32), shape(hidden // BLK, MAP, ROW, BLK, dtype=BF16)
    map4 = pltpu.VMEM((MAP, MAP, IMG, channels), F32)
    pad = pltpu.VMEM((MAP + 2, MAP + 2, IMG, channels), F32)
    sums = pltpu.VMEM((2, 8, channels), F32)
    small = pltpu.VMEM((6, 8, channels), F32)
    upsum = pltpu.VMEM((8, hidden), F32)
    ksum = pltpu.VMEM((9, 8, channels), F32)
    unite_space = pltpu.VMEM((3 * channels, channels), BF16)
    blocks = hidden // BLK
    groups = 2 * blocks * (BLK // GROUP_LANES) + -(-3 * channels // GROUP_LANES)
    assert groups == 4 * PER_QUARTER
    block = (PER_QUARTER, 4 * channels // BLOCKS, GROUP_LANES)
    half = shape(BLOCKS // 2, *block, dtype=BF16)
    buf = pltpu.VMEM((BLOCKS, *block), BF16)

    kernels = conv_kernel.transpose(1, 2, 0, 3)
    down_t = down_weight.transpose(0, 2, 1)
    unite_t = unite_weight.transpose(0, 2, 1)
    mix_width = mix_width.transpose(1, 0, 2)
    mix_height = mix_height.transpose(1, 0, 2)

    x_pieces = to_whole(patches[:, 0].transpose(1, 2, 0, 3), tile)
    first = run(
        kernel_first,
        "conv_first",
        10**7,
        dict(tile=tile_arg, **{f"p{k}": x_pieces[k] for k in range(4)}, kernels=kernels),
        dict(x=c_bf, a=c_f32, stats=shape(2, channels)),
        dict(pad=pad, sums=sums),
        tight=True,
    )
    taps = run(
        kernel_taps,
        "taps",
        10**8,
        dict(x=Late(first.x), a=Late(first.a), stats=first.stats),
        dict(out=shape(24, channels)),
        dict(pad=pad, alone=ksum, times=ksum),
        tight=True,
    ).out
    stats0, (cotangent, taps) = total_moments(first.stats, float(local_cells), [cotangent, taps])
    times = taps[9:18] + (taps[18:19] - stats0[0:1]) * taps[0:9]
    cot_pieces = to_whole(cotangent[:, 0].transpose(1, 2, 0, 3), tile)

    def forward_ins(layer):
        return dict(
            batch_gain=batch_gain, batch_shift=batch_shift,
            mix_width=mix_width, mix_width_bias=mix_width_bias, mix_height=mix_height, mix_height_bias=mix_height_bias,
            unite_t=Late(unite_t, layer), up=Late(up_weight, layer), down=Late(down_t, layer),
            unite_bias=unite_bias, norm_gain=norm_gain, norm_shift=norm_shift, up_bias=up_bias, down_bias=down_bias,
        )

    fwd = run(
        lambda r: kernel_forward(cells, r),
        "block_forward",
        6 * 10**9,
        dict(a=Late(first.a), stats=stats0, **forward_ins(0), x=Late(first.x), kernels=kernels),
        dict(
            nb=Stream(c_bf), pw=Stream(c_bf), ph=Stream(c_bf), zhat=Stream(c_f32), s=Stream(rows(1, F32)), zb=Stream(c_bf),
            g=Stream(h_bf), d=Stream(h_bf), u=Stream(c_f32), a2=Stream(c_f32), stats2=shape(2, channels),
        ),
        dict(pad=pad, sums=sums, unite=unite_space),
    )
    stats1, *cot_pieces = tie(fwd.stats2, *cot_pieces)
    stats1 = total_moments(stats1, float(local_cells))

    turn = run(
        lambda r: kernel_turn(cells, r),
        "block_turn",
        14 * 10**9,
        dict(
            tile=tile_arg, index=index_arg, a=Late(fwd.a2), stats=stats1, u=Late(fwd.u), **{f"c{k}": Late(cot_pieces[k]) for k in range(4)},
            **forward_ins(1),
        ),
        dict(
            **{f"f{k}": Stream(piece) for k in range(4)}, dm=Stream(c_f32), dn=Stream(c_f32), small_out=shape(SMALL_ROWS, channels),
            mine=Place(half), sent=Place(half),
        ),
        dict(
            nb=vmem(c_bf), pw=vmem(c_bf), ph=vmem(c_bf), zb=vmem(c_bf), do=vmem(c_bf), df=vmem(c_bf), dpw=vmem(c_bf), dph=vmem(c_bf),
            cot=map4, out=vmem(c_f32), zhat=vmem(c_f32), s=vmem(rows(1, F32)), dz=vmem(c_f32), small=small, upsum=upsum, buf=buf, unite=unite_space,
        ),
    )
    features = [turn.f0, turn.f1, turn.f2, turn.f3]

    near = masks(GROUPS[0])[0]
    part1 = narrow_add([turn.mine, flat_partner(turn.sent, near)])
    rows_free = [turn.small_out[:TAPS_ROW], taps[0:9], times, turn.small_out[KERNEL_ROW + 9 :]]
    total1, (part1,) = total_sum(jnp.concatenate(rows_free, 0), [part1], 2)
    total1, part1 = tie(total1, part1)
    mid = run(
        lambda r: kernel_conv_middle(cells, r),
        "conv_middle",
        2 * 10**9,
        dict(a=Late(fwd.a2, step=2), dn=Late(turn.dn, step=2), x=Late(fwd.u, step=2), dm=Late(turn.dm), stats=stats1, totals=total1, kernels=kernels, batch_gain=batch_gain),
        dict(du=Stream(c_f32), kgrad=shape(16, channels)),
        dict(padx=pad, padd=pad, ksum=ksum),
    )
    part1 = scatter_stage(part1, GROUPS[1])
    du, part1, *features = tie(mid.du, part1, *features)
    features = swap_pieces(features)
    back = run(
        lambda r: kernel_back(cells, r),
        "block_back",
        14 * 10**9,
        dict(
            index=index_arg, down=Late(down_t, 0), du=Late(du), up=Late(up_weight, 0), d=Late(fwd.d), zb=Late(fwd.zb), g=Late(fwd.g), unite_t=Late(unite_t, 0),
            zhat=Late(fwd.zhat), s=Late(fwd.s), nb=Late(fwd.nb), pw=Late(fwd.pw), ph=Late(fwd.ph), a=Late(first.a), x=Late(first.x),
            kgrad=mid.kgrad, norm_gain=norm_gain, stats=stats0, mix_width=mix_width, mix_height=mix_height,
        ),
        dict(dm=Stream(c_f32), dn=Stream(c_f32), small_out=shape(SMALL_ROWS, channels), mine=Place(half), sent=Place(half)),
        dict(do=vmem(c_bf), df=vmem(c_bf), dpw=vmem(c_bf), dph=vmem(c_bf), dz=vmem(c_f32), small=small, upsum=upsum, buf=buf, unite=unite_space, pad=pad, taps=ksum),
    )
    part1 = extra_sum(scatter_stage(part1, GROUPS[2]))
    small0, mine0, sent0, part1, *features = tie(back.small_out, back.mine, back.sent, part1, *features)
    gathered = lax.all_gather(part1, ("dp", "tile"), axis=0, tiled=True)[:BLOCKS]
    part0 = narrow_add([mine0, flat_partner(sent0, near)])
    total0, (part0,) = total_sum(small0, [part0], 2)
    part0 = scatter_stage(part0, GROUPS[1])
    last = run(
        lambda r: kernel_last(cells, r),
        "conv_last",
        2 * 10**9,
        dict(tile=tile_arg, a=Late(first.a, step=2), dn=Late(back.dn, step=2), dm=Late(back.dm), stats=stats0, totals=total0, kernels=kernels, batch_gain=batch_gain),
        {f"o{k}": piece for k in range(4)},
        dict(padd=pad, du=map4),
    )
    part0, *grads = tie(part0, last.o0, last.o1, last.o2, last.o3)
    grads = swap_pieces(grads)
    part0 = extra_sum(scatter_stage(part0, GROUPS[2]))
    part0 = gather_stage(part0, GROUPS[2])
    part0, *grads = tie(part0, *grads)
    part0 = gather_stage(part0, GROUPS[1])
    features_out = join_pieces(features, tile)
    grads = join_pieces(grads, tile)
    part0, features_out, grads, gathered = tie(part0, features_out, grads, gathered)
    far = flat_partner(part0, near)

    grad_shapes = dict(up=shape(2, channels, hidden), down=shape(2, channels, hidden), unite=shape(2, channels, 3 * channels))
    whole = run(
        kernel_unpack_gathered,
        "unpack_1",
        10**7,
        dict(blocks=Late(gathered)),
        {key: Stream(value, 1) for key, value in grad_shapes.items()},
        tight=True,
    )
    whole = run(
        kernel_unpack,
        "unpack_0",
        10**7,
        dict(index=index_arg, near=Late(part0), far=Late(far), up_in=Kept(whole.up), down_in=Kept(whole.down), unite_in=Kept(whole.unite)),
        {key: Stream(value, 0) for key, value in grad_shapes.items()},
        aliases={3: 0, 4: 1, 5: 2},
        tight=True,
    )
    line = shape(2, channels)
    fin = run(
        lambda r: kernel_finish(cells, r),
        "finish",
        10**6,
        dict(total0=total0, total1=total1, stats=stats0, gain=batch_gain),
        dict(
            batch_shift=line, batch_gain=line, norm_gain=line, norm_shift=line, down_bias=line, unite_bias=line, up_bias=shape(2, hidden),
            kernel=shape(3, 3, 2, channels), mix_width=shape(MAP, 2, MAP), mix_height=shape(MAP, 2, MAP), mix_width_bias=shape(2, MAP), mix_height_bias=shape(2, MAP),
        ),
    )

    def to_output(field):
        return field.transpose(2, 0, 1, 3)[:, None]

    return (
        to_output(features_out),
        to_output(grads),
        fin.kernel.transpose(2, 0, 1, 3),
        fin.batch_gain,
        fin.batch_shift,
        fin.mix_width.transpose(1, 0, 2),
        fin.mix_width_bias,
        fin.mix_height.transpose(1, 0, 2),
        fin.mix_height_bias,
        whole.unite.transpose(0, 2, 1),
        fin.unite_bias,
        fin.norm_gain,
        fin.norm_shift,
        whole.up,
        fin.up_bias,
        whole.down.transpose(0, 2, 1),
        fin.down_bias,
    )


def solution(mesh):
    field = P("dp", "tile", None, None, None)
    return jax.shard_map(
        on_device,
        mesh=mesh,
        in_specs=(field,) + (P(),) * 15 + (field,),
        out_specs=(field, field) + (P(),) * 15,
        check_vma=False,
    )
```

```python
import math

import jax
import jax.numpy as jnp
from jax import lax
from jax.experimental import pallas as pl
from jax.experimental.pallas import tpu as pltpu
from jax.sharding import PartitionSpec as P

F32 = jnp.float32
BF16 = jnp.bfloat16
norm_epsilon = 1e-05
layer_epsilon = 1e-06
ROOT_HALF = 0.7071067811865476
INV_ROOT_TAU = 0.3989422804014327
LOG2E = 1.4426950408889634

TS = 7
MAP = 14
IMG = 8
ROW = MAP * IMG
PIECE = TS * TS * IMG
VMEM_BYTES = 58 * 1024 * 1024
MARGIN = 8 * 1024 * 1024
BLK = 256


def partner(x, axis, distance):
    count = lax.axis_size(axis)
    return lax.ppermute(x, axis, [(i, i ^ distance) for i in range(count)])


def stages():
    result = [("tile", (1, 2, 3))]
    count = lax.axis_size("dp")
    step = 1
    if count > 1 and (count.bit_length() - 1) % 2 == 1:
        result.append(("dp", (1,)))
        step = 2
    while step < count:
        result.append(("dp", (step, 2 * step, 3 * step)))
        step *= 4
    return result


def total_sum(x, after=None, when=2):
    for step, (axis, distances) in enumerate(stages()):
        if step == when and after is not None:
            x, *after = tie(x, *after)
        got = [partner(x, axis, d) for d in distances]
        if len(got) == 1:
            x = x + got[0]
        else:
            x = (x + got[0]) + (got[1] + got[2])
    return x if after is None else (x, after)


def total_moments(stats, count, after=None):
    for step, (axis, distances) in enumerate(stages()):
        if step == 2 and after is not None:
            stats, *after = tie(stats, *after)
        parts = [stats] + [partner(stats, axis, d) for d in distances]
        if len(parts) == 2:
            mean = (parts[0][0] + parts[1][0]) * 0.5
            dev = [jnp.square(p[0] - mean) for p in parts]
            square = (parts[0][1] + parts[1][1]) + count * (dev[0] + dev[1])
        else:
            mean = ((parts[0][0] + parts[1][0]) + (parts[2][0] + parts[3][0])) * 0.25
            dev = [jnp.square(p[0] - mean) for p in parts]
            square = ((parts[0][1] + parts[1][1]) + (parts[2][1] + parts[3][1])) + count * (
                (dev[0] + dev[1]) + (dev[2] + dev[3])
            )
        count = count * len(parts)
        stats = jnp.stack([mean, square])
    return stats if after is None else (stats, after)


def to_whole(field, tile):
    share = field.shape[2] // lax.axis_size("tile")
    pieces = []
    for k in range(4):
        part = lax.dynamic_slice_in_dim(field, (tile ^ k) * share, share, 2)
        part = part.reshape(TS * TS * share, field.shape[3])
        pieces.append(part if k == 0 else partner(part, "tile", k))
    return pieces


def swap_pieces(pieces):
    return [pieces[0]] + [partner(pieces[k], "tile", k) for k in range(1, 4)]


def join_pieces(pieces, tile):
    channels = pieces[0].shape[-1]
    share = pieces[0].shape[0] // (TS * TS)
    result = jnp.zeros((TS, TS, share * lax.axis_size("tile"), channels), pieces[0].dtype)
    for k in range(4):
        part = pieces[k].reshape(TS, TS, share, channels)
        result = lax.dynamic_update_slice_in_dim(result, part, (tile ^ k) * share, 2)
    return result


def flat_partner(x, mask):
    axes = ("dp", "tile")
    count = lax.axis_size("dp") * lax.axis_size("tile")
    return lax.ppermute(x, axes, [(i, i ^ mask) for i in range(count)])


GROUPS = ((0,), (1, 2), (3, 4))
BLOCKS = 32


def block_index():
    flat = lax.axis_index("dp") * lax.axis_size("tile") + lax.axis_index("tile")
    index = jnp.zeros((), jnp.int32)
    for group in GROUPS:
        for bit in group:
            index = index * 2 + ((flat >> bit) & 1)
    return index


def masks(group):
    if len(group) == 1:
        return [1 << group[0]]
    return [1 << group[1], 1 << group[0], (1 << group[0]) | (1 << group[1])]


def narrow_add(parts):
    parts = [p.astype(F32) for p in parts]
    total = parts[0] + parts[1]
    if len(parts) == 4:
        total = total + (parts[2] + parts[3])
    return total.astype(BF16)


def scatter_stage(x, group):
    wide = masks(group)
    size = x.shape[0] // (len(wide) + 1)
    got = [flat_partner(x[(j + 1) * size : (j + 2) * size], mask) for j, mask in enumerate(wide)]
    return narrow_add([x[:size]] + got)


def extra_sum(x):
    count = lax.axis_size("dp") * lax.axis_size("tile")
    mask = BLOCKS
    while mask < count:
        x = narrow_add([x, flat_partner(x, mask)])
        mask *= 2
    return x


def gather_stage(x, group):
    return jnp.concatenate([x] + [flat_partner(x, mask) for mask in masks(group)], 0)


def tie(*values):
    return lax.optimization_barrier(values)


def dot(a, b):
    return lax.dot_general(a, b, (((1,), (0,)), ((), ())), preferred_element_type=F32)


def dot_nt(a, b):
    return lax.dot_general(a, b, (((1,), (1,)), ((), ())), preferred_element_type=F32)


def dot_tn(a, b):
    return lax.dot_general(a, b, (((0,), (0,)), ((), ())), preferred_element_type=F32)


def spread(ref, layer, repeat, turned=False):
    matrix = ref[...].astype(F32)[:, layer, :].astype(BF16)
    size = MAP * repeat
    shift = repeat.bit_length() - 1
    row = lax.broadcasted_iota(jnp.int32, (size, MAP), 0)
    col = lax.broadcasted_iota(jnp.int32, (size, MAP), 1)
    pick = jnp.where((row >> shift) == col, 1.0, 0.0).astype(BF16)
    half = dot_nt(pick, matrix) if turned else dot(pick, matrix)
    wide = dot_nt(half.astype(BF16), pick)
    row = lax.broadcasted_iota(jnp.int32, (size, size), 0)
    col = lax.broadcasted_iota(jnp.int32, (size, size), 1)
    return jnp.where((row & (repeat - 1)) == (col & (repeat - 1)), wide, 0.0).astype(BF16)


def spread_bias(ref, layer, repeat):
    size = MAP * repeat
    shift = repeat.bit_length() - 1
    row = lax.broadcasted_iota(jnp.int32, (size, MAP), 0)
    col = lax.broadcasted_iota(jnp.int32, (size, MAP), 1)
    return jnp.sum(jnp.where((row >> shift) == col, ref[layer : layer + 1], 0.0), axis=1, keepdims=True)


def collapse(product, repeat):
    size = MAP * repeat
    shift = repeat.bit_length() - 1
    row = lax.broadcasted_iota(jnp.int32, (size, size), 0)
    col = lax.broadcasted_iota(jnp.int32, (size, size), 1)
    kept = jnp.where((row & (repeat - 1)) == (col & (repeat - 1)), product, 0.0)
    kept = jnp.sum(kept.reshape(MAP, repeat, size), axis=1)
    row = lax.broadcasted_iota(jnp.int32, (size, MAP), 0)
    col = lax.broadcasted_iota(jnp.int32, (size, MAP), 1)
    pick = jnp.where((row >> shift) == col, 1.0, 0.0).astype(F32)
    return lax.dot_general(
        kept, pick, (((1,), (0,)), ((), ())), preferred_element_type=F32, precision=lax.Precision.HIGHEST
    )


def lane_groups(channels):
    return [(lo, min(lo + 128, channels)) for lo in range(0, channels, 128)]


def zero_border(pad):
    shape = pad.shape
    pad[0] = jnp.zeros(shape[1:], F32)
    pad[MAP + 1] = jnp.zeros(shape[1:], F32)
    for h in range(1, MAP + 1):
        pad[h, 0] = jnp.zeros(shape[2:], F32)
        pad[h, MAP + 1] = jnp.zeros(shape[2:], F32)


def pick_columns(field, w0):
    return jnp.where(w0 == 0, field[:, :TS], field[:, TS:])


def corner(tile, k):
    other = tile ^ k
    return (other >> 1) * TS, (other & 1) * TS


def conv_rows(pad, kernel_ref, layer, out_ref, stats_ref, sums, then=None):
    channels = pad.shape[-1]
    sums[...] = jnp.zeros(sums.shape, F32)

    def body(h, carry):
        for lo, hi in lane_groups(channels):
            acc = None
            for r in range(3):
                for s in range(3):
                    term = pad[h + r, s : s + MAP, :, lo:hi] * kernel_ref[r, s, layer : layer + 1, lo:hi]
                    acc = term if acc is None else acc + term
            out_ref[h, :, lo:hi] = acc.reshape(ROW, hi - lo)
            sums[0, :, lo:hi] += jnp.sum(acc, axis=0)
        if then is not None:
            then(h)
        return carry

    lax.fori_loop(0, MAP, body, 0)
    count = MAP * ROW
    mean = jnp.sum(sums[0], axis=0, keepdims=True) * (1.0 / count)

    def again(h, carry):
        for lo, hi in lane_groups(channels):
            dev = out_ref[h, :, lo:hi] - mean[:, lo:hi]
            sums[1, :, lo:hi] += jnp.sum((dev * dev).reshape(MAP, IMG, hi - lo), axis=0)
        return carry

    lax.fori_loop(0, MAP, again, 0)
    stats_ref[0:1] = mean
    stats_ref[1:2] = jnp.sum(sums[1], axis=0, keepdims=True)


def scale_of(stats_ref, cells):
    mean = stats_ref[0:1]
    return mean, lax.rsqrt(stats_ref[1:2] * (1.0 / cells) + norm_epsilon)


JOINED = 1024
MAIN = 256


def joined_places(channels):
    rest = channels - MAIN
    return [(i, 0, MAIN, i * MAIN) for i in range(3)] + [(i, MAIN, rest, 3 * MAIN + i * rest) for i in range(3)]


def put_joined(ref, rows, i, value):
    for part, first, size, lane in joined_places(value.shape[-1]):
        if part == i:
            ref[rows + (slice(lane, lane + size),)] = value[..., first : first + size]


def get_joined(value, i, channels):
    pieces = [value[..., lane : lane + size] for part, first, size, lane in joined_places(channels) if part == i]
    return jnp.concatenate(pieces, axis=-1)


def mix_forward(layer, cells, a_ref, stats_ref, gain_ref, shift_ref, mw_ref, mwb_ref, mh_ref, mhb_ref, joined):
    mean, rstd = scale_of(stats_ref, cells)
    channels = a_ref.shape[-1]
    gain = gain_ref[layer : layer + 1]
    shift = shift_ref[layer : layer + 1]
    width = spread(mw_ref, layer, IMG)
    height = spread(mh_ref, layer, 16)
    width_bias = spread_bias(mwb_ref, layer, IMG)
    height_bias = spread_bias(mhb_ref, layer, 16)
    used = 3 * channels
    joined[:, :, used:] = jnp.zeros(joined.shape[:2] + (joined.shape[2] - used,), BF16)
    whole = slice(None)
    for h in range(MAP):
        value = (((a_ref[h] - mean) * rstd) * gain + shift).astype(BF16)
        put_joined(joined, (h, whole), 0, value)
        put_joined(joined, (h, whole), 1, (dot(width, value) + width_bias).astype(BF16))
    for j in range(ROW // 16):
        cols = slice(16 * j, 16 * j + 16)
        value = get_joined(joined[:, cols, :], 0, channels).reshape(MAP * 16, channels)
        mixed = (dot(height, value) + height_bias).astype(BF16)
        put_joined(joined, (whole, cols), 2, mixed.reshape(MAP, 16, channels))


def gelu_pair(v):
    t = 1.0 / (1.0 + (0.3275911 * ROOT_HALF) * jnp.abs(v))
    e = jnp.exp2(v * v * (-0.5 * LOG2E))
    q = ((((0.5 * 1.061405429 * t - 0.5 * 1.453152027) * t + 0.5 * 1.421413741) * t - 0.5 * 0.284496736) * t + 0.5 * 0.254829592) * t * e
    phi = jnp.where(v >= 0, 1.0 - q, q)
    return v * phi, phi + v * e * INV_ROOT_TAU


HALVES = 2
PART = MAP // HALVES


def half_rows(ref, p):
    value = ref[p * PART : (p + 1) * PART]
    return value.reshape(PART * ROW, value.shape[-1])


def put_half(ref, p, value):
    ref[p * PART : (p + 1) * PART] = value.reshape(PART, ROW, value.shape[-1])


def add_half(ref, p, value):
    ref[p * PART : (p + 1) * PART] += value.reshape(PART, ROW, value.shape[-1])


def column_sums(value):
    return jnp.sum(value.reshape(-1, 8, value.shape[-1]), axis=0)


def unite_norm(r, layer, p, residual):
    one = slice(layer, layer + 1)
    m = residual + r.unite_bias[one] + dot(half_rows(r.joined.ref, p), r.unite[...])
    centre = jnp.mean(m, axis=-1, keepdims=True)
    dev = m - centre
    s = lax.rsqrt(jnp.mean(dev * dev, axis=-1, keepdims=True) + layer_epsilon)
    zhat = dev * s
    zb = (zhat * r.norm_gain[one] + r.norm_shift[one]).astype(BF16)
    return m, zhat, s, zb


def hidden_block(r, layer, j):
    blk = slice(j * BLK, (j + 1) * BLK) if isinstance(j, int) else pl.ds(pl.multiple_of(j * BLK, BLK), BLK)
    return blk, r.up.ref[:, blk], r.down.ref[:, blk]


def block_half(value):
    return value.reshape(PART, ROW, BLK)


def norm_backward(r, layer, p, do32, zhat, s, dz, df_ref):
    one = slice(layer, layer + 1)
    channels = do32.shape[-1]
    e = dz * r.norm_gain[one]
    mean_e = jnp.mean(e, axis=-1, keepdims=True)
    mean_ez = jnp.mean(e * zhat, axis=-1, keepdims=True)
    dm = do32 + s * (e - mean_e - zhat * mean_ez)
    put_half(r.dm.ref, p, dm)
    df = dm.astype(BF16)
    put_half(df_ref, p, df)
    r.small[2] += column_sums(dz * zhat)
    r.small[3] += column_sums(dz)
    r.small[4] += column_sums(do32)
    r.small[5] += column_sums(dm)
    dj = dot_nt(df, r.unite[...])
    put_half(r.dn.ref, p, get_joined(dj, 0, channels))
    put_half(r.dpw, p, get_joined(dj, 1, channels).astype(BF16))
    put_half(r.dph, p, get_joined(dj, 2, channels).astype(BF16))


GROUP_LANES = 128
PER_QUARTER = 7


def put_group(r, q, value):
    size = r.buf.shape[2]
    count = value.shape[0] // size
    quarter = q // PER_QUARTER if isinstance(q, int) else lax.div(q, PER_QUARTER)
    lane = q - quarter * PER_QUARTER
    for b in range(count):
        r.buf[(quarter * count + b) ^ r.index[0], lane] = value[b * size : (b + 1) * size].astype(BF16)


def put_columns(r, q, value):
    for i in range(value.shape[-1] // GROUP_LANES):
        put_group(r, q + i, value[:, i * GROUP_LANES : (i + 1) * GROUP_LANES])


def flat_rows(value):
    return value.reshape(MAP * ROW, value.shape[-1])


def hidden_gradients(r, j, blocks, zb, do, g, dh):
    per = BLK // GROUP_LANES
    put_columns(r, per * j, dot_tn(flat_rows(zb[...]), dh))
    put_columns(r, per * (j + blocks), dot_tn(flat_rows(do[...]), g))


def mix_backward(layer, cells, a_ref, stats_ref, mw_ref, mh_ref, dpw, dph, dn_ref, small, send):
    mean, rstd = scale_of(stats_ref, cells)
    width = spread(mw_ref, layer, IMG, turned=True)
    height = spread(mh_ref, layer, 16, turned=True)
    for j in range(ROW // 16):
        cols = slice(16 * j, 16 * j + 16)
        value = dph[:, cols, :].reshape(MAP * 16, -1)
        dn_ref[:, cols, :] += dot(height, value).reshape(MAP, 16, -1)

    totals = [small[0], small[1]]
    for h in range(MAP):
        dn = dn_ref[h] + dot(width, dpw[h])
        dn_ref[h] = dn
        send(h)
        xhat = (a_ref[h] - mean) * rstd
        totals[0] = totals[0] + jnp.sum(dn.reshape(MAP, IMG, -1), axis=0)
        totals[1] = totals[1] + jnp.sum((dn * xhat).reshape(MAP, IMG, -1), axis=0)
    small[0], small[1] = totals


def unite_gradients(r, blocks, df_ref, out_ref):
    df = flat_rows(df_ref[...])
    channels = df.shape[-1]
    joined, dpw, dph = r.joined.ref, r.dpw, r.dph
    put_columns(r, 2 * blocks * (BLK // GROUP_LANES), dot_tn(df, flat_rows(joined[...])))

    wide = jnp.zeros((ROW, ROW), F32)
    bias = jnp.zeros((ROW, channels), F32)
    for h in range(MAP):
        wide = wide + dot_nt(dpw[h], get_joined(joined[h], 0, channels))
        bias = bias + dpw[h].astype(F32)
    tall = jnp.zeros((MAP * 16, MAP * 16), F32)
    tall_bias = jnp.zeros((MAP, 16, channels), F32)
    for j in range(ROW // 16):
        cols = slice(16 * j, 16 * j + 16)
        value = dph[:, cols, :]
        tall = tall + dot_nt(value.reshape(MAP * 16, channels), get_joined(joined[:, cols, :], 0, channels).reshape(MAP * 16, channels))
        tall_bias = tall_bias + value.astype(F32)
    diagonal = lax.broadcasted_iota(jnp.int32, (MAP, MAP), 0) == lax.broadcasted_iota(jnp.int32, (MAP, MAP), 1)

    def as_row(field):
        col = jnp.sum(jnp.sum(field, axis=1), axis=-1, keepdims=True)
        return jnp.sum(jnp.where(diagonal, col, 0.0), axis=0, keepdims=True)

    width = jnp.concatenate([collapse(wide, IMG), as_row(bias.reshape(MAP, IMG, channels))], axis=0)
    height = jnp.concatenate([collapse(tall, 16), as_row(tall_bias)], axis=0)
    for v in range(MAP + 1):
        row, lane = mix_place(v)
        out_ref[row : row + 1, lane : lane + MAP] = width[v : v + 1]
        out_ref[row : row + 1, lane + 16 : lane + 16 + MAP] = height[v : v + 1]


MIX_ROW = 10
TAPS_ROW = 12
KERNEL_ROW = 21
SMALL_ROWS = 32


def mix_place(v):
    return MIX_ROW + v // 10, 32 * (v % 10)


def put_small(out_ref, small, upsum):
    channels = out_ref.shape[-1]
    for i in range(6):
        out_ref[i : i + 1] = jnp.sum(small[i], axis=0, keepdims=True)
    up = jnp.sum(upsum[...], axis=0, keepdims=True)
    for i in range(up.shape[-1] // channels):
        out_ref[6 + i : 7 + i] = up[:, i * channels : (i + 1) * channels]


def tap_sums(value, pad, h, lo, hi, total):
    for r in range(3):
        for s in range(3):
            total[3 * r + s, :, lo:hi] += jnp.sum(value * pad[h + r, s : s + MAP, :, lo:hi], axis=0)


def put_taps(out_ref, row, total):
    for i in range(9):
        out_ref[row + i : row + i + 1] = jnp.sum(total[i], axis=0, keepdims=True)


def conv_backward(layer, cells, a, stats_ref, totals_ref, gain, kernel_ref, dn, dm, emit, padd, x=None, padx=None, ksum=None, send=None):
    mean, rstd = scale_of(stats_ref, cells)
    scale = rstd * gain[layer : layer + 1]
    shift_mean = totals_ref[0:1] * (1.0 / cells)
    gain_mean = totals_ref[1:2] * (1.0 / cells)
    channels = padd.shape[-1]
    arriving = [part for part in (a, dn, dm, x) if part is not None]
    for c in range(MAP // 2):
        for part in arriving:
            part.start_part(c)
    zero_border(padd)
    if x is not None:
        zero_border(padx)
        ksum[...] = jnp.zeros(ksum.shape, F32)

    def fill(c):
        for part in arriving:
            part.wait(c)
        for i in range(2):
            h = 2 * c + i
            xhat = (a.ref[h] - mean) * rstd
            da = scale * (dn.ref[h] - shift_mean - xhat * gain_mean)
            padd[h + 1, 1 : MAP + 1] = da.reshape(MAP, IMG, -1)
            if x is not None:
                padx[h + 1, 1 : MAP + 1] = x.ref[h].astype(BF16).astype(F32).reshape(MAP, IMG, -1)

    def rows(c):
        for i in range(2):
            h = 2 * c + i
            for lo, hi in lane_groups(channels):
                acc = dm.ref[h, :, lo:hi].reshape(MAP, IMG, hi - lo)
                da = padd[h + 1, 1 : MAP + 1, :, lo:hi]
                for r in range(3):
                    for s in range(3):
                        acc = acc + padd[h + 2 - r, 2 - s : 2 - s + MAP, :, lo:hi] * kernel_ref[r, s, layer : layer + 1, lo:hi]
                if x is not None:
                    tap_sums(da, padx, h, lo, hi, ksum)
                emit(h, lo, hi, acc)
        if send is not None:
            send(c)

    fill(0)

    def body(c, carry):
        fill(c + 1)
        rows(c)
        return carry

    lax.fori_loop(0, MAP // 2 - 1, body, 0)
    rows(MAP // 2 - 1)


def fill_pad(pad, x_ref):
    def body(h, carry):
        pad[h + 1, 1 : MAP + 1] = x_ref[h].astype(F32).reshape(MAP, IMG, -1)
        return carry

    lax.fori_loop(0, MAP, body, 0)


def kernel_taps(r):
    r.x.wait_all()
    zero_border(r.pad)
    fill_pad(r.pad, r.x.ref)
    r.a.wait_all()
    mean = r.stats[0:1]
    for total in (r.alone, r.times):
        total[...] = jnp.zeros(total.shape, F32)

    def body(h, carry):
        for lo, hi in lane_groups(r.pad.shape[-1]):
            value = (r.a.ref[h, :, lo:hi] - mean[:, lo:hi]).reshape(MAP, IMG, hi - lo)
            for i in range(3):
                for s in range(3):
                    window = r.pad[h + i, s : s + MAP, :, lo:hi]
                    r.alone[3 * i + s, :, lo:hi] += jnp.sum(window, axis=0)
                    r.times[3 * i + s, :, lo:hi] += jnp.sum(value * window, axis=0)
        return carry

    lax.fori_loop(0, MAP, body, 0)
    r.out[...] = jnp.zeros(r.out.shape, F32)
    put_taps(r.out, 0, r.alone)
    put_taps(r.out, 9, r.times)
    r.out[18:19] = mean


def kernel_first(r):
    tile = r.tile[0]
    zero_border(r.pad)
    for k, piece in enumerate((r.p0, r.p1, r.p2, r.p3)):
        h0, w0 = corner(tile, k)
        value = piece[...].astype(F32).reshape(TS, TS, IMG, -1)
        r.pad[pl.ds(1 + h0, TS), pl.ds(1 + w0, TS)] = value

    def body(h, carry):
        r.x[h] = r.pad[h + 1, 1 : MAP + 1].reshape(ROW, -1).astype(BF16)
        return carry

    lax.fori_loop(0, MAP, body, 0)
    conv_rows(r.pad, r.kernels, 0, r.a, r.stats, r.sums)


def turn_unite(r):
    r.unite_t.wait_all()
    channels = r.unite.shape[-1]
    for part, first, size, lane in joined_places(channels):
        r.unite[lane : lane + size] = r.unite_t.ref[:, part * channels + first : part * channels + first + size].T
    r.unite[3 * channels :] = jnp.zeros((JOINED - 3 * channels, channels), BF16)


def forward_front(r, layer, cells, later):
    r.a.wait_all()
    for part in later:
        part.start()
    mix_forward(layer, cells, r.a.ref, r.stats, r.batch_gain, r.batch_shift, r.mix_width, r.mix_width_bias, r.mix_height, r.mix_height_bias, r.joined.ref)


def kernel_forward(cells, r):
    forward_front(r, 0, cells, (r.unite_t, r.x, r.up, r.down))
    r.joined.send_all()
    turn_unite(r)
    zero_border(r.pad)
    r.x.wait_all()
    for p in range(HALVES):
        m, zhat, s, zb = unite_norm(r, 0, p, half_rows(r.x.ref, p).astype(F32))
        put_half(r.u.ref, p, m + r.down_bias[0:1])
        put_half(r.zhat.ref, p, zhat)
        put_half(r.s.ref, p, s)
        put_half(r.zb.ref, p, zb)
        for stream in (r.zhat, r.s, r.zb):
            stream.send(p)
    r.up.wait_all()
    r.down.wait_all()

    def body(j):
        blk, up, down = hidden_block(r, 0, j)
        for p in range(HALVES):
            g, d = gelu_pair(dot(half_rows(r.zb.ref, p), up) + r.up_bias[0:1, blk])
            g = g.astype(BF16)
            r.g.ref[j, p * PART : (p + 1) * PART] = block_half(g)
            r.d.ref[j, p * PART : (p + 1) * PART] = block_half(d.astype(BF16))
            add_half(r.u.ref, p, dot_nt(g, down))
        r.g.send(j)
        r.d.send(j)

    lax.fori_loop(0, r.up_bias.shape[-1] // BLK, lambda j, c: (body(j), c)[1], 0)
    r.u.send_all()

    def fill(h, carry):
        rounded = r.u.ref[h].astype(BF16).astype(F32)
        r.pad[h + 1, 1 : MAP + 1] = rounded.reshape(MAP, IMG, -1)
        return carry

    lax.fori_loop(0, MAP, fill, 0)
    conv_rows(r.pad, r.kernels, 1, r.a2.ref, r.stats2, r.sums, r.a2.send)


def clear(r):
    r.small[...] = jnp.zeros(r.small.shape, F32)
    r.upsum[...] = jnp.zeros(r.upsum.shape, F32)


def send_blocks(r):
    half = BLOCKS // 2
    r.mine.start(r.buf.at[pl.ds(0, half)])
    r.sent.start(r.buf.at[pl.ds(half, half)])


def kernel_turn(cells, r):
    tile = r.tile[0]
    clear(r)
    r.joined = Held(r.joined)
    forward_front(r, 1, cells, (r.unite_t, r.u, r.c0, r.c1, r.c2, r.c3, r.up, r.down))
    turn_unite(r)
    for k, piece in enumerate((r.c0, r.c1, r.c2, r.c3)):
        piece.wait_all()
        h0, w0 = corner(tile, k)
        r.cot[pl.ds(h0, TS), pl.ds(w0, TS)] = piece.ref[...].astype(F32).reshape(TS, TS, IMG, -1)
    r.u.wait_all()

    def cotangent(p):
        return r.cot[p * PART : (p + 1) * PART].reshape(PART * ROW, -1)

    for p in range(HALVES):
        m, zhat, s, zb = unite_norm(r, 1, p, half_rows(r.u.ref, p))
        put_half(r.out, p, m + r.down_bias[1:2])
        put_half(r.zhat, p, zhat)
        put_half(r.s, p, s)
        put_half(r.zb, p, zb)
        put_half(r.do, p, cotangent(p).astype(BF16))
    r.up.wait_all()
    r.down.wait_all()
    r.dz[...] = jnp.zeros(r.dz.shape, F32)
    blocks = r.up_bias.shape[-1] // BLK

    def body(j):
        blk, up, down = hidden_block(r, 1, j)
        gs, dhs = [], []
        for p in range(HALVES):
            g, d = gelu_pair(dot(half_rows(r.zb, p), up) + r.up_bias[1:2, blk])
            g = g.astype(BF16)
            add_half(r.out, p, dot_nt(g, down))
            dh = dot(half_rows(r.do, p), down) * d
            r.upsum[:, blk] += column_sums(dh)
            dh = dh.astype(BF16)
            add_half(r.dz, p, dot_nt(dh, up))
            gs.append(g)
            dhs.append(dh)
        return jnp.concatenate(gs, 0), jnp.concatenate(dhs, 0)

    done = []
    for j in range(blocks):
        done.append(body(j))
        if j > 0:
            hidden_gradients(r, j - 1, blocks, r.zb, r.do, *done[j - 1])
    hidden_gradients(r, blocks - 1, blocks, r.zb, r.do, *done[blocks - 1])
    for k, piece in enumerate((r.f0, r.f1, r.f2, r.f3)):
        h0, w0 = corner(tile, k)
        field = r.out[pl.ds(h0, TS)].reshape(TS, MAP, IMG, -1)
        piece.ref[...] = pick_columns(field, w0).reshape(PIECE, -1).astype(BF16)
        piece.send_all()
    for p in range(HALVES):
        norm_backward(r, 1, p, cotangent(p), half_rows(r.zhat, p), half_rows(r.s, p), half_rows(r.dz, p), r.df)
        r.dm.send(p)
    mix_backward(1, cells, r.a.ref, r.stats, r.mix_width, r.mix_height, r.dpw, r.dph, r.dn.ref, r.small, r.dn.send)
    r.small_out[...] = jnp.zeros(r.small_out.shape, F32)
    put_small(r.small_out, r.small, r.upsum)
    r.small_out[TAPS_ROW : TAPS_ROW + 18] = r.taps[...]
    unite_gradients(r, blocks, r.df, r.small_out)
    send_blocks(r)


def kernel_conv_middle(cells, r):
    def emit(h, lo, hi, value):
        r.du.ref[h, :, lo:hi] = value.reshape(ROW, hi - lo)
        r.do.ref[h, :, lo:hi] = value.reshape(ROW, hi - lo).astype(BF16)

    def send(c):
        r.do.send(c)
        r.du.send(c)

    conv_backward(1, cells, r.a, r.stats, r.totals, r.batch_gain, r.kernels, r.dn, r.dm, emit, r.padd, r.x, r.padx, r.ksum, send)
    put_taps(r.kgrad, 0, r.ksum)


def kernel_back(cells, r):
    for part in (r.do_in, r.down, r.up):
        part.start()
    r.d.start_part(0)
    r.zb.start()
    r.g.start_part(0)
    clear(r)
    r.do = r.do_in.ref
    for part in (r.do_in, r.up, r.down):
        part.wait_all()
    for j in range(1, r.d.parts):
        r.d.start_part(j)
        r.g.start_part(j)
    for part in (r.zhat, r.s, r.unite_t, r.du, r.joined, r.a, r.x):
        part.start()
    r.dz[...] = jnp.zeros(r.dz.shape, F32)
    blocks = r.upsum.shape[-1] // BLK

    def body(j):
        blk, up, down = hidden_block(r, 0, j)
        r.d.wait(j)
        dhs = []
        for p in range(HALVES):
            d = r.d.ref[j, p * PART : (p + 1) * PART].reshape(PART * ROW, BLK).astype(F32)
            dh = dot(half_rows(r.do, p), down) * d
            r.upsum[:, blk] += column_sums(dh)
            dh = dh.astype(BF16)
            add_half(r.dz, p, dot_nt(dh, up))
            dhs.append(dh)
        return jnp.concatenate(dhs, 0)

    def gradients(j, dh):
        if j == 0:
            r.zb.wait_all()
        r.g.wait(j)
        hidden_gradients(r, j, blocks, r.zb.ref, r.do, flat_rows(r.g.ref[j]), dh)

    done = []
    for j in range(blocks):
        done.append(body(j))
        if j > 0:
            gradients(j - 1, done[j - 1])
    gradients(blocks - 1, done[blocks - 1])
    turn_unite(r)
    r.du.wait_all()
    r.zhat.wait_all()
    r.s.wait_all()
    for p in range(HALVES):
        norm_backward(r, 0, p, half_rows(r.du.ref, p), half_rows(r.zhat.ref, p), half_rows(r.s.ref, p), half_rows(r.dz, p), r.df)
        r.dm.send(p)
    r.joined.wait_all()
    r.small_out[...] = jnp.zeros(r.small_out.shape, F32)
    unite_gradients(r, blocks, r.df, r.small_out)
    send_blocks(r)
    for part in (r.a, r.x):
        part.wait_all()
    zero_border(r.pad)
    fill_pad(r.pad, r.x.ref)
    r.taps[...] = jnp.zeros(r.taps.shape, F32)

    mix_backward(0, cells, r.a.ref, r.stats, r.mix_width, r.mix_height, r.dpw, r.dph, r.dn.ref, r.small, r.dn.send)

    def windows(h, carry):
        for lo, hi in lane_groups(r.pad.shape[-1]):
            tap_sums(r.dn.ref[h, :, lo:hi].reshape(MAP, IMG, hi - lo), r.pad, h, lo, hi, r.taps)
        return carry

    lax.fori_loop(0, MAP, windows, 0)
    put_small(r.small_out, r.small, r.upsum)
    put_taps(r.small_out, TAPS_ROW, r.taps)
    r.small_out[KERNEL_ROW : KERNEL_ROW + 9] = r.kgrad[0:9]


def kernel_last(cells, r):
    tile = r.tile[0]

    def emit(h, lo, hi, value):
        r.du[h, :, :, lo:hi] = value

    conv_backward(0, cells, r.a, r.stats, r.totals, r.batch_gain, r.kernels, r.dn, r.dm, emit, r.padd)
    for k, piece in enumerate((r.o0, r.o1, r.o2, r.o3)):
        h0, w0 = corner(tile, k)
        piece[...] = r.du[pl.ds(h0, TS), pl.ds(w0, TS)].reshape(PIECE, -1).astype(BF16)


def unpack_put(r, value, quarter, row):
    channels, hidden = r.up.ref.shape
    rows = pl.ds(row, value.shape[1])
    for i in range(value.shape[0]):
        base = (quarter * value.shape[0] + i) * GROUP_LANES
        if base < hidden:
            r.up.ref[rows, base : base + GROUP_LANES] = value[i]
        elif base < 2 * hidden:
            r.down.ref[rows, base - hidden : base - hidden + GROUP_LANES] = value[i]
        else:
            base -= 2 * hidden
            for part, first, size, lane in joined_places(channels):
                lo, hi = max(lane, base), min(lane + size, base + GROUP_LANES)
                if lo < hi:
                    target = part * channels + first + lo - lane
                    r.unite.ref[rows, target : target + hi - lo] = value[i, :, lo - base : hi - base]


def unpack_all(r, block):
    channels, hidden = r.up.ref.shape
    size = 4 * channels // BLOCKS
    per = channels // size
    lanes = PER_QUARTER * GROUP_LANES
    for quarter in range(4):
        for b in range(per):
            unpack_put(r, block(quarter * per + b), quarter, b * size)
        if (quarter + 1) * lanes >= hidden and quarter * lanes < hidden:
            r.up.send_all()
        if (quarter + 1) * lanes >= 2 * hidden and quarter * lanes < 2 * hidden:
            r.down.send_all()
    r.unite.send_all()


def kernel_unpack_gathered(r):
    r.blocks.wait_all()
    bits = [bit for group in GROUPS for bit in group]

    def block(p):
        place = sum(((p >> (len(bits) - 1 - i)) & 1) << bit for i, bit in enumerate(bits))
        return r.blocks.ref[place].astype(F32)

    unpack_all(r, block)


def kernel_unpack(r):
    index = r.index[0]
    half = BLOCKS // 2
    flip = index & (half - 1)
    own = index // half
    r.near.wait_all()
    r.far.wait_all()

    def block(p):
        place = (p & (half - 1)) ^ flip
        near, far = r.near.ref[place].astype(F32), r.far.ref[place].astype(F32)
        return jnp.where(own == p // half, near, far)

    unpack_all(r, block)


def kernel_finish(cells, r):
    channels = r.total0.shape[-1]
    for layer, total in enumerate((r.total0, r.total1)):
        one = slice(layer, layer + 1)
        r.batch_shift[one] = total[0:1]
        r.batch_gain[one] = total[1:2]
        r.norm_gain[one] = total[2:3]
        r.norm_shift[one] = total[3:4]
        r.down_bias[one] = total[4:5]
        r.unite_bias[one] = total[5:6]
        for i in range(r.up_bias.shape[-1] // channels):
            r.up_bias[one, i * channels : (i + 1) * channels] = total[6 + i : 7 + i]
        for v in range(MAP + 1):
            row, lane = mix_place(v)
            width, height = total[row : row + 1, lane : lane + MAP], total[row : row + 1, lane + 16 : lane + 16 + MAP]
            if v < MAP:
                r.mix_width[v, one], r.mix_height[v, one] = width, height
            else:
                r.mix_width_bias[one], r.mix_height_bias[one] = width, height
    mean, rstd = scale_of(r.stats, cells)
    shift_mean, gain_mean = r.total0[0:1] * (1.0 / cells), r.total0[1:2] * (1.0 / cells)
    for i in range(9):
        alone, times = r.total1[TAPS_ROW + i : TAPS_ROW + i + 1], r.total1[KERNEL_ROW + i : KERNEL_ROW + i + 1]
        value = r.total0[TAPS_ROW + i : TAPS_ROW + i + 1] - shift_mean * alone - gain_mean * rstd * times
        r.kernel[i // 3, i % 3, 0:1] = rstd * r.gain[0:1] * value
        r.kernel[i // 3, i % 3, 1:2] = r.total0[KERNEL_ROW + i : KERNEL_ROW + i + 1]


class Kept:
    def __init__(self, array):
        self.array = array


class Smem:
    def __init__(self, array):
        self.array = array


class Layer:
    def __init__(self, array, layer):
        self.array, self.layer = array, layer


def chunk_step(shape, step=None):
    if len(shape) == 4 and shape[1:3] == (MAP, ROW):
        return 1
    if len(shape) == 3 and shape[:2] == (MAP, ROW):
        return step or PART
    return shape[0]


class Late:
    def __init__(self, array, layer=None, step=None, hold=False):
        self.array, self.layer, self.hold = array, layer, hold
        self.step = chunk_step(self.shape, step)

    @property
    def shape(self):
        return self.array.shape if self.layer is None else self.array.shape[1:]

    @property
    def parts(self):
        return self.shape[0] // self.step


class LateRef:
    def __init__(self, late, source, ref, sems):
        self.parts, self.step = late.parts, late.step
        self.source = source if late.layer is None else source.at[late.layer]
        self.ref, self.sems = ref, sems

    def copy(self, c):
        if self.parts == 1:
            return pltpu.make_async_copy(self.source, self.ref, self.sems.at[0])
        rows = pl.ds(self.step * c, self.step)
        return pltpu.make_async_copy(self.source.at[rows], self.ref.at[rows], self.sems.at[c])

    def start(self):
        for c in range(self.parts):
            self.copy(c).start()

    def start_part(self, c):
        self.copy(c).start()

    def wait(self, c):
        self.copy(c).wait()

    def wait_all(self):
        for c in range(self.parts):
            self.copy(c).wait()


class Stream:
    def __init__(self, out, layer=None, step=None):
        self.out, self.layer = out, layer
        self.step = chunk_step(self.shape, step)

    @property
    def shape(self):
        return self.out.shape if self.layer is None else self.out.shape[1:]


class Place:
    def __init__(self, out):
        self.out = out


class StreamRef:
    def __init__(self, stream, target, ref, sem):
        self.target, self.ref, self.sem = target if stream.layer is None else target.at[stream.layer], ref, sem
        self.step = stream.step

    def send(self, c):
        rows = pl.ds(self.step * c, self.step)
        pltpu.make_async_copy(self.ref.at[rows], self.target.at[rows], self.sem).start()

    def send_all(self):
        pltpu.make_async_copy(self.ref, self.target, self.sem).start()

    def finish(self):
        pltpu.make_async_copy(self.ref, self.target, self.sem).wait()


class PlaceRef:
    def __init__(self, target, sem):
        self.target, self.sem = target, sem

    def start(self, source):
        self.copy = pltpu.make_async_copy(source, self.target, self.sem)
        self.copy.start()

    def finish(self):
        self.copy.wait()


class Held:
    def __init__(self, ref):
        self.ref = ref


class Refs:
    pass


def full(array):
    rank = len(array.shape)
    return pl.BlockSpec(array.shape, lambda i: (0,) * rank)


ANY = pl.BlockSpec(memory_space=pl.ANY)


def _padded(array):
    shape = list(array.shape)
    if len(shape) > 1:
        shape[-2] = -(-shape[-2] // 16) * 16
    shape[-1] = -(-shape[-1] // 128) * 128
    return math.prod(shape) * jnp.dtype(array.dtype).itemsize


def run(body, name, flops, ins, outs, scratch=None, aliases=None, tight=False):
    scratch = dict(scratch or {})
    arrays, in_specs, out_specs, out_shapes, spaces = [], [], [], [], []
    for key, operand in ins.items():
        if isinstance(operand, Smem):
            in_specs.append(pl.BlockSpec(memory_space=pltpu.SMEM))
        elif isinstance(operand, Layer):
            shape, layer = operand.array.shape, operand.layer
            in_specs.append(pl.BlockSpec((None,) + shape[1:], lambda i, layer=layer, rank=len(shape): (layer,) + (0,) * (rank - 1)))
        elif isinstance(operand, Kept):
            in_specs.append(ANY)
        elif isinstance(operand, Late):
            in_specs.append(ANY)
            spaces += [pltpu.VMEM(operand.shape, operand.array.dtype), pltpu.SemaphoreType.DMA((operand.parts,))]
        else:
            in_specs.append(full(operand))
        arrays.append(getattr(operand, "array", operand))
    for key, out in outs.items():
        if isinstance(out, (Stream, Place)):
            out_specs.append(ANY)
            out_shapes.append(out.out)
            if isinstance(out, Stream):
                spaces.append(pltpu.VMEM(out.shape, out.out.dtype))
            spaces.append(pltpu.SemaphoreType.DMA)
        elif isinstance(out, Layer):
            shape, layer = out.array.shape, out.layer
            out_specs.append(pl.BlockSpec((None,) + shape[1:], lambda i, layer=layer, rank=len(shape): (layer,) + (0,) * (rank - 1)))
            out_shapes.append(out.array)
        else:
            out_specs.append(full(out))
            out_shapes.append(out)
    spaces += list(scratch.values())

    def wrapped(*refs):
        refs = list(refs)
        r = Refs()
        main, extra = refs[: len(ins) + len(outs)], refs[len(ins) + len(outs) :]
        late, streams = [], []
        for key, operand in ins.items():
            ref = main.pop(0)
            if isinstance(operand, Late):
                ref = LateRef(operand, ref, extra.pop(0), extra.pop(0))
                if not operand.hold:
                    late.append(ref)
            setattr(r, key, ref)
        for key, out in outs.items():
            ref = main.pop(0)
            if isinstance(out, Stream):
                ref = StreamRef(out, ref, extra.pop(0), extra.pop(0))
                streams.append(ref)
            elif isinstance(out, Place):
                ref = PlaceRef(ref, extra.pop(0))
                streams.append(ref)
            setattr(r, key, ref)
        for key in scratch:
            setattr(r, key, extra.pop(0))
        for part in late:
            part.start()
        body(r)
        for stream in streams:
            stream.finish()

    held = [a for a, spec in zip(arrays + out_shapes, in_specs + out_specs) if spec is not ANY]
    held += [space for space in spaces if getattr(space, "memory_space", None) == pltpu.VMEM]
    need = sum(_padded(a) for a in held)
    limit = min(VMEM_BYTES, need + need // 4 + MARGIN) if tight else VMEM_BYTES
    size = sum(a.size * a.dtype.itemsize for a in arrays) + sum(o.size * o.dtype.itemsize for o in out_shapes)
    results = pl.pallas_call(
        wrapped,
        grid=(1,),
        in_specs=in_specs,
        out_specs=out_specs,
        out_shape=out_shapes,
        scratch_shapes=spaces,
        input_output_aliases=aliases or {},
        compiler_params=pltpu.CompilerParams(vmem_limit_bytes=limit),
        cost_estimate=pl.CostEstimate(flops=flops, bytes_accessed=size, transcendentals=0),
        name=name,
    )(*arrays)
    named = Refs()
    for key, value in zip(outs, results):
        setattr(named, key, value)
    return named


def on_device(
    patches,
    conv_kernel,
    batch_gain,
    batch_shift,
    mix_width,
    mix_width_bias,
    mix_height,
    mix_height_bias,
    unite_weight,
    unite_bias,
    norm_gain,
    norm_shift,
    up_weight,
    up_bias,
    down_weight,
    down_bias,
    cotangent,
):
    channels = patches.shape[-1]
    hidden = up_weight.shape[-1]
    tile = lax.axis_index("tile")
    tile_arg = Smem(tile.astype(jnp.int32).reshape(1))
    index_arg = Smem(block_index().reshape(1))
    local_cells = MAP * ROW
    cells = local_cells * lax.axis_size("dp") * lax.axis_size("tile")

    def rows(lanes, dtype):
        return jax.ShapeDtypeStruct((MAP, ROW, lanes), dtype)

    def shape(*dims, dtype=F32):
        return jax.ShapeDtypeStruct(dims, dtype)

    def vmem(struct):
        return pltpu.VMEM(struct.shape, struct.dtype)

    piece = shape(PIECE, channels, dtype=BF16)
    c_bf, c_f32, h_bf = rows(channels, BF16), rows(channels, F32), shape(hidden // BLK, MAP, ROW, BLK, dtype=BF16)
    map4 = pltpu.VMEM((MAP, MAP, IMG, channels), F32)
    pad = pltpu.VMEM((MAP + 2, MAP + 2, IMG, channels), F32)
    sums = pltpu.VMEM((2, 8, channels), F32)
    small = pltpu.VMEM((6, 8, channels), F32)
    upsum = pltpu.VMEM((8, hidden), F32)
    ksum = pltpu.VMEM((9, 8, channels), F32)
    unite_space = pltpu.VMEM((JOINED, channels), BF16)
    blocks = hidden // BLK
    groups = 2 * blocks * (BLK // GROUP_LANES) + JOINED // GROUP_LANES
    assert groups == 4 * PER_QUARTER
    block = (PER_QUARTER, 4 * channels // BLOCKS, GROUP_LANES)
    half = shape(BLOCKS // 2, *block, dtype=BF16)
    buf = pltpu.VMEM((BLOCKS, *block), BF16)

    kernels = conv_kernel.transpose(1, 2, 0, 3)
    down_t = down_weight.transpose(0, 2, 1)
    unite_t = unite_weight.transpose(0, 2, 1)
    mix_width = mix_width.transpose(1, 0, 2)
    mix_height = mix_height.transpose(1, 0, 2)

    x_pieces = to_whole(patches[:, 0].transpose(1, 2, 0, 3), tile)
    first = run(
        kernel_first,
        "conv_first",
        10**7,
        dict(tile=tile_arg, **{f"p{k}": x_pieces[k] for k in range(4)}, kernels=kernels),
        dict(x=c_bf, a=c_f32, stats=shape(2, channels)),
        dict(pad=pad, sums=sums),
        tight=True,
    )
    taps = run(
        kernel_taps,
        "taps",
        10**8,
        dict(x=Late(first.x), a=Late(first.a), stats=first.stats),
        dict(out=shape(24, channels)),
        dict(pad=pad, alone=ksum, times=ksum),
        tight=True,
    ).out
    stats0, (cotangent, taps) = total_moments(first.stats, float(local_cells), [cotangent, taps])
    taps = jnp.concatenate([taps[0:9], taps[9:18] + (taps[18:19] - stats0[0:1]) * taps[0:9]], 0)
    cot_pieces = to_whole(cotangent[:, 0].transpose(1, 2, 0, 3), tile)

    def forward_ins(layer):
        return dict(
            batch_gain=batch_gain, batch_shift=batch_shift,
            mix_width=mix_width, mix_width_bias=mix_width_bias, mix_height=mix_height, mix_height_bias=mix_height_bias,
            unite_t=Late(unite_t, layer, hold=True), up=Late(up_weight, layer, hold=True), down=Late(down_t, layer, hold=True),
            unite_bias=unite_bias, norm_gain=norm_gain, norm_shift=norm_shift, up_bias=up_bias, down_bias=down_bias,
        )

    fwd = run(
        lambda r: kernel_forward(cells, r),
        "block_forward",
        6 * 10**9,
        dict(a=Late(first.a), stats=stats0, **forward_ins(0), x=Late(first.x, hold=True), kernels=kernels),
        dict(
            joined=Stream(rows(JOINED, BF16)), zhat=Stream(c_f32), s=Stream(rows(1, F32)), zb=Stream(c_bf),
            g=Stream(h_bf), d=Stream(h_bf), u=Stream(c_f32), a2=Stream(c_f32, step=1), stats2=shape(2, channels),
        ),
        dict(pad=pad, sums=sums, unite=unite_space),
    )
    stats1, *cot_pieces = tie(fwd.stats2, *cot_pieces)
    stats1 = total_moments(stats1, float(local_cells))

    turn = run(
        lambda r: kernel_turn(cells, r),
        "block_turn",
        14 * 10**9,
        dict(
            tile=tile_arg, index=index_arg, a=Late(fwd.a2), stats=stats1, u=Late(fwd.u, hold=True), **{f"c{k}": Late(cot_pieces[k], hold=True) for k in range(4)},
            **forward_ins(1), taps=taps,
        ),
        dict(
            **{f"f{k}": Stream(piece) for k in range(4)}, dm=Stream(c_f32), dn=Stream(c_f32, step=1), small_out=shape(SMALL_ROWS, channels),
            mine=Place(half), sent=Place(half),
        ),
        dict(
            joined=vmem(rows(JOINED, BF16)), zb=vmem(c_bf), do=vmem(c_bf), df=vmem(c_bf), dpw=vmem(c_bf), dph=vmem(c_bf),
            cot=map4, out=vmem(c_f32), zhat=vmem(c_f32), s=vmem(rows(1, F32)), dz=vmem(c_f32), small=small, upsum=upsum, buf=buf, unite=unite_space,
        ),
    )
    features = [turn.f0, turn.f1, turn.f2, turn.f3]

    near = masks(GROUPS[0])[0]
    part1 = narrow_add([turn.mine, flat_partner(turn.sent, near)])
    total1, (part1,) = total_sum(turn.small_out, [part1], 2)
    total1, part1 = tie(total1, part1)
    mid = run(
        lambda r: kernel_conv_middle(cells, r),
        "conv_middle",
        2 * 10**9,
        dict(**{key: Late(value, step=2, hold=True) for key, value in dict(a=fwd.a2, dn=turn.dn, x=fwd.u, dm=turn.dm).items()}, stats=stats1, totals=total1, kernels=kernels, batch_gain=batch_gain),
        dict(do=Stream(c_bf, step=2), du=Stream(c_f32, step=2), kgrad=shape(16, channels)),
        dict(padx=pad, padd=pad, ksum=ksum),
    )
    part1 = scatter_stage(part1, GROUPS[1])
    do, part1, *features = tie(mid.do, part1, *features)
    features = swap_pieces(features)
    back = run(
        lambda r: kernel_back(cells, r),
        "block_back",
        14 * 10**9,
        dict(
            index=index_arg,
            **{
                key: Late(value, layer, hold=True)
                for key, (value, layer) in dict(
                    down=(down_t, 0), do_in=(do, None), du=(mid.du, None), up=(up_weight, 0), d=(fwd.d, None), zb=(fwd.zb, None), g=(fwd.g, None), unite_t=(unite_t, 0),
                    zhat=(fwd.zhat, None), s=(fwd.s, None), joined=(fwd.joined, None), a=(first.a, None), x=(first.x, None),
                ).items()
            },
            kgrad=mid.kgrad, norm_gain=norm_gain, stats=stats0, mix_width=mix_width, mix_height=mix_height,
        ),
        dict(dm=Stream(c_f32), dn=Stream(c_f32, step=1), small_out=shape(SMALL_ROWS, channels), mine=Place(half), sent=Place(half)),
        dict(df=vmem(c_bf), dpw=vmem(c_bf), dph=vmem(c_bf), dz=vmem(c_f32), small=small, upsum=upsum, buf=buf, unite=unite_space, pad=pad, taps=ksum),
    )
    part1 = extra_sum(scatter_stage(part1, GROUPS[2]))
    small0, mine0, sent0, part1, *features = tie(back.small_out, back.mine, back.sent, part1, *features)
    gathered = lax.all_gather(part1, ("dp", "tile"), axis=0, tiled=True)[:BLOCKS]
    part0 = narrow_add([mine0, flat_partner(sent0, near)])
    total0, (part0,) = total_sum(small0, [part0], 1)
    part0 = scatter_stage(part0, GROUPS[1])
    total0, part0 = tie(total0, part0)
    part0 = extra_sum(scatter_stage(part0, GROUPS[2]))
    last = run(
        lambda r: kernel_last(cells, r),
        "conv_last",
        2 * 10**9,
        dict(tile=tile_arg, **{key: Late(value, step=2, hold=True) for key, value in dict(a=first.a, dn=back.dn, dm=back.dm).items()}, stats=stats0, totals=total0, kernels=kernels, batch_gain=batch_gain),
        {f"o{k}": piece for k in range(4)},
        dict(padd=pad, du=map4),
    )
    part0, *grads = tie(part0, last.o0, last.o1, last.o2, last.o3)
    grads = swap_pieces(grads)
    part0 = gather_stage(part0, GROUPS[2])
    part0, *grads = tie(part0, *grads)
    got0 = [flat_partner(part0, mask) for mask in masks(GROUPS[1])]
    features_out = join_pieces(features, tile)
    grads = join_pieces(grads, tile)
    grad_shapes = dict(up=shape(2, channels, hidden), down=shape(2, channels, hidden), unite=shape(2, channels, 3 * channels))
    whole = run(
        kernel_unpack_gathered,
        "unpack_1",
        10**7,
        dict(blocks=Late(gathered)),
        {key: Stream(value, 1) for key, value in grad_shapes.items()},
        tight=True,
    )
    line = shape(2, channels)
    fin = run(
        lambda r: kernel_finish(cells, r),
        "finish",
        10**6,
        dict(total0=total0, total1=total1, stats=stats0, gain=batch_gain),
        dict(
            batch_shift=line, batch_gain=line, norm_gain=line, norm_shift=line, down_bias=line, unite_bias=line, up_bias=shape(2, hidden),
            kernel=shape(3, 3, 2, channels), mix_width=shape(MAP, 2, MAP), mix_height=shape(MAP, 2, MAP), mix_width_bias=shape(2, MAP), mix_height_bias=shape(2, MAP),
        ),
    )
    whole_1 = (whole.up, whole.down, whole.unite)
    part0, features_out, grads, *rest = tie(part0, features_out, grads, *whole_1, *got0)
    whole_1, got0 = rest[:3], rest[3:]
    part0 = jnp.concatenate([part0, *got0], 0)
    far = flat_partner(part0, near)
    whole = run(
        kernel_unpack,
        "unpack_0",
        10**7,
        dict(index=index_arg, near=Late(part0), far=Late(far), up_in=Kept(whole_1[0]), down_in=Kept(whole_1[1]), unite_in=Kept(whole_1[2])),
        {key: Stream(value, 0) for key, value in grad_shapes.items()},
        aliases={3: 0, 4: 1, 5: 2},
        tight=True,
    )

    def to_output(field):
        return field.transpose(2, 0, 1, 3)[:, None]

    return (
        to_output(features_out),
        to_output(grads),
        fin.kernel.transpose(2, 0, 1, 3),
        fin.batch_gain,
        fin.batch_shift,
        fin.mix_width.transpose(1, 0, 2),
        fin.mix_width_bias,
        fin.mix_height.transpose(1, 0, 2),
        fin.mix_height_bias,
        whole.unite.transpose(0, 2, 1),
        fin.unite_bias,
        fin.norm_gain,
        fin.norm_shift,
        whole.up,
        fin.up_bias,
        whole.down.transpose(0, 2, 1),
        fin.down_bias,
    )


def solution(mesh):
    field = P("dp", "tile", None, None, None)
    return jax.shard_map(
        on_device,
        mesh=mesh,
        in_specs=(field,) + (P(),) * 15 + (field,),
        out_specs=(field, field) + (P(),) * 15,
        check_vma=False,
    )
```

```python
import math

import jax
import jax.numpy as jnp
from jax import lax
from jax.experimental import pallas as pl
from jax.experimental.pallas import tpu as pltpu
from jax.sharding import PartitionSpec as P

F32 = jnp.float32
BF16 = jnp.bfloat16
norm_epsilon = 1e-05
layer_epsilon = 1e-06
ROOT_HALF = 0.7071067811865476
INV_ROOT_TAU = 0.3989422804014327
LOG2E = 1.4426950408889634

TS = 7
MAP = 14
IMG = 8
ROW = MAP * IMG
PIECE = TS * TS * IMG
VMEM_BYTES = 58 * 1024 * 1024
MARGIN = 8 * 1024 * 1024
BLK = 256


def partner(x, axis, distance):
    count = lax.axis_size(axis)
    return lax.ppermute(x, axis, [(i, i ^ distance) for i in range(count)])


def stages():
    result = [("tile", (1, 2, 3))]
    count = lax.axis_size("dp")
    step = 1
    if count > 1 and (count.bit_length() - 1) % 2 == 1:
        result.append(("dp", (1,)))
        step = 2
    while step < count:
        result.append(("dp", (step, 2 * step, 3 * step)))
        step *= 4
    return result


def sum_stage(x, stage):
    axis, distances = stage
    got = [partner(x, axis, d) for d in distances]
    if len(got) == 1:
        return x + got[0]
    return (x + got[0]) + (got[1] + got[2])


def total_sum(x, after=None, when=2):
    for step, stage in enumerate(stages()):
        if step == when and after is not None:
            x, *after = tie(x, *after)
        x = sum_stage(x, stage)
    return x if after is None else (x, after)


def total_moments(stats, count, after=None):
    for step, (axis, distances) in enumerate(stages()):
        if step == 2 and after is not None:
            stats, *after = tie(stats, *after)
        parts = [stats] + [partner(stats, axis, d) for d in distances]
        if len(parts) == 2:
            mean = (parts[0][0] + parts[1][0]) * 0.5
            dev = [jnp.square(p[0] - mean) for p in parts]
            square = (parts[0][1] + parts[1][1]) + count * (dev[0] + dev[1])
        else:
            mean = ((parts[0][0] + parts[1][0]) + (parts[2][0] + parts[3][0])) * 0.25
            dev = [jnp.square(p[0] - mean) for p in parts]
            square = ((parts[0][1] + parts[1][1]) + (parts[2][1] + parts[3][1])) + count * (
                (dev[0] + dev[1]) + (dev[2] + dev[3])
            )
        count = count * len(parts)
        stats = jnp.stack([mean, square])
    return stats if after is None else (stats, after)


def to_whole(field, tile):
    share = field.shape[2] // lax.axis_size("tile")
    pieces = []
    for k in range(4):
        part = lax.dynamic_slice_in_dim(field, (tile ^ k) * share, share, 2)
        part = part.reshape(TS * TS * share, field.shape[3])
        pieces.append(part if k == 0 else partner(part, "tile", k))
    return pieces


def swap_pieces(pieces):
    return [pieces[0]] + [partner(pieces[k], "tile", k) for k in range(1, 4)]


def join_pieces(pieces, tile):
    channels = pieces[0].shape[-1]
    share = pieces[0].shape[0] // (TS * TS)
    result = jnp.zeros((TS, TS, share * lax.axis_size("tile"), channels), pieces[0].dtype)
    for k in range(4):
        part = pieces[k].reshape(TS, TS, share, channels)
        result = lax.dynamic_update_slice_in_dim(result, part, (tile ^ k) * share, 2)
    return result


def flat_partner(x, mask):
    axes = ("dp", "tile")
    count = lax.axis_size("dp") * lax.axis_size("tile")
    return lax.ppermute(x, axes, [(i, i ^ mask) for i in range(count)])


GROUPS = ((0,), (1, 2), (3, 4))
BLOCKS = 32


def block_index():
    flat = lax.axis_index("dp") * lax.axis_size("tile") + lax.axis_index("tile")
    index = jnp.zeros((), jnp.int32)
    for group in GROUPS:
        for bit in group:
            index = index * 2 + ((flat >> bit) & 1)
    return index


def masks(group):
    if len(group) == 1:
        return [1 << group[0]]
    return [1 << group[1], 1 << group[0], (1 << group[0]) | (1 << group[1])]


def narrow_add(parts):
    parts = [p.astype(F32) for p in parts]
    total = parts[0] + parts[1]
    if len(parts) == 4:
        total = total + (parts[2] + parts[3])
    return total.astype(BF16)


def scatter_stage(x, group):
    wide = masks(group)
    size = x.shape[0] // (len(wide) + 1)
    got = [flat_partner(x[(j + 1) * size : (j + 2) * size], mask) for j, mask in enumerate(wide)]
    return narrow_add([x[:size]] + got)


def scatter_sends(x, group):
    wide = masks(group)
    size = x.shape[0] // (len(wide) + 1)
    return [flat_partner(x[(j + 1) * size : (j + 2) * size], mask) for j, mask in enumerate(wide)]


def extra_sum(x):
    count = lax.axis_size("dp") * lax.axis_size("tile")
    mask = BLOCKS
    while mask < count:
        x = narrow_add([x, flat_partner(x, mask)])
        mask *= 2
    return x


def gather_stage(x, group):
    return jnp.concatenate([x] + [flat_partner(x, mask) for mask in masks(group)], 0)


def tie(*values):
    return lax.optimization_barrier(values)


def dot(a, b):
    return lax.dot_general(a, b, (((1,), (0,)), ((), ())), preferred_element_type=F32)


def dot_nt(a, b):
    return lax.dot_general(a, b, (((1,), (1,)), ((), ())), preferred_element_type=F32)


def dot_tn(a, b):
    return lax.dot_general(a, b, (((0,), (0,)), ((), ())), preferred_element_type=F32)


def spread(ref, layer, repeat, turned=False):
    matrix = ref[...].astype(F32)[:, layer, :].astype(BF16)
    size = MAP * repeat
    shift = repeat.bit_length() - 1
    row = lax.broadcasted_iota(jnp.int32, (size, MAP), 0)
    col = lax.broadcasted_iota(jnp.int32, (size, MAP), 1)
    pick = jnp.where((row >> shift) == col, 1.0, 0.0).astype(BF16)
    half = dot_nt(pick, matrix) if turned else dot(pick, matrix)
    wide = dot_nt(half.astype(BF16), pick)
    row = lax.broadcasted_iota(jnp.int32, (size, size), 0)
    col = lax.broadcasted_iota(jnp.int32, (size, size), 1)
    return jnp.where((row & (repeat - 1)) == (col & (repeat - 1)), wide, 0.0).astype(BF16)


def spread_bias(ref, layer, repeat):
    size = MAP * repeat
    shift = repeat.bit_length() - 1
    row = lax.broadcasted_iota(jnp.int32, (size, MAP), 0)
    col = lax.broadcasted_iota(jnp.int32, (size, MAP), 1)
    return jnp.sum(jnp.where((row >> shift) == col, ref[layer : layer + 1], 0.0), axis=1, keepdims=True)


def collapse(product, repeat):
    size = MAP * repeat
    shift = repeat.bit_length() - 1
    row = lax.broadcasted_iota(jnp.int32, (size, size), 0)
    col = lax.broadcasted_iota(jnp.int32, (size, size), 1)
    kept = jnp.where((row & (repeat - 1)) == (col & (repeat - 1)), product, 0.0)
    kept = jnp.sum(kept.reshape(MAP, repeat, size), axis=1)
    row = lax.broadcasted_iota(jnp.int32, (size, MAP), 0)
    col = lax.broadcasted_iota(jnp.int32, (size, MAP), 1)
    pick = jnp.where((row >> shift) == col, 1.0, 0.0).astype(F32)
    return lax.dot_general(
        kept, pick, (((1,), (0,)), ((), ())), preferred_element_type=F32, precision=lax.Precision.HIGHEST
    )


def lane_groups(channels):
    return [(lo, min(lo + 128, channels)) for lo in range(0, channels, 128)]


def zero_border(pad):
    shape = pad.shape
    pad[0] = jnp.zeros(shape[1:], F32)
    pad[MAP + 1] = jnp.zeros(shape[1:], F32)
    for h in range(1, MAP + 1):
        pad[h, 0] = jnp.zeros(shape[2:], F32)
        pad[h, MAP + 1] = jnp.zeros(shape[2:], F32)


def pick_columns(field, w0):
    return jnp.where(w0 == 0, field[:, :TS], field[:, TS:])


def corner(tile, k):
    other = tile ^ k
    return (other >> 1) * TS, (other & 1) * TS


def conv_rows(pad, kernel_ref, layer, out_ref, stats_ref, sums, then=None):
    channels = pad.shape[-1]
    sums[...] = jnp.zeros(sums.shape, F32)

    def body(h, carry):
        for lo, hi in lane_groups(channels):
            acc = None
            for r in range(3):
                for s in range(3):
                    term = pad[h + r, s : s + MAP, :, lo:hi] * kernel_ref[r, s, layer : layer + 1, lo:hi]
                    acc = term if acc is None else acc + term
            out_ref[h, :, lo:hi] = acc.reshape(ROW, hi - lo)
            sums[0, :, lo:hi] += jnp.sum(acc, axis=0)
        if then is not None:
            then(h)
        return carry

    lax.fori_loop(0, MAP, body, 0)
    count = MAP * ROW
    mean = jnp.sum(sums[0], axis=0, keepdims=True) * (1.0 / count)

    def again(h, carry):
        for lo, hi in lane_groups(channels):
            dev = out_ref[h, :, lo:hi] - mean[:, lo:hi]
            sums[1, :, lo:hi] += jnp.sum((dev * dev).reshape(MAP, IMG, hi - lo), axis=0)
        return carry

    lax.fori_loop(0, MAP, again, 0)
    stats_ref[0:1] = mean
    stats_ref[1:2] = jnp.sum(sums[1], axis=0, keepdims=True)


def scale_of(stats_ref, cells):
    mean = stats_ref[0:1]
    return mean, lax.rsqrt(stats_ref[1:2] * (1.0 / cells) + norm_epsilon)


JOINED = 1024
MAIN = 256


def joined_places(channels):
    rest = channels - MAIN
    return [(i, 0, MAIN, i * MAIN) for i in range(3)] + [(i, MAIN, rest, 3 * MAIN + i * rest) for i in range(3)]


def put_joined(ref, rows, i, value):
    for part, first, size, lane in joined_places(value.shape[-1]):
        if part == i:
            ref[rows + (slice(lane, lane + size),)] = value[..., first : first + size]


def get_joined(value, i, channels):
    pieces = [value[..., lane : lane + size] for part, first, size, lane in joined_places(channels) if part == i]
    return jnp.concatenate(pieces, axis=-1)


def mix_forward(layer, cells, a_ref, stats_ref, gain_ref, shift_ref, mw_ref, mwb_ref, mh_ref, mhb_ref, joined):
    mean, rstd = scale_of(stats_ref, cells)
    channels = a_ref.shape[-1]
    gain = gain_ref[layer : layer + 1]
    shift = shift_ref[layer : layer + 1]
    width = spread(mw_ref, layer, IMG)
    height = spread(mh_ref, layer, 16)
    width_bias = spread_bias(mwb_ref, layer, IMG)
    height_bias = spread_bias(mhb_ref, layer, 16)
    used = 3 * channels
    joined[:, :, used:] = jnp.zeros(joined.shape[:2] + (joined.shape[2] - used,), BF16)
    whole = slice(None)
    for h in range(MAP):
        value = (((a_ref[h] - mean) * rstd) * gain + shift).astype(BF16)
        put_joined(joined, (h, whole), 0, value)
        put_joined(joined, (h, whole), 1, (dot(width, value) + width_bias).astype(BF16))
    for j in range(ROW // 16):
        cols = slice(16 * j, 16 * j + 16)
        value = get_joined(joined[:, cols, :], 0, channels).reshape(MAP * 16, channels)
        mixed = (dot(height, value) + height_bias).astype(BF16)
        put_joined(joined, (whole, cols), 2, mixed.reshape(MAP, 16, channels))


def gelu_pair(v):
    t = 1.0 / (1.0 + (0.3275911 * ROOT_HALF) * jnp.abs(v))
    e = jnp.exp2(v * v * (-0.5 * LOG2E))
    q = ((((0.5 * 1.061405429 * t - 0.5 * 1.453152027) * t + 0.5 * 1.421413741) * t - 0.5 * 0.284496736) * t + 0.5 * 0.254829592) * t * e
    phi = jnp.where(v >= 0, 1.0 - q, q)
    return v * phi, phi + v * e * INV_ROOT_TAU


HALVES = 2
PART = MAP // HALVES


def half_rows(ref, p):
    value = ref[p * PART : (p + 1) * PART]
    return value.reshape(PART * ROW, value.shape[-1])


def put_half(ref, p, value):
    ref[p * PART : (p + 1) * PART] = value.reshape(PART, ROW, value.shape[-1])


def add_half(ref, p, value):
    ref[p * PART : (p + 1) * PART] += value.reshape(PART, ROW, value.shape[-1])


def column_sums(value):
    return jnp.sum(value.reshape(-1, 8, value.shape[-1]), axis=0)


def unite_norm(r, layer, p, residual):
    one = slice(layer, layer + 1)
    m = residual + r.unite_bias[one] + dot(half_rows(r.joined.ref, p), r.unite[...])
    centre = jnp.mean(m, axis=-1, keepdims=True)
    dev = m - centre
    s = lax.rsqrt(jnp.mean(dev * dev, axis=-1, keepdims=True) + layer_epsilon)
    zhat = dev * s
    zb = (zhat * r.norm_gain[one] + r.norm_shift[one]).astype(BF16)
    return m, zhat, s, zb


def hidden_block(r, layer, j):
    blk = slice(j * BLK, (j + 1) * BLK) if isinstance(j, int) else pl.ds(pl.multiple_of(j * BLK, BLK), BLK)
    return blk, r.up.ref[:, blk], r.down.ref[:, blk]


def block_half(value):
    return value.reshape(PART, ROW, BLK)


def norm_backward(r, layer, p, do32, zhat, s, dz, df_ref):
    one = slice(layer, layer + 1)
    channels = do32.shape[-1]
    e = dz * r.norm_gain[one]
    mean_e = jnp.mean(e, axis=-1, keepdims=True)
    mean_ez = jnp.mean(e * zhat, axis=-1, keepdims=True)
    dm = do32 + s * (e - mean_e - zhat * mean_ez)
    put_half(r.dm.ref, p, dm)
    df = dm.astype(BF16)
    put_half(df_ref, p, df)
    r.small[2] += column_sums(dz * zhat)
    r.small[3] += column_sums(dz)
    r.small[4] += column_sums(do32)
    r.small[5] += column_sums(dm)
    dj = dot_nt(df, r.unite[...])
    put_half(r.dn.ref, p, get_joined(dj, 0, channels))
    put_half(r.dpw, p, get_joined(dj, 1, channels).astype(BF16))
    put_half(r.dph, p, get_joined(dj, 2, channels).astype(BF16))


GROUP_LANES = 128
PER_QUARTER = 7


def put_group(r, q, value):
    size = r.buf.shape[2]
    count = value.shape[0] // size
    quarter = q // PER_QUARTER if isinstance(q, int) else lax.div(q, PER_QUARTER)
    lane = q - quarter * PER_QUARTER
    for b in range(count):
        r.buf[(quarter * count + b) ^ r.index[0], lane] = value[b * size : (b + 1) * size].astype(BF16)


def put_columns(r, q, value):
    for i in range(value.shape[-1] // GROUP_LANES):
        put_group(r, q + i, value[:, i * GROUP_LANES : (i + 1) * GROUP_LANES])


def flat_rows(value):
    return value.reshape(MAP * ROW, value.shape[-1])


def hidden_gradients(r, j, blocks, zb, do, g, dh):
    per = BLK // GROUP_LANES
    put_columns(r, per * j, dot_tn(flat_rows(zb[...]), dh))
    put_columns(r, per * (j + blocks), dot_tn(flat_rows(do[...]), g))


def mix_backward(layer, cells, a_ref, stats_ref, mw_ref, mh_ref, dpw, dph, dn_ref, small, send):
    mean, rstd = scale_of(stats_ref, cells)
    width = spread(mw_ref, layer, IMG, turned=True)
    height = spread(mh_ref, layer, 16, turned=True)
    for j in range(ROW // 16):
        cols = slice(16 * j, 16 * j + 16)
        value = dph[:, cols, :].reshape(MAP * 16, -1)
        dn_ref[:, cols, :] += dot(height, value).reshape(MAP, 16, -1)

    totals = [small[0], small[1]]
    for h in range(MAP):
        dn = dn_ref[h] + dot(width, dpw[h])
        dn_ref[h] = dn
        send(h)
        xhat = (a_ref[h] - mean) * rstd
        totals[0] = totals[0] + jnp.sum(dn.reshape(MAP, IMG, -1), axis=0)
        totals[1] = totals[1] + jnp.sum((dn * xhat).reshape(MAP, IMG, -1), axis=0)
    small[0], small[1] = totals


def unite_gradients(r, blocks, df_ref, out_ref):
    df = flat_rows(df_ref[...])
    channels = df.shape[-1]
    joined, dpw, dph = r.joined.ref, r.dpw, r.dph
    put_columns(r, 2 * blocks * (BLK // GROUP_LANES), dot_tn(df, flat_rows(joined[...])))

    wide = jnp.zeros((ROW, ROW), F32)
    bias = jnp.zeros((ROW, channels), F32)
    for h in range(MAP):
        wide = wide + dot_nt(dpw[h], get_joined(joined[h], 0, channels))
        bias = bias + dpw[h].astype(F32)
    tall = jnp.zeros((MAP * 16, MAP * 16), F32)
    tall_bias = jnp.zeros((MAP, 16, channels), F32)
    for j in range(ROW // 16):
        cols = slice(16 * j, 16 * j + 16)
        value = dph[:, cols, :]
        tall = tall + dot_nt(value.reshape(MAP * 16, channels), get_joined(joined[:, cols, :], 0, channels).reshape(MAP * 16, channels))
        tall_bias = tall_bias + value.astype(F32)
    diagonal = lax.broadcasted_iota(jnp.int32, (MAP, MAP), 0) == lax.broadcasted_iota(jnp.int32, (MAP, MAP), 1)

    def as_row(field):
        col = jnp.sum(jnp.sum(field, axis=1), axis=-1, keepdims=True)
        return jnp.sum(jnp.where(diagonal, col, 0.0), axis=0, keepdims=True)

    width = jnp.concatenate([collapse(wide, IMG), as_row(bias.reshape(MAP, IMG, channels))], axis=0)
    height = jnp.concatenate([collapse(tall, 16), as_row(tall_bias)], axis=0)
    for v in range(MAP + 1):
        row, lane = mix_place(v)
        out_ref[row : row + 1, lane : lane + MAP] = width[v : v + 1]
        out_ref[row : row + 1, lane + 16 : lane + 16 + MAP] = height[v : v + 1]


MIX_ROW = 10
TAPS_ROW = 12
KERNEL_ROW = 21
SMALL_ROWS = 32


def mix_place(v):
    return MIX_ROW + v // 10, 32 * (v % 10)


def put_small(out_ref, small, upsum):
    channels = out_ref.shape[-1]
    for i in range(6):
        out_ref[i : i + 1] = jnp.sum(small[i], axis=0, keepdims=True)
    up = jnp.sum(upsum[...], axis=0, keepdims=True)
    for i in range(up.shape[-1] // channels):
        out_ref[6 + i : 7 + i] = up[:, i * channels : (i + 1) * channels]


def tap_sums(value, pad, h, lo, hi, total):
    for r in range(3):
        for s in range(3):
            total[3 * r + s, :, lo:hi] += jnp.sum(value * pad[h + r, s : s + MAP, :, lo:hi], axis=0)


def put_taps(out_ref, row, total):
    for i in range(9):
        out_ref[row + i : row + i + 1] = jnp.sum(total[i], axis=0, keepdims=True)


def conv_backward(layer, cells, a, stats_ref, totals_ref, gain, kernel_ref, dn, dm, emit, padd, x=None, padx=None, ksum=None, send=None):
    mean, rstd = scale_of(stats_ref, cells)
    scale = rstd * gain[layer : layer + 1]
    shift_mean = totals_ref[0:1] * (1.0 / cells)
    gain_mean = totals_ref[1:2] * (1.0 / cells)
    channels = padd.shape[-1]
    arriving = [part for part in (a, dn, dm, x) if part is not None]
    for c in range(MAP // 2):
        for part in arriving:
            part.start_part(c)
    zero_border(padd)
    if x is not None:
        zero_border(padx)
        ksum[...] = jnp.zeros(ksum.shape, F32)

    def fill(c):
        for part in arriving:
            part.wait(c)
        for i in range(2):
            h = 2 * c + i
            xhat = (a.ref[h] - mean) * rstd
            da = scale * (dn.ref[h] - shift_mean - xhat * gain_mean)
            padd[h + 1, 1 : MAP + 1] = da.reshape(MAP, IMG, -1)
            if x is not None:
                padx[h + 1, 1 : MAP + 1] = x.ref[h].astype(BF16).astype(F32).reshape(MAP, IMG, -1)

    def rows(c):
        for i in range(2):
            h = 2 * c + i
            for lo, hi in lane_groups(channels):
                acc = dm.ref[h, :, lo:hi].reshape(MAP, IMG, hi - lo)
                da = padd[h + 1, 1 : MAP + 1, :, lo:hi]
                for r in range(3):
                    for s in range(3):
                        acc = acc + padd[h + 2 - r, 2 - s : 2 - s + MAP, :, lo:hi] * kernel_ref[r, s, layer : layer + 1, lo:hi]
                if x is not None:
                    tap_sums(da, padx, h, lo, hi, ksum)
                emit(h, lo, hi, acc)
        if send is not None:
            send(c)

    fill(0)

    def body(c, carry):
        fill(c + 1)
        rows(c)
        return carry

    lax.fori_loop(0, MAP // 2 - 1, body, 0)
    rows(MAP // 2 - 1)


def fill_pad(pad, x_ref):
    def body(h, carry):
        pad[h + 1, 1 : MAP + 1] = x_ref[h].astype(F32).reshape(MAP, IMG, -1)
        return carry

    lax.fori_loop(0, MAP, body, 0)


def kernel_taps(r):
    r.x.wait_all()
    zero_border(r.pad)
    fill_pad(r.pad, r.x.ref)
    r.a.wait_all()
    mean = r.stats[0:1]
    for total in (r.alone, r.times):
        total[...] = jnp.zeros(total.shape, F32)

    def body(h, carry):
        for lo, hi in lane_groups(r.pad.shape[-1]):
            value = (r.a.ref[h, :, lo:hi] - mean[:, lo:hi]).reshape(MAP, IMG, hi - lo)
            for i in range(3):
                for s in range(3):
                    window = r.pad[h + i, s : s + MAP, :, lo:hi]
                    r.alone[3 * i + s, :, lo:hi] += jnp.sum(window, axis=0)
                    r.times[3 * i + s, :, lo:hi] += jnp.sum(value * window, axis=0)
        return carry

    lax.fori_loop(0, MAP, body, 0)
    r.out[...] = jnp.zeros(r.out.shape, F32)
    put_taps(r.out, 0, r.alone)
    put_taps(r.out, 9, r.times)
    r.out[18:19] = mean


def kernel_first(r):
    tile = r.tile[0]
    zero_border(r.pad)
    for k, piece in enumerate((r.p0, r.p1, r.p2, r.p3)):
        h0, w0 = corner(tile, k)
        value = piece[...].astype(F32).reshape(TS, TS, IMG, -1)
        r.pad[pl.ds(1 + h0, TS), pl.ds(1 + w0, TS)] = value

    def body(h, carry):
        r.x[h] = r.pad[h + 1, 1 : MAP + 1].reshape(ROW, -1).astype(BF16)
        return carry

    lax.fori_loop(0, MAP, body, 0)
    conv_rows(r.pad, r.kernels, 0, r.a, r.stats, r.sums)


def turn_unite(r):
    r.unite_t.wait_all()
    channels = r.unite.shape[-1]
    for part, first, size, lane in joined_places(channels):
        r.unite[lane : lane + size] = r.unite_t.ref[:, part * channels + first : part * channels + first + size].T
    r.unite[3 * channels :] = jnp.zeros((JOINED - 3 * channels, channels), BF16)


def forward_front(r, layer, cells, later):
    r.a.wait_all()
    for part in later:
        part.start()
    mix_forward(layer, cells, r.a.ref, r.stats, r.batch_gain, r.batch_shift, r.mix_width, r.mix_width_bias, r.mix_height, r.mix_height_bias, r.joined.ref)


def kernel_forward(cells, r):
    forward_front(r, 0, cells, (r.unite_t, r.x, r.up, r.down))
    r.joined.send_all()
    turn_unite(r)
    zero_border(r.pad)
    r.x.wait_all()
    for p in range(HALVES):
        m, zhat, s, zb = unite_norm(r, 0, p, half_rows(r.x.ref, p).astype(F32))
        put_half(r.u.ref, p, m + r.down_bias[0:1])
        put_half(r.zhat.ref, p, zhat)
        put_half(r.s.ref, p, s)
        put_half(r.zb.ref, p, zb)
        for stream in (r.zhat, r.s, r.zb):
            stream.send(p)
    r.up.wait_all()
    r.down.wait_all()

    def body(j):
        blk, up, down = hidden_block(r, 0, j)
        for p in range(HALVES):
            g, d = gelu_pair(dot(half_rows(r.zb.ref, p), up) + r.up_bias[0:1, blk])
            g = g.astype(BF16)
            r.g.ref[j, p * PART : (p + 1) * PART] = block_half(g)
            r.d.ref[j, p * PART : (p + 1) * PART] = block_half(d.astype(BF16))
            add_half(r.u.ref, p, dot_nt(g, down))
        r.g.send(j)
        r.d.send(j)

    lax.fori_loop(0, r.up_bias.shape[-1] // BLK, lambda j, c: (body(j), c)[1], 0)
    r.u.send_all()

    def fill(h, carry):
        rounded = r.u.ref[h].astype(BF16).astype(F32)
        r.pad[h + 1, 1 : MAP + 1] = rounded.reshape(MAP, IMG, -1)
        return carry

    lax.fori_loop(0, MAP, fill, 0)
    conv_rows(r.pad, r.kernels, 1, r.a2.ref, r.stats2, r.sums, r.a2.send)


def clear(r):
    r.small[...] = jnp.zeros(r.small.shape, F32)
    r.upsum[...] = jnp.zeros(r.upsum.shape, F32)


def send_blocks(r):
    half = BLOCKS // 2
    r.mine.start(r.buf.at[pl.ds(0, half)])
    r.sent.start(r.buf.at[pl.ds(half, half)])


def kernel_turn(cells, r):
    tile = r.tile[0]
    clear(r)
    r.joined = Held(r.joined)
    forward_front(r, 1, cells, (r.unite_t, r.u, r.c0, r.c1, r.c2, r.c3, r.up, r.down))
    turn_unite(r)
    for k, piece in enumerate((r.c0, r.c1, r.c2, r.c3)):
        piece.wait_all()
        h0, w0 = corner(tile, k)
        r.cot[pl.ds(h0, TS), pl.ds(w0, TS)] = piece.ref[...].astype(F32).reshape(TS, TS, IMG, -1)
    r.u.wait_all()

    def cotangent(p):
        return r.cot[p * PART : (p + 1) * PART].reshape(PART * ROW, -1)

    for p in range(HALVES):
        m, zhat, s, zb = unite_norm(r, 1, p, half_rows(r.u.ref, p))
        put_half(r.out, p, m + r.down_bias[1:2])
        put_half(r.zhat, p, zhat)
        put_half(r.s, p, s)
        put_half(r.zb, p, zb)
        put_half(r.do, p, cotangent(p).astype(BF16))
    r.up.wait_all()
    r.down.wait_all()
    r.dz[...] = jnp.zeros(r.dz.shape, F32)
    blocks = r.up_bias.shape[-1] // BLK

    def body(j):
        blk, up, down = hidden_block(r, 1, j)
        gs, dhs = [], []
        for p in range(HALVES):
            g, d = gelu_pair(dot(half_rows(r.zb, p), up) + r.up_bias[1:2, blk])
            g = g.astype(BF16)
            add_half(r.out, p, dot_nt(g, down))
            dh = dot(half_rows(r.do, p), down) * d
            r.upsum[:, blk] += column_sums(dh)
            dh = dh.astype(BF16)
            add_half(r.dz, p, dot_nt(dh, up))
            gs.append(g)
            dhs.append(dh)
        return jnp.concatenate(gs, 0), jnp.concatenate(dhs, 0)

    done = []
    for j in range(blocks):
        done.append(body(j))
        if j > 0:
            hidden_gradients(r, j - 1, blocks, r.zb, r.do, *done[j - 1])
    hidden_gradients(r, blocks - 1, blocks, r.zb, r.do, *done[blocks - 1])
    for k, piece in enumerate((r.f0, r.f1, r.f2, r.f3)):
        h0, w0 = corner(tile, k)
        field = r.out[pl.ds(h0, TS)].reshape(TS, MAP, IMG, -1)
        piece.ref[...] = pick_columns(field, w0).reshape(PIECE, -1).astype(BF16)
        piece.send_all()
    for p in range(HALVES):
        norm_backward(r, 1, p, cotangent(p), half_rows(r.zhat, p), half_rows(r.s, p), half_rows(r.dz, p), r.df)
        r.dm.send(p)
    mix_backward(1, cells, r.a.ref, r.stats, r.mix_width, r.mix_height, r.dpw, r.dph, r.dn.ref, r.small, r.dn.send)
    r.small_out[...] = jnp.zeros(r.small_out.shape, F32)
    put_small(r.small_out, r.small, r.upsum)
    r.small_out[TAPS_ROW : TAPS_ROW + 18] = r.taps[...]
    unite_gradients(r, blocks, r.df, r.small_out)
    send_blocks(r)


def kernel_conv_middle(cells, r):
    def emit(h, lo, hi, value):
        r.du.ref[h, :, lo:hi] = value.reshape(ROW, hi - lo)
        r.do.ref[h, :, lo:hi] = value.reshape(ROW, hi - lo).astype(BF16)

    def send(c):
        r.do.send(c)
        r.du.send(c)

    conv_backward(1, cells, r.a, r.stats, r.totals, r.batch_gain, r.kernels, r.dn, r.dm, emit, r.padd, r.x, r.padx, r.ksum, send)
    put_taps(r.kgrad, 0, r.ksum)


def kernel_back(cells, r):
    for part in (r.do_in, r.down, r.up):
        part.start()
    r.d.start_part(0)
    r.zb.start()
    r.g.start_part(0)
    clear(r)
    r.do = r.do_in.ref
    for part in (r.do_in, r.up, r.down):
        part.wait_all()
    for j in range(1, r.d.parts):
        r.d.start_part(j)
        r.g.start_part(j)
    for part in (r.zhat, r.s, r.unite_t, r.du, r.joined, r.a, r.x):
        part.start()
    r.dz[...] = jnp.zeros(r.dz.shape, F32)
    blocks = r.upsum.shape[-1] // BLK

    def body(j):
        blk, up, down = hidden_block(r, 0, j)
        r.d.wait(j)
        dhs = []
        for p in range(HALVES):
            d = r.d.ref[j, p * PART : (p + 1) * PART].reshape(PART * ROW, BLK).astype(F32)
            dh = dot(half_rows(r.do, p), down) * d
            r.upsum[:, blk] += column_sums(dh)
            dh = dh.astype(BF16)
            add_half(r.dz, p, dot_nt(dh, up))
            dhs.append(dh)
        return jnp.concatenate(dhs, 0)

    def gradients(j, dh):
        if j == 0:
            r.zb.wait_all()
        r.g.wait(j)
        hidden_gradients(r, j, blocks, r.zb.ref, r.do, flat_rows(r.g.ref[j]), dh)

    done = []
    for j in range(blocks):
        done.append(body(j))
        if j > 0:
            gradients(j - 1, done[j - 1])
    gradients(blocks - 1, done[blocks - 1])
    turn_unite(r)
    r.du.wait_all()
    r.zhat.wait_all()
    r.s.wait_all()
    for p in range(HALVES):
        norm_backward(r, 0, p, half_rows(r.du.ref, p), half_rows(r.zhat.ref, p), half_rows(r.s.ref, p), half_rows(r.dz, p), r.df)
        r.dm.send(p)
    r.joined.wait_all()
    r.small_out[...] = jnp.zeros(r.small_out.shape, F32)
    unite_gradients(r, blocks, r.df, r.small_out)
    send_blocks(r)
    for part in (r.a, r.x):
        part.wait_all()
    zero_border(r.pad)
    fill_pad(r.pad, r.x.ref)
    r.taps[...] = jnp.zeros(r.taps.shape, F32)

    mix_backward(0, cells, r.a.ref, r.stats, r.mix_width, r.mix_height, r.dpw, r.dph, r.dn.ref, r.small, r.dn.send)

    def windows(h, carry):
        for lo, hi in lane_groups(r.pad.shape[-1]):
            tap_sums(r.dn.ref[h, :, lo:hi].reshape(MAP, IMG, hi - lo), r.pad, h, lo, hi, r.taps)
        return carry

    lax.fori_loop(0, MAP, windows, 0)
    put_small(r.small_out, r.small, r.upsum)
    put_taps(r.small_out, TAPS_ROW, r.taps)
    r.small_out[KERNEL_ROW : KERNEL_ROW + 9] = r.kgrad[0:9]


def kernel_last(cells, r):
    tile = r.tile[0]

    def emit(h, lo, hi, value):
        r.du[h, :, :, lo:hi] = value

    conv_backward(0, cells, r.a, r.stats, r.totals, r.batch_gain, r.kernels, r.dn, r.dm, emit, r.padd)
    for k, piece in enumerate((r.o0, r.o1, r.o2, r.o3)):
        h0, w0 = corner(tile, k)
        piece[...] = r.du[pl.ds(h0, TS), pl.ds(w0, TS)].reshape(PIECE, -1).astype(BF16)


def unpack_put(r, value, quarter, row):
    channels, hidden = r.up.ref.shape
    rows = pl.ds(row, value.shape[1])
    for i in range(value.shape[0]):
        base = (quarter * value.shape[0] + i) * GROUP_LANES
        if base < hidden:
            r.up.ref[rows, base : base + GROUP_LANES] = value[i]
        elif base < 2 * hidden:
            r.down.ref[rows, base - hidden : base - hidden + GROUP_LANES] = value[i]
        else:
            base -= 2 * hidden
            for part, first, size, lane in joined_places(channels):
                lo, hi = max(lane, base), min(lane + size, base + GROUP_LANES)
                if lo < hi:
                    target = part * channels + first + lo - lane
                    r.unite.ref[rows, target : target + hi - lo] = value[i, :, lo - base : hi - base]


def unpack_all(r, block):
    channels, hidden = r.up.ref.shape
    size = 4 * channels // BLOCKS
    per = channels // size
    lanes = PER_QUARTER * GROUP_LANES
    for quarter in range(4):
        for b in range(per):
            unpack_put(r, block(quarter * per + b), quarter, b * size)
        if (quarter + 1) * lanes >= hidden and quarter * lanes < hidden:
            r.up.send_all()
        if (quarter + 1) * lanes >= 2 * hidden and quarter * lanes < 2 * hidden:
            r.down.send_all()
    r.unite.send_all()


def kernel_unpack(r):
    index = r.index[0]
    half = BLOCKS // 2
    flip = index & (half - 1)
    own = index // half
    r.near.wait_all()
    r.far.wait_all()

    def block(p):
        place = (p & (half - 1)) ^ flip
        near, far = r.near.ref[place].astype(F32), r.far.ref[place].astype(F32)
        return jnp.where(own == p // half, near, far)

    unpack_all(r, block)


def kernel_finish(cells, r):
    channels = r.total0.shape[-1]
    for layer, total in enumerate((r.total0, r.total1)):
        one = slice(layer, layer + 1)
        r.batch_shift[one] = total[0:1]
        r.batch_gain[one] = total[1:2]
        r.norm_gain[one] = total[2:3]
        r.norm_shift[one] = total[3:4]
        r.down_bias[one] = total[4:5]
        r.unite_bias[one] = total[5:6]
        for i in range(r.up_bias.shape[-1] // channels):
            r.up_bias[one, i * channels : (i + 1) * channels] = total[6 + i : 7 + i]
        for v in range(MAP + 1):
            row, lane = mix_place(v)
            width, height = total[row : row + 1, lane : lane + MAP], total[row : row + 1, lane + 16 : lane + 16 + MAP]
            if v < MAP:
                r.mix_width[v, one], r.mix_height[v, one] = width, height
            else:
                r.mix_width_bias[one], r.mix_height_bias[one] = width, height
    mean, rstd = scale_of(r.stats, cells)
    shift_mean, gain_mean = r.total0[0:1] * (1.0 / cells), r.total0[1:2] * (1.0 / cells)
    for i in range(9):
        alone, times = r.total1[TAPS_ROW + i : TAPS_ROW + i + 1], r.total1[KERNEL_ROW + i : KERNEL_ROW + i + 1]
        value = r.total0[TAPS_ROW + i : TAPS_ROW + i + 1] - shift_mean * alone - gain_mean * rstd * times
        r.kernel[i // 3, i % 3, 0:1] = rstd * r.gain[0:1] * value
        r.kernel[i // 3, i % 3, 1:2] = r.total0[KERNEL_ROW + i : KERNEL_ROW + i + 1]


class Kept:
    def __init__(self, array):
        self.array = array


class Smem:
    def __init__(self, array):
        self.array = array


class Layer:
    def __init__(self, array, layer):
        self.array, self.layer = array, layer


def chunk_step(shape, step=None):
    if len(shape) == 4 and shape[1:3] == (MAP, ROW):
        return 1
    if len(shape) == 3 and shape[:2] == (MAP, ROW):
        return step or PART
    return shape[0]


class Late:
    def __init__(self, array, layer=None, step=None, hold=False):
        self.array, self.layer, self.hold = array, layer, hold
        self.step = chunk_step(self.shape, step)

    @property
    def shape(self):
        return self.array.shape if self.layer is None else self.array.shape[1:]

    @property
    def parts(self):
        return self.shape[0] // self.step


class LateJoin:
    def __init__(self, arrays):
        self.arrays = arrays
        self.dtype = arrays[0].dtype
        self.shape = (sum(a.shape[0] for a in arrays),) + arrays[0].shape[1:]


class LateJoinRef:
    def __init__(self, sources, ref, sems):
        self.ref, self.copies, row = ref, [], 0
        for i, source in enumerate(sources):
            size = source.shape[0]
            self.copies.append(pltpu.make_async_copy(source, ref.at[pl.ds(row, size)], sems.at[i]))
            row += size

    def start(self):
        for copy in self.copies:
            copy.start()

    def wait_all(self):
        for copy in self.copies:
            copy.wait()


class LateRef:
    def __init__(self, late, source, ref, sems):
        self.parts, self.step = late.parts, late.step
        self.source = source if late.layer is None else source.at[late.layer]
        self.ref, self.sems = ref, sems

    def copy(self, c):
        if self.parts == 1:
            return pltpu.make_async_copy(self.source, self.ref, self.sems.at[0])
        rows = pl.ds(self.step * c, self.step)
        return pltpu.make_async_copy(self.source.at[rows], self.ref.at[rows], self.sems.at[c])

    def start(self):
        for c in range(self.parts):
            self.copy(c).start()

    def start_part(self, c):
        self.copy(c).start()

    def wait(self, c):
        self.copy(c).wait()

    def wait_all(self):
        for c in range(self.parts):
            self.copy(c).wait()


class Stream:
    def __init__(self, out, layer=None, step=None):
        self.out, self.layer = out, layer
        self.step = chunk_step(self.shape, step)

    @property
    def shape(self):
        return self.out.shape if self.layer is None else self.out.shape[1:]


class Place:
    def __init__(self, out):
        self.out = out


class StreamRef:
    def __init__(self, stream, target, ref, sem):
        self.target, self.ref, self.sem = target if stream.layer is None else target.at[stream.layer], ref, sem
        self.step = stream.step

    def send(self, c):
        rows = pl.ds(self.step * c, self.step)
        pltpu.make_async_copy(self.ref.at[rows], self.target.at[rows], self.sem).start()

    def send_all(self):
        pltpu.make_async_copy(self.ref, self.target, self.sem).start()

    def finish(self):
        pltpu.make_async_copy(self.ref, self.target, self.sem).wait()


class PlaceRef:
    def __init__(self, target, sem):
        self.target, self.sem = target, sem

    def start(self, source):
        self.copy = pltpu.make_async_copy(source, self.target, self.sem)
        self.copy.start()

    def finish(self):
        self.copy.wait()


class Held:
    def __init__(self, ref):
        self.ref = ref


class Refs:
    pass


def full(array):
    rank = len(array.shape)
    return pl.BlockSpec(array.shape, lambda i: (0,) * rank)


ANY = pl.BlockSpec(memory_space=pl.ANY)
FINISHED = (
    "batch_shift", "batch_gain", "norm_gain", "norm_shift", "down_bias", "unite_bias", "up_bias",
    "kernel", "mix_width", "mix_height", "mix_width_bias", "mix_height_bias",
)


def _padded(array):
    shape = list(array.shape)
    if len(shape) > 1:
        shape[-2] = -(-shape[-2] // 16) * 16
    shape[-1] = -(-shape[-1] // 128) * 128
    return math.prod(shape) * jnp.dtype(array.dtype).itemsize


def run(body, name, flops, ins, outs, scratch=None, aliases=None, tight=False):
    scratch = dict(scratch or {})
    arrays, in_specs, out_specs, out_shapes, spaces = [], [], [], [], []
    for key, operand in ins.items():
        if isinstance(operand, Smem):
            in_specs.append(pl.BlockSpec(memory_space=pltpu.SMEM))
        elif isinstance(operand, Layer):
            shape, layer = operand.array.shape, operand.layer
            in_specs.append(pl.BlockSpec((None,) + shape[1:], lambda i, layer=layer, rank=len(shape): (layer,) + (0,) * (rank - 1)))
        elif isinstance(operand, Kept):
            in_specs.append(ANY)
        elif isinstance(operand, LateJoin):
            in_specs += [ANY] * len(operand.arrays)
            arrays += operand.arrays
            spaces += [pltpu.VMEM(operand.shape, operand.dtype), pltpu.SemaphoreType.DMA((len(operand.arrays),))]
            continue
        elif isinstance(operand, Late):
            in_specs.append(ANY)
            spaces += [pltpu.VMEM(operand.shape, operand.array.dtype), pltpu.SemaphoreType.DMA((operand.parts,))]
        else:
            in_specs.append(full(operand))
        arrays.append(getattr(operand, "array", operand))
    for key, out in outs.items():
        if isinstance(out, (Stream, Place)):
            out_specs.append(ANY)
            out_shapes.append(out.out)
            if isinstance(out, Stream):
                spaces.append(pltpu.VMEM(out.shape, out.out.dtype))
            spaces.append(pltpu.SemaphoreType.DMA)
        elif isinstance(out, Layer):
            shape, layer = out.array.shape, out.layer
            out_specs.append(pl.BlockSpec((None,) + shape[1:], lambda i, layer=layer, rank=len(shape): (layer,) + (0,) * (rank - 1)))
            out_shapes.append(out.array)
        else:
            out_specs.append(full(out))
            out_shapes.append(out)
    spaces += list(scratch.values())

    def wrapped(*refs):
        refs = list(refs)
        r = Refs()
        main, extra = refs[: len(arrays) + len(outs)], refs[len(arrays) + len(outs) :]
        late, streams = [], []
        for key, operand in ins.items():
            if isinstance(operand, LateJoin):
                sources = [main.pop(0) for _ in operand.arrays]
                ref = LateJoinRef(sources, extra.pop(0), extra.pop(0))
                late.append(ref)
                setattr(r, key, ref)
                continue
            ref = main.pop(0)
            if isinstance(operand, Late):
                ref = LateRef(operand, ref, extra.pop(0), extra.pop(0))
                if not operand.hold:
                    late.append(ref)
            setattr(r, key, ref)
        for key, out in outs.items():
            ref = main.pop(0)
            if isinstance(out, Stream):
                ref = StreamRef(out, ref, extra.pop(0), extra.pop(0))
                streams.append(ref)
            elif isinstance(out, Place):
                ref = PlaceRef(ref, extra.pop(0))
                streams.append(ref)
            setattr(r, key, ref)
        for key in scratch:
            setattr(r, key, extra.pop(0))
        for part in late:
            part.start()
        body(r)
        for stream in streams:
            stream.finish()

    held = [a for a, spec in zip(arrays + out_shapes, in_specs + out_specs) if spec is not ANY]
    held += [space for space in spaces if getattr(space, "memory_space", None) == pltpu.VMEM]
    need = sum(_padded(a) for a in held)
    limit = min(VMEM_BYTES, need + need // 4 + MARGIN) if tight else VMEM_BYTES
    size = sum(a.size * a.dtype.itemsize for a in arrays) + sum(o.size * o.dtype.itemsize for o in out_shapes)
    results = pl.pallas_call(
        wrapped,
        grid=(1,),
        in_specs=in_specs,
        out_specs=out_specs,
        out_shape=out_shapes,
        scratch_shapes=spaces,
        input_output_aliases=aliases or {},
        compiler_params=pltpu.CompilerParams(vmem_limit_bytes=limit),
        cost_estimate=pl.CostEstimate(flops=flops, bytes_accessed=size, transcendentals=0),
        name=name,
    )(*arrays)
    named = Refs()
    for key, value in zip(outs, results):
        setattr(named, key, value)
    return named


def on_device(
    patches,
    conv_kernel,
    batch_gain,
    batch_shift,
    mix_width,
    mix_width_bias,
    mix_height,
    mix_height_bias,
    unite_weight,
    unite_bias,
    norm_gain,
    norm_shift,
    up_weight,
    up_bias,
    down_weight,
    down_bias,
    cotangent,
):
    channels = patches.shape[-1]
    hidden = up_weight.shape[-1]
    tile = lax.axis_index("tile")
    tile_arg = Smem(tile.astype(jnp.int32).reshape(1))
    index_arg = Smem(block_index().reshape(1))
    local_cells = MAP * ROW
    cells = local_cells * lax.axis_size("dp") * lax.axis_size("tile")

    def rows(lanes, dtype):
        return jax.ShapeDtypeStruct((MAP, ROW, lanes), dtype)

    def shape(*dims, dtype=F32):
        return jax.ShapeDtypeStruct(dims, dtype)

    def vmem(struct):
        return pltpu.VMEM(struct.shape, struct.dtype)

    piece = shape(PIECE, channels, dtype=BF16)
    c_bf, c_f32, h_bf = rows(channels, BF16), rows(channels, F32), shape(hidden // BLK, MAP, ROW, BLK, dtype=BF16)
    map4 = pltpu.VMEM((MAP, MAP, IMG, channels), F32)
    pad = pltpu.VMEM((MAP + 2, MAP + 2, IMG, channels), F32)
    sums = pltpu.VMEM((2, 8, channels), F32)
    small = pltpu.VMEM((6, 8, channels), F32)
    upsum = pltpu.VMEM((8, hidden), F32)
    ksum = pltpu.VMEM((9, 8, channels), F32)
    unite_space = pltpu.VMEM((JOINED, channels), BF16)
    blocks = hidden // BLK
    groups = 2 * blocks * (BLK // GROUP_LANES) + JOINED // GROUP_LANES
    assert groups == 4 * PER_QUARTER
    block = (PER_QUARTER, 4 * channels // BLOCKS, GROUP_LANES)
    half = shape(BLOCKS // 2, *block, dtype=BF16)
    buf = pltpu.VMEM((BLOCKS, *block), BF16)

    kernels = conv_kernel.transpose(1, 2, 0, 3)
    down_t = down_weight.transpose(0, 2, 1)
    unite_t = unite_weight.transpose(0, 2, 1)
    mix_width = mix_width.transpose(1, 0, 2)
    mix_height = mix_height.transpose(1, 0, 2)

    x_pieces = to_whole(patches[:, 0].transpose(1, 2, 0, 3), tile)
    first = run(
        kernel_first,
        "conv_first",
        10**7,
        dict(tile=tile_arg, **{f"p{k}": x_pieces[k] for k in range(4)}, kernels=kernels),
        dict(x=c_bf, a=c_f32, stats=shape(2, channels)),
        dict(pad=pad, sums=sums),
        tight=True,
    )
    taps = run(
        kernel_taps,
        "taps",
        10**8,
        dict(x=Late(first.x), a=Late(first.a), stats=first.stats),
        dict(out=shape(24, channels)),
        dict(pad=pad, alone=ksum, times=ksum),
        tight=True,
    ).out
    stats0, (cotangent, taps) = total_moments(first.stats, float(local_cells), [cotangent, taps])
    taps = jnp.concatenate([taps[0:9], taps[9:18] + (taps[18:19] - stats0[0:1]) * taps[0:9]], 0)
    cot_pieces = to_whole(cotangent[:, 0].transpose(1, 2, 0, 3), tile)

    def forward_ins(layer):
        return dict(
            batch_gain=batch_gain, batch_shift=batch_shift,
            mix_width=mix_width, mix_width_bias=mix_width_bias, mix_height=mix_height, mix_height_bias=mix_height_bias,
            unite_t=Late(unite_t, layer, hold=True), up=Late(up_weight, layer, hold=True), down=Late(down_t, layer, hold=True),
            unite_bias=unite_bias, norm_gain=norm_gain, norm_shift=norm_shift, up_bias=up_bias, down_bias=down_bias,
        )

    fwd = run(
        lambda r: kernel_forward(cells, r),
        "block_forward",
        6 * 10**9,
        dict(a=Late(first.a), stats=stats0, **forward_ins(0), x=Late(first.x, hold=True), kernels=kernels),
        dict(
            joined=Stream(rows(JOINED, BF16)), zhat=Stream(c_f32), s=Stream(rows(1, F32)), zb=Stream(c_bf),
            g=Stream(h_bf), d=Stream(h_bf), u=Stream(c_f32), a2=Stream(c_f32, step=1), stats2=shape(2, channels),
        ),
        dict(pad=pad, sums=sums, unite=unite_space),
    )
    stats1, *cot_pieces = tie(fwd.stats2, *cot_pieces)
    stats1 = total_moments(stats1, float(local_cells))

    turn = run(
        lambda r: kernel_turn(cells, r),
        "block_turn",
        14 * 10**9,
        dict(
            tile=tile_arg, index=index_arg, a=Late(fwd.a2), stats=stats1, u=Late(fwd.u, hold=True), **{f"c{k}": Late(cot_pieces[k], hold=True) for k in range(4)},
            **forward_ins(1), taps=taps,
        ),
        dict(
            **{f"f{k}": Stream(piece) for k in range(4)}, dm=Stream(c_f32), dn=Stream(c_f32, step=1), small_out=shape(SMALL_ROWS, channels),
            mine=Place(half), sent=Place(half),
        ),
        dict(
            joined=vmem(rows(JOINED, BF16)), zb=vmem(c_bf), do=vmem(c_bf), df=vmem(c_bf), dpw=vmem(c_bf), dph=vmem(c_bf),
            cot=map4, out=vmem(c_f32), zhat=vmem(c_f32), s=vmem(rows(1, F32)), dz=vmem(c_f32), small=small, upsum=upsum, buf=buf, unite=unite_space,
        ),
    )
    features = [turn.f0, turn.f1, turn.f2, turn.f3]

    near = masks(GROUPS[0])[0]
    got = flat_partner(turn.sent, near)
    first_stage, *later_stages = stages()
    total1 = sum_stage(turn.small_out, first_stage)
    total1, mine1, got = tie(total1, turn.mine, got)
    part1 = narrow_add([mine1, got])
    got1 = scatter_sends(part1, GROUPS[1])
    for stage in later_stages:
        total1 = sum_stage(total1, stage)
    total1, part1, *got1 = tie(total1, part1[: part1.shape[0] // 4], *got1)
    part1 = narrow_add([part1, *got1])
    got1 = scatter_sends(part1, GROUPS[2])
    mid = run(
        lambda r: kernel_conv_middle(cells, r),
        "conv_middle",
        2 * 10**9,
        dict(**{key: Late(value, step=2, hold=True) for key, value in dict(a=fwd.a2, dn=turn.dn, x=fwd.u, dm=turn.dm).items()}, stats=stats1, totals=total1, kernels=kernels, batch_gain=batch_gain),
        dict(do=Stream(c_bf, step=2), du=Stream(c_f32, step=2), kgrad=shape(16, channels)),
        dict(padx=pad, padd=pad, ksum=ksum),
    )
    do, part1, *rest = tie(mid.do, part1[:1], *got1, *features)
    got1, features = rest[:3], rest[3:]
    part1 = extra_sum(narrow_add([part1, *got1]))
    got1 = [flat_partner(part1, mask) for mask in masks(GROUPS[2])]
    features = swap_pieces(features)
    back = run(
        lambda r: kernel_back(cells, r),
        "block_back",
        14 * 10**9,
        dict(
            index=index_arg,
            **{
                key: Late(value, layer, hold=True)
                for key, (value, layer) in dict(
                    down=(down_t, 0), do_in=(do, None), du=(mid.du, None), up=(up_weight, 0), d=(fwd.d, None), zb=(fwd.zb, None), g=(fwd.g, None), unite_t=(unite_t, 0),
                    zhat=(fwd.zhat, None), s=(fwd.s, None), joined=(fwd.joined, None), a=(first.a, None), x=(first.x, None),
                ).items()
            },
            kgrad=mid.kgrad, norm_gain=norm_gain, stats=stats0, mix_width=mix_width, mix_height=mix_height,
        ),
        dict(dm=Stream(c_f32), dn=Stream(c_f32, step=1), small_out=shape(SMALL_ROWS, channels), mine=Place(half), sent=Place(half)),
        dict(df=vmem(c_bf), dpw=vmem(c_bf), dph=vmem(c_bf), dz=vmem(c_f32), small=small, upsum=upsum, buf=buf, unite=unite_space, pad=pad, taps=ksum),
    )
    small0, mine0, sent0, part1, *rest = tie(back.small_out, back.mine, back.sent, part1, *got1, *features)
    part1 = jnp.concatenate([part1, *rest[:3]], 0)
    features = rest[3:]
    got = flat_partner(sent0, near)
    total0 = sum_stage(small0, first_stage)
    total0, mine0, got = tie(total0, mine0, got)
    part0 = narrow_add([mine0, got])
    got0 = scatter_sends(part0, GROUPS[1])
    for stage in later_stages[:-1]:
        total0 = sum_stage(total0, stage)
    total0, part1 = tie(total0, part1)
    got1 = [flat_partner(part1, mask) for mask in masks(GROUPS[1])]
    total0 = sum_stage(total0, later_stages[-1])
    total0, part0, *got0 = tie(total0, part0[: part0.shape[0] // 4], *got0)
    part0 = narrow_add([part0, *got0])
    got0 = scatter_sends(part0, GROUPS[2])
    last = run(
        lambda r: kernel_last(cells, r),
        "conv_last",
        2 * 10**9,
        dict(tile=tile_arg, **{key: Late(value, step=2, hold=True) for key, value in dict(a=first.a, dn=back.dn, dm=back.dm).items()}, stats=stats0, totals=total0, kernels=kernels, batch_gain=batch_gain),
        {f"o{k}": piece for k in range(4)},
        dict(padd=pad, du=map4),
    )
    part0, *rest = tie(part0, last.o0, last.o1, last.o2, last.o3, *got0, part1, *got1)
    grads, got0, parts1 = rest[:4], rest[4:7], rest[7:]
    grads = swap_pieces(grads)
    part0 = extra_sum(narrow_add([part0[:1], *got0]))
    got0 = [flat_partner(part0, mask) for mask in masks(GROUPS[2])]
    part0, *rest = tie(part0, *got0, *grads, *parts1)
    part0 = jnp.concatenate([part0, *rest[:3]], 0)
    grads, parts1 = rest[3:7], rest[7:]
    got0 = [flat_partner(part0, mask) for mask in masks(GROUPS[1])]
    far1 = [flat_partner(part, near) for part in parts1]
    features_out = join_pieces(features, tile)
    grads = join_pieces(grads, tile)
    grad_shapes = dict(up=shape(2, channels, hidden), down=shape(2, channels, hidden), unite=shape(2, channels, 3 * channels))
    whole = run(
        kernel_unpack,
        "unpack_1",
        10**7,
        dict(index=index_arg, near=LateJoin(parts1), far=LateJoin(far1)),
        {key: Stream(value, 1) for key, value in grad_shapes.items()},
        tight=True,
    )
    line = shape(2, channels)
    fin = run(
        lambda r: kernel_finish(cells, r),
        "finish",
        10**6,
        dict(total0=total0, total1=total1, stats=stats0, gain=batch_gain),
        dict(
            batch_shift=line, batch_gain=line, norm_gain=line, norm_shift=line, down_bias=line, unite_bias=line, up_bias=shape(2, hidden),
            kernel=shape(3, 3, 2, channels), mix_width=shape(MAP, 2, MAP), mix_height=shape(MAP, 2, MAP), mix_width_bias=shape(2, MAP), mix_height_bias=shape(2, MAP),
        ),
    )
    whole_1 = (whole.up, whole.down, whole.unite)
    small_results = [getattr(fin, key) for key in FINISHED]
    grads, features_out, *rest = tie(grads, features_out, part0, *got0, *whole_1, *small_results)
    parts0, whole_1, small_results = rest[:4], rest[4:7], rest[7:]
    for key, value in zip(FINISHED, small_results):
        setattr(fin, key, value)
    far = [flat_partner(part, near) for part in parts0]
    whole = run(
        kernel_unpack,
        "unpack_0",
        10**7,
        dict(index=index_arg, near=LateJoin(parts0), far=LateJoin(far), up_in=Kept(whole_1[0]), down_in=Kept(whole_1[1]), unite_in=Kept(whole_1[2])),
        {key: Stream(value, 0) for key, value in grad_shapes.items()},
        aliases={9: 0, 10: 1, 11: 2},
        tight=True,
    )

    def to_output(field):
        return field.transpose(2, 0, 1, 3)[:, None]

    return (
        to_output(features_out),
        to_output(grads),
        fin.kernel.transpose(2, 0, 1, 3),
        fin.batch_gain,
        fin.batch_shift,
        fin.mix_width.transpose(1, 0, 2),
        fin.mix_width_bias,
        fin.mix_height.transpose(1, 0, 2),
        fin.mix_height_bias,
        whole.unite.transpose(0, 2, 1),
        fin.unite_bias,
        fin.norm_gain,
        fin.norm_shift,
        whole.up,
        fin.up_bias,
        whole.down.transpose(0, 2, 1),
        fin.down_bias,
    )


def solution(mesh):
    field = P("dp", "tile", None, None, None)
    return jax.shard_map(
        on_device,
        mesh=mesh,
        in_specs=(field,) + (P(),) * 15 + (field,),
        out_specs=(field, field) + (P(),) * 15,
        check_vma=False,
    )
```

```python
import math

import jax
import jax.numpy as jnp
from jax import lax
from jax.experimental import pallas as pl
from jax.experimental.pallas import tpu as pltpu
from jax.sharding import PartitionSpec as P

F32 = jnp.float32
BF16 = jnp.bfloat16
norm_epsilon = 1e-05
layer_epsilon = 1e-06
ROOT_HALF = 0.7071067811865476
INV_ROOT_TAU = 0.3989422804014327
LOG2E = 1.4426950408889634

TS = 7
MAP = 14
IMG = 8
ROW = MAP * IMG
PIECE = TS * TS * IMG
VMEM_BYTES = 58 * 1024 * 1024
MARGIN = 8 * 1024 * 1024
BLK = 256


def partner(x, axis, distance):
    count = lax.axis_size(axis)
    return lax.ppermute(x, axis, [(i, i ^ distance) for i in range(count)])


def stages():
    result = [("tile", (1, 2, 3))]
    count = lax.axis_size("dp")
    step = 1
    if count > 1 and (count.bit_length() - 1) % 2 == 1:
        result.append(("dp", (1,)))
        step = 2
    while step < count:
        result.append(("dp", (step, 2 * step, 3 * step)))
        step *= 4
    return result


def sum_stage(x, stage):
    axis, distances = stage
    got = [partner(x, axis, d) for d in distances]
    if len(got) == 1:
        return x + got[0]
    return (x + got[0]) + (got[1] + got[2])


def total_sum(x, after=None, when=2):
    for step, stage in enumerate(stages()):
        if step == when and after is not None:
            x, *after = tie(x, *after)
        x = sum_stage(x, stage)
    return x if after is None else (x, after)


def total_moments(stats, count, after=None):
    for step, (axis, distances) in enumerate(stages()):
        if step == 2 and after is not None:
            stats, *after = tie(stats, *after)
        parts = [stats] + [partner(stats, axis, d) for d in distances]
        if len(parts) == 2:
            mean = (parts[0][0] + parts[1][0]) * 0.5
            dev = [jnp.square(p[0] - mean) for p in parts]
            square = (parts[0][1] + parts[1][1]) + count * (dev[0] + dev[1])
        else:
            mean = ((parts[0][0] + parts[1][0]) + (parts[2][0] + parts[3][0])) * 0.25
            dev = [jnp.square(p[0] - mean) for p in parts]
            square = ((parts[0][1] + parts[1][1]) + (parts[2][1] + parts[3][1])) + count * (
                (dev[0] + dev[1]) + (dev[2] + dev[3])
            )
        count = count * len(parts)
        stats = jnp.stack([mean, square])
    return stats if after is None else (stats, after)


def to_whole(field, tile):
    share = field.shape[2] // lax.axis_size("tile")
    pieces = []
    for k in range(4):
        part = lax.dynamic_slice_in_dim(field, (tile ^ k) * share, share, 2)
        part = part.reshape(TS * TS * share, field.shape[3])
        pieces.append(part if k == 0 else partner(part, "tile", k))
    return pieces


def swap_pieces(pieces):
    return [pieces[0]] + [partner(pieces[k], "tile", k) for k in range(1, 4)]


def join_pieces(pieces, tile):
    channels = pieces[0].shape[-1]
    share = pieces[0].shape[0] // (TS * TS)
    result = jnp.zeros((TS, TS, share * lax.axis_size("tile"), channels), pieces[0].dtype)
    for k in range(4):
        part = pieces[k].reshape(TS, TS, share, channels)
        result = lax.dynamic_update_slice_in_dim(result, part, (tile ^ k) * share, 2)
    return result


def flat_partner(x, mask):
    axes = ("dp", "tile")
    count = lax.axis_size("dp") * lax.axis_size("tile")
    return lax.ppermute(x, axes, [(i, i ^ mask) for i in range(count)])


GROUPS = ((0,), (1, 2))
SPLIT_BITS = 3
QUAD = 4
BLOCKS = 32


def block_index():
    flat = lax.axis_index("dp") * lax.axis_size("tile") + lax.axis_index("tile")
    index = jnp.zeros((), jnp.int32)
    for group in GROUPS:
        for bit in group:
            index = index * 2 + ((flat >> bit) & 1)
    return index * QUAD


def masks(group):
    if len(group) == 1:
        return [1 << group[0]]
    return [1 << group[1], 1 << group[0], (1 << group[0]) | (1 << group[1])]


def narrow_add(parts):
    parts = [p.astype(F32) for p in parts]
    total = parts[0] + parts[1]
    if len(parts) == 4:
        total = total + (parts[2] + parts[3])
    return total.astype(BF16)


def scatter_sends(x, group):
    wide = masks(group)
    size = x.shape[0] // (len(wide) + 1)
    return [flat_partner(x[(j + 1) * size : (j + 2) * size], mask) for j, mask in enumerate(wide)]


def far_masks():
    count = lax.axis_size("dp") * lax.axis_size("tile")
    return [1 << bit for bit in range(SPLIT_BITS, count.bit_length() - 1)]


def add_partner(x, mask):
    return narrow_add([x, flat_partner(x, mask)])


def tie(*values):
    return lax.optimization_barrier(values)


def dot(a, b):
    return lax.dot_general(a, b, (((1,), (0,)), ((), ())), preferred_element_type=F32)


def dot_nt(a, b):
    return lax.dot_general(a, b, (((1,), (1,)), ((), ())), preferred_element_type=F32)


def dot_tn(a, b):
    return lax.dot_general(a, b, (((0,), (0,)), ((), ())), preferred_element_type=F32)


def spread(ref, layer, repeat, turned=False):
    matrix = ref[...].astype(F32)[:, layer, :].astype(BF16)
    size = MAP * repeat
    shift = repeat.bit_length() - 1
    row = lax.broadcasted_iota(jnp.int32, (size, MAP), 0)
    col = lax.broadcasted_iota(jnp.int32, (size, MAP), 1)
    pick = jnp.where((row >> shift) == col, 1.0, 0.0).astype(BF16)
    half = dot_nt(pick, matrix) if turned else dot(pick, matrix)
    wide = dot_nt(half.astype(BF16), pick)
    row = lax.broadcasted_iota(jnp.int32, (size, size), 0)
    col = lax.broadcasted_iota(jnp.int32, (size, size), 1)
    return jnp.where((row & (repeat - 1)) == (col & (repeat - 1)), wide, 0.0).astype(BF16)


def spread_bias(ref, layer, repeat):
    size = MAP * repeat
    shift = repeat.bit_length() - 1
    row = lax.broadcasted_iota(jnp.int32, (size, MAP), 0)
    col = lax.broadcasted_iota(jnp.int32, (size, MAP), 1)
    return jnp.sum(jnp.where((row >> shift) == col, ref[layer : layer + 1], 0.0), axis=1, keepdims=True)


def collapse(product, repeat):
    size = MAP * repeat
    shift = repeat.bit_length() - 1
    row = lax.broadcasted_iota(jnp.int32, (size, size), 0)
    col = lax.broadcasted_iota(jnp.int32, (size, size), 1)
    kept = jnp.where((row & (repeat - 1)) == (col & (repeat - 1)), product, 0.0)
    kept = jnp.sum(kept.reshape(MAP, repeat, size), axis=1)
    row = lax.broadcasted_iota(jnp.int32, (size, MAP), 0)
    col = lax.broadcasted_iota(jnp.int32, (size, MAP), 1)
    pick = jnp.where((row >> shift) == col, 1.0, 0.0).astype(F32)
    return lax.dot_general(
        kept, pick, (((1,), (0,)), ((), ())), preferred_element_type=F32, precision=lax.Precision.HIGHEST
    )


def lane_groups(channels):
    return [(lo, min(lo + 128, channels)) for lo in range(0, channels, 128)]


def zero_border(pad):
    shape = pad.shape
    pad[0] = jnp.zeros(shape[1:], F32)
    pad[MAP + 1] = jnp.zeros(shape[1:], F32)
    for h in range(1, MAP + 1):
        pad[h, 0] = jnp.zeros(shape[2:], F32)
        pad[h, MAP + 1] = jnp.zeros(shape[2:], F32)


def pick_columns(field, w0):
    return jnp.where(w0 == 0, field[:, :TS], field[:, TS:])


def corner(tile, k):
    other = tile ^ k
    return (other >> 1) * TS, (other & 1) * TS


def conv_rows(pad, kernel_ref, layer, out_ref, stats_ref, sums, then=None):
    channels = pad.shape[-1]
    sums[...] = jnp.zeros(sums.shape, F32)

    def body(h, carry):
        for lo, hi in lane_groups(channels):
            acc = None
            for r in range(3):
                for s in range(3):
                    term = pad[h + r, s : s + MAP, :, lo:hi] * kernel_ref[r, s, layer : layer + 1, lo:hi]
                    acc = term if acc is None else acc + term
            out_ref[h, :, lo:hi] = acc.reshape(ROW, hi - lo)
            sums[0, :, lo:hi] += jnp.sum(acc, axis=0)
        if then is not None:
            then(h)
        return carry

    lax.fori_loop(0, MAP, body, 0)
    count = MAP * ROW
    mean = jnp.sum(sums[0], axis=0, keepdims=True) * (1.0 / count)

    def again(h, carry):
        for lo, hi in lane_groups(channels):
            dev = out_ref[h, :, lo:hi] - mean[:, lo:hi]
            sums[1, :, lo:hi] += jnp.sum((dev * dev).reshape(MAP, IMG, hi - lo), axis=0)
        return carry

    lax.fori_loop(0, MAP, again, 0)
    stats_ref[0:1] = mean
    stats_ref[1:2] = jnp.sum(sums[1], axis=0, keepdims=True)


def scale_of(stats_ref, cells):
    mean = stats_ref[0:1]
    return mean, lax.rsqrt(stats_ref[1:2] * (1.0 / cells) + norm_epsilon)


JOINED = 1024
MAIN = 256


def joined_places(channels):
    rest = channels - MAIN
    return [(i, 0, MAIN, i * MAIN) for i in range(3)] + [(i, MAIN, rest, 3 * MAIN + i * rest) for i in range(3)]


def put_joined(ref, rows, i, value):
    for part, first, size, lane in joined_places(value.shape[-1]):
        if part == i:
            ref[rows + (slice(lane, lane + size),)] = value[..., first : first + size]


def get_joined(value, i, channels):
    pieces = [value[..., lane : lane + size] for part, first, size, lane in joined_places(channels) if part == i]
    return jnp.concatenate(pieces, axis=-1)


def mix_forward(layer, cells, arrive, a_ref, stats_ref, gain_ref, shift_ref, mw_ref, mwb_ref, mh_ref, mhb_ref, joined):
    mean, rstd = scale_of(stats_ref, cells)
    channels = a_ref.shape[-1]
    gain = gain_ref[layer : layer + 1]
    shift = shift_ref[layer : layer + 1]
    width = spread(mw_ref, layer, IMG)
    height = spread(mh_ref, layer, 16)
    width_bias = spread_bias(mwb_ref, layer, IMG)
    height_bias = spread_bias(mhb_ref, layer, 16)
    used = 3 * channels
    joined[:, :, used:] = jnp.zeros(joined.shape[:2] + (joined.shape[2] - used,), BF16)
    whole = slice(None)
    for h in range(MAP):
        if h % PART == 0:
            arrive(h // PART)
        value = (((a_ref[h] - mean) * rstd) * gain + shift).astype(BF16)
        put_joined(joined, (h, whole), 0, value)
        put_joined(joined, (h, whole), 1, (dot(width, value) + width_bias).astype(BF16))
    for j in range(ROW // 16):
        cols = slice(16 * j, 16 * j + 16)
        value = get_joined(joined[:, cols, :], 0, channels).reshape(MAP * 16, channels)
        mixed = (dot(height, value) + height_bias).astype(BF16)
        put_joined(joined, (whole, cols), 2, mixed.reshape(MAP, 16, channels))


def gelu_pair(v):
    t = 1.0 / (1.0 + (0.3275911 * ROOT_HALF) * jnp.abs(v))
    e = jnp.exp2(v * v * (-0.5 * LOG2E))
    q = ((((0.5 * 1.061405429 * t - 0.5 * 1.453152027) * t + 0.5 * 1.421413741) * t - 0.5 * 0.284496736) * t + 0.5 * 0.254829592) * t * e
    phi = jnp.where(v >= 0, 1.0 - q, q)
    return v * phi, phi + v * e * INV_ROOT_TAU


HALVES = 2
PART = MAP // HALVES


def half_rows(ref, p):
    value = ref[p * PART : (p + 1) * PART]
    return value.reshape(PART * ROW, value.shape[-1])


def put_half(ref, p, value):
    ref[p * PART : (p + 1) * PART] = value.reshape(PART, ROW, value.shape[-1])


def add_half(ref, p, value):
    ref[p * PART : (p + 1) * PART] += value.reshape(PART, ROW, value.shape[-1])


def column_sums(value):
    return jnp.sum(value.reshape(-1, 8, value.shape[-1]), axis=0)


def unite_norm(r, layer, p, residual):
    one = slice(layer, layer + 1)
    m = residual + r.unite_bias[one] + dot(half_rows(r.joined.ref, p), r.unite[...])
    centre = jnp.mean(m, axis=-1, keepdims=True)
    dev = m - centre
    s = lax.rsqrt(jnp.mean(dev * dev, axis=-1, keepdims=True) + layer_epsilon)
    zhat = dev * s
    zb = (zhat * r.norm_gain[one] + r.norm_shift[one]).astype(BF16)
    return m, zhat, s, zb


def hidden_block(r, layer, j):
    blk = slice(j * BLK, (j + 1) * BLK) if isinstance(j, int) else pl.ds(pl.multiple_of(j * BLK, BLK), BLK)
    return blk, r.up.ref[:, blk], r.down.ref[:, blk]


def block_half(value):
    return value.reshape(PART, ROW, BLK)


def norm_backward(r, layer, p, do32, zhat, s, dz, df_ref):
    one = slice(layer, layer + 1)
    channels = do32.shape[-1]
    e = dz * r.norm_gain[one]
    mean_e = jnp.mean(e, axis=-1, keepdims=True)
    mean_ez = jnp.mean(e * zhat, axis=-1, keepdims=True)
    dm = do32 + s * (e - mean_e - zhat * mean_ez)
    put_half(r.dm.ref, p, dm)
    df = dm.astype(BF16)
    put_half(df_ref, p, df)
    r.small[2] += column_sums(dz * zhat)
    r.small[3] += column_sums(dz)
    r.small[4] += column_sums(do32)
    r.small[5] += column_sums(dm)
    dj = dot_nt(df, r.unite[...])
    put_half(r.dn.ref, p, get_joined(dj, 0, channels))
    put_half(r.dpw, p, get_joined(dj, 1, channels).astype(BF16))
    put_half(r.dph, p, get_joined(dj, 2, channels).astype(BF16))


GROUP_LANES = 128
PER_QUARTER = 7


def put_group(r, q, value):
    size = r.buf.shape[2]
    count = value.shape[0] // size
    quarter = q // PER_QUARTER if isinstance(q, int) else lax.div(q, PER_QUARTER)
    lane = q - quarter * PER_QUARTER
    for b in range(count):
        r.buf[(quarter * count + b) ^ r.index[0], lane] = value[b * size : (b + 1) * size].astype(BF16)


def put_columns(r, q, value):
    for i in range(value.shape[-1] // GROUP_LANES):
        put_group(r, q + i, value[:, i * GROUP_LANES : (i + 1) * GROUP_LANES])


def flat_rows(value):
    return value.reshape(MAP * ROW, value.shape[-1])


def hidden_gradients(r, j, blocks, zb, do, g, dh):
    per = BLK // GROUP_LANES
    put_columns(r, per * j, dot_tn(flat_rows(zb[...]), dh))
    put_columns(r, per * (j + blocks), dot_tn(flat_rows(do[...]), g))


def mix_backward(layer, cells, a_ref, stats_ref, mw_ref, mh_ref, dpw, dph, dn_ref, small, send):
    mean, rstd = scale_of(stats_ref, cells)
    width = spread(mw_ref, layer, IMG, turned=True)
    height = spread(mh_ref, layer, 16, turned=True)
    for j in range(ROW // 16):
        cols = slice(16 * j, 16 * j + 16)
        value = dph[:, cols, :].reshape(MAP * 16, -1)
        dn_ref[:, cols, :] += dot(height, value).reshape(MAP, 16, -1)

    totals = [small[0], small[1]]
    for h in range(MAP):
        dn = dn_ref[h] + dot(width, dpw[h])
        dn_ref[h] = dn
        send(h)
        xhat = (a_ref[h] - mean) * rstd
        totals[0] = totals[0] + jnp.sum(dn.reshape(MAP, IMG, -1), axis=0)
        totals[1] = totals[1] + jnp.sum((dn * xhat).reshape(MAP, IMG, -1), axis=0)
    small[0], small[1] = totals


def unite_gradients(r, blocks, df_ref, out_ref):
    df = flat_rows(df_ref[...])
    channels = df.shape[-1]
    joined, dpw, dph = r.joined.ref, r.dpw, r.dph
    put_columns(r, 2 * blocks * (BLK // GROUP_LANES), dot_tn(df, flat_rows(joined[...])))

    wide = jnp.zeros((ROW, ROW), F32)
    bias = jnp.zeros((ROW, channels), F32)
    for h in range(MAP):
        wide = wide + dot_nt(dpw[h], get_joined(joined[h], 0, channels))
        bias = bias + dpw[h].astype(F32)
    tall = jnp.zeros((MAP * 16, MAP * 16), F32)
    tall_bias = jnp.zeros((MAP, 16, channels), F32)
    for j in range(ROW // 16):
        cols = slice(16 * j, 16 * j + 16)
        value = dph[:, cols, :]
        tall = tall + dot_nt(value.reshape(MAP * 16, channels), get_joined(joined[:, cols, :], 0, channels).reshape(MAP * 16, channels))
        tall_bias = tall_bias + value.astype(F32)
    diagonal = lax.broadcasted_iota(jnp.int32, (MAP, MAP), 0) == lax.broadcasted_iota(jnp.int32, (MAP, MAP), 1)

    def as_row(field):
        col = jnp.sum(jnp.sum(field, axis=1), axis=-1, keepdims=True)
        return jnp.sum(jnp.where(diagonal, col, 0.0), axis=0, keepdims=True)

    width = jnp.concatenate([collapse(wide, IMG), as_row(bias.reshape(MAP, IMG, channels))], axis=0)
    height = jnp.concatenate([collapse(tall, 16), as_row(tall_bias)], axis=0)
    for v in range(MAP + 1):
        row, lane = mix_place(v)
        out_ref[row : row + 1, lane : lane + MAP] = width[v : v + 1]
        out_ref[row : row + 1, lane + 16 : lane + 16 + MAP] = height[v : v + 1]


MIX_ROW = 10
TAPS_ROW = 12
KERNEL_ROW = 21
SMALL_ROWS = 32


def mix_place(v):
    return MIX_ROW + v // 10, 32 * (v % 10)


def put_small(out_ref, small, upsum):
    channels = out_ref.shape[-1]
    for i in range(6):
        out_ref[i : i + 1] = jnp.sum(small[i], axis=0, keepdims=True)
    up = jnp.sum(upsum[...], axis=0, keepdims=True)
    for i in range(up.shape[-1] // channels):
        out_ref[6 + i : 7 + i] = up[:, i * channels : (i + 1) * channels]


def tap_sums(value, pad, h, lo, hi, total):
    for r in range(3):
        for s in range(3):
            total[3 * r + s, :, lo:hi] += jnp.sum(value * pad[h + r, s : s + MAP, :, lo:hi], axis=0)


def put_taps(out_ref, row, total):
    for i in range(9):
        out_ref[row + i : row + i + 1] = jnp.sum(total[i], axis=0, keepdims=True)


def conv_backward(layer, cells, a, stats_ref, totals_ref, gain, kernel_ref, dn, dm, emit, padd, x=None, padx=None, ksum=None, send=None):
    mean, rstd = scale_of(stats_ref, cells)
    scale = rstd * gain[layer : layer + 1]
    shift_mean = totals_ref[0:1] * (1.0 / cells)
    gain_mean = totals_ref[1:2] * (1.0 / cells)
    channels = padd.shape[-1]
    arriving = [part for part in (a, dn, dm, x) if part is not None]
    for c in range(MAP // 2):
        for part in arriving:
            part.start_part(c)
    zero_border(padd)
    if x is not None:
        zero_border(padx)
        ksum[...] = jnp.zeros(ksum.shape, F32)

    def fill(c):
        for part in arriving:
            part.wait(c)
        for i in range(2):
            h = 2 * c + i
            xhat = (a.ref[h] - mean) * rstd
            da = scale * (dn.ref[h] - shift_mean - xhat * gain_mean)
            padd[h + 1, 1 : MAP + 1] = da.reshape(MAP, IMG, -1)
            if x is not None:
                padx[h + 1, 1 : MAP + 1] = x.ref[h].astype(BF16).astype(F32).reshape(MAP, IMG, -1)

    def rows(c):
        for i in range(2):
            h = 2 * c + i
            for lo, hi in lane_groups(channels):
                acc = dm.ref[h, :, lo:hi].reshape(MAP, IMG, hi - lo)
                da = padd[h + 1, 1 : MAP + 1, :, lo:hi]
                for r in range(3):
                    for s in range(3):
                        acc = acc + padd[h + 2 - r, 2 - s : 2 - s + MAP, :, lo:hi] * kernel_ref[r, s, layer : layer + 1, lo:hi]
                if x is not None:
                    tap_sums(da, padx, h, lo, hi, ksum)
                emit(h, lo, hi, acc)
        if send is not None:
            send(c)

    fill(0)

    def body(c, carry):
        fill(c + 1)
        rows(c)
        return carry

    lax.fori_loop(0, MAP // 2 - 1, body, 0)
    rows(MAP // 2 - 1)


def fill_pad(pad, x_ref):
    def body(h, carry):
        pad[h + 1, 1 : MAP + 1] = x_ref[h].astype(F32).reshape(MAP, IMG, -1)
        return carry

    lax.fori_loop(0, MAP, body, 0)


def kernel_taps(r):
    r.x.wait_all()
    zero_border(r.pad)
    fill_pad(r.pad, r.x.ref)
    r.a.wait_all()
    mean = r.stats[0:1]
    for total in (r.alone, r.times):
        total[...] = jnp.zeros(total.shape, F32)

    def body(h, carry):
        for lo, hi in lane_groups(r.pad.shape[-1]):
            value = (r.a.ref[h, :, lo:hi] - mean[:, lo:hi]).reshape(MAP, IMG, hi - lo)
            for i in range(3):
                for s in range(3):
                    window = r.pad[h + i, s : s + MAP, :, lo:hi]
                    r.alone[3 * i + s, :, lo:hi] += jnp.sum(window, axis=0)
                    r.times[3 * i + s, :, lo:hi] += jnp.sum(value * window, axis=0)
        return carry

    lax.fori_loop(0, MAP, body, 0)
    r.out[...] = jnp.zeros(r.out.shape, F32)
    put_taps(r.out, 0, r.alone)
    put_taps(r.out, 9, r.times)
    r.out[18:19] = mean


def kernel_first(r):
    tile = r.tile[0]
    zero_border(r.pad)
    for k, piece in enumerate((r.p0, r.p1, r.p2, r.p3)):
        h0, w0 = corner(tile, k)
        value = piece[...].astype(F32).reshape(TS, TS, IMG, -1)
        r.pad[pl.ds(1 + h0, TS), pl.ds(1 + w0, TS)] = value

    def body(h, carry):
        r.x[h] = r.pad[h + 1, 1 : MAP + 1].reshape(ROW, -1).astype(BF16)
        return carry

    lax.fori_loop(0, MAP, body, 0)
    conv_rows(r.pad, r.kernels, 0, r.a, r.stats, r.sums)


def turn_unite(r):
    r.unite_t.wait_all()
    channels = r.unite.shape[-1]
    for part, first, size, lane in joined_places(channels):
        r.unite[lane : lane + size] = r.unite_t.ref[:, part * channels + first : part * channels + first + size].T
    r.unite[3 * channels :] = jnp.zeros((JOINED - 3 * channels, channels), BF16)


def forward_front(r, layer, cells, later):
    def arrive(p):
        r.a.wait(p)
        if p == HALVES - 1:
            for part in later:
                part.start()

    mix_forward(layer, cells, arrive, r.a.ref, r.stats, r.batch_gain, r.batch_shift, r.mix_width, r.mix_width_bias, r.mix_height, r.mix_height_bias, r.joined.ref)


def kernel_forward(cells, r):
    forward_front(r, 0, cells, (r.unite_t, r.x, r.up, r.down))
    r.joined.send_all()
    turn_unite(r)
    zero_border(r.pad)
    r.x.wait_all()
    for p in range(HALVES):
        m, zhat, s, zb = unite_norm(r, 0, p, half_rows(r.x.ref, p).astype(F32))
        put_half(r.u.ref, p, m + r.down_bias[0:1])
        put_half(r.zhat.ref, p, zhat)
        put_half(r.s.ref, p, s)
        put_half(r.zb.ref, p, zb)
        for stream in (r.zhat, r.s, r.zb):
            stream.send(p)
    r.up.wait_all()
    r.down.wait_all()

    def body(j):
        blk, up, down = hidden_block(r, 0, j)
        for p in range(HALVES):
            g, d = gelu_pair(dot(half_rows(r.zb.ref, p), up) + r.up_bias[0:1, blk])
            g = g.astype(BF16)
            r.g.ref[j, p * PART : (p + 1) * PART] = block_half(g)
            r.d.ref[j, p * PART : (p + 1) * PART] = block_half(d.astype(BF16))
            add_half(r.u.ref, p, dot_nt(g, down))
        r.g.send(j)
        r.d.send(j)

    lax.fori_loop(0, r.up_bias.shape[-1] // BLK, lambda j, c: (body(j), c)[1], 0)
    r.u.send_all()

    def fill(h, carry):
        rounded = r.u.ref[h].astype(BF16).astype(F32)
        r.pad[h + 1, 1 : MAP + 1] = rounded.reshape(MAP, IMG, -1)
        return carry

    lax.fori_loop(0, MAP, fill, 0)
    conv_rows(r.pad, r.kernels, 1, r.a2.ref, r.stats2, r.sums, r.a2.send)


def clear(r):
    r.small[...] = jnp.zeros(r.small.shape, F32)
    r.upsum[...] = jnp.zeros(r.upsum.shape, F32)


def send_blocks(r):
    half = BLOCKS // 2
    r.mine.start(r.buf.at[pl.ds(0, half)])
    r.sent.start(r.buf.at[pl.ds(half, half)])


def kernel_whole_map(r):
    tile = r.tile[0]
    for k, piece in enumerate((r.p0, r.p1, r.p2, r.p3)):
        h0, w0 = corner(tile, k)
        r.field[pl.ds(h0, TS), pl.ds(w0, TS)] = piece[...].astype(F32).reshape(TS, TS, IMG, -1)
    for h in range(MAP):
        r.out[h] = r.field[h].reshape(ROW, -1).astype(BF16)


def kernel_pieces(r):
    tile = r.tile[0]
    for k, piece in enumerate((r.p0, r.p1, r.p2, r.p3)):
        h0, w0 = corner(tile, k)
        field = r.field[pl.ds(h0, TS)].astype(F32).reshape(TS, MAP, IMG, -1)
        piece[...] = pick_columns(field, w0).reshape(PIECE, -1).astype(BF16)


def kernel_turn(cells, r):
    clear(r)
    r.do = r.do_in.ref
    r.joined = Held(r.joined)
    forward_front(r, 1, cells, (r.unite_t, r.u, r.up, r.down, r.do_in))
    turn_unite(r)
    r.u.wait_all()

    def cotangent(p):
        return half_rows(r.do, p).astype(F32)

    for p in range(HALVES):
        m, zhat, s, zb = unite_norm(r, 1, p, half_rows(r.u.ref, p))
        put_half(r.out, p, m + r.down_bias[1:2])
        put_half(r.zhat, p, zhat)
        put_half(r.s, p, s)
        put_half(r.zb, p, zb)
    for part in (r.up, r.down, r.do_in):
        part.wait_all()
    r.dz[...] = jnp.zeros(r.dz.shape, F32)
    blocks = r.up_bias.shape[-1] // BLK

    def body(j):
        blk, up, down = hidden_block(r, 1, j)
        gs, dhs = [], []
        for p in range(HALVES):
            g, d = gelu_pair(dot(half_rows(r.zb, p), up) + r.up_bias[1:2, blk])
            g = g.astype(BF16)
            add_half(r.out, p, dot_nt(g, down))
            dh = dot(half_rows(r.do, p), down) * d
            r.upsum[:, blk] += column_sums(dh)
            dh = dh.astype(BF16)
            add_half(r.dz, p, dot_nt(dh, up))
            gs.append(g)
            dhs.append(dh)
        return jnp.concatenate(gs, 0), jnp.concatenate(dhs, 0)

    done = []
    for j in range(blocks):
        done.append(body(j))
        if j > 0:
            hidden_gradients(r, j - 1, blocks, r.zb, r.do, *done[j - 1])
    hidden_gradients(r, blocks - 1, blocks, r.zb, r.do, *done[blocks - 1])
    r.features.ref[...] = r.out[...].astype(BF16)
    r.features.send_all()
    for p in range(HALVES):
        norm_backward(r, 1, p, cotangent(p), half_rows(r.zhat, p), half_rows(r.s, p), half_rows(r.dz, p), r.df)
        r.dm.send(p)
    r.small_out[...] = jnp.zeros(r.small_out.shape, F32)
    unite_gradients(r, blocks, r.df, r.small_out)
    send_blocks(r)
    mix_backward(1, cells, r.a.ref, r.stats, r.mix_width, r.mix_height, r.dpw, r.dph, r.dn.ref, r.small, r.dn.send)
    put_small(r.small_out, r.small, r.upsum)
    r.small_out[TAPS_ROW : TAPS_ROW + 18] = r.taps[...]


def kernel_conv_middle(cells, r):
    def emit(h, lo, hi, value):
        r.du.ref[h, :, lo:hi] = value.reshape(ROW, hi - lo)
        r.do.ref[h, :, lo:hi] = value.reshape(ROW, hi - lo).astype(BF16)

    def send(c):
        r.do.send(c)
        r.du.send(c)

    conv_backward(1, cells, r.a, r.stats, r.totals, r.batch_gain, r.kernels, r.dn, r.dm, emit, r.padd, r.x, r.padx, r.ksum, send)
    put_taps(r.kgrad, 0, r.ksum)


def kernel_back(cells, r):
    for part in (r.do_in, r.down, r.up):
        part.start()
    r.d.start_part(0)
    clear(r)
    r.do = r.do_in.ref
    for part in (r.do_in, r.up, r.down):
        part.wait_all()
    r.d.start_part(1)
    r.zb.start()
    r.g.start_part(0)
    r.dz[...] = jnp.zeros(r.dz.shape, F32)
    blocks = r.upsum.shape[-1] // BLK
    later = {blocks - 2: (r.zhat, r.s, r.unite_t, r.du), blocks - 1: (r.joined, r.a, r.x)}

    def body(j):
        blk, up, down = hidden_block(r, 0, j)
        r.d.wait(j)
        if j > 0:
            if j + 1 < blocks:
                r.d.start_part(j + 1)
            r.g.start_part(j)
        for part in later.get(j, ()):
            part.start()
        dhs = []
        for p in range(HALVES):
            d = r.d.ref[j, p * PART : (p + 1) * PART].reshape(PART * ROW, BLK).astype(F32)
            dh = dot(half_rows(r.do, p), down) * d
            r.upsum[:, blk] += column_sums(dh)
            dh = dh.astype(BF16)
            add_half(r.dz, p, dot_nt(dh, up))
            dhs.append(dh)
        return jnp.concatenate(dhs, 0)

    def gradients(j, dh):
        if j == 0:
            r.zb.wait_all()
        r.g.wait(j)
        hidden_gradients(r, j, blocks, r.zb.ref, r.do, flat_rows(r.g.ref[j]), dh)

    done = []
    for j in range(blocks):
        done.append(body(j))
        if j > 0:
            gradients(j - 1, done[j - 1])
    gradients(blocks - 1, done[blocks - 1])
    turn_unite(r)
    r.du.wait_all()
    r.zhat.wait_all()
    r.s.wait_all()
    for p in range(HALVES):
        norm_backward(r, 0, p, half_rows(r.du.ref, p), half_rows(r.zhat.ref, p), half_rows(r.s.ref, p), half_rows(r.dz, p), r.df)
        r.dm.send(p)
    r.joined.wait_all()
    r.small_out[...] = jnp.zeros(r.small_out.shape, F32)
    unite_gradients(r, blocks, r.df, r.small_out)
    send_blocks(r)
    for part in (r.a, r.x):
        part.wait_all()
    zero_border(r.pad)
    fill_pad(r.pad, r.x.ref)
    r.taps[...] = jnp.zeros(r.taps.shape, F32)

    mix_backward(0, cells, r.a.ref, r.stats, r.mix_width, r.mix_height, r.dpw, r.dph, r.dn.ref, r.small, r.dn.send)

    def windows(h, carry):
        for lo, hi in lane_groups(r.pad.shape[-1]):
            tap_sums(r.dn.ref[h, :, lo:hi].reshape(MAP, IMG, hi - lo), r.pad, h, lo, hi, r.taps)
        return carry

    lax.fori_loop(0, MAP, windows, 0)
    put_small(r.small_out, r.small, r.upsum)
    put_taps(r.small_out, TAPS_ROW, r.taps)
    r.small_out[KERNEL_ROW : KERNEL_ROW + 9] = r.kgrad[0:9]


def kernel_last(cells, r):
    tile = r.tile[0]

    def emit(h, lo, hi, value):
        r.du[h, :, :, lo:hi] = value

    conv_backward(0, cells, r.a, r.stats, r.totals, r.batch_gain, r.kernels, r.dn, r.dm, emit, r.padd)
    for k, piece in enumerate((r.o0, r.o1, r.o2, r.o3)):
        h0, w0 = corner(tile, k)
        piece[...] = r.du[pl.ds(h0, TS), pl.ds(w0, TS)].reshape(PIECE, -1).astype(BF16)


def unpack_put(r, value, quarter, row):
    channels, hidden = r.up.ref.shape
    rows = pl.ds(row, value.shape[1])
    for i in range(value.shape[0]):
        base = (quarter * value.shape[0] + i) * GROUP_LANES
        if base < hidden:
            r.up.ref[rows, base : base + GROUP_LANES] = value[i]
        elif base < 2 * hidden:
            r.down.ref[rows, base - hidden : base - hidden + GROUP_LANES] = value[i]
        else:
            base -= 2 * hidden
            for part, first, size, lane in joined_places(channels):
                lo, hi = max(lane, base), min(lane + size, base + GROUP_LANES)
                if lo < hi:
                    target = part * channels + first + lo - lane
                    r.unite.ref[rows, target : target + hi - lo] = value[i, :, lo - base : hi - base]


def unpack_all(r, block):
    channels, hidden = r.up.ref.shape
    size = 4 * channels // BLOCKS
    per = channels // size
    lanes = PER_QUARTER * GROUP_LANES
    for quarter in range(4):
        for b in range(per):
            unpack_put(r, block(quarter * per + b), quarter, b * size)
        if (quarter + 1) * lanes >= hidden and quarter * lanes < hidden:
            r.up.send_all()
        if (quarter + 1) * lanes >= 2 * hidden and quarter * lanes < 2 * hidden:
            r.down.send_all()
    r.unite.send_all()


def kernel_unpack(r):
    index = r.index[0]
    half = BLOCKS // 2
    flip = index & (half - 1)
    own = index // half
    r.near.wait_all()
    r.far.wait_all()

    def block(p):
        place = (p & (half - 1)) ^ flip
        near, far = r.near.ref[place].astype(F32), r.far.ref[place].astype(F32)
        return jnp.where(own == p // half, near, far)

    unpack_all(r, block)


def kernel_finish(cells, r):
    channels = r.total0.shape[-1]
    for layer, total in enumerate((r.total0, r.total1)):
        one = slice(layer, layer + 1)
        r.batch_shift[one] = total[0:1]
        r.batch_gain[one] = total[1:2]
        r.norm_gain[one] = total[2:3]
        r.norm_shift[one] = total[3:4]
        r.down_bias[one] = total[4:5]
        r.unite_bias[one] = total[5:6]
        for i in range(r.up_bias.shape[-1] // channels):
            r.up_bias[one, i * channels : (i + 1) * channels] = total[6 + i : 7 + i]
        for v in range(MAP + 1):
            row, lane = mix_place(v)
            width, height = total[row : row + 1, lane : lane + MAP], total[row : row + 1, lane + 16 : lane + 16 + MAP]
            if v < MAP:
                r.mix_width[v, one], r.mix_height[v, one] = width, height
            else:
                r.mix_width_bias[one], r.mix_height_bias[one] = width, height
    mean, rstd = scale_of(r.stats, cells)
    shift_mean, gain_mean = r.total0[0:1] * (1.0 / cells), r.total0[1:2] * (1.0 / cells)
    for i in range(9):
        alone, times = r.total1[TAPS_ROW + i : TAPS_ROW + i + 1], r.total1[KERNEL_ROW + i : KERNEL_ROW + i + 1]
        value = r.total0[TAPS_ROW + i : TAPS_ROW + i + 1] - shift_mean * alone - gain_mean * rstd * times
        r.kernel[i // 3, i % 3, 0:1] = rstd * r.gain[0:1] * value
        r.kernel[i // 3, i % 3, 1:2] = r.total0[KERNEL_ROW + i : KERNEL_ROW + i + 1]


class Kept:
    def __init__(self, array):
        self.array = array


class Smem:
    def __init__(self, array):
        self.array = array


class Layer:
    def __init__(self, array, layer):
        self.array, self.layer = array, layer


def chunk_step(shape, step=None):
    if len(shape) == 4 and shape[1:3] == (MAP, ROW):
        return 1
    if len(shape) == 3 and shape[:2] == (MAP, ROW):
        return step or PART
    return shape[0]


class Late:
    def __init__(self, array, layer=None, step=None, hold=False):
        self.array, self.layer, self.hold = array, layer, hold
        self.step = chunk_step(self.shape, step)

    @property
    def shape(self):
        return self.array.shape if self.layer is None else self.array.shape[1:]

    @property
    def parts(self):
        return self.shape[0] // self.step


class LateJoin:
    def __init__(self, arrays):
        self.arrays = arrays
        self.dtype = arrays[0].dtype
        self.shape = (sum(a.shape[0] for a in arrays),) + arrays[0].shape[1:]


class LateJoinRef:
    def __init__(self, sources, ref, sems):
        self.ref, self.copies, row = ref, [], 0
        for i, source in enumerate(sources):
            size = source.shape[0]
            self.copies.append(pltpu.make_async_copy(source, ref.at[pl.ds(row, size)], sems.at[i]))
            row += size

    def start(self):
        for copy in self.copies:
            copy.start()

    def wait_all(self):
        for copy in self.copies:
            copy.wait()


class LateRef:
    def __init__(self, late, source, ref, sems):
        self.parts, self.step = late.parts, late.step
        self.source = source if late.layer is None else source.at[late.layer]
        self.ref, self.sems = ref, sems

    def copy(self, c):
        if self.parts == 1:
            return pltpu.make_async_copy(self.source, self.ref, self.sems.at[0])
        rows = pl.ds(self.step * c, self.step)
        return pltpu.make_async_copy(self.source.at[rows], self.ref.at[rows], self.sems.at[c])

    def start(self):
        for c in range(self.parts):
            self.copy(c).start()

    def start_part(self, c):
        self.copy(c).start()

    def wait(self, c):
        self.copy(c).wait()

    def wait_all(self):
        for c in range(self.parts):
            self.copy(c).wait()


class Stream:
    def __init__(self, out, layer=None, step=None):
        self.out, self.layer = out, layer
        self.step = chunk_step(self.shape, step)

    @property
    def shape(self):
        return self.out.shape if self.layer is None else self.out.shape[1:]


class Place:
    def __init__(self, out):
        self.out = out


class StreamRef:
    def __init__(self, stream, target, ref, sem):
        self.target, self.ref, self.sem = target if stream.layer is None else target.at[stream.layer], ref, sem
        self.step = stream.step

    def send(self, c):
        rows = pl.ds(self.step * c, self.step)
        pltpu.make_async_copy(self.ref.at[rows], self.target.at[rows], self.sem).start()

    def send_all(self):
        pltpu.make_async_copy(self.ref, self.target, self.sem).start()

    def finish(self):
        pltpu.make_async_copy(self.ref, self.target, self.sem).wait()


class PlaceRef:
    def __init__(self, target, sem):
        self.target, self.sem = target, sem

    def start(self, source):
        self.copy = pltpu.make_async_copy(source, self.target, self.sem)
        self.copy.start()

    def finish(self):
        self.copy.wait()


class Held:
    def __init__(self, ref):
        self.ref = ref


class Refs:
    pass


def full(array):
    rank = len(array.shape)
    return pl.BlockSpec(array.shape, lambda i: (0,) * rank)


ANY = pl.BlockSpec(memory_space=pl.ANY)
FINISHED = (
    "batch_shift", "batch_gain", "norm_gain", "norm_shift", "down_bias", "unite_bias", "up_bias",
    "kernel", "mix_width", "mix_height", "mix_width_bias", "mix_height_bias",
)


def _padded(array):
    shape = list(array.shape)
    if len(shape) > 1:
        shape[-2] = -(-shape[-2] // 16) * 16
    shape[-1] = -(-shape[-1] // 128) * 128
    return math.prod(shape) * jnp.dtype(array.dtype).itemsize


def run(body, name, flops, ins, outs, scratch=None, aliases=None, tight=False):
    scratch = dict(scratch or {})
    arrays, in_specs, out_specs, out_shapes, spaces = [], [], [], [], []
    for key, operand in ins.items():
        if isinstance(operand, Smem):
            in_specs.append(pl.BlockSpec(memory_space=pltpu.SMEM))
        elif isinstance(operand, Layer):
            shape, layer = operand.array.shape, operand.layer
            in_specs.append(pl.BlockSpec((None,) + shape[1:], lambda i, layer=layer, rank=len(shape): (layer,) + (0,) * (rank - 1)))
        elif isinstance(operand, Kept):
            in_specs.append(ANY)
        elif isinstance(operand, LateJoin):
            in_specs += [ANY] * len(operand.arrays)
            arrays += operand.arrays
            spaces += [pltpu.VMEM(operand.shape, operand.dtype), pltpu.SemaphoreType.DMA((len(operand.arrays),))]
            continue
        elif isinstance(operand, Late):
            in_specs.append(ANY)
            spaces += [pltpu.VMEM(operand.shape, operand.array.dtype), pltpu.SemaphoreType.DMA((operand.parts,))]
        else:
            in_specs.append(full(operand))
        arrays.append(getattr(operand, "array", operand))
    for key, out in outs.items():
        if isinstance(out, (Stream, Place)):
            out_specs.append(ANY)
            out_shapes.append(out.out)
            if isinstance(out, Stream):
                spaces.append(pltpu.VMEM(out.shape, out.out.dtype))
            spaces.append(pltpu.SemaphoreType.DMA)
        elif isinstance(out, Layer):
            shape, layer = out.array.shape, out.layer
            out_specs.append(pl.BlockSpec((None,) + shape[1:], lambda i, layer=layer, rank=len(shape): (layer,) + (0,) * (rank - 1)))
            out_shapes.append(out.array)
        else:
            out_specs.append(full(out))
            out_shapes.append(out)
    spaces += list(scratch.values())

    def wrapped(*refs):
        refs = list(refs)
        r = Refs()
        main, extra = refs[: len(arrays) + len(outs)], refs[len(arrays) + len(outs) :]
        late, streams = [], []
        for key, operand in ins.items():
            if isinstance(operand, LateJoin):
                sources = [main.pop(0) for _ in operand.arrays]
                ref = LateJoinRef(sources, extra.pop(0), extra.pop(0))
                late.append(ref)
                setattr(r, key, ref)
                continue
            ref = main.pop(0)
            if isinstance(operand, Late):
                ref = LateRef(operand, ref, extra.pop(0), extra.pop(0))
                if not operand.hold:
                    late.append(ref)
            setattr(r, key, ref)
        for key, out in outs.items():
            ref = main.pop(0)
            if isinstance(out, Stream):
                ref = StreamRef(out, ref, extra.pop(0), extra.pop(0))
                streams.append(ref)
            elif isinstance(out, Place):
                ref = PlaceRef(ref, extra.pop(0))
                streams.append(ref)
            setattr(r, key, ref)
        for key in scratch:
            setattr(r, key, extra.pop(0))
        for part in late:
            part.start()
        body(r)
        for stream in streams:
            stream.finish()

    held = [a for a, spec in zip(arrays + out_shapes, in_specs + out_specs) if spec is not ANY]
    held += [space for space in spaces if getattr(space, "memory_space", None) == pltpu.VMEM]
    need = sum(_padded(a) for a in held)
    limit = min(VMEM_BYTES, need + need // 4 + MARGIN) if tight else VMEM_BYTES
    size = sum(a.size * a.dtype.itemsize for a in arrays) + sum(o.size * o.dtype.itemsize for o in out_shapes)
    results = pl.pallas_call(
        wrapped,
        grid=(1,),
        in_specs=in_specs,
        out_specs=out_specs,
        out_shape=out_shapes,
        scratch_shapes=spaces,
        input_output_aliases=aliases or {},
        compiler_params=pltpu.CompilerParams(vmem_limit_bytes=limit),
        cost_estimate=pl.CostEstimate(flops=flops, bytes_accessed=size, transcendentals=0),
        name=name,
    )(*arrays)
    named = Refs()
    for key, value in zip(outs, results):
        setattr(named, key, value)
    return named


def on_device(
    patches,
    conv_kernel,
    batch_gain,
    batch_shift,
    mix_width,
    mix_width_bias,
    mix_height,
    mix_height_bias,
    unite_weight,
    unite_bias,
    norm_gain,
    norm_shift,
    up_weight,
    up_bias,
    down_weight,
    down_bias,
    cotangent,
):
    channels = patches.shape[-1]
    hidden = up_weight.shape[-1]
    tile = lax.axis_index("tile")
    tile_arg = Smem(tile.astype(jnp.int32).reshape(1))
    index_arg = Smem(block_index().reshape(1))
    local_cells = MAP * ROW
    cells = local_cells * lax.axis_size("dp") * lax.axis_size("tile")

    def rows(lanes, dtype):
        return jax.ShapeDtypeStruct((MAP, ROW, lanes), dtype)

    def shape(*dims, dtype=F32):
        return jax.ShapeDtypeStruct(dims, dtype)

    def vmem(struct):
        return pltpu.VMEM(struct.shape, struct.dtype)

    piece = shape(PIECE, channels, dtype=BF16)
    c_bf, c_f32, h_bf = rows(channels, BF16), rows(channels, F32), shape(hidden // BLK, MAP, ROW, BLK, dtype=BF16)
    map4 = pltpu.VMEM((MAP, MAP, IMG, channels), F32)
    pad = pltpu.VMEM((MAP + 2, MAP + 2, IMG, channels), F32)
    sums = pltpu.VMEM((2, 8, channels), F32)
    small = pltpu.VMEM((6, 8, channels), F32)
    upsum = pltpu.VMEM((8, hidden), F32)
    ksum = pltpu.VMEM((9, 8, channels), F32)
    unite_space = pltpu.VMEM((JOINED, channels), BF16)
    blocks = hidden // BLK
    groups = 2 * blocks * (BLK // GROUP_LANES) + JOINED // GROUP_LANES
    assert groups == 4 * PER_QUARTER
    block = (PER_QUARTER, 4 * channels // BLOCKS, GROUP_LANES)
    half = shape(BLOCKS // 2, *block, dtype=BF16)
    buf = pltpu.VMEM((BLOCKS, *block), BF16)

    kernels = conv_kernel.transpose(1, 2, 0, 3)
    down_t = down_weight.transpose(0, 2, 1)
    unite_t = unite_weight.transpose(0, 2, 1)
    mix_width = mix_width.transpose(1, 0, 2)
    mix_height = mix_height.transpose(1, 0, 2)

    x_pieces = to_whole(patches[:, 0].transpose(1, 2, 0, 3), tile)
    first = run(
        kernel_first,
        "conv_first",
        10**7,
        dict(tile=tile_arg, **{f"p{k}": x_pieces[k] for k in range(4)}, kernels=kernels),
        dict(x=c_bf, a=c_f32, stats=shape(2, channels)),
        dict(pad=pad, sums=sums),
        tight=True,
    )
    taps = run(
        kernel_taps,
        "taps",
        10**8,
        dict(x=Late(first.x), a=Late(first.a), stats=first.stats),
        dict(out=shape(24, channels)),
        dict(pad=pad, alone=ksum, times=ksum),
        tight=True,
    ).out
    stats0, (cotangent, taps) = total_moments(first.stats, float(local_cells), [cotangent, taps])
    taps = jnp.concatenate([taps[0:9], taps[9:18] + (taps[18:19] - stats0[0:1]) * taps[0:9]], 0)
    cot_pieces = to_whole(cotangent[:, 0].transpose(1, 2, 0, 3), tile)

    def forward_ins(layer):
        return dict(
            batch_gain=batch_gain, batch_shift=batch_shift,
            mix_width=mix_width, mix_width_bias=mix_width_bias, mix_height=mix_height, mix_height_bias=mix_height_bias,
            unite_t=Late(unite_t, layer, hold=True), up=Late(up_weight, layer, hold=True), down=Late(down_t, layer, hold=True),
            unite_bias=unite_bias, norm_gain=norm_gain, norm_shift=norm_shift, up_bias=up_bias, down_bias=down_bias,
        )

    fwd = run(
        lambda r: kernel_forward(cells, r),
        "block_forward",
        6 * 10**9,
        dict(a=Late(first.a), stats=stats0, **forward_ins(0), x=Late(first.x, hold=True), kernels=kernels),
        dict(
            joined=Stream(rows(JOINED, BF16)), zhat=Stream(c_f32), s=Stream(rows(1, F32)), zb=Stream(c_bf),
            g=Stream(h_bf), d=Stream(h_bf), u=Stream(c_f32), a2=Stream(c_f32, step=1), stats2=shape(2, channels),
        ),
        dict(pad=pad, sums=sums, unite=unite_space),
    )
    stats1, *cot_pieces = tie(fwd.stats2, *cot_pieces)
    cot_map = run(
        kernel_whole_map,
        "cotangent_map",
        10**7,
        dict(tile=tile_arg, **{f"p{k}": cot_pieces[k] for k in range(4)}),
        dict(out=c_bf),
        dict(field=map4),
        tight=True,
    ).out
    stats1 = total_moments(stats1, float(local_cells))

    turn = run(
        lambda r: kernel_turn(cells, r),
        "block_turn",
        14 * 10**9,
        dict(
            index=index_arg, a=Late(fwd.a2), stats=stats1, u=Late(fwd.u, hold=True), do_in=Late(cot_map, hold=True),
            **forward_ins(1), taps=taps,
        ),
        dict(
            features=Stream(c_bf), dm=Stream(c_f32), dn=Stream(c_f32, step=1), small_out=shape(SMALL_ROWS, channels),
            mine=Place(half), sent=Place(half),
        ),
        dict(
            joined=vmem(rows(JOINED, BF16)), zb=vmem(c_bf), df=vmem(c_bf), dpw=vmem(c_bf), dph=vmem(c_bf),
            out=vmem(c_f32), zhat=vmem(c_f32), s=vmem(rows(1, F32)), dz=vmem(c_f32), small=small, upsum=upsum, buf=buf, unite=unite_space,
        ),
    )
    cut = run(
        kernel_pieces,
        "feature_pieces",
        10**7,
        dict(tile=tile_arg, field=turn.features),
        {f"p{k}": piece for k in range(4)},
        tight=True,
    )
    features = [cut.p0, cut.p1, cut.p2, cut.p3]

    near = masks(GROUPS[0])[0]
    got = flat_partner(turn.sent, near)
    first_stage, *later_stages = stages()
    total1 = sum_stage(turn.small_out, first_stage)
    total1, mine1, got = tie(total1, turn.mine, got)
    part1 = narrow_add([mine1, got])
    got1 = scatter_sends(part1, GROUPS[1])
    for stage in later_stages:
        total1 = sum_stage(total1, stage)
    total1, part1, *rest = tie(total1, part1[: part1.shape[0] // 4], *got1, *features)
    got1, features = rest[:3], rest[3:]
    part1 = narrow_add([part1, *got1])
    far = far_masks()
    got1 = flat_partner(part1, far[0])
    mid = run(
        lambda r: kernel_conv_middle(cells, r),
        "conv_middle",
        2 * 10**9,
        dict(**{key: Late(value, step=2, hold=True) for key, value in dict(a=fwd.a2, dn=turn.dn, x=fwd.u, dm=turn.dm).items()}, stats=stats1, totals=total1, kernels=kernels, batch_gain=batch_gain),
        dict(do=Stream(c_bf, step=2), du=Stream(c_f32, step=2), kgrad=shape(16, channels)),
        dict(padx=pad, padd=pad, ksum=ksum),
    )
    do, part1, got1, *features = tie(mid.do, part1, got1, *features)
    part1 = narrow_add([part1, got1])
    got1 = flat_partner(part1, far[1])
    features = swap_pieces(features)
    back = run(
        lambda r: kernel_back(cells, r),
        "block_back",
        14 * 10**9,
        dict(
            index=index_arg,
            **{
                key: Late(value, layer, hold=True)
                for key, (value, layer) in dict(
                    down=(down_t, 0), do_in=(do, None), du=(mid.du, None), up=(up_weight, 0), d=(fwd.d, None), zb=(fwd.zb, None), g=(fwd.g, None), unite_t=(unite_t, 0),
                    zhat=(fwd.zhat, None), s=(fwd.s, None), joined=(fwd.joined, None), a=(first.a, None), x=(first.x, None),
                ).items()
            },
            kgrad=mid.kgrad, norm_gain=norm_gain, stats=stats0, mix_width=mix_width, mix_height=mix_height,
        ),
        dict(dm=Stream(c_f32), dn=Stream(c_f32, step=1), small_out=shape(SMALL_ROWS, channels), mine=Place(half), sent=Place(half)),
        dict(df=vmem(c_bf), dpw=vmem(c_bf), dph=vmem(c_bf), dz=vmem(c_f32), small=small, upsum=upsum, buf=buf, unite=unite_space, pad=pad, taps=ksum),
    )
    small0, mine0, sent0, part1, got1, *features = tie(back.small_out, back.mine, back.sent, part1, got1, *features)
    part1 = narrow_add([part1, got1])
    for mask in far[2:]:
        part1 = add_partner(part1, mask)
    got = flat_partner(sent0, near)
    total0 = sum_stage(small0, first_stage)
    total0, mine0, got = tie(total0, mine0, got)
    part0 = narrow_add([mine0, got])
    got0 = scatter_sends(part0, GROUPS[1])
    for stage in later_stages[:-1]:
        total0 = sum_stage(total0, stage)
    total0, part1 = tie(total0, part1)
    got1 = [flat_partner(part1, mask) for mask in masks(GROUPS[1])]
    total0 = sum_stage(total0, later_stages[-1])
    total0, part0, *got0 = tie(total0, part0[: part0.shape[0] // 4], *got0)
    part0 = narrow_add([part0, *got0])
    got0 = flat_partner(part0, far[0])
    last = run(
        lambda r: kernel_last(cells, r),
        "conv_last",
        2 * 10**9,
        dict(tile=tile_arg, **{key: Late(value, step=2, hold=True) for key, value in dict(a=first.a, dn=back.dn, dm=back.dm).items()}, stats=stats0, totals=total0, kernels=kernels, batch_gain=batch_gain),
        {f"o{k}": piece for k in range(4)},
        dict(padd=pad, du=map4),
    )
    o3, part0, got0, *parts1 = tie(last.o3, part0, got0, part1, *got1)
    grads = swap_pieces([last.o0, last.o1, last.o2, o3])
    part0 = narrow_add([part0, got0])
    got0 = flat_partner(part0, far[1])
    part0, got0, *rest = tie(part0, got0, *grads, *parts1)
    part0 = narrow_add([part0, got0])
    for mask in far[2:]:
        part0 = add_partner(part0, mask)
    grads, parts1 = rest[:4], rest[4:]
    got0 = [flat_partner(part0, mask) for mask in masks(GROUPS[1])]
    far1 = [flat_partner(part, near) for part in parts1]
    features_out = join_pieces(features, tile)
    grads = join_pieces(grads, tile)
    grad_shapes = dict(up=shape(2, channels, hidden), down=shape(2, channels, hidden), unite=shape(2, channels, 3 * channels))
    whole = run(
        kernel_unpack,
        "unpack_1",
        10**7,
        dict(index=index_arg, near=LateJoin(parts1), far=LateJoin(far1)),
        {key: Stream(value, 1) for key, value in grad_shapes.items()},
        tight=True,
    )
    line = shape(2, channels)
    fin = run(
        lambda r: kernel_finish(cells, r),
        "finish",
        10**6,
        dict(total0=total0, total1=total1, stats=stats0, gain=batch_gain),
        dict(
            batch_shift=line, batch_gain=line, norm_gain=line, norm_shift=line, down_bias=line, unite_bias=line, up_bias=shape(2, hidden),
            kernel=shape(3, 3, 2, channels), mix_width=shape(MAP, 2, MAP), mix_height=shape(MAP, 2, MAP), mix_width_bias=shape(2, MAP), mix_height_bias=shape(2, MAP),
        ),
    )
    whole_1 = (whole.up, whole.down, whole.unite)
    small_results = [getattr(fin, key) for key in FINISHED]
    grads, features_out, *rest = tie(grads, features_out, part0, *got0, *whole_1, *small_results)
    parts0, whole_1, small_results = rest[:4], rest[4:7], rest[7:]
    for key, value in zip(FINISHED, small_results):
        setattr(fin, key, value)
    far0 = [flat_partner(part, near) for part in parts0]
    whole = run(
        kernel_unpack,
        "unpack_0",
        10**7,
        dict(index=index_arg, near=LateJoin(parts0), far=LateJoin(far0), up_in=Kept(whole_1[0]), down_in=Kept(whole_1[1]), unite_in=Kept(whole_1[2])),
        {key: Stream(value, 0) for key, value in grad_shapes.items()},
        aliases={9: 0, 10: 1, 11: 2},
        tight=True,
    )

    def to_output(field):
        return field.transpose(2, 0, 1, 3)[:, None]

    return (
        to_output(features_out),
        to_output(grads),
        fin.kernel.transpose(2, 0, 1, 3),
        fin.batch_gain,
        fin.batch_shift,
        fin.mix_width.transpose(1, 0, 2),
        fin.mix_width_bias,
        fin.mix_height.transpose(1, 0, 2),
        fin.mix_height_bias,
        whole.unite.transpose(0, 2, 1),
        fin.unite_bias,
        fin.norm_gain,
        fin.norm_shift,
        whole.up,
        fin.up_bias,
        whole.down.transpose(0, 2, 1),
        fin.down_bias,
    )


def solution(mesh):
    field = P("dp", "tile", None, None, None)
    return jax.shard_map(
        on_device,
        mesh=mesh,
        in_specs=(field,) + (P(),) * 15 + (field,),
        out_specs=(field, field) + (P(),) * 15,
        check_vma=False,
    )
```

```python
import math

import jax
import jax.numpy as jnp
from jax import lax
from jax.experimental import pallas as pl
from jax.experimental.pallas import tpu as pltpu
from jax.sharding import PartitionSpec as P

F32 = jnp.float32
BF16 = jnp.bfloat16
norm_epsilon = 1e-05
layer_epsilon = 1e-06
ROOT_HALF = 0.7071067811865476
INV_ROOT_TAU = 0.3989422804014327
LOG2E = 1.4426950408889634

TS = 7
MAP = 14
IMG = 8
ROW = MAP * IMG
PIECE = TS * TS * IMG
VMEM_BYTES = 58 * 1024 * 1024
MARGIN = 8 * 1024 * 1024
BLK = 256


def partner(x, axis, distance):
    count = lax.axis_size(axis)
    return lax.ppermute(x, axis, [(i, i ^ distance) for i in range(count)])


def stages():
    result = [("tile", (1, 2, 3))]
    count = lax.axis_size("dp")
    step = 1
    if count > 1 and (count.bit_length() - 1) % 2 == 1:
        result.append(("dp", (1,)))
        step = 2
    while step < count:
        result.append(("dp", (step, 2 * step, 3 * step)))
        step *= 4
    return result


def sum_stage(x, stage):
    axis, distances = stage
    got = [partner(x, axis, d) for d in distances]
    if len(got) == 1:
        return x + got[0]
    return (x + got[0]) + (got[1] + got[2])


def total_sum(x, after=None, when=2):
    for step, stage in enumerate(stages()):
        if step == when and after is not None:
            x, *after = tie(x, *after)
        x = sum_stage(x, stage)
    return x if after is None else (x, after)


def total_moments(stats, count, after=None):
    for step, (axis, distances) in enumerate(stages()):
        if step == 2 and after is not None:
            stats, *after = tie(stats, *after)
        parts = [stats] + [partner(stats, axis, d) for d in distances]
        if len(parts) == 2:
            mean = (parts[0][0] + parts[1][0]) * 0.5
            dev = [jnp.square(p[0] - mean) for p in parts]
            square = (parts[0][1] + parts[1][1]) + count * (dev[0] + dev[1])
        else:
            mean = ((parts[0][0] + parts[1][0]) + (parts[2][0] + parts[3][0])) * 0.25
            dev = [jnp.square(p[0] - mean) for p in parts]
            square = ((parts[0][1] + parts[1][1]) + (parts[2][1] + parts[3][1])) + count * (
                (dev[0] + dev[1]) + (dev[2] + dev[3])
            )
        count = count * len(parts)
        stats = jnp.stack([mean, square])
    return stats if after is None else (stats, after)


def to_whole(field, tile):
    share = field.shape[2] // lax.axis_size("tile")
    pieces = []
    for k in range(4):
        part = lax.dynamic_slice_in_dim(field, (tile ^ k) * share, share, 2)
        part = part.reshape(TS * TS * share, field.shape[3])
        pieces.append(part if k == 0 else partner(part, "tile", k))
    return pieces


def swap_pieces(pieces):
    return [pieces[0]] + [partner(pieces[k], "tile", k) for k in range(1, 4)]


def join_pieces(pieces, tile):
    channels = pieces[0].shape[-1]
    share = pieces[0].shape[0] // (TS * TS)
    result = jnp.zeros((TS, TS, share * lax.axis_size("tile"), channels), pieces[0].dtype)
    for k in range(4):
        part = pieces[k].reshape(TS, TS, share, channels)
        result = lax.dynamic_update_slice_in_dim(result, part, (tile ^ k) * share, 2)
    return result


def flat_partner(x, mask):
    axes = ("dp", "tile")
    count = lax.axis_size("dp") * lax.axis_size("tile")
    return lax.ppermute(x, axes, [(i, i ^ mask) for i in range(count)])


GROUPS = ((0,), (1, 2))
SPLIT_BITS = 3
QUAD = 4
BLOCKS = 32


def block_index():
    flat = lax.axis_index("dp") * lax.axis_size("tile") + lax.axis_index("tile")
    index = jnp.zeros((), jnp.int32)
    for group in GROUPS:
        for bit in group:
            index = index * 2 + ((flat >> bit) & 1)
    return index * QUAD


def masks(group):
    if len(group) == 1:
        return [1 << group[0]]
    return [1 << group[1], 1 << group[0], (1 << group[0]) | (1 << group[1])]


def narrow_add(parts):
    parts = [p.astype(F32) for p in parts]
    total = parts[0] + parts[1]
    if len(parts) == 4:
        total = total + (parts[2] + parts[3])
    return total.astype(BF16)


def scatter_sends(x, group):
    wide = masks(group)
    size = x.shape[0] // (len(wide) + 1)
    return [flat_partner(x[(j + 1) * size : (j + 2) * size], mask) for j, mask in enumerate(wide)]


def far_masks():
    count = lax.axis_size("dp") * lax.axis_size("tile")
    return [1 << bit for bit in range(SPLIT_BITS, count.bit_length() - 1)]


def add_partner(x, mask):
    return narrow_add([x, flat_partner(x, mask)])


def tie(*values):
    return lax.optimization_barrier(values)


def dot(a, b):
    return lax.dot_general(a, b, (((1,), (0,)), ((), ())), preferred_element_type=F32)


def dot_nt(a, b):
    return lax.dot_general(a, b, (((1,), (1,)), ((), ())), preferred_element_type=F32)


def dot_tn(a, b):
    return lax.dot_general(a, b, (((0,), (0,)), ((), ())), preferred_element_type=F32)


def spread(ref, layer, repeat, turned=False):
    matrix = ref[...].astype(F32)[:, layer, :].astype(BF16)
    size = MAP * repeat
    shift = repeat.bit_length() - 1
    row = lax.broadcasted_iota(jnp.int32, (size, MAP), 0)
    col = lax.broadcasted_iota(jnp.int32, (size, MAP), 1)
    pick = jnp.where((row >> shift) == col, 1.0, 0.0).astype(BF16)
    half = dot_nt(pick, matrix) if turned else dot(pick, matrix)
    wide = dot_nt(half.astype(BF16), pick)
    row = lax.broadcasted_iota(jnp.int32, (size, size), 0)
    col = lax.broadcasted_iota(jnp.int32, (size, size), 1)
    return jnp.where((row & (repeat - 1)) == (col & (repeat - 1)), wide, 0.0).astype(BF16)


def spread_bias(ref, layer, repeat):
    size = MAP * repeat
    shift = repeat.bit_length() - 1
    row = lax.broadcasted_iota(jnp.int32, (size, MAP), 0)
    col = lax.broadcasted_iota(jnp.int32, (size, MAP), 1)
    return jnp.sum(jnp.where((row >> shift) == col, ref[layer : layer + 1], 0.0), axis=1, keepdims=True)


def collapse(product, repeat):
    size = MAP * repeat
    shift = repeat.bit_length() - 1
    row = lax.broadcasted_iota(jnp.int32, (size, size), 0)
    col = lax.broadcasted_iota(jnp.int32, (size, size), 1)
    kept = jnp.where((row & (repeat - 1)) == (col & (repeat - 1)), product, 0.0)
    kept = jnp.sum(kept.reshape(MAP, repeat, size), axis=1)
    row = lax.broadcasted_iota(jnp.int32, (size, MAP), 0)
    col = lax.broadcasted_iota(jnp.int32, (size, MAP), 1)
    pick = jnp.where((row >> shift) == col, 1.0, 0.0).astype(F32)
    return lax.dot_general(
        kept, pick, (((1,), (0,)), ((), ())), preferred_element_type=F32, precision=lax.Precision.HIGHEST
    )


def lane_groups(channels):
    return [(lo, min(lo + 128, channels)) for lo in range(0, channels, 128)]


def zero_border(pad):
    shape = pad.shape
    pad[0] = jnp.zeros(shape[1:], F32)
    pad[MAP + 1] = jnp.zeros(shape[1:], F32)
    for h in range(1, MAP + 1):
        pad[h, 0] = jnp.zeros(shape[2:], F32)
        pad[h, MAP + 1] = jnp.zeros(shape[2:], F32)


def pick_columns(field, w0):
    return jnp.where(w0 == 0, field[:, :TS], field[:, TS:])


def corner(tile, k):
    other = tile ^ k
    return (other >> 1) * TS, (other & 1) * TS


def conv_rows(pad, kernel_ref, layer, out_ref, stats_ref, sums, then=None):
    channels = pad.shape[-1]
    sums[...] = jnp.zeros(sums.shape, F32)

    def body(h, carry):
        for lo, hi in lane_groups(channels):
            acc = None
            for r in range(3):
                for s in range(3):
                    term = pad[h + r, s : s + MAP, :, lo:hi] * kernel_ref[r, s, layer : layer + 1, lo:hi]
                    acc = term if acc is None else acc + term
            out_ref[h, :, lo:hi] = acc.reshape(ROW, hi - lo)
            sums[0, :, lo:hi] += jnp.sum(acc, axis=0)
        if then is not None:
            then(h)
        return carry

    lax.fori_loop(0, MAP, body, 0)
    count = MAP * ROW
    mean = jnp.sum(sums[0], axis=0, keepdims=True) * (1.0 / count)

    def again(h, carry):
        for lo, hi in lane_groups(channels):
            dev = out_ref[h, :, lo:hi] - mean[:, lo:hi]
            sums[1, :, lo:hi] += jnp.sum((dev * dev).reshape(MAP, IMG, hi - lo), axis=0)
        return carry

    lax.fori_loop(0, MAP, again, 0)
    stats_ref[0:1] = mean
    stats_ref[1:2] = jnp.sum(sums[1], axis=0, keepdims=True)


def scale_of(stats_ref, cells):
    mean = stats_ref[0:1]
    return mean, lax.rsqrt(stats_ref[1:2] * (1.0 / cells) + norm_epsilon)


JOINED = 1024
MAIN = 256


def joined_places(channels):
    rest = channels - MAIN
    return [(i, 0, MAIN, i * MAIN) for i in range(3)] + [(i, MAIN, rest, 3 * MAIN + i * rest) for i in range(3)]


def put_joined(ref, rows, i, value):
    for part, first, size, lane in joined_places(value.shape[-1]):
        if part == i:
            ref[rows + (slice(lane, lane + size),)] = value[..., first : first + size]


def get_joined(value, i, channels):
    pieces = [value[..., lane : lane + size] for part, first, size, lane in joined_places(channels) if part == i]
    return jnp.concatenate(pieces, axis=-1)


def mix_forward(layer, cells, arrive, a_ref, stats_ref, gain_ref, shift_ref, mw_ref, mwb_ref, mh_ref, mhb_ref, joined):
    mean, rstd = scale_of(stats_ref, cells)
    channels = a_ref.shape[-1]
    gain = gain_ref[layer : layer + 1]
    shift = shift_ref[layer : layer + 1]
    width = spread(mw_ref, layer, IMG)
    height = spread(mh_ref, layer, 16)
    width_bias = spread_bias(mwb_ref, layer, IMG)
    height_bias = spread_bias(mhb_ref, layer, 16)
    used = 3 * channels
    joined[:, :, used:] = jnp.zeros(joined.shape[:2] + (joined.shape[2] - used,), BF16)
    whole = slice(None)
    for h in range(MAP):
        if h % PART == 0:
            arrive(h // PART)
        value = (((a_ref[h] - mean) * rstd) * gain + shift).astype(BF16)
        put_joined(joined, (h, whole), 0, value)
        put_joined(joined, (h, whole), 1, (dot(width, value) + width_bias).astype(BF16))
    for j in range(ROW // 16):
        cols = slice(16 * j, 16 * j + 16)
        value = get_joined(joined[:, cols, :], 0, channels).reshape(MAP * 16, channels)
        mixed = (dot(height, value) + height_bias).astype(BF16)
        put_joined(joined, (whole, cols), 2, mixed.reshape(MAP, 16, channels))


def gelu_pair(v):
    t = 1.0 / (1.0 + (0.3275911 * ROOT_HALF) * jnp.abs(v))
    e = jnp.exp2(v * v * (-0.5 * LOG2E))
    q = ((((0.5 * 1.061405429 * t - 0.5 * 1.453152027) * t + 0.5 * 1.421413741) * t - 0.5 * 0.284496736) * t + 0.5 * 0.254829592) * t * e
    phi = jnp.where(v >= 0, 1.0 - q, q)
    return v * phi, phi + v * e * INV_ROOT_TAU


HALVES = 2
PART = MAP // HALVES


def half_rows(ref, p):
    value = ref[p * PART : (p + 1) * PART]
    return value.reshape(PART * ROW, value.shape[-1])


def put_half(ref, p, value):
    ref[p * PART : (p + 1) * PART] = value.reshape(PART, ROW, value.shape[-1])


def add_half(ref, p, value):
    ref[p * PART : (p + 1) * PART] += value.reshape(PART, ROW, value.shape[-1])


def column_sums(value):
    return jnp.sum(value.reshape(-1, 8, value.shape[-1]), axis=0)


def unite_norm(r, layer, p, residual):
    one = slice(layer, layer + 1)
    m = residual + r.unite_bias[one] + dot(half_rows(r.joined.ref, p), r.unite[...])
    centre = jnp.mean(m, axis=-1, keepdims=True)
    dev = m - centre
    s = lax.rsqrt(jnp.mean(dev * dev, axis=-1, keepdims=True) + layer_epsilon)
    zhat = dev * s
    zb = (zhat * r.norm_gain[one] + r.norm_shift[one]).astype(BF16)
    return m, zhat, s, zb


def hidden_block(r, layer, j):
    blk = slice(j * BLK, (j + 1) * BLK) if isinstance(j, int) else pl.ds(pl.multiple_of(j * BLK, BLK), BLK)
    return blk, r.up.ref[:, blk], r.down.ref[:, blk]


def block_half(value):
    return value.reshape(PART, ROW, BLK)


def norm_backward(r, layer, p, do32, zhat, s, dz, df_ref):
    one = slice(layer, layer + 1)
    channels = do32.shape[-1]
    e = dz * r.norm_gain[one]
    mean_e = jnp.mean(e, axis=-1, keepdims=True)
    mean_ez = jnp.mean(e * zhat, axis=-1, keepdims=True)
    dm = do32 + s * (e - mean_e - zhat * mean_ez)
    put_half(r.dm.ref, p, dm)
    df = dm.astype(BF16)
    put_half(df_ref, p, df)
    r.small[2] += column_sums(dz * zhat)
    r.small[3] += column_sums(dz)
    r.small[4] += column_sums(do32)
    r.small[5] += column_sums(dm)
    dj = dot_nt(df, r.unite[...])
    put_half(r.dn.ref, p, get_joined(dj, 0, channels))
    put_half(r.dpw, p, get_joined(dj, 1, channels).astype(BF16))
    put_half(r.dph, p, get_joined(dj, 2, channels).astype(BF16))


GROUP_LANES = 128
PER_QUARTER = 7


def put_group(r, q, value):
    size = r.buf.shape[2]
    count = value.shape[0] // size
    quarter = q // PER_QUARTER if isinstance(q, int) else lax.div(q, PER_QUARTER)
    lane = q - quarter * PER_QUARTER
    for b in range(count):
        r.buf[(quarter * count + b) ^ r.index[0], lane] = value[b * size : (b + 1) * size].astype(BF16)


def put_columns(r, q, value):
    for i in range(value.shape[-1] // GROUP_LANES):
        put_group(r, q + i, value[:, i * GROUP_LANES : (i + 1) * GROUP_LANES])


def flat_rows(value):
    return value.reshape(MAP * ROW, value.shape[-1])


def hidden_gradients(r, j, blocks, zb, do, g, dh):
    per = BLK // GROUP_LANES
    put_columns(r, per * j, dot_tn(flat_rows(zb[...]), dh))
    put_columns(r, per * (j + blocks), dot_tn(flat_rows(do[...]), g))


def mix_backward(layer, cells, a_ref, stats_ref, mw_ref, mh_ref, dpw, dph, dn_ref, small, send):
    mean, rstd = scale_of(stats_ref, cells)
    width = spread(mw_ref, layer, IMG, turned=True)
    height = spread(mh_ref, layer, 16, turned=True)
    for j in range(ROW // 16):
        cols = slice(16 * j, 16 * j + 16)
        value = dph[:, cols, :].reshape(MAP * 16, -1)
        dn_ref[:, cols, :] += dot(height, value).reshape(MAP, 16, -1)

    totals = [small[0], small[1]]
    for h in range(MAP):
        dn = dn_ref[h] + dot(width, dpw[h])
        dn_ref[h] = dn
        send(h)
        xhat = (a_ref[h] - mean) * rstd
        totals[0] = totals[0] + jnp.sum(dn.reshape(MAP, IMG, -1), axis=0)
        totals[1] = totals[1] + jnp.sum((dn * xhat).reshape(MAP, IMG, -1), axis=0)
    small[0], small[1] = totals


def unite_gradients(r, blocks, df_ref, out_ref):
    df = flat_rows(df_ref[...])
    channels = df.shape[-1]
    joined, dpw, dph = r.joined.ref, r.dpw, r.dph
    put_columns(r, 2 * blocks * (BLK // GROUP_LANES), dot_tn(df, flat_rows(joined[...])))

    wide = jnp.zeros((ROW, ROW), F32)
    bias = jnp.zeros((ROW, channels), F32)
    for h in range(MAP):
        wide = wide + dot_nt(dpw[h], get_joined(joined[h], 0, channels))
        bias = bias + dpw[h].astype(F32)
    tall = jnp.zeros((MAP * 16, MAP * 16), F32)
    tall_bias = jnp.zeros((MAP, 16, channels), F32)
    for j in range(ROW // 16):
        cols = slice(16 * j, 16 * j + 16)
        value = dph[:, cols, :]
        tall = tall + dot_nt(value.reshape(MAP * 16, channels), get_joined(joined[:, cols, :], 0, channels).reshape(MAP * 16, channels))
        tall_bias = tall_bias + value.astype(F32)
    diagonal = lax.broadcasted_iota(jnp.int32, (MAP, MAP), 0) == lax.broadcasted_iota(jnp.int32, (MAP, MAP), 1)

    def as_row(field):
        col = jnp.sum(jnp.sum(field, axis=1), axis=-1, keepdims=True)
        return jnp.sum(jnp.where(diagonal, col, 0.0), axis=0, keepdims=True)

    width = jnp.concatenate([collapse(wide, IMG), as_row(bias.reshape(MAP, IMG, channels))], axis=0)
    height = jnp.concatenate([collapse(tall, 16), as_row(tall_bias)], axis=0)
    for v in range(MAP + 1):
        row, lane = mix_place(v)
        out_ref[row : row + 1, lane : lane + MAP] = width[v : v + 1]
        out_ref[row : row + 1, lane + 16 : lane + 16 + MAP] = height[v : v + 1]


MIX_ROW = 10
TAPS_ROW = 12
KERNEL_ROW = 21
SMALL_ROWS = 32


def mix_place(v):
    return MIX_ROW + v // 10, 32 * (v % 10)


def put_small(out_ref, small, upsum):
    channels = out_ref.shape[-1]
    for i in range(6):
        out_ref[i : i + 1] = jnp.sum(small[i], axis=0, keepdims=True)
    up = jnp.sum(upsum[...], axis=0, keepdims=True)
    for i in range(up.shape[-1] // channels):
        out_ref[6 + i : 7 + i] = up[:, i * channels : (i + 1) * channels]


def tap_sums(value, pad, h, lo, hi, total):
    for r in range(3):
        for s in range(3):
            total[3 * r + s, :, lo:hi] += jnp.sum(value * pad[h + r, s : s + MAP, :, lo:hi], axis=0)


def put_taps(out_ref, row, total):
    for i in range(9):
        out_ref[row + i : row + i + 1] = jnp.sum(total[i], axis=0, keepdims=True)


def conv_backward(layer, cells, a, stats_ref, totals_ref, gain, kernel_ref, dn, dm, emit, padd, x=None, padx=None, ksum=None, send=None):
    mean, rstd = scale_of(stats_ref, cells)
    scale = rstd * gain[layer : layer + 1]
    shift_mean = totals_ref[0:1] * (1.0 / cells)
    gain_mean = totals_ref[1:2] * (1.0 / cells)
    channels = padd.shape[-1]
    arriving = [part for part in (a, dn, dm, x) if part is not None]
    for c in range(MAP // 2):
        for part in arriving:
            part.start_part(c)
    zero_border(padd)
    if x is not None:
        zero_border(padx)
        ksum[...] = jnp.zeros(ksum.shape, F32)

    def fill(c):
        for part in arriving:
            part.wait(c)
        for i in range(2):
            h = 2 * c + i
            xhat = (a.ref[h] - mean) * rstd
            da = scale * (dn.ref[h] - shift_mean - xhat * gain_mean)
            padd[h + 1, 1 : MAP + 1] = da.reshape(MAP, IMG, -1)
            if x is not None:
                padx[h + 1, 1 : MAP + 1] = x.ref[h].astype(BF16).astype(F32).reshape(MAP, IMG, -1)

    def rows(c):
        for i in range(2):
            h = 2 * c + i
            for lo, hi in lane_groups(channels):
                acc = dm.ref[h, :, lo:hi].reshape(MAP, IMG, hi - lo)
                da = padd[h + 1, 1 : MAP + 1, :, lo:hi]
                for r in range(3):
                    for s in range(3):
                        acc = acc + padd[h + 2 - r, 2 - s : 2 - s + MAP, :, lo:hi] * kernel_ref[r, s, layer : layer + 1, lo:hi]
                if x is not None:
                    tap_sums(da, padx, h, lo, hi, ksum)
                emit(h, lo, hi, acc)
        if send is not None:
            send(c)

    fill(0)

    def body(c, carry):
        fill(c + 1)
        rows(c)
        return carry

    lax.fori_loop(0, MAP // 2 - 1, body, 0)
    rows(MAP // 2 - 1)


def fill_pad(pad, x_ref):
    def body(h, carry):
        pad[h + 1, 1 : MAP + 1] = x_ref[h].astype(F32).reshape(MAP, IMG, -1)
        return carry

    lax.fori_loop(0, MAP, body, 0)


def kernel_taps(r):
    r.x.wait_all()
    zero_border(r.pad)
    fill_pad(r.pad, r.x.ref)
    r.a.wait_all()
    mean = r.stats[0:1]
    r.times[...] = jnp.zeros(r.times.shape, F32)
    r.alone[0] = jnp.zeros(r.alone.shape[1:], F32)

    def body(h, carry):
        for lo, hi in lane_groups(r.pad.shape[-1]):
            value = (r.a.ref[h, :, lo:hi] - mean[:, lo:hi]).reshape(MAP, IMG, hi - lo)
            tap_sums(value, r.pad, h, lo, hi, r.times)
            r.alone[0, :, lo:hi] += jnp.sum(r.pad[h + 1, 1 : MAP + 1, :, lo:hi], axis=0)
        return carry

    lax.fori_loop(0, MAP, body, 0)
    whole = r.alone[0]
    ends = {0: MAP, 2: 1}
    out_rows = {i: jnp.sum(r.pad[at, 1 : MAP + 1], axis=0) for i, at in ends.items()}
    out_cols = {i: jnp.sum(r.pad[1 : MAP + 1, at], axis=0) for i, at in ends.items()}
    for i in range(3):
        for k in range(3):
            value = whole
            if i != 1:
                value = value - out_rows[i]
            if k != 1:
                value = value - out_cols[k]
            if i != 1 and k != 1:
                value = value + r.pad[ends[i], ends[k]]
            r.alone[3 * i + k] = value
    r.out[...] = jnp.zeros(r.out.shape, F32)
    put_taps(r.out, 0, r.alone)
    put_taps(r.out, 9, r.times)
    r.out[18:19] = mean


def kernel_first(r):
    tile = r.tile[0]
    zero_border(r.pad)
    for k, piece in enumerate((r.p0, r.p1, r.p2, r.p3)):
        h0, w0 = corner(tile, k)
        value = piece[...].astype(F32).reshape(TS, TS, IMG, -1)
        r.pad[pl.ds(1 + h0, TS), pl.ds(1 + w0, TS)] = value

    def body(h, carry):
        r.x[h] = r.pad[h + 1, 1 : MAP + 1].reshape(ROW, -1).astype(BF16)
        return carry

    lax.fori_loop(0, MAP, body, 0)
    conv_rows(r.pad, r.kernels, 0, r.a, r.stats, r.sums)


def turn_unite(r):
    r.unite_t.wait_all()
    channels = r.unite.shape[-1]
    for part, first, size, lane in joined_places(channels):
        r.unite[lane : lane + size] = r.unite_t.ref[:, part * channels + first : part * channels + first + size].T
    r.unite[3 * channels :] = jnp.zeros((JOINED - 3 * channels, channels), BF16)


def forward_front(r, layer, cells, later):
    def arrive(p):
        r.a.wait(p)
        if p == HALVES - 1:
            for part in later:
                part.start()

    mix_forward(layer, cells, arrive, r.a.ref, r.stats, r.batch_gain, r.batch_shift, r.mix_width, r.mix_width_bias, r.mix_height, r.mix_height_bias, r.joined.ref)


def kernel_forward(cells, r):
    forward_front(r, 0, cells, (r.unite_t, r.x, r.up, r.down))
    r.joined.send_all()
    turn_unite(r)
    zero_border(r.pad)
    r.x.wait_all()
    for p in range(HALVES):
        m, zhat, s, zb = unite_norm(r, 0, p, half_rows(r.x.ref, p).astype(F32))
        put_half(r.u.ref, p, m + r.down_bias[0:1])
        put_half(r.zhat.ref, p, zhat)
        put_half(r.s.ref, p, s)
        put_half(r.zb.ref, p, zb)
        for stream in (r.zhat, r.s, r.zb):
            stream.send(p)
    r.up.wait_all()
    r.down.wait_all()

    def body(j):
        blk, up, down = hidden_block(r, 0, j)
        for p in range(HALVES):
            g, d = gelu_pair(dot(half_rows(r.zb.ref, p), up) + r.up_bias[0:1, blk])
            g = g.astype(BF16)
            r.g.ref[j, p * PART : (p + 1) * PART] = block_half(g)
            r.d.ref[j, p * PART : (p + 1) * PART] = block_half(d.astype(BF16))
            add_half(r.u.ref, p, dot_nt(g, down))
        r.g.send(j)
        r.d.send(j)

    lax.fori_loop(0, r.up_bias.shape[-1] // BLK, lambda j, c: (body(j), c)[1], 0)
    r.u.send_all()

    def fill(h, carry):
        rounded = r.u.ref[h].astype(BF16).astype(F32)
        r.pad[h + 1, 1 : MAP + 1] = rounded.reshape(MAP, IMG, -1)
        return carry

    lax.fori_loop(0, MAP, fill, 0)
    conv_rows(r.pad, r.kernels, 1, r.a2.ref, r.stats2, r.sums, r.a2.send)


def clear(r):
    r.small[...] = jnp.zeros(r.small.shape, F32)
    r.upsum[...] = jnp.zeros(r.upsum.shape, F32)


def send_blocks(r):
    half = BLOCKS // 2
    r.mine.start(r.buf.at[pl.ds(0, half)])
    r.sent.start(r.buf.at[pl.ds(half, half)])


def kernel_whole_map(r):
    tile = r.tile[0]
    for k, piece in enumerate((r.p0, r.p1, r.p2, r.p3)):
        h0, w0 = corner(tile, k)
        r.field[pl.ds(h0, TS), pl.ds(w0, TS)] = piece[...].astype(F32).reshape(TS, TS, IMG, -1)
    for h in range(MAP):
        r.out[h] = r.field[h].reshape(ROW, -1).astype(BF16)


def kernel_pieces(r):
    tile = r.tile[0]
    for k, piece in enumerate((r.p0, r.p1, r.p2, r.p3)):
        h0, w0 = corner(tile, k)
        field = r.field[pl.ds(h0, TS)].astype(F32).reshape(TS, MAP, IMG, -1)
        piece[...] = pick_columns(field, w0).reshape(PIECE, -1).astype(BF16)


def kernel_turn(cells, r):
    clear(r)
    r.do = r.do_in.ref
    r.joined = Held(r.joined)
    forward_front(r, 1, cells, (r.unite_t, r.u, r.up, r.down, r.do_in))
    turn_unite(r)
    r.u.wait_all()

    def cotangent(p):
        return half_rows(r.do, p).astype(F32)

    for p in range(HALVES):
        m, zhat, s, zb = unite_norm(r, 1, p, half_rows(r.u.ref, p))
        put_half(r.out, p, m + r.down_bias[1:2])
        put_half(r.zhat, p, zhat)
        put_half(r.s, p, s)
        put_half(r.zb, p, zb)
    for part in (r.up, r.down, r.do_in):
        part.wait_all()
    r.dz[...] = jnp.zeros(r.dz.shape, F32)
    blocks = r.up_bias.shape[-1] // BLK

    def body(j):
        blk, up, down = hidden_block(r, 1, j)
        gs, dhs = [], []
        for p in range(HALVES):
            g, d = gelu_pair(dot(half_rows(r.zb, p), up) + r.up_bias[1:2, blk])
            g = g.astype(BF16)
            add_half(r.out, p, dot_nt(g, down))
            dh = dot(half_rows(r.do, p), down) * d
            r.upsum[:, blk] += column_sums(dh)
            dh = dh.astype(BF16)
            add_half(r.dz, p, dot_nt(dh, up))
            gs.append(g)
            dhs.append(dh)
        return jnp.concatenate(gs, 0), jnp.concatenate(dhs, 0)

    done = []
    for j in range(blocks):
        done.append(body(j))
        if j > 0:
            hidden_gradients(r, j - 1, blocks, r.zb, r.do, *done[j - 1])
    hidden_gradients(r, blocks - 1, blocks, r.zb, r.do, *done[blocks - 1])
    r.features.ref[...] = r.out[...].astype(BF16)
    r.features.send_all()
    for p in range(HALVES):
        norm_backward(r, 1, p, cotangent(p), half_rows(r.zhat, p), half_rows(r.s, p), half_rows(r.dz, p), r.df)
        r.dm.send(p)
    r.small_out[...] = jnp.zeros(r.small_out.shape, F32)
    unite_gradients(r, blocks, r.df, r.small_out)
    send_blocks(r)
    mix_backward(1, cells, r.a.ref, r.stats, r.mix_width, r.mix_height, r.dpw, r.dph, r.dn.ref, r.small, r.dn.send)
    put_small(r.small_out, r.small, r.upsum)
    r.small_out[TAPS_ROW : TAPS_ROW + 18] = r.taps[...]


def kernel_conv_middle(cells, r):
    def emit(h, lo, hi, value):
        r.du.ref[h, :, lo:hi] = value.reshape(ROW, hi - lo)
        r.do.ref[h, :, lo:hi] = value.reshape(ROW, hi - lo).astype(BF16)

    def send(c):
        r.do.send(c)
        r.du.send(c)

    conv_backward(1, cells, r.a, r.stats, r.totals, r.batch_gain, r.kernels, r.dn, r.dm, emit, r.padd, r.x, r.padx, r.ksum, send)
    put_taps(r.kgrad, 0, r.ksum)


def kernel_back(cells, r):
    for part in (r.do_in, r.down, r.up):
        part.start()
    r.d.start_part(0)
    clear(r)
    r.do = r.do_in.ref
    for part in (r.do_in, r.up, r.down):
        part.wait_all()
    r.d.start_part(1)
    r.zb.start()
    r.g.start_part(0)
    r.dz[...] = jnp.zeros(r.dz.shape, F32)
    blocks = r.upsum.shape[-1] // BLK
    later = {blocks - 2: (r.zhat, r.s, r.unite_t, r.du), blocks - 1: (r.joined, r.a, r.x)}

    def body(j):
        blk, up, down = hidden_block(r, 0, j)
        r.d.wait(j)
        if j > 0:
            if j + 1 < blocks:
                r.d.start_part(j + 1)
            r.g.start_part(j)
        for part in later.get(j, ()):
            part.start()
        dhs = []
        for p in range(HALVES):
            d = r.d.ref[j, p * PART : (p + 1) * PART].reshape(PART * ROW, BLK).astype(F32)
            dh = dot(half_rows(r.do, p), down) * d
            r.upsum[:, blk] += column_sums(dh)
            dh = dh.astype(BF16)
            add_half(r.dz, p, dot_nt(dh, up))
            dhs.append(dh)
        return jnp.concatenate(dhs, 0)

    def gradients(j, dh):
        if j == 0:
            r.zb.wait_all()
        r.g.wait(j)
        hidden_gradients(r, j, blocks, r.zb.ref, r.do, flat_rows(r.g.ref[j]), dh)

    done = []
    for j in range(blocks):
        done.append(body(j))
        if j > 0:
            gradients(j - 1, done[j - 1])
    gradients(blocks - 1, done[blocks - 1])
    turn_unite(r)
    r.du.wait_all()
    r.zhat.wait_all()
    r.s.wait_all()
    for p in range(HALVES):
        norm_backward(r, 0, p, half_rows(r.du.ref, p), half_rows(r.zhat.ref, p), half_rows(r.s.ref, p), half_rows(r.dz, p), r.df)
        r.dm.send(p)
    r.joined.wait_all()
    r.small_out[...] = jnp.zeros(r.small_out.shape, F32)
    unite_gradients(r, blocks, r.df, r.small_out)
    send_blocks(r)
    for part in (r.a, r.x):
        part.wait_all()
    zero_border(r.pad)
    fill_pad(r.pad, r.x.ref)
    r.taps[...] = jnp.zeros(r.taps.shape, F32)

    mix_backward(0, cells, r.a.ref, r.stats, r.mix_width, r.mix_height, r.dpw, r.dph, r.dn.ref, r.small, r.dn.send)

    def windows(h, carry):
        for lo, hi in lane_groups(r.pad.shape[-1]):
            tap_sums(r.dn.ref[h, :, lo:hi].reshape(MAP, IMG, hi - lo), r.pad, h, lo, hi, r.taps)
        return carry

    lax.fori_loop(0, MAP, windows, 0)
    put_small(r.small_out, r.small, r.upsum)
    put_taps(r.small_out, TAPS_ROW, r.taps)
    r.small_out[KERNEL_ROW : KERNEL_ROW + 9] = r.kgrad[0:9]


def kernel_last(cells, r):
    tile = r.tile[0]

    def emit(h, lo, hi, value):
        r.du[h, :, :, lo:hi] = value

    conv_backward(0, cells, r.a, r.stats, r.totals, r.batch_gain, r.kernels, r.dn, r.dm, emit, r.padd)
    for k, piece in enumerate((r.o0, r.o1, r.o2, r.o3)):
        h0, w0 = corner(tile, k)
        piece[...] = r.du[pl.ds(h0, TS), pl.ds(w0, TS)].reshape(PIECE, -1).astype(BF16)


def unpack_put(r, value, quarter, row):
    channels, hidden = r.up.ref.shape
    rows = pl.ds(row, value.shape[1])
    for i in range(value.shape[0]):
        base = (quarter * value.shape[0] + i) * GROUP_LANES
        if base < hidden:
            r.up.ref[rows, base : base + GROUP_LANES] = value[i]
        elif base < 2 * hidden:
            r.down.ref[rows, base - hidden : base - hidden + GROUP_LANES] = value[i]
        else:
            base -= 2 * hidden
            for part, first, size, lane in joined_places(channels):
                lo, hi = max(lane, base), min(lane + size, base + GROUP_LANES)
                if lo < hi:
                    target = part * channels + first + lo - lane
                    r.unite.ref[rows, target : target + hi - lo] = value[i, :, lo - base : hi - base]


def unpack_all(r, block):
    channels, hidden = r.up.ref.shape
    size = 4 * channels // BLOCKS
    per = channels // size
    lanes = PER_QUARTER * GROUP_LANES
    for quarter in range(4):
        for b in range(per):
            unpack_put(r, block(quarter * per + b), quarter, b * size)
        if (quarter + 1) * lanes >= hidden and quarter * lanes < hidden:
            r.up.send_all()
        if (quarter + 1) * lanes >= 2 * hidden and quarter * lanes < 2 * hidden:
            r.down.send_all()
    r.unite.send_all()


def kernel_unpack(r):
    index = r.index[0]
    half = BLOCKS // 2
    flip = index & (half - 1)
    own = index // half
    r.near.wait_all()
    r.far.wait_all()

    def block(p):
        place = (p & (half - 1)) ^ flip
        near, far = r.near.ref[place].astype(F32), r.far.ref[place].astype(F32)
        return jnp.where(own == p // half, near, far)

    unpack_all(r, block)


def kernel_finish(cells, r):
    channels = r.total0.shape[-1]
    for layer, total in enumerate((r.total0, r.total1)):
        one = slice(layer, layer + 1)
        r.batch_shift[one] = total[0:1]
        r.batch_gain[one] = total[1:2]
        r.norm_gain[one] = total[2:3]
        r.norm_shift[one] = total[3:4]
        r.down_bias[one] = total[4:5]
        r.unite_bias[one] = total[5:6]
        for i in range(r.up_bias.shape[-1] // channels):
            r.up_bias[one, i * channels : (i + 1) * channels] = total[6 + i : 7 + i]
        for v in range(MAP + 1):
            row, lane = mix_place(v)
            width, height = total[row : row + 1, lane : lane + MAP], total[row : row + 1, lane + 16 : lane + 16 + MAP]
            if v < MAP:
                r.mix_width[v, one], r.mix_height[v, one] = width, height
            else:
                r.mix_width_bias[one], r.mix_height_bias[one] = width, height
    mean, rstd = scale_of(r.stats, cells)
    shift_mean, gain_mean = r.total0[0:1] * (1.0 / cells), r.total0[1:2] * (1.0 / cells)
    for i in range(9):
        alone, times = r.total1[TAPS_ROW + i : TAPS_ROW + i + 1], r.total1[KERNEL_ROW + i : KERNEL_ROW + i + 1]
        value = r.total0[TAPS_ROW + i : TAPS_ROW + i + 1] - shift_mean * alone - gain_mean * rstd * times
        r.kernel[i // 3, i % 3, 0:1] = rstd * r.gain[0:1] * value
        r.kernel[i // 3, i % 3, 1:2] = r.total0[KERNEL_ROW + i : KERNEL_ROW + i + 1]


class Kept:
    def __init__(self, array):
        self.array = array


class Smem:
    def __init__(self, array):
        self.array = array


class Layer:
    def __init__(self, array, layer):
        self.array, self.layer = array, layer


def chunk_step(shape, step=None):
    if len(shape) == 4 and shape[1:3] == (MAP, ROW):
        return 1
    if len(shape) == 3 and shape[:2] == (MAP, ROW):
        return step or PART
    return shape[0]


class Late:
    def __init__(self, array, layer=None, step=None, hold=False):
        self.array, self.layer, self.hold = array, layer, hold
        self.step = chunk_step(self.shape, step)

    @property
    def shape(self):
        return self.array.shape if self.layer is None else self.array.shape[1:]

    @property
    def parts(self):
        return self.shape[0] // self.step


class LateJoin:
    def __init__(self, arrays):
        self.arrays = arrays
        self.dtype = arrays[0].dtype
        self.shape = (sum(a.shape[0] for a in arrays),) + arrays[0].shape[1:]


class LateJoinRef:
    def __init__(self, sources, ref, sems):
        self.ref, self.copies, row = ref, [], 0
        for i, source in enumerate(sources):
            size = source.shape[0]
            self.copies.append(pltpu.make_async_copy(source, ref.at[pl.ds(row, size)], sems.at[i]))
            row += size

    def start(self):
        for copy in self.copies:
            copy.start()

    def wait_all(self):
        for copy in self.copies:
            copy.wait()


class LateRef:
    def __init__(self, late, source, ref, sems):
        self.parts, self.step = late.parts, late.step
        self.source = source if late.layer is None else source.at[late.layer]
        self.ref, self.sems = ref, sems

    def copy(self, c):
        if self.parts == 1:
            return pltpu.make_async_copy(self.source, self.ref, self.sems.at[0])
        rows = pl.ds(self.step * c, self.step)
        return pltpu.make_async_copy(self.source.at[rows], self.ref.at[rows], self.sems.at[c])

    def start(self):
        for c in range(self.parts):
            self.copy(c).start()

    def start_part(self, c):
        self.copy(c).start()

    def wait(self, c):
        self.copy(c).wait()

    def wait_all(self):
        for c in range(self.parts):
            self.copy(c).wait()


class Stream:
    def __init__(self, out, layer=None, step=None):
        self.out, self.layer = out, layer
        self.step = chunk_step(self.shape, step)

    @property
    def shape(self):
        return self.out.shape if self.layer is None else self.out.shape[1:]


class Place:
    def __init__(self, out):
        self.out = out


class StreamRef:
    def __init__(self, stream, target, ref, sem):
        self.target, self.ref, self.sem = target if stream.layer is None else target.at[stream.layer], ref, sem
        self.step = stream.step

    def send(self, c):
        rows = pl.ds(self.step * c, self.step)
        pltpu.make_async_copy(self.ref.at[rows], self.target.at[rows], self.sem).start()

    def send_all(self):
        pltpu.make_async_copy(self.ref, self.target, self.sem).start()

    def finish(self):
        pltpu.make_async_copy(self.ref, self.target, self.sem).wait()


class PlaceRef:
    def __init__(self, target, sem):
        self.target, self.sem = target, sem

    def start(self, source):
        self.copy = pltpu.make_async_copy(source, self.target, self.sem)
        self.copy.start()

    def finish(self):
        self.copy.wait()


class Held:
    def __init__(self, ref):
        self.ref = ref


class Refs:
    pass


def full(array):
    rank = len(array.shape)
    return pl.BlockSpec(array.shape, lambda i: (0,) * rank)


ANY = pl.BlockSpec(memory_space=pl.ANY)
FINISHED = (
    "batch_shift", "batch_gain", "norm_gain", "norm_shift", "down_bias", "unite_bias", "up_bias",
    "kernel", "mix_width", "mix_height", "mix_width_bias", "mix_height_bias",
)


def _padded(array):
    shape = list(array.shape)
    if len(shape) > 1:
        shape[-2] = -(-shape[-2] // 16) * 16
    shape[-1] = -(-shape[-1] // 128) * 128
    return math.prod(shape) * jnp.dtype(array.dtype).itemsize


def run(body, name, flops, ins, outs, scratch=None, aliases=None, tight=False):
    scratch = dict(scratch or {})
    arrays, in_specs, out_specs, out_shapes, spaces = [], [], [], [], []
    for key, operand in ins.items():
        if isinstance(operand, Smem):
            in_specs.append(pl.BlockSpec(memory_space=pltpu.SMEM))
        elif isinstance(operand, Layer):
            shape, layer = operand.array.shape, operand.layer
            in_specs.append(pl.BlockSpec((None,) + shape[1:], lambda i, layer=layer, rank=len(shape): (layer,) + (0,) * (rank - 1)))
        elif isinstance(operand, Kept):
            in_specs.append(ANY)
        elif isinstance(operand, LateJoin):
            in_specs += [ANY] * len(operand.arrays)
            arrays += operand.arrays
            spaces += [pltpu.VMEM(operand.shape, operand.dtype), pltpu.SemaphoreType.DMA((len(operand.arrays),))]
            continue
        elif isinstance(operand, Late):
            in_specs.append(ANY)
            spaces += [pltpu.VMEM(operand.shape, operand.array.dtype), pltpu.SemaphoreType.DMA((operand.parts,))]
        else:
            in_specs.append(full(operand))
        arrays.append(getattr(operand, "array", operand))
    for key, out in outs.items():
        if isinstance(out, (Stream, Place)):
            out_specs.append(ANY)
            out_shapes.append(out.out)
            if isinstance(out, Stream):
                spaces.append(pltpu.VMEM(out.shape, out.out.dtype))
            spaces.append(pltpu.SemaphoreType.DMA)
        elif isinstance(out, Layer):
            shape, layer = out.array.shape, out.layer
            out_specs.append(pl.BlockSpec((None,) + shape[1:], lambda i, layer=layer, rank=len(shape): (layer,) + (0,) * (rank - 1)))
            out_shapes.append(out.array)
        else:
            out_specs.append(full(out))
            out_shapes.append(out)
    spaces += list(scratch.values())

    def wrapped(*refs):
        refs = list(refs)
        r = Refs()
        main, extra = refs[: len(arrays) + len(outs)], refs[len(arrays) + len(outs) :]
        late, streams = [], []
        for key, operand in ins.items():
            if isinstance(operand, LateJoin):
                sources = [main.pop(0) for _ in operand.arrays]
                ref = LateJoinRef(sources, extra.pop(0), extra.pop(0))
                late.append(ref)
                setattr(r, key, ref)
                continue
            ref = main.pop(0)
            if isinstance(operand, Late):
                ref = LateRef(operand, ref, extra.pop(0), extra.pop(0))
                if not operand.hold:
                    late.append(ref)
            setattr(r, key, ref)
        for key, out in outs.items():
            ref = main.pop(0)
            if isinstance(out, Stream):
                ref = StreamRef(out, ref, extra.pop(0), extra.pop(0))
                streams.append(ref)
            elif isinstance(out, Place):
                ref = PlaceRef(ref, extra.pop(0))
                streams.append(ref)
            setattr(r, key, ref)
        for key in scratch:
            setattr(r, key, extra.pop(0))
        for part in late:
            part.start()
        body(r)
        for stream in streams:
            stream.finish()

    held = [a for a, spec in zip(arrays + out_shapes, in_specs + out_specs) if spec is not ANY]
    held += [space for space in spaces if getattr(space, "memory_space", None) == pltpu.VMEM]
    need = sum(_padded(a) for a in held)
    limit = min(VMEM_BYTES, need + need // 4 + MARGIN) if tight else VMEM_BYTES
    size = sum(a.size * a.dtype.itemsize for a in arrays) + sum(o.size * o.dtype.itemsize for o in out_shapes)
    results = pl.pallas_call(
        wrapped,
        grid=(1,),
        in_specs=in_specs,
        out_specs=out_specs,
        out_shape=out_shapes,
        scratch_shapes=spaces,
        input_output_aliases=aliases or {},
        compiler_params=pltpu.CompilerParams(vmem_limit_bytes=limit),
        cost_estimate=pl.CostEstimate(flops=flops, bytes_accessed=size, transcendentals=0),
        name=name,
    )(*arrays)
    named = Refs()
    for key, value in zip(outs, results):
        setattr(named, key, value)
    return named


def on_device(
    patches,
    conv_kernel,
    batch_gain,
    batch_shift,
    mix_width,
    mix_width_bias,
    mix_height,
    mix_height_bias,
    unite_weight,
    unite_bias,
    norm_gain,
    norm_shift,
    up_weight,
    up_bias,
    down_weight,
    down_bias,
    cotangent,
):
    channels = patches.shape[-1]
    hidden = up_weight.shape[-1]
    tile = lax.axis_index("tile")
    tile_arg = Smem(tile.astype(jnp.int32).reshape(1))
    index_arg = Smem(block_index().reshape(1))
    local_cells = MAP * ROW
    cells = local_cells * lax.axis_size("dp") * lax.axis_size("tile")

    def rows(lanes, dtype):
        return jax.ShapeDtypeStruct((MAP, ROW, lanes), dtype)

    def shape(*dims, dtype=F32):
        return jax.ShapeDtypeStruct(dims, dtype)

    def vmem(struct):
        return pltpu.VMEM(struct.shape, struct.dtype)

    piece = shape(PIECE, channels, dtype=BF16)
    c_bf, c_f32, h_bf = rows(channels, BF16), rows(channels, F32), shape(hidden // BLK, MAP, ROW, BLK, dtype=BF16)
    map4 = pltpu.VMEM((MAP, MAP, IMG, channels), F32)
    pad = pltpu.VMEM((MAP + 2, MAP + 2, IMG, channels), F32)
    sums = pltpu.VMEM((2, 8, channels), F32)
    small = pltpu.VMEM((6, 8, channels), F32)
    upsum = pltpu.VMEM((8, hidden), F32)
    ksum = pltpu.VMEM((9, 8, channels), F32)
    unite_space = pltpu.VMEM((JOINED, channels), BF16)
    blocks = hidden // BLK
    groups = 2 * blocks * (BLK // GROUP_LANES) + JOINED // GROUP_LANES
    assert groups == 4 * PER_QUARTER
    block = (PER_QUARTER, 4 * channels // BLOCKS, GROUP_LANES)
    half = shape(BLOCKS // 2, *block, dtype=BF16)
    buf = pltpu.VMEM((BLOCKS, *block), BF16)

    kernels = conv_kernel.transpose(1, 2, 0, 3)
    down_t = down_weight.transpose(0, 2, 1)
    unite_t = unite_weight.transpose(0, 2, 1)
    mix_width = mix_width.transpose(1, 0, 2)
    mix_height = mix_height.transpose(1, 0, 2)

    x_pieces = to_whole(patches[:, 0].transpose(1, 2, 0, 3), tile)
    first = run(
        kernel_first,
        "conv_first",
        10**7,
        dict(tile=tile_arg, **{f"p{k}": x_pieces[k] for k in range(4)}, kernels=kernels),
        dict(x=c_bf, a=c_f32, stats=shape(2, channels)),
        dict(pad=pad, sums=sums),
        tight=True,
    )
    taps = run(
        kernel_taps,
        "taps",
        10**8,
        dict(x=Late(first.x), a=Late(first.a), stats=first.stats),
        dict(out=shape(24, channels)),
        dict(pad=pad, alone=ksum, times=ksum),
        tight=True,
    ).out
    stats0, (cotangent, taps) = total_moments(first.stats, float(local_cells), [cotangent, taps])
    taps = jnp.concatenate([taps[0:9], taps[9:18] + (taps[18:19] - stats0[0:1]) * taps[0:9]], 0)
    cot_pieces = to_whole(cotangent[:, 0].transpose(1, 2, 0, 3), tile)

    def forward_ins(layer):
        return dict(
            batch_gain=batch_gain, batch_shift=batch_shift,
            mix_width=mix_width, mix_width_bias=mix_width_bias, mix_height=mix_height, mix_height_bias=mix_height_bias,
            unite_t=Late(unite_t, layer, hold=True), up=Late(up_weight, layer, hold=True), down=Late(down_t, layer, hold=True),
            unite_bias=unite_bias, norm_gain=norm_gain, norm_shift=norm_shift, up_bias=up_bias, down_bias=down_bias,
        )

    fwd = run(
        lambda r: kernel_forward(cells, r),
        "block_forward",
        6 * 10**9,
        dict(a=Late(first.a), stats=stats0, **forward_ins(0), x=Late(first.x, hold=True), kernels=kernels),
        dict(
            joined=Stream(rows(JOINED, BF16)), zhat=Stream(c_f32), s=Stream(rows(1, F32)), zb=Stream(c_bf),
            g=Stream(h_bf), d=Stream(h_bf), u=Stream(c_f32), a2=Stream(c_f32, step=1), stats2=shape(2, channels),
        ),
        dict(pad=pad, sums=sums, unite=unite_space),
    )
    stats1, *cot_pieces = tie(fwd.stats2, *cot_pieces)
    cot_map = run(
        kernel_whole_map,
        "cotangent_map",
        10**7,
        dict(tile=tile_arg, **{f"p{k}": cot_pieces[k] for k in range(4)}),
        dict(out=c_bf),
        dict(field=map4),
        tight=True,
    ).out
    stats1 = total_moments(stats1, float(local_cells))

    turn = run(
        lambda r: kernel_turn(cells, r),
        "block_turn",
        14 * 10**9,
        dict(
            index=index_arg, a=Late(fwd.a2), stats=stats1, u=Late(fwd.u, hold=True), do_in=Late(cot_map, hold=True),
            **forward_ins(1), taps=taps,
        ),
        dict(
            features=Stream(c_bf), dm=Stream(c_f32), dn=Stream(c_f32, step=1), small_out=shape(SMALL_ROWS, channels),
            mine=Place(half), sent=Place(half),
        ),
        dict(
            joined=vmem(rows(JOINED, BF16)), zb=vmem(c_bf), df=vmem(c_bf), dpw=vmem(c_bf), dph=vmem(c_bf),
            out=vmem(c_f32), zhat=vmem(c_f32), s=vmem(rows(1, F32)), dz=vmem(c_f32), small=small, upsum=upsum, buf=buf, unite=unite_space,
        ),
    )
    cut = run(
        kernel_pieces,
        "feature_pieces",
        10**7,
        dict(tile=tile_arg, field=turn.features),
        {f"p{k}": piece for k in range(4)},
        tight=True,
    )
    features = [cut.p0, cut.p1, cut.p2, cut.p3]

    near = masks(GROUPS[0])[0]
    got = flat_partner(turn.sent, near)
    first_stage, *later_stages = stages()
    total1 = sum_stage(turn.small_out, first_stage)
    total1, mine1, got = tie(total1, turn.mine, got)
    part1 = narrow_add([mine1, got])
    got1 = scatter_sends(part1, GROUPS[1])
    for stage in later_stages:
        total1 = sum_stage(total1, stage)
    total1, part1, *rest = tie(total1, part1[: part1.shape[0] // 4], *got1, *features)
    got1, features = rest[:3], rest[3:]
    part1 = narrow_add([part1, *got1])
    far = far_masks()
    got1 = flat_partner(part1, far[0])
    mid = run(
        lambda r: kernel_conv_middle(cells, r),
        "conv_middle",
        2 * 10**9,
        dict(**{key: Late(value, step=2, hold=True) for key, value in dict(a=fwd.a2, dn=turn.dn, x=fwd.u, dm=turn.dm).items()}, stats=stats1, totals=total1, kernels=kernels, batch_gain=batch_gain),
        dict(do=Stream(c_bf, step=2), du=Stream(c_f32, step=2), kgrad=shape(16, channels)),
        dict(padx=pad, padd=pad, ksum=ksum),
    )
    do, part1, got1, *features = tie(mid.do, part1, got1, *features)
    part1 = narrow_add([part1, got1])
    got1 = flat_partner(part1, far[1])
    features = swap_pieces(features)
    back = run(
        lambda r: kernel_back(cells, r),
        "block_back",
        14 * 10**9,
        dict(
            index=index_arg,
            **{
                key: Late(value, layer, hold=True)
                for key, (value, layer) in dict(
                    down=(down_t, 0), do_in=(do, None), du=(mid.du, None), up=(up_weight, 0), d=(fwd.d, None), zb=(fwd.zb, None), g=(fwd.g, None), unite_t=(unite_t, 0),
                    zhat=(fwd.zhat, None), s=(fwd.s, None), joined=(fwd.joined, None), a=(first.a, None), x=(first.x, None),
                ).items()
            },
            kgrad=mid.kgrad, norm_gain=norm_gain, stats=stats0, mix_width=mix_width, mix_height=mix_height,
        ),
        dict(dm=Stream(c_f32), dn=Stream(c_f32, step=1), small_out=shape(SMALL_ROWS, channels), mine=Place(half), sent=Place(half)),
        dict(df=vmem(c_bf), dpw=vmem(c_bf), dph=vmem(c_bf), dz=vmem(c_f32), small=small, upsum=upsum, buf=buf, unite=unite_space, pad=pad, taps=ksum),
    )
    small0, mine0, sent0, part1, got1, *features = tie(back.small_out, back.mine, back.sent, part1, got1, *features)
    part1 = narrow_add([part1, got1])
    for mask in far[2:]:
        part1 = add_partner(part1, mask)
    got = flat_partner(sent0, near)
    total0 = sum_stage(small0, first_stage)
    total0, mine0, got = tie(total0, mine0, got)
    part0 = narrow_add([mine0, got])
    got0 = scatter_sends(part0, GROUPS[1])
    for stage in later_stages[:-1]:
        total0 = sum_stage(total0, stage)
    total0, part1 = tie(total0, part1)
    x_mask, y_mask, _ = masks(GROUPS[1])
    got1 = [flat_partner(part1, y_mask), flat_partner(part1, x_mask)]
    total0 = sum_stage(total0, later_stages[-1])
    total0, part0, *got0 = tie(total0, part0[: part0.shape[0] // 4], *got0)
    part0 = narrow_add([part0, *got0])
    halves0 = [part0[: QUAD // 2], part0[QUAD // 2 :]]
    got0 = [flat_partner(halves0[0], far[0]), flat_partner(halves0[1], far[1])]
    last = run(
        lambda r: kernel_last(cells, r),
        "conv_last",
        2 * 10**9,
        dict(tile=tile_arg, **{key: Late(value, step=2, hold=True) for key, value in dict(a=first.a, dn=back.dn, dm=back.dm).items()}, stats=stats0, totals=total0, kernels=kernels, batch_gain=batch_gain),
        {f"o{k}": piece for k in range(4)},
        dict(padd=pad, du=map4),
    )
    o3, *rest = tie(last.o3, *halves0, *got0, part1, *got1)
    halves0, got0, (part1, from_y, from_x) = rest[:2], rest[2:4], rest[4:]
    parts1 = [part1, from_x, from_y, flat_partner(from_y, x_mask)]
    grads = swap_pieces([last.o0, last.o1, last.o2, o3])
    halves0 = [narrow_add([half0, got]) for half0, got in zip(halves0, got0)]
    got0 = [flat_partner(halves0[0], far[1]), flat_partner(halves0[1], far[0])]
    rest = tie(*halves0, *got0, *grads, *parts1)
    part0 = jnp.concatenate([narrow_add([half0, got]) for half0, got in zip(rest[:2], rest[2:4])], 0)
    for mask in far[2:]:
        part0 = add_partner(part0, mask)
    grads, parts1 = rest[4:8], rest[8:]
    got0 = [flat_partner(part0, mask) for mask in masks(GROUPS[1])]
    far1 = [flat_partner(part, near) for part in parts1]
    features_out = join_pieces(features, tile)
    grads = join_pieces(grads, tile)
    grad_shapes = dict(up=shape(2, channels, hidden), down=shape(2, channels, hidden), unite=shape(2, channels, 3 * channels))
    whole = run(
        kernel_unpack,
        "unpack_1",
        10**7,
        dict(index=index_arg, near=LateJoin(parts1), far=LateJoin(far1)),
        {key: Stream(value, 1) for key, value in grad_shapes.items()},
        tight=True,
    )
    line = shape(2, channels)
    fin = run(
        lambda r: kernel_finish(cells, r),
        "finish",
        10**6,
        dict(total0=total0, total1=total1, stats=stats0, gain=batch_gain),
        dict(
            batch_shift=line, batch_gain=line, norm_gain=line, norm_shift=line, down_bias=line, unite_bias=line, up_bias=shape(2, hidden),
            kernel=shape(3, 3, 2, channels), mix_width=shape(MAP, 2, MAP), mix_height=shape(MAP, 2, MAP), mix_width_bias=shape(2, MAP), mix_height_bias=shape(2, MAP),
        ),
    )
    whole_1 = (whole.up, whole.down, whole.unite)
    small_results = [getattr(fin, key) for key in FINISHED]
    grads, features_out, *rest = tie(grads, features_out, part0, *got0, *whole_1, *small_results)
    parts0, whole_1, small_results = rest[:4], rest[4:7], rest[7:]
    for key, value in zip(FINISHED, small_results):
        setattr(fin, key, value)
    far0 = [flat_partner(part, near) for part in parts0]
    whole = run(
        kernel_unpack,
        "unpack_0",
        10**7,
        dict(index=index_arg, near=LateJoin(parts0), far=LateJoin(far0), up_in=Kept(whole_1[0]), down_in=Kept(whole_1[1]), unite_in=Kept(whole_1[2])),
        {key: Stream(value, 0) for key, value in grad_shapes.items()},
        aliases={9: 0, 10: 1, 11: 2},
        tight=True,
    )

    def to_output(field):
        return field.transpose(2, 0, 1, 3)[:, None]

    return (
        to_output(features_out),
        to_output(grads),
        fin.kernel.transpose(2, 0, 1, 3),
        fin.batch_gain,
        fin.batch_shift,
        fin.mix_width.transpose(1, 0, 2),
        fin.mix_width_bias,
        fin.mix_height.transpose(1, 0, 2),
        fin.mix_height_bias,
        whole.unite.transpose(0, 2, 1),
        fin.unite_bias,
        fin.norm_gain,
        fin.norm_shift,
        whole.up,
        fin.up_bias,
        whole.down.transpose(0, 2, 1),
        fin.down_bias,
    )


def solution(mesh):
    field = P("dp", "tile", None, None, None)
    return jax.shard_map(
        on_device,
        mesh=mesh,
        in_specs=(field,) + (P(),) * 15 + (field,),
        out_specs=(field, field) + (P(),) * 15,
        check_vma=False,
    )
```

```python
import math

import jax
import jax.numpy as jnp
from jax import lax
from jax.experimental import pallas as pl
from jax.experimental.pallas import tpu as pltpu
from jax.sharding import PartitionSpec as P

F32 = jnp.float32
BF16 = jnp.bfloat16
norm_epsilon = 1e-05
layer_epsilon = 1e-06
ROOT_HALF = 0.7071067811865476
INV_ROOT_TAU = 0.3989422804014327
LOG2E = 1.4426950408889634

TS = 7
MAP = 14
IMG = 8
ROW = MAP * IMG
PIECE = TS * TS * IMG
VMEM_BYTES = 58 * 1024 * 1024
MARGIN = 8 * 1024 * 1024
BLK = 256


def partner(x, axis, distance):
    count = lax.axis_size(axis)
    return lax.ppermute(x, axis, [(i, i ^ distance) for i in range(count)])


def stages():
    result = [("tile", (1, 2, 3))]
    count = lax.axis_size("dp")
    step = 1
    if count > 1 and (count.bit_length() - 1) % 2 == 1:
        result.append(("dp", (1,)))
        step = 2
    while step < count:
        result.append(("dp", (step, 2 * step, 3 * step)))
        step *= 4
    return result


def sum_stage(x, stage):
    axis, distances = stage
    got = [partner(x, axis, d) for d in distances]
    if len(got) == 1:
        return x + got[0]
    return (x + got[0]) + (got[1] + got[2])


def total_sum(x, after=None, when=2):
    for step, stage in enumerate(stages()):
        if step == when and after is not None:
            x, *after = tie(x, *after)
        x = sum_stage(x, stage)
    return x if after is None else (x, after)


def total_moments(stats, count, after=None):
    for step, (axis, distances) in enumerate(stages()):
        if step == 2 and after is not None:
            stats, *after = tie(stats, *after)
        parts = [stats] + [partner(stats, axis, d) for d in distances]
        if len(parts) == 2:
            mean = (parts[0][0] + parts[1][0]) * 0.5
            dev = [jnp.square(p[0] - mean) for p in parts]
            square = (parts[0][1] + parts[1][1]) + count * (dev[0] + dev[1])
        else:
            mean = ((parts[0][0] + parts[1][0]) + (parts[2][0] + parts[3][0])) * 0.25
            dev = [jnp.square(p[0] - mean) for p in parts]
            square = ((parts[0][1] + parts[1][1]) + (parts[2][1] + parts[3][1])) + count * (
                (dev[0] + dev[1]) + (dev[2] + dev[3])
            )
        count = count * len(parts)
        stats = jnp.stack([mean, square])
    return stats if after is None else (stats, after)


def to_whole(field, tile):
    share = field.shape[2] // lax.axis_size("tile")
    pieces = []
    for k in range(4):
        part = lax.dynamic_slice_in_dim(field, (tile ^ k) * share, share, 2)
        part = part.reshape(TS * TS * share, field.shape[3])
        pieces.append(part if k == 0 else partner(part, "tile", k))
    return pieces


def swap_pieces(pieces):
    return [pieces[0]] + [partner(pieces[k], "tile", k) for k in range(1, 4)]


def join_pieces(pieces, tile):
    channels = pieces[0].shape[-1]
    share = pieces[0].shape[0] // (TS * TS)
    result = jnp.zeros((TS, TS, share * lax.axis_size("tile"), channels), pieces[0].dtype)
    for k in range(4):
        part = pieces[k].reshape(TS, TS, share, channels)
        result = lax.dynamic_update_slice_in_dim(result, part, (tile ^ k) * share, 2)
    return result


def flat_partner(x, mask):
    axes = ("dp", "tile")
    count = lax.axis_size("dp") * lax.axis_size("tile")
    return lax.ppermute(x, axes, [(i, i ^ mask) for i in range(count)])


GROUPS = ((0,), (1, 2))
SPLIT_BITS = 3
QUAD = 4
BLOCKS = 32


def block_index():
    flat = lax.axis_index("dp") * lax.axis_size("tile") + lax.axis_index("tile")
    index = jnp.zeros((), jnp.int32)
    for group in GROUPS:
        for bit in group:
            index = index * 2 + ((flat >> bit) & 1)
    return index * QUAD


def masks(group):
    if len(group) == 1:
        return [1 << group[0]]
    return [1 << group[1], 1 << group[0], (1 << group[0]) | (1 << group[1])]


def narrow_add(parts):
    parts = [p.astype(F32) for p in parts]
    total = parts[0] + parts[1]
    if len(parts) == 4:
        total = total + (parts[2] + parts[3])
    return total.astype(BF16)


def scatter_sends(x, group):
    wide = masks(group)
    size = x.shape[0] // (len(wide) + 1)
    return [flat_partner(x[(j + 1) * size : (j + 2) * size], mask) for j, mask in enumerate(wide)]


def far_masks():
    count = lax.axis_size("dp") * lax.axis_size("tile")
    return [1 << bit for bit in range(SPLIT_BITS, count.bit_length() - 1)]


def add_partner(x, mask):
    return narrow_add([x, flat_partner(x, mask)])


def tie(*values):
    return lax.optimization_barrier(values)


def dot(a, b):
    return lax.dot_general(a, b, (((1,), (0,)), ((), ())), preferred_element_type=F32)


def dot_nt(a, b):
    return lax.dot_general(a, b, (((1,), (1,)), ((), ())), preferred_element_type=F32)


def dot_tn(a, b):
    return lax.dot_general(a, b, (((0,), (0,)), ((), ())), preferred_element_type=F32)


def spread(ref, layer, repeat, turned=False):
    matrix = ref[...].astype(F32)[:, layer, :].astype(BF16)
    size = MAP * repeat
    shift = repeat.bit_length() - 1
    row = lax.broadcasted_iota(jnp.int32, (size, MAP), 0)
    col = lax.broadcasted_iota(jnp.int32, (size, MAP), 1)
    pick = jnp.where((row >> shift) == col, 1.0, 0.0).astype(BF16)
    half = dot_nt(pick, matrix) if turned else dot(pick, matrix)
    wide = dot_nt(half.astype(BF16), pick)
    row = lax.broadcasted_iota(jnp.int32, (size, size), 0)
    col = lax.broadcasted_iota(jnp.int32, (size, size), 1)
    return jnp.where((row & (repeat - 1)) == (col & (repeat - 1)), wide, 0.0).astype(BF16)


def spread_bias(ref, layer, repeat):
    size = MAP * repeat
    shift = repeat.bit_length() - 1
    row = lax.broadcasted_iota(jnp.int32, (size, MAP), 0)
    col = lax.broadcasted_iota(jnp.int32, (size, MAP), 1)
    return jnp.sum(jnp.where((row >> shift) == col, ref[layer : layer + 1], 0.0), axis=1, keepdims=True)


def collapse(product, repeat):
    size = MAP * repeat
    shift = repeat.bit_length() - 1
    row = lax.broadcasted_iota(jnp.int32, (size, size), 0)
    col = lax.broadcasted_iota(jnp.int32, (size, size), 1)
    kept = jnp.where((row & (repeat - 1)) == (col & (repeat - 1)), product, 0.0)
    kept = jnp.sum(kept.reshape(MAP, repeat, size), axis=1)
    row = lax.broadcasted_iota(jnp.int32, (size, MAP), 0)
    col = lax.broadcasted_iota(jnp.int32, (size, MAP), 1)
    pick = jnp.where((row >> shift) == col, 1.0, 0.0).astype(F32)
    return lax.dot_general(
        kept, pick, (((1,), (0,)), ((), ())), preferred_element_type=F32, precision=lax.Precision.HIGHEST
    )


def lane_groups(channels):
    return [(lo, min(lo + 128, channels)) for lo in range(0, channels, 128)]


def zero_border(pad):
    shape = pad.shape
    pad[0] = jnp.zeros(shape[1:], F32)
    pad[MAP + 1] = jnp.zeros(shape[1:], F32)
    for h in range(1, MAP + 1):
        pad[h, 0] = jnp.zeros(shape[2:], F32)
        pad[h, MAP + 1] = jnp.zeros(shape[2:], F32)


def pick_columns(field, w0):
    return jnp.where(w0 == 0, field[:, :TS], field[:, TS:])


def corner(tile, k):
    other = tile ^ k
    return (other >> 1) * TS, (other & 1) * TS


def conv_rows(pad, kernel_ref, layer, out_ref, stats_ref, sums, then=None):
    channels = pad.shape[-1]
    sums[...] = jnp.zeros(sums.shape, F32)

    def body(h, carry):
        for lo, hi in lane_groups(channels):
            acc = None
            for r in range(3):
                for s in range(3):
                    term = pad[h + r, s : s + MAP, :, lo:hi] * kernel_ref[r, s, layer : layer + 1, lo:hi]
                    acc = term if acc is None else acc + term
            out_ref[h, :, lo:hi] = acc.reshape(ROW, hi - lo)
            sums[0, :, lo:hi] += jnp.sum(acc, axis=0)
        if then is not None:
            then(h)
        return carry

    lax.fori_loop(0, MAP, body, 0)
    count = MAP * ROW
    mean = jnp.sum(sums[0], axis=0, keepdims=True) * (1.0 / count)

    def again(h, carry):
        for lo, hi in lane_groups(channels):
            dev = out_ref[h, :, lo:hi] - mean[:, lo:hi]
            sums[1, :, lo:hi] += jnp.sum((dev * dev).reshape(MAP, IMG, hi - lo), axis=0)
        return carry

    lax.fori_loop(0, MAP, again, 0)
    stats_ref[0:1] = mean
    stats_ref[1:2] = jnp.sum(sums[1], axis=0, keepdims=True)


def scale_of(stats_ref, cells):
    mean = stats_ref[0:1]
    return mean, lax.rsqrt(stats_ref[1:2] * (1.0 / cells) + norm_epsilon)


JOINED = 1024
MAIN = 256


def joined_places(channels):
    rest = channels - MAIN
    return [(i, 0, MAIN, i * MAIN) for i in range(3)] + [(i, MAIN, rest, 3 * MAIN + i * rest) for i in range(3)]


def put_joined(ref, rows, i, value):
    for part, first, size, lane in joined_places(value.shape[-1]):
        if part == i:
            ref[rows + (slice(lane, lane + size),)] = value[..., first : first + size]


def get_joined(value, i, channels):
    pieces = [value[..., lane : lane + size] for part, first, size, lane in joined_places(channels) if part == i]
    return jnp.concatenate(pieces, axis=-1)


def mix_forward(layer, cells, arrive, a_ref, stats_ref, gain_ref, shift_ref, mw_ref, mwb_ref, mh_ref, mhb_ref, joined):
    mean, rstd = scale_of(stats_ref, cells)
    channels = a_ref.shape[-1]
    gain = gain_ref[layer : layer + 1]
    shift = shift_ref[layer : layer + 1]
    width = spread(mw_ref, layer, IMG)
    height = spread(mh_ref, layer, 16)
    width_bias = spread_bias(mwb_ref, layer, IMG)
    height_bias = spread_bias(mhb_ref, layer, 16)
    used = 3 * channels
    joined[:, :, used:] = jnp.zeros(joined.shape[:2] + (joined.shape[2] - used,), BF16)
    whole = slice(None)
    for h in range(MAP):
        if h % PART == 0:
            arrive(h // PART)
        value = (((a_ref[h] - mean) * rstd) * gain + shift).astype(BF16)
        put_joined(joined, (h, whole), 0, value)
        put_joined(joined, (h, whole), 1, (dot(width, value) + width_bias).astype(BF16))
    for j in range(ROW // 16):
        cols = slice(16 * j, 16 * j + 16)
        value = get_joined(joined[:, cols, :], 0, channels).reshape(MAP * 16, channels)
        mixed = (dot(height, value) + height_bias).astype(BF16)
        put_joined(joined, (whole, cols), 2, mixed.reshape(MAP, 16, channels))


def gelu_pair(v):
    t = 1.0 / (1.0 + (0.3275911 * ROOT_HALF) * jnp.abs(v))
    e = jnp.exp2(v * v * (-0.5 * LOG2E))
    q = ((((0.5 * 1.061405429 * t - 0.5 * 1.453152027) * t + 0.5 * 1.421413741) * t - 0.5 * 0.284496736) * t + 0.5 * 0.254829592) * t * e
    phi = jnp.where(v >= 0, 1.0 - q, q)
    return v * phi, phi + v * e * INV_ROOT_TAU


HALVES = 2
PART = MAP // HALVES


def half_rows(ref, p):
    value = ref[p * PART : (p + 1) * PART]
    return value.reshape(PART * ROW, value.shape[-1])


def put_half(ref, p, value):
    ref[p * PART : (p + 1) * PART] = value.reshape(PART, ROW, value.shape[-1])


def add_half(ref, p, value):
    ref[p * PART : (p + 1) * PART] += value.reshape(PART, ROW, value.shape[-1])


def column_sums(value):
    return jnp.sum(value.reshape(-1, 8, value.shape[-1]), axis=0)


def unite_norm(r, layer, p, residual):
    one = slice(layer, layer + 1)
    m = residual + r.unite_bias[one] + dot(half_rows(r.joined.ref, p), r.unite[...])
    centre = jnp.mean(m, axis=-1, keepdims=True)
    dev = m - centre
    s = lax.rsqrt(jnp.mean(dev * dev, axis=-1, keepdims=True) + layer_epsilon)
    zhat = dev * s
    zb = (zhat * r.norm_gain[one] + r.norm_shift[one]).astype(BF16)
    return m, zhat, s, zb


def hidden_block(r, layer, j):
    blk = slice(j * BLK, (j + 1) * BLK) if isinstance(j, int) else pl.ds(pl.multiple_of(j * BLK, BLK), BLK)
    return blk, r.up.ref[:, blk], r.down.ref[:, blk]


def block_half(value):
    return value.reshape(PART, ROW, BLK)


def norm_backward(r, layer, p, do32, zhat, s, dz, df_ref):
    one = slice(layer, layer + 1)
    channels = do32.shape[-1]
    e = dz * r.norm_gain[one]
    mean_e = jnp.mean(e, axis=-1, keepdims=True)
    mean_ez = jnp.mean(e * zhat, axis=-1, keepdims=True)
    dm = do32 + s * (e - mean_e - zhat * mean_ez)
    put_half(r.dm.ref, p, dm)
    df = dm.astype(BF16)
    put_half(df_ref, p, df)
    r.small[2] += column_sums(dz * zhat)
    r.small[3] += column_sums(dz)
    r.small[4] += column_sums(do32)
    r.small[5] += column_sums(dm)
    dj = dot_nt(df, r.unite[...])
    put_half(r.dn.ref, p, get_joined(dj, 0, channels))
    put_half(r.dpw, p, get_joined(dj, 1, channels).astype(BF16))
    put_half(r.dph, p, get_joined(dj, 2, channels).astype(BF16))


GROUP_LANES = 128
PER_QUARTER = 7


def put_group(r, q, value):
    size = r.buf.shape[2]
    count = value.shape[0] // size
    quarter = q // PER_QUARTER if isinstance(q, int) else lax.div(q, PER_QUARTER)
    lane = q - quarter * PER_QUARTER
    for b in range(count):
        r.buf[(quarter * count + b) ^ r.index[0], lane] = value[b * size : (b + 1) * size].astype(BF16)


def put_columns(r, q, value):
    for i in range(value.shape[-1] // GROUP_LANES):
        put_group(r, q + i, value[:, i * GROUP_LANES : (i + 1) * GROUP_LANES])


def flat_rows(value):
    return value.reshape(MAP * ROW, value.shape[-1])


def hidden_gradients(r, j, blocks, zb, do, g, dh):
    per = BLK // GROUP_LANES
    put_columns(r, per * j, dot_tn(flat_rows(zb[...]), dh))
    put_columns(r, per * (j + blocks), dot_tn(flat_rows(do[...]), g))


def mix_backward(layer, cells, a_ref, stats_ref, mw_ref, mh_ref, dpw, dph, dn_ref, small, send):
    mean, rstd = scale_of(stats_ref, cells)
    width = spread(mw_ref, layer, IMG, turned=True)
    height = spread(mh_ref, layer, 16, turned=True)
    for j in range(ROW // 16):
        cols = slice(16 * j, 16 * j + 16)
        value = dph[:, cols, :].reshape(MAP * 16, -1)
        dn_ref[:, cols, :] += dot(height, value).reshape(MAP, 16, -1)

    totals = [small[0], small[1]]
    for h in range(MAP):
        dn = dn_ref[h] + dot(width, dpw[h])
        dn_ref[h] = dn
        send(h)
        xhat = (a_ref[h] - mean) * rstd
        totals[0] = totals[0] + jnp.sum(dn.reshape(MAP, IMG, -1), axis=0)
        totals[1] = totals[1] + jnp.sum((dn * xhat).reshape(MAP, IMG, -1), axis=0)
    small[0], small[1] = totals


def unite_gradients(r, blocks, df_ref, out_ref):
    df = flat_rows(df_ref[...])
    channels = df.shape[-1]
    joined, dpw, dph = r.joined.ref, r.dpw, r.dph
    put_columns(r, 2 * blocks * (BLK // GROUP_LANES), dot_tn(df, flat_rows(joined[...])))

    wide = jnp.zeros((ROW, ROW), F32)
    bias = jnp.zeros((ROW, channels), F32)
    for h in range(MAP):
        wide = wide + dot_nt(dpw[h], get_joined(joined[h], 0, channels))
        bias = bias + dpw[h].astype(F32)
    tall = jnp.zeros((MAP * 16, MAP * 16), F32)
    tall_bias = jnp.zeros((MAP, 16, channels), F32)
    for j in range(ROW // 16):
        cols = slice(16 * j, 16 * j + 16)
        value = dph[:, cols, :]
        tall = tall + dot_nt(value.reshape(MAP * 16, channels), get_joined(joined[:, cols, :], 0, channels).reshape(MAP * 16, channels))
        tall_bias = tall_bias + value.astype(F32)
    diagonal = lax.broadcasted_iota(jnp.int32, (MAP, MAP), 0) == lax.broadcasted_iota(jnp.int32, (MAP, MAP), 1)

    def as_row(field):
        col = jnp.sum(jnp.sum(field, axis=1), axis=-1, keepdims=True)
        return jnp.sum(jnp.where(diagonal, col, 0.0), axis=0, keepdims=True)

    width = jnp.concatenate([collapse(wide, IMG), as_row(bias.reshape(MAP, IMG, channels))], axis=0)
    height = jnp.concatenate([collapse(tall, 16), as_row(tall_bias)], axis=0)
    for v in range(MAP + 1):
        row, lane = mix_place(v)
        out_ref[row : row + 1, lane : lane + MAP] = width[v : v + 1]
        out_ref[row : row + 1, lane + 16 : lane + 16 + MAP] = height[v : v + 1]


MIX_ROW = 10
TAPS_ROW = 12
KERNEL_ROW = 21
SMALL_ROWS = 32


def mix_place(v):
    return MIX_ROW + v // 10, 32 * (v % 10)


def put_small(out_ref, small, upsum):
    channels = out_ref.shape[-1]
    for i in range(6):
        out_ref[i : i + 1] = jnp.sum(small[i], axis=0, keepdims=True)
    up = jnp.sum(upsum[...], axis=0, keepdims=True)
    for i in range(up.shape[-1] // channels):
        out_ref[6 + i : 7 + i] = up[:, i * channels : (i + 1) * channels]


def tap_sums(value, pad, h, lo, hi, total):
    for r in range(3):
        for s in range(3):
            total[3 * r + s, :, lo:hi] += jnp.sum(value * pad[h + r, s : s + MAP, :, lo:hi], axis=0)


def put_taps(out_ref, row, total):
    for i in range(9):
        out_ref[row + i : row + i + 1] = jnp.sum(total[i], axis=0, keepdims=True)


def conv_backward(layer, cells, a, stats_ref, totals_ref, gain, kernel_ref, dn, dm, emit, padd, x=None, padx=None, ksum=None, send=None):
    mean, rstd = scale_of(stats_ref, cells)
    scale = rstd * gain[layer : layer + 1]
    shift_mean = totals_ref[0:1] * (1.0 / cells)
    gain_mean = totals_ref[1:2] * (1.0 / cells)
    channels = padd.shape[-1]
    arriving = [part for part in (a, dn, dm, x) if part is not None]
    for c in range(MAP // 2):
        for part in arriving:
            part.start_part(c)
    zero_border(padd)
    if x is not None:
        zero_border(padx)
        ksum[...] = jnp.zeros(ksum.shape, F32)

    def fill(c):
        for part in arriving:
            part.wait(c)
        for i in range(2):
            h = 2 * c + i
            xhat = (a.ref[h] - mean) * rstd
            da = scale * (dn.ref[h] - shift_mean - xhat * gain_mean)
            padd[h + 1, 1 : MAP + 1] = da.reshape(MAP, IMG, -1)
            if x is not None:
                padx[h + 1, 1 : MAP + 1] = x.ref[h].astype(BF16).astype(F32).reshape(MAP, IMG, -1)

    def rows(c):
        for i in range(2):
            h = 2 * c + i
            for lo, hi in lane_groups(channels):
                acc = dm.ref[h, :, lo:hi].reshape(MAP, IMG, hi - lo)
                da = padd[h + 1, 1 : MAP + 1, :, lo:hi]
                for r in range(3):
                    for s in range(3):
                        acc = acc + padd[h + 2 - r, 2 - s : 2 - s + MAP, :, lo:hi] * kernel_ref[r, s, layer : layer + 1, lo:hi]
                if x is not None:
                    tap_sums(da, padx, h, lo, hi, ksum)
                emit(h, lo, hi, acc)
        if send is not None:
            send(c)

    fill(0)

    def body(c, carry):
        fill(c + 1)
        rows(c)
        return carry

    lax.fori_loop(0, MAP // 2 - 1, body, 0)
    rows(MAP // 2 - 1)


def fill_pad(pad, x_ref):
    def body(h, carry):
        pad[h + 1, 1 : MAP + 1] = x_ref[h].astype(F32).reshape(MAP, IMG, -1)
        return carry

    lax.fori_loop(0, MAP, body, 0)


def kernel_taps(r):
    r.x.wait_all()
    zero_border(r.pad)
    fill_pad(r.pad, r.x.ref)
    r.a.wait_all()
    mean = r.stats[0:1]
    r.times[...] = jnp.zeros(r.times.shape, F32)
    r.alone[0] = jnp.zeros(r.alone.shape[1:], F32)

    def body(h, carry):
        for lo, hi in lane_groups(r.pad.shape[-1]):
            value = (r.a.ref[h, :, lo:hi] - mean[:, lo:hi]).reshape(MAP, IMG, hi - lo)
            tap_sums(value, r.pad, h, lo, hi, r.times)
            r.alone[0, :, lo:hi] += jnp.sum(r.pad[h + 1, 1 : MAP + 1, :, lo:hi], axis=0)
        return carry

    lax.fori_loop(0, MAP, body, 0)
    whole = r.alone[0]
    ends = {0: MAP, 2: 1}
    out_rows = {i: jnp.sum(r.pad[at, 1 : MAP + 1], axis=0) for i, at in ends.items()}
    out_cols = {i: jnp.sum(r.pad[1 : MAP + 1, at], axis=0) for i, at in ends.items()}
    for i in range(3):
        for k in range(3):
            value = whole
            if i != 1:
                value = value - out_rows[i]
            if k != 1:
                value = value - out_cols[k]
            if i != 1 and k != 1:
                value = value + r.pad[ends[i], ends[k]]
            r.alone[3 * i + k] = value
    r.out[...] = jnp.zeros(r.out.shape, F32)
    put_taps(r.out, 0, r.alone)
    put_taps(r.out, 9, r.times)
    r.out[18:19] = mean


def kernel_first(r):
    tile = r.tile[0]
    zero_border(r.pad)
    for k, piece in enumerate((r.p0, r.p1, r.p2, r.p3)):
        h0, w0 = corner(tile, k)
        value = piece[...].astype(F32).reshape(TS, TS, IMG, -1)
        r.pad[pl.ds(1 + h0, TS), pl.ds(1 + w0, TS)] = value

    def body(h, carry):
        r.x[h] = r.pad[h + 1, 1 : MAP + 1].reshape(ROW, -1).astype(BF16)
        return carry

    lax.fori_loop(0, MAP, body, 0)
    conv_rows(r.pad, r.kernels, 0, r.a, r.stats, r.sums)


def turn_unite(r):
    r.unite_t.wait_all()
    channels = r.unite.shape[-1]
    for part, first, size, lane in joined_places(channels):
        r.unite[lane : lane + size] = r.unite_t.ref[:, part * channels + first : part * channels + first + size].T
    r.unite[3 * channels :] = jnp.zeros((JOINED - 3 * channels, channels), BF16)


def forward_front(r, layer, cells, later):
    def arrive(p):
        r.a.wait(p)
        if p == HALVES - 1:
            for part in later:
                part.start()

    mix_forward(layer, cells, arrive, r.a.ref, r.stats, r.batch_gain, r.batch_shift, r.mix_width, r.mix_width_bias, r.mix_height, r.mix_height_bias, r.joined.ref)


def kernel_forward(cells, r):
    forward_front(r, 0, cells, (r.unite_t, r.x, r.up, r.down))
    r.joined.send_all()
    turn_unite(r)
    zero_border(r.pad)
    r.x.wait_all()
    for p in range(HALVES):
        m, zhat, s, zb = unite_norm(r, 0, p, half_rows(r.x.ref, p).astype(F32))
        put_half(r.u.ref, p, m + r.down_bias[0:1])
        put_half(r.zhat.ref, p, zhat)
        put_half(r.s.ref, p, s)
        put_half(r.zb.ref, p, zb)
        for stream in (r.zhat, r.s, r.zb):
            stream.send(p)
    r.up.wait_all()
    r.down.wait_all()

    def body(j):
        blk, up, down = hidden_block(r, 0, j)
        for p in range(HALVES):
            g, d = gelu_pair(dot(half_rows(r.zb.ref, p), up) + r.up_bias[0:1, blk])
            g = g.astype(BF16)
            r.g.ref[j, p * PART : (p + 1) * PART] = block_half(g)
            r.d.ref[j, p * PART : (p + 1) * PART] = block_half(d.astype(BF16))
            add_half(r.u.ref, p, dot_nt(g, down))
        r.g.send(j)
        r.d.send(j)

    lax.fori_loop(0, r.up_bias.shape[-1] // BLK, lambda j, c: (body(j), c)[1], 0)
    r.u.send_all()

    def fill(h, carry):
        rounded = r.u.ref[h].astype(BF16).astype(F32)
        r.pad[h + 1, 1 : MAP + 1] = rounded.reshape(MAP, IMG, -1)
        return carry

    lax.fori_loop(0, MAP, fill, 0)
    conv_rows(r.pad, r.kernels, 1, r.a2.ref, r.stats2, r.sums, r.a2.send)


def clear(r):
    r.small[...] = jnp.zeros(r.small.shape, F32)
    r.upsum[...] = jnp.zeros(r.upsum.shape, F32)


def send_blocks(r):
    half = BLOCKS // 2
    r.mine.start(r.buf.at[pl.ds(0, half)])
    r.sent.start(r.buf.at[pl.ds(half, half)])


def kernel_whole_map(r):
    tile = r.tile[0]
    for k, piece in enumerate((r.p0, r.p1, r.p2, r.p3)):
        h0, w0 = corner(tile, k)
        r.field[pl.ds(h0, TS), pl.ds(w0, TS)] = piece[...].astype(F32).reshape(TS, TS, IMG, -1)
    for h in range(MAP):
        r.out.ref[h] = r.field[h].reshape(ROW, -1).astype(BF16)
    r.out.send_all()


def kernel_pieces(r):
    tile = r.tile[0]
    for k, piece in enumerate((r.p0, r.p1, r.p2, r.p3)):
        h0, w0 = corner(tile, k)
        field = r.field[pl.ds(h0, TS)].astype(F32).reshape(TS, MAP, IMG, -1)
        piece[...] = pick_columns(field, w0).reshape(PIECE, -1).astype(BF16)


def kernel_turn(cells, r):
    clear(r)
    r.do = r.do_in.ref
    r.joined = Held(r.joined)
    forward_front(r, 1, cells, (r.unite_t, r.u, r.up, r.down, r.do_in))
    turn_unite(r)
    r.u.wait_all()

    def cotangent(p):
        return half_rows(r.do, p).astype(F32)

    for p in range(HALVES):
        m, zhat, s, zb = unite_norm(r, 1, p, half_rows(r.u.ref, p))
        put_half(r.out, p, m + r.down_bias[1:2])
        put_half(r.zhat, p, zhat)
        put_half(r.s, p, s)
        put_half(r.zb, p, zb)
    for part in (r.up, r.down, r.do_in):
        part.wait_all()
    r.dz[...] = jnp.zeros(r.dz.shape, F32)
    blocks = r.up_bias.shape[-1] // BLK

    def body(j):
        blk, up, down = hidden_block(r, 1, j)
        gs, dhs = [], []
        for p in range(HALVES):
            g, d = gelu_pair(dot(half_rows(r.zb, p), up) + r.up_bias[1:2, blk])
            g = g.astype(BF16)
            add_half(r.out, p, dot_nt(g, down))
            dh = dot(half_rows(r.do, p), down) * d
            r.upsum[:, blk] += column_sums(dh)
            dh = dh.astype(BF16)
            add_half(r.dz, p, dot_nt(dh, up))
            gs.append(g)
            dhs.append(dh)
        return jnp.concatenate(gs, 0), jnp.concatenate(dhs, 0)

    done = []
    for j in range(blocks):
        done.append(body(j))
        if j > 0:
            hidden_gradients(r, j - 1, blocks, r.zb, r.do, *done[j - 1])
    hidden_gradients(r, blocks - 1, blocks, r.zb, r.do, *done[blocks - 1])
    r.features.ref[...] = r.out[...].astype(BF16)
    r.features.send_all()
    for p in range(HALVES):
        norm_backward(r, 1, p, cotangent(p), half_rows(r.zhat, p), half_rows(r.s, p), half_rows(r.dz, p), r.df)
        r.dm.send(p)
    r.small_out[...] = jnp.zeros(r.small_out.shape, F32)
    unite_gradients(r, blocks, r.df, r.small_out)
    send_blocks(r)
    mix_backward(1, cells, r.a.ref, r.stats, r.mix_width, r.mix_height, r.dpw, r.dph, r.dn.ref, r.small, r.dn.send)
    put_small(r.small_out, r.small, r.upsum)
    r.small_out[TAPS_ROW : TAPS_ROW + 18] = r.taps[...]


def kernel_conv_middle(cells, r):
    def emit(h, lo, hi, value):
        r.du.ref[h, :, lo:hi] = value.reshape(ROW, hi - lo)
        r.do.ref[h, :, lo:hi] = value.reshape(ROW, hi - lo).astype(BF16)

    def send(c):
        r.do.send(c)
        r.du.send(c)

    conv_backward(1, cells, r.a, r.stats, r.totals, r.batch_gain, r.kernels, r.dn, r.dm, emit, r.padd, r.x, r.padx, r.ksum, send)
    put_taps(r.kgrad, 0, r.ksum)


def kernel_back(cells, r):
    for part in (r.do_in, r.down, r.up):
        part.start()
    r.d.start_part(0)
    clear(r)
    r.do = r.do_in.ref
    for part in (r.do_in, r.up, r.down):
        part.wait_all()
    r.d.start_part(1)
    r.zb.start()
    r.g.start_part(0)
    r.dz[...] = jnp.zeros(r.dz.shape, F32)
    blocks = r.upsum.shape[-1] // BLK
    later = {blocks - 2: (r.zhat, r.s, r.unite_t, r.du), blocks - 1: (r.joined, r.a, r.x)}

    def body(j):
        blk, up, down = hidden_block(r, 0, j)
        r.d.wait(j)
        if j > 0:
            if j + 1 < blocks:
                r.d.start_part(j + 1)
            r.g.start_part(j)
        for part in later.get(j, ()):
            part.start()
        dhs = []
        for p in range(HALVES):
            d = r.d.ref[j, p * PART : (p + 1) * PART].reshape(PART * ROW, BLK).astype(F32)
            dh = dot(half_rows(r.do, p), down) * d
            r.upsum[:, blk] += column_sums(dh)
            dh = dh.astype(BF16)
            add_half(r.dz, p, dot_nt(dh, up))
            dhs.append(dh)
        return jnp.concatenate(dhs, 0)

    def gradients(j, dh):
        if j == 0:
            r.zb.wait_all()
        r.g.wait(j)
        hidden_gradients(r, j, blocks, r.zb.ref, r.do, flat_rows(r.g.ref[j]), dh)

    done = []
    for j in range(blocks):
        done.append(body(j))
        if j > 0:
            gradients(j - 1, done[j - 1])
    gradients(blocks - 1, done[blocks - 1])
    turn_unite(r)
    r.du.wait_all()
    r.zhat.wait_all()
    r.s.wait_all()
    for p in range(HALVES):
        norm_backward(r, 0, p, half_rows(r.du.ref, p), half_rows(r.zhat.ref, p), half_rows(r.s.ref, p), half_rows(r.dz, p), r.df)
        r.dm.send(p)
    r.joined.wait_all()
    r.small_out[...] = jnp.zeros(r.small_out.shape, F32)
    unite_gradients(r, blocks, r.df, r.small_out)
    send_blocks(r)
    for part in (r.a, r.x):
        part.wait_all()
    zero_border(r.pad)
    fill_pad(r.pad, r.x.ref)
    r.taps[...] = jnp.zeros(r.taps.shape, F32)

    mix_backward(0, cells, r.a.ref, r.stats, r.mix_width, r.mix_height, r.dpw, r.dph, r.dn.ref, r.small, r.dn.send)

    def windows(h, carry):
        for lo, hi in lane_groups(r.pad.shape[-1]):
            tap_sums(r.dn.ref[h, :, lo:hi].reshape(MAP, IMG, hi - lo), r.pad, h, lo, hi, r.taps)
        return carry

    lax.fori_loop(0, MAP, windows, 0)
    put_small(r.small_out, r.small, r.upsum)
    put_taps(r.small_out, TAPS_ROW, r.taps)
    r.small_out[KERNEL_ROW : KERNEL_ROW + 9] = r.kgrad[0:9]


def kernel_last(cells, r):
    tile = r.tile[0]

    def emit(h, lo, hi, value):
        r.du[h, :, :, lo:hi] = value

    conv_backward(0, cells, r.a, r.stats, r.totals, r.batch_gain, r.kernels, r.dn, r.dm, emit, r.padd)
    for k, piece in enumerate((r.o0, r.o1, r.o2, r.o3)):
        h0, w0 = corner(tile, k)
        piece[...] = r.du[pl.ds(h0, TS), pl.ds(w0, TS)].reshape(PIECE, -1).astype(BF16)


def unpack_put(r, value, quarter, row):
    channels, hidden = r.up.ref.shape
    rows = pl.ds(row, value.shape[1])
    for i in range(value.shape[0]):
        base = (quarter * value.shape[0] + i) * GROUP_LANES
        if base < hidden:
            r.up.ref[rows, base : base + GROUP_LANES] = value[i]
        elif base < 2 * hidden:
            r.down.ref[rows, base - hidden : base - hidden + GROUP_LANES] = value[i]
        else:
            base -= 2 * hidden
            for part, first, size, lane in joined_places(channels):
                lo, hi = max(lane, base), min(lane + size, base + GROUP_LANES)
                if lo < hi:
                    target = part * channels + first + lo - lane
                    r.unite.ref[rows, target : target + hi - lo] = value[i, :, lo - base : hi - base]


def unpack_all(r, block):
    channels, hidden = r.up.ref.shape
    size = 4 * channels // BLOCKS
    per = channels // size
    lanes = PER_QUARTER * GROUP_LANES
    for quarter in range(4):
        for b in range(per):
            unpack_put(r, block(quarter * per + b), quarter, b * size)
        if (quarter + 1) * lanes >= hidden and quarter * lanes < hidden:
            r.up.send_all()
        if (quarter + 1) * lanes >= 2 * hidden and quarter * lanes < 2 * hidden:
            r.down.send_all()
    r.unite.send_all()


def kernel_unpack(r):
    index = r.index[0]
    half = BLOCKS // 2
    flip = index & (half - 1)
    own = index // half
    r.near.wait_all()
    r.far.wait_all()

    def block(p):
        place = (p & (half - 1)) ^ flip
        near, far = r.near.ref[place].astype(F32), r.far.ref[place].astype(F32)
        return jnp.where(own == p // half, near, far)

    unpack_all(r, block)


def kernel_finish(cells, r):
    channels = r.total0.shape[-1]
    for layer, total in enumerate((r.total0, r.total1)):
        one = slice(layer, layer + 1)
        r.batch_shift[one] = total[0:1]
        r.batch_gain[one] = total[1:2]
        r.norm_gain[one] = total[2:3]
        r.norm_shift[one] = total[3:4]
        r.down_bias[one] = total[4:5]
        r.unite_bias[one] = total[5:6]
        for i in range(r.up_bias.shape[-1] // channels):
            r.up_bias[one, i * channels : (i + 1) * channels] = total[6 + i : 7 + i]
        for v in range(MAP + 1):
            row, lane = mix_place(v)
            width, height = total[row : row + 1, lane : lane + MAP], total[row : row + 1, lane + 16 : lane + 16 + MAP]
            if v < MAP:
                r.mix_width[v, one], r.mix_height[v, one] = width, height
            else:
                r.mix_width_bias[one], r.mix_height_bias[one] = width, height
    mean, rstd = scale_of(r.stats, cells)
    shift_mean, gain_mean = r.total0[0:1] * (1.0 / cells), r.total0[1:2] * (1.0 / cells)
    for i in range(9):
        alone, times = r.total1[TAPS_ROW + i : TAPS_ROW + i + 1], r.total1[KERNEL_ROW + i : KERNEL_ROW + i + 1]
        value = r.total0[TAPS_ROW + i : TAPS_ROW + i + 1] - shift_mean * alone - gain_mean * rstd * times
        r.kernel[i // 3, i % 3, 0:1] = rstd * r.gain[0:1] * value
        r.kernel[i // 3, i % 3, 1:2] = r.total0[KERNEL_ROW + i : KERNEL_ROW + i + 1]


class Kept:
    def __init__(self, array):
        self.array = array


class Smem:
    def __init__(self, array):
        self.array = array


class Layer:
    def __init__(self, array, layer):
        self.array, self.layer = array, layer


def chunk_step(shape, step=None):
    if len(shape) == 4 and shape[1:3] == (MAP, ROW):
        return 1
    if len(shape) == 3 and shape[:2] == (MAP, ROW):
        return step or PART
    return shape[0]


class Late:
    def __init__(self, array, layer=None, step=None, hold=False):
        self.array, self.layer, self.hold = array, layer, hold
        self.step = chunk_step(self.shape, step)

    @property
    def shape(self):
        return self.array.shape if self.layer is None else self.array.shape[1:]

    @property
    def parts(self):
        return self.shape[0] // self.step


class LateJoin:
    def __init__(self, arrays):
        self.arrays = arrays
        self.dtype = arrays[0].dtype
        self.shape = (sum(a.shape[0] for a in arrays),) + arrays[0].shape[1:]


class LateJoinRef:
    def __init__(self, sources, ref, sems):
        self.ref, self.copies, row = ref, [], 0
        for i, source in enumerate(sources):
            size = source.shape[0]
            self.copies.append(pltpu.make_async_copy(source, ref.at[pl.ds(row, size)], sems.at[i]))
            row += size

    def start(self):
        for copy in self.copies:
            copy.start()

    def wait_all(self):
        for copy in self.copies:
            copy.wait()


class LateRef:
    def __init__(self, late, source, ref, sems):
        self.parts, self.step = late.parts, late.step
        self.source = source if late.layer is None else source.at[late.layer]
        self.ref, self.sems = ref, sems

    def copy(self, c):
        if self.parts == 1:
            return pltpu.make_async_copy(self.source, self.ref, self.sems.at[0])
        rows = pl.ds(self.step * c, self.step)
        return pltpu.make_async_copy(self.source.at[rows], self.ref.at[rows], self.sems.at[c])

    def start(self):
        for c in range(self.parts):
            self.copy(c).start()

    def start_part(self, c):
        self.copy(c).start()

    def wait(self, c):
        self.copy(c).wait()

    def wait_all(self):
        for c in range(self.parts):
            self.copy(c).wait()


class Stream:
    def __init__(self, out, layer=None, step=None):
        self.out, self.layer = out, layer
        self.step = chunk_step(self.shape, step)

    @property
    def shape(self):
        return self.out.shape if self.layer is None else self.out.shape[1:]


class Place:
    def __init__(self, out):
        self.out = out


class StreamRef:
    def __init__(self, stream, target, ref, sem):
        self.target, self.ref, self.sem = target if stream.layer is None else target.at[stream.layer], ref, sem
        self.step = stream.step

    def send(self, c):
        rows = pl.ds(self.step * c, self.step)
        pltpu.make_async_copy(self.ref.at[rows], self.target.at[rows], self.sem).start()

    def send_all(self):
        pltpu.make_async_copy(self.ref, self.target, self.sem).start()

    def finish(self):
        pltpu.make_async_copy(self.ref, self.target, self.sem).wait()


class PlaceRef:
    def __init__(self, target, sem):
        self.target, self.sem = target, sem

    def start(self, source):
        self.copy = pltpu.make_async_copy(source, self.target, self.sem)
        self.copy.start()

    def finish(self):
        self.copy.wait()


class Held:
    def __init__(self, ref):
        self.ref = ref


class Refs:
    pass


def full(array):
    rank = len(array.shape)
    return pl.BlockSpec(array.shape, lambda i: (0,) * rank)


ANY = pl.BlockSpec(memory_space=pl.ANY)
FINISHED = (
    "batch_shift", "batch_gain", "norm_gain", "norm_shift", "down_bias", "unite_bias", "up_bias",
    "kernel", "mix_width", "mix_height", "mix_width_bias", "mix_height_bias",
)


def _padded(array):
    shape = list(array.shape)
    if len(shape) > 1:
        shape[-2] = -(-shape[-2] // 16) * 16
    shape[-1] = -(-shape[-1] // 128) * 128
    return math.prod(shape) * jnp.dtype(array.dtype).itemsize


def run(body, name, flops, ins, outs, scratch=None, aliases=None, tight=False):
    scratch = dict(scratch or {})
    arrays, in_specs, out_specs, out_shapes, spaces = [], [], [], [], []
    for key, operand in ins.items():
        if isinstance(operand, Smem):
            in_specs.append(pl.BlockSpec(memory_space=pltpu.SMEM))
        elif isinstance(operand, Layer):
            shape, layer = operand.array.shape, operand.layer
            in_specs.append(pl.BlockSpec((None,) + shape[1:], lambda i, layer=layer, rank=len(shape): (layer,) + (0,) * (rank - 1)))
        elif isinstance(operand, Kept):
            in_specs.append(ANY)
        elif isinstance(operand, LateJoin):
            in_specs += [ANY] * len(operand.arrays)
            arrays += operand.arrays
            spaces += [pltpu.VMEM(operand.shape, operand.dtype), pltpu.SemaphoreType.DMA((len(operand.arrays),))]
            continue
        elif isinstance(operand, Late):
            in_specs.append(ANY)
            spaces += [pltpu.VMEM(operand.shape, operand.array.dtype), pltpu.SemaphoreType.DMA((operand.parts,))]
        else:
            in_specs.append(full(operand))
        arrays.append(getattr(operand, "array", operand))
    for key, out in outs.items():
        if isinstance(out, (Stream, Place)):
            out_specs.append(ANY)
            out_shapes.append(out.out)
            if isinstance(out, Stream):
                spaces.append(pltpu.VMEM(out.shape, out.out.dtype))
            spaces.append(pltpu.SemaphoreType.DMA)
        elif isinstance(out, Layer):
            shape, layer = out.array.shape, out.layer
            out_specs.append(pl.BlockSpec((None,) + shape[1:], lambda i, layer=layer, rank=len(shape): (layer,) + (0,) * (rank - 1)))
            out_shapes.append(out.array)
        else:
            out_specs.append(full(out))
            out_shapes.append(out)
    spaces += list(scratch.values())

    def wrapped(*refs):
        refs = list(refs)
        r = Refs()
        main, extra = refs[: len(arrays) + len(outs)], refs[len(arrays) + len(outs) :]
        late, streams = [], []
        for key, operand in ins.items():
            if isinstance(operand, LateJoin):
                sources = [main.pop(0) for _ in operand.arrays]
                ref = LateJoinRef(sources, extra.pop(0), extra.pop(0))
                late.append(ref)
                setattr(r, key, ref)
                continue
            ref = main.pop(0)
            if isinstance(operand, Late):
                ref = LateRef(operand, ref, extra.pop(0), extra.pop(0))
                if not operand.hold:
                    late.append(ref)
            setattr(r, key, ref)
        for key, out in outs.items():
            ref = main.pop(0)
            if isinstance(out, Stream):
                ref = StreamRef(out, ref, extra.pop(0), extra.pop(0))
                streams.append(ref)
            elif isinstance(out, Place):
                ref = PlaceRef(ref, extra.pop(0))
                streams.append(ref)
            setattr(r, key, ref)
        for key in scratch:
            setattr(r, key, extra.pop(0))
        for part in late:
            part.start()
        body(r)
        for stream in streams:
            stream.finish()

    held = [a for a, spec in zip(arrays + out_shapes, in_specs + out_specs) if spec is not ANY]
    held += [space for space in spaces if getattr(space, "memory_space", None) == pltpu.VMEM]
    need = sum(_padded(a) for a in held)
    limit = min(VMEM_BYTES, need + need // 4 + MARGIN) if tight else VMEM_BYTES
    size = sum(a.size * a.dtype.itemsize for a in arrays) + sum(o.size * o.dtype.itemsize for o in out_shapes)
    results = pl.pallas_call(
        wrapped,
        grid=(1,),
        in_specs=in_specs,
        out_specs=out_specs,
        out_shape=out_shapes,
        scratch_shapes=spaces,
        input_output_aliases=aliases or {},
        compiler_params=pltpu.CompilerParams(vmem_limit_bytes=limit),
        cost_estimate=pl.CostEstimate(flops=flops, bytes_accessed=size, transcendentals=0),
        name=name,
    )(*arrays)
    named = Refs()
    for key, value in zip(outs, results):
        setattr(named, key, value)
    return named


def on_device(
    patches,
    conv_kernel,
    batch_gain,
    batch_shift,
    mix_width,
    mix_width_bias,
    mix_height,
    mix_height_bias,
    unite_weight,
    unite_bias,
    norm_gain,
    norm_shift,
    up_weight,
    up_bias,
    down_weight,
    down_bias,
    cotangent,
):
    channels = patches.shape[-1]
    hidden = up_weight.shape[-1]
    tile = lax.axis_index("tile")
    tile_arg = Smem(tile.astype(jnp.int32).reshape(1))
    index_arg = Smem(block_index().reshape(1))
    local_cells = MAP * ROW
    cells = local_cells * lax.axis_size("dp") * lax.axis_size("tile")

    def rows(lanes, dtype):
        return jax.ShapeDtypeStruct((MAP, ROW, lanes), dtype)

    def shape(*dims, dtype=F32):
        return jax.ShapeDtypeStruct(dims, dtype)

    def vmem(struct):
        return pltpu.VMEM(struct.shape, struct.dtype)

    piece = shape(PIECE, channels, dtype=BF16)
    c_bf, c_f32, h_bf = rows(channels, BF16), rows(channels, F32), shape(hidden // BLK, MAP, ROW, BLK, dtype=BF16)
    map4 = pltpu.VMEM((MAP, MAP, IMG, channels), F32)
    pad = pltpu.VMEM((MAP + 2, MAP + 2, IMG, channels), F32)
    sums = pltpu.VMEM((2, 8, channels), F32)
    small = pltpu.VMEM((6, 8, channels), F32)
    upsum = pltpu.VMEM((8, hidden), F32)
    ksum = pltpu.VMEM((9, 8, channels), F32)
    unite_space = pltpu.VMEM((JOINED, channels), BF16)
    blocks = hidden // BLK
    groups = 2 * blocks * (BLK // GROUP_LANES) + JOINED // GROUP_LANES
    assert groups == 4 * PER_QUARTER
    block = (PER_QUARTER, 4 * channels // BLOCKS, GROUP_LANES)
    half = shape(BLOCKS // 2, *block, dtype=BF16)
    buf = pltpu.VMEM((BLOCKS, *block), BF16)

    kernels = conv_kernel.transpose(1, 2, 0, 3)
    down_t = down_weight.transpose(0, 2, 1)
    unite_t = unite_weight.transpose(0, 2, 1)
    mix_width = mix_width.transpose(1, 0, 2)
    mix_height = mix_height.transpose(1, 0, 2)

    x_pieces = to_whole(patches[:, 0].transpose(1, 2, 0, 3), tile)
    first = run(
        kernel_first,
        "conv_first",
        10**7,
        dict(tile=tile_arg, **{f"p{k}": x_pieces[k] for k in range(4)}, kernels=kernels),
        dict(x=c_bf, a=c_f32, stats=shape(2, channels)),
        dict(pad=pad, sums=sums),
        tight=True,
    )
    taps = run(
        kernel_taps,
        "taps",
        10**8,
        dict(x=Late(first.x), a=Late(first.a), stats=first.stats),
        dict(out=shape(24, channels)),
        dict(pad=pad, alone=ksum, times=ksum),
        tight=True,
    ).out
    stats0, (cotangent, taps) = total_moments(first.stats, float(local_cells), [cotangent, taps])
    taps = jnp.concatenate([taps[0:9], taps[9:18] + (taps[18:19] - stats0[0:1]) * taps[0:9]], 0)
    cot_pieces = to_whole(cotangent[:, 0].transpose(1, 2, 0, 3), tile)

    def forward_ins(layer):
        return dict(
            batch_gain=batch_gain, batch_shift=batch_shift,
            mix_width=mix_width, mix_width_bias=mix_width_bias, mix_height=mix_height, mix_height_bias=mix_height_bias,
            unite_t=Late(unite_t, layer, hold=True), up=Late(up_weight, layer, hold=True), down=Late(down_t, layer, hold=True),
            unite_bias=unite_bias, norm_gain=norm_gain, norm_shift=norm_shift, up_bias=up_bias, down_bias=down_bias,
        )

    fwd = run(
        lambda r: kernel_forward(cells, r),
        "block_forward",
        6 * 10**9,
        dict(a=Late(first.a), stats=stats0, **forward_ins(0), x=Late(first.x, hold=True), kernels=kernels),
        dict(
            joined=Stream(rows(JOINED, BF16)), zhat=Stream(c_f32), s=Stream(rows(1, F32)), zb=Stream(c_bf),
            g=Stream(h_bf), d=Stream(h_bf), u=Stream(c_f32), a2=Stream(c_f32, step=1), stats2=shape(2, channels),
        ),
        dict(pad=pad, sums=sums, unite=unite_space),
    )
    stats1, *cot_pieces = tie(fwd.stats2, *cot_pieces)
    cot_map = run(
        kernel_whole_map,
        "cotangent_map",
        10**7,
        dict(tile=tile_arg, **{f"p{k}": cot_pieces[k] for k in range(4)}),
        dict(out=Stream(c_bf)),
        dict(field=map4),
    ).out
    stats1 = total_moments(stats1, float(local_cells))

    turn = run(
        lambda r: kernel_turn(cells, r),
        "block_turn",
        14 * 10**9,
        dict(
            index=index_arg, a=Late(fwd.a2), stats=stats1, u=Late(fwd.u, hold=True), do_in=Late(cot_map, hold=True),
            **forward_ins(1), taps=taps,
        ),
        dict(
            features=Stream(c_bf), dm=Stream(c_f32), dn=Stream(c_f32, step=1), small_out=shape(SMALL_ROWS, channels),
            mine=Place(half), sent=Place(half),
        ),
        dict(
            joined=vmem(rows(JOINED, BF16)), zb=vmem(c_bf), df=vmem(c_bf), dpw=vmem(c_bf), dph=vmem(c_bf),
            out=vmem(c_f32), zhat=vmem(c_f32), s=vmem(rows(1, F32)), dz=vmem(c_f32), small=small, upsum=upsum, buf=buf, unite=unite_space,
        ),
    )
    cut = run(
        kernel_pieces,
        "feature_pieces",
        10**7,
        dict(tile=tile_arg, field=turn.features),
        {f"p{k}": piece for k in range(4)},
        tight=True,
    )
    features = [cut.p0, cut.p1, cut.p2, cut.p3]

    near = masks(GROUPS[0])[0]
    got = flat_partner(turn.sent, near)
    first_stage, *later_stages = stages()
    total1 = sum_stage(turn.small_out, first_stage)
    total1, mine1, got = tie(total1, turn.mine, got)
    part1 = narrow_add([mine1, got])
    got1 = scatter_sends(part1, GROUPS[1])
    for stage in later_stages:
        total1 = sum_stage(total1, stage)
    total1, part1, *rest = tie(total1, part1[: part1.shape[0] // 4], *got1, *features)
    got1, features = rest[:3], rest[3:]
    part1 = narrow_add([part1, *got1])
    far = far_masks()
    got1 = flat_partner(part1, far[0])
    mid = run(
        lambda r: kernel_conv_middle(cells, r),
        "conv_middle",
        2 * 10**9,
        dict(**{key: Late(value, step=2, hold=True) for key, value in dict(a=fwd.a2, dn=turn.dn, x=fwd.u, dm=turn.dm).items()}, stats=stats1, totals=total1, kernels=kernels, batch_gain=batch_gain),
        dict(do=Stream(c_bf, step=2), du=Stream(c_f32, step=2), kgrad=shape(16, channels)),
        dict(padx=pad, padd=pad, ksum=ksum),
    )
    do, part1, got1, *features = tie(mid.do, part1, got1, *features)
    part1 = narrow_add([part1, got1])
    got1 = flat_partner(part1, far[1])
    features = swap_pieces(features)
    back = run(
        lambda r: kernel_back(cells, r),
        "block_back",
        14 * 10**9,
        dict(
            index=index_arg,
            **{
                key: Late(value, layer, hold=True)
                for key, (value, layer) in dict(
                    down=(down_t, 0), do_in=(do, None), du=(mid.du, None), up=(up_weight, 0), d=(fwd.d, None), zb=(fwd.zb, None), g=(fwd.g, None), unite_t=(unite_t, 0),
                    zhat=(fwd.zhat, None), s=(fwd.s, None), joined=(fwd.joined, None), a=(first.a, None), x=(first.x, None),
                ).items()
            },
            kgrad=mid.kgrad, norm_gain=norm_gain, stats=stats0, mix_width=mix_width, mix_height=mix_height,
        ),
        dict(dm=Stream(c_f32), dn=Stream(c_f32, step=1), small_out=shape(SMALL_ROWS, channels), mine=Place(half), sent=Place(half)),
        dict(df=vmem(c_bf), dpw=vmem(c_bf), dph=vmem(c_bf), dz=vmem(c_f32), small=small, upsum=upsum, buf=buf, unite=unite_space, pad=pad, taps=ksum),
    )
    small0, mine0, sent0, part1, got1, *features = tie(back.small_out, back.mine, back.sent, part1, got1, *features)
    part1 = narrow_add([part1, got1])
    for mask in far[2:]:
        part1 = add_partner(part1, mask)
    got = flat_partner(sent0, near)
    total0 = sum_stage(small0, first_stage)
    total0, mine0, got = tie(total0, mine0, got)
    part0 = narrow_add([mine0, got])
    got0 = scatter_sends(part0, GROUPS[1])
    for stage in later_stages[:-1]:
        total0 = sum_stage(total0, stage)
    total0, part1 = tie(total0, part1)
    x_mask, y_mask, _ = masks(GROUPS[1])
    got1 = [flat_partner(part1, y_mask), flat_partner(part1, x_mask)]
    total0 = sum_stage(total0, later_stages[-1])
    total0, part0, *got0 = tie(total0, part0[: part0.shape[0] // 4], *got0)
    part0 = narrow_add([part0, *got0])
    halves0 = [part0[: QUAD // 2], part0[QUAD // 2 :]]
    got0 = [flat_partner(halves0[0], far[0]), flat_partner(halves0[1], far[1])]
    last = run(
        lambda r: kernel_last(cells, r),
        "conv_last",
        2 * 10**9,
        dict(tile=tile_arg, **{key: Late(value, step=2, hold=True) for key, value in dict(a=first.a, dn=back.dn, dm=back.dm).items()}, stats=stats0, totals=total0, kernels=kernels, batch_gain=batch_gain),
        {f"o{k}": piece for k in range(4)},
        dict(padd=pad, du=map4),
    )
    o3, *rest = tie(last.o3, *halves0, *got0, part1, *got1)
    halves0, got0, (part1, from_y, from_x) = rest[:2], rest[2:4], rest[4:]
    parts1 = [part1, from_x, from_y, flat_partner(from_y, x_mask)]
    grads = swap_pieces([last.o0, last.o1, last.o2, o3])
    halves0 = [narrow_add([half0, got]) for half0, got in zip(halves0, got0)]
    got0 = [flat_partner(halves0[0], far[1]), flat_partner(halves0[1], far[0])]
    rest = tie(*halves0, *got0, *grads, *parts1)
    part0 = jnp.concatenate([narrow_add([half0, got]) for half0, got in zip(rest[:2], rest[2:4])], 0)
    for mask in far[2:]:
        part0 = add_partner(part0, mask)
    grads, parts1 = rest[4:8], rest[8:]
    got0 = [flat_partner(part0, mask) for mask in masks(GROUPS[1])]
    far1 = [flat_partner(part, near) for part in parts1]
    features_out = join_pieces(features, tile)
    grads = join_pieces(grads, tile)
    grad_shapes = dict(up=shape(2, channels, hidden), down=shape(2, channels, hidden), unite=shape(2, channels, 3 * channels))
    whole = run(
        kernel_unpack,
        "unpack_1",
        10**7,
        dict(index=index_arg, near=LateJoin(parts1), far=LateJoin(far1)),
        {key: Stream(value, 1) for key, value in grad_shapes.items()},
        tight=True,
    )
    line = shape(2, channels)
    fin = run(
        lambda r: kernel_finish(cells, r),
        "finish",
        10**6,
        dict(total0=total0, total1=total1, stats=stats0, gain=batch_gain),
        dict(
            batch_shift=line, batch_gain=line, norm_gain=line, norm_shift=line, down_bias=line, unite_bias=line, up_bias=shape(2, hidden),
            kernel=shape(3, 3, 2, channels), mix_width=shape(MAP, 2, MAP), mix_height=shape(MAP, 2, MAP), mix_width_bias=shape(2, MAP), mix_height_bias=shape(2, MAP),
        ),
    )
    whole_1 = (whole.up, whole.down, whole.unite)
    small_results = [getattr(fin, key) for key in FINISHED]
    grads, features_out, *rest = tie(grads, features_out, part0, *got0, *whole_1, *small_results)
    parts0, whole_1, small_results = rest[:4], rest[4:7], rest[7:]
    for key, value in zip(FINISHED, small_results):
        setattr(fin, key, value)
    far0 = [flat_partner(part, near) for part in parts0]
    whole = run(
        kernel_unpack,
        "unpack_0",
        10**7,
        dict(index=index_arg, near=LateJoin(parts0), far=LateJoin(far0), up_in=Kept(whole_1[0]), down_in=Kept(whole_1[1]), unite_in=Kept(whole_1[2])),
        {key: Stream(value, 0) for key, value in grad_shapes.items()},
        aliases={9: 0, 10: 1, 11: 2},
        tight=True,
    )

    def to_output(field):
        return field.transpose(2, 0, 1, 3)[:, None]

    return (
        to_output(features_out),
        to_output(grads),
        fin.kernel.transpose(2, 0, 1, 3),
        fin.batch_gain,
        fin.batch_shift,
        fin.mix_width.transpose(1, 0, 2),
        fin.mix_width_bias,
        fin.mix_height.transpose(1, 0, 2),
        fin.mix_height_bias,
        whole.unite.transpose(0, 2, 1),
        fin.unite_bias,
        fin.norm_gain,
        fin.norm_shift,
        whole.up,
        fin.up_bias,
        whole.down.transpose(0, 2, 1),
        fin.down_bias,
    )


def solution(mesh):
    field = P("dp", "tile", None, None, None)
    return jax.shard_map(
        on_device,
        mesh=mesh,
        in_specs=(field,) + (P(),) * 15 + (field,),
        out_specs=(field, field) + (P(),) * 15,
        check_vma=False,
    )
```
